32 devices in a mesh: dp: 16 (over z, y, core), blk: 2 (over x).
Axes of the slice: x: 2, y: 2, z: 4, core: 2. Of those that a mesh axis runs over, the one named last changes fastest.
Arguments:
- tokens: bfloat16 [48, 1024, 768], P('dp', 'blk'), may hold values from -6 to 6
- query_weight: bfloat16 [768, 768], replicated, may hold values from -0.21875 to 0.21875
- query_bias: bfloat16 [768], replicated, may hold values from -3 to 3
- key_weight: bfloat16 [768, 768], replicated, may hold values from -0.21875 to 0.21875
- value_weight: bfloat16 [768, 768], replicated, may hold values from -0.21875 to 0.21875
- value_bias: bfloat16 [768], replicated, may hold values from -3 to 3
- out_weight: bfloat16 [768, 768], replicated, may hold values from -1.75 to 1.75
- out_bias: bfloat16 [768], replicated, may hold values from -3 to 3
- gain_one: bfloat16 [768], replicated, may hold values from 0.099609375 to 1.8984375
- shift_one: bfloat16 [768], replicated, may hold values from -3 to 3
- up_weight: bfloat16 [768, 3072], replicated, may hold values from -0.21875 to 0.21875
- up_bias: bfloat16 [3072], replicated, may hold values from -3 to 3
- down_weight: bfloat16 [3072, 768], replicated, may hold values from -0.109375 to 0.109375
- down_bias: bfloat16 [768], replicated, may hold values from -3 to 3
- gain_two: bfloat16 [768], replicated, may hold values from 0.099609375 to 1.8984375
- shift_two: bfloat16 [768], replicated, may hold values from -3 to 3
- group_ids: int32 [48, 1024], P('dp', 'blk'), may hold values from 0 to 4, as said below
- valid_mask: int32 [48, 1024], P('dp', 'blk'), may hold values from 0 to 1, as said below
- cotangent: bfloat16 [48, 1024, 768], P('dp', 'blk'), may hold values from -6 to 6
Outputs:
- block_out: bfloat16 [48, 1024, 768], P('dp', 'blk')
- tokens_gradient: bfloat16 [48, 1024, 768], P('dp', 'blk')
- query_weight_gradient: float32 [768, 768], P(('dp', 'blk'))
- query_bias_gradient: float32 [768], P(('dp', 'blk'))
- key_weight_gradient: float32 [768, 768], P(('dp', 'blk'))
- value_weight_gradient: float32 [768, 768], P(('dp', 'blk'))
- value_bias_gradient: float32 [768], P(('dp', 'blk'))
- out_weight_gradient: float32 [768, 768], P(('dp', 'blk'))
- out_bias_gradient: float32 [768], P(('dp', 'blk'))
- gain_one_gradient: float32 [768], P(('dp', 'blk'))
- shift_one_gradient: float32 [768], P(('dp', 'blk'))
- up_weight_gradient: float32 [768, 3072], P(('dp', 'blk'))
- up_bias_gradient: float32 [3072], P(('dp', 'blk'))
- down_weight_gradient: float32 [3072, 768], P(('dp', 'blk'))
- down_bias_gradient: float32 [768], P(('dp', 'blk'))
- gain_two_gradient: float32 [768], P(('dp', 'blk'))
- shift_two_gradient: float32 [768], P(('dp', 'blk'))
The draws below stay inside these ranges and needn't reach their ends.
Inputs may be any that keep to these rules, and one draw needn't show every extreme that they name: `group_ids`: group numbers never fall along a sequence and every group has a used slot. In each aligned block of 3 sequences one sequence, drawn from the seed, is group 0 in all its slots; the others have 5 groups. `valid_mask`: the unused slots of a group are its last ones.
All inputs are finite; a program needn't handle non-finite values.
Results may differ from the reference program's by a relative error of at most 0.02.
Values may be sent and summed in bfloat16 or wider, within the bound.
A program may use at most 320 MiB of HBM per device.

```python
import jax
import jax.numpy as jnp
from jax import lax

D = 768
HEAD = 64
FF = 3072
CAPTIONS = 5
LEN = 1024
SEQ_GRP = 3
SEQS = 48


def slot_layout(key):
    share_key, tail_key, pick_key = jax.random.split(key, 3)
    shares = jax.random.randint(share_key, (SEQS, CAPTIONS), 2, 7, dtype=jnp.int32)
    bounds = LEN * jnp.cumsum(shares, axis=1) // jnp.sum(shares, axis=1, keepdims=True)
    starts = jnp.concatenate([jnp.zeros((SEQS, 1), jnp.int32), bounds[:, :-1]], axis=1)
    slots = jnp.arange(LEN, dtype=jnp.int32)
    groups = jnp.sum((slots[None, :, None] >= bounds[:, None, :-1]).astype(jnp.int32), axis=2)
    eighths = jax.random.randint(tail_key, (SEQS, CAPTIONS), 0, 3, dtype=jnp.int32)
    finish = bounds - (bounds - starts) * eighths // 8
    chosen = jax.random.randint(pick_key, (SEQS // SEQ_GRP, 1), 0, SEQ_GRP, dtype=jnp.int32)
    single = (jnp.arange(SEQ_GRP, dtype=jnp.int32)[None, :] == chosen).reshape(SEQS)
    groups = jnp.where(single[:, None], 0, groups)
    onehot = (groups[:, :, None] == jnp.arange(CAPTIONS, dtype=jnp.int32)[None, None, :]).astype(jnp.int32)
    slot_end = jnp.sum(onehot * finish[:, None, :], axis=2)
    single_end = LEN - LEN * eighths[:, :1] // 8
    slot_end = jnp.where(single[:, None], single_end, slot_end)
    usable = (slots[None, :] < slot_end).astype(jnp.int32)
    return (groups.astype(jnp.int32), usable)


def draw_group_ids(key, part):
    groups, usable = slot_layout(key)
    return groups


def draw_valid_mask(key, part):
    groups, usable = slot_layout(key)
    return usable


def levels(own_key, dims, pieces, low, largest):
    def one(position, shards_of):
        heights = jax.random.uniform(jax.random.fold_in(jax.random.fold_in(own_key, 6), position), (shards_of,), jnp.float32, low / len(pieces), largest / len(pieces))
        return jnp.repeat(jnp.exp(heights), dims[position] // shards_of).reshape((-1,) + (1,) * (len(dims) - position - 1))

    factor_of = one(*pieces[0])
    for cut in pieces[1:]:
        factor_of = factor_of * one(*cut)
    return factor_of


def bell_draw(rng, dims, deviation, most, shards=(), held_as=jnp.bfloat16):
    level = levels(rng, dims, shards, -0.22, 0.18) if shards else 1.0
    values = jax.random.normal(rng, dims, jnp.float32) * deviation * level
    return jnp.minimum(jnp.maximum(values, -most), most).astype(held_as)


def setup_inputs(seed: int = 0) -> dict:
    arg_keys = jax.random.split(jax.random.key(seed), 20)
    return {
        "tokens": bell_draw(arg_keys[0], (SEQS, LEN, D), 1.0, 6.0, ((0, 16), (1, 2))),
        "query_weight": bell_draw(arg_keys[1], (D, D), D ** -0.5, 0.21875),
        "query_bias": bell_draw(arg_keys[2], (D,), 0.5, 3.0),
        "key_weight": bell_draw(arg_keys[3], (D, D), D ** -0.5, 0.21875),
        "value_weight": bell_draw(arg_keys[4], (D, D), D ** -0.5, 0.21875),
        "value_bias": bell_draw(arg_keys[5], (D,), 0.5, 3.0),
        "out_weight": bell_draw(arg_keys[6], (D, D), (D // 64) ** -0.5, 1.75),
        "out_bias": bell_draw(arg_keys[7], (D,), 0.5, 3.0),
        "gain_one": jnp.clip(1.0 + 0.18 * jax.random.normal(arg_keys[8], (D,), jnp.float32), 0.099609375, 1.8984375).astype(jnp.bfloat16),
        "shift_one": bell_draw(arg_keys[9], (D,), 0.5, 3.0),
        "up_weight": bell_draw(arg_keys[10], (D, FF), D ** -0.5, 0.21875),
        "up_bias": bell_draw(arg_keys[11], (FF,), 0.5, 3.0),
        "down_weight": bell_draw(arg_keys[12], (FF, D), FF ** -0.5, 0.109375),
        "down_bias": bell_draw(arg_keys[13], (D,), 0.5, 3.0),
        "gain_two": jnp.clip(1.0 + 0.18 * jax.random.normal(arg_keys[14], (D,), jnp.float32), 0.099609375, 1.8984375).astype(jnp.bfloat16),
        "shift_two": bell_draw(arg_keys[15], (D,), 0.5, 3.0),
        "group_ids": draw_group_ids(jax.random.fold_in(arg_keys[19], 71), 0),
        "valid_mask": draw_valid_mask(jax.random.fold_in(arg_keys[19], 71), 0),
        "cotangent": bell_draw(arg_keys[18], (SEQS, LEN, D), 1.0, 6.0, ((0, 16), (1, 2))),
    }


@jax.custom_vjp
def low(v):
    return lax.optimization_barrier(v.astype(jnp.bfloat16)).astype(jnp.float32)

@jax.custom_vjp
def low_back(v):
    return v

def low_keep(v):
    return (low(v), None)

def low_pass(kept, grad):
    return (grad,)

def back_keep(v):
    return (v, None)

def back_low(kept, grad):
    return (low(grad),)
low.defvjp(low_keep, low_pass)
low_back.defvjp(back_keep, back_low)
highest = lax.Precision.HIGHEST
epsilon = 1e-12
masked = -1e+30

def matmul(left, right):
    return jnp.dot(left, right, precision=highest, preferred_element_type=jnp.float32)

def layer_norm(values, gain, shift):
    centred = values - lax.optimization_barrier(jnp.mean(values, axis=-1, keepdims=True))
    spread = lax.optimization_barrier(jnp.mean(centred * centred, axis=-1, keepdims=True))
    return centred * lax.rsqrt(spread + epsilon) * gain + shift

def forward(inputs, params, groups, usable):
    query_weight, query_bias, key_weight, value_weight, value_bias, out_weight, out_bias, gain_one, shift_one, up_weight, up_bias, down_weight, down_bias, gain_two, shift_two = params
    sequences, length, features = inputs.shape
    head_shape = (sequences, length, features // HEAD, HEAD)
    flattened = inputs.reshape(-1, features)
    queries = low_back(low(matmul(flattened, query_weight) + query_bias))
    keys_all = low_back(low(matmul(flattened, key_weight)))
    values_all = low_back(low(matmul(flattened, value_weight) + value_bias))
    logits = jnp.einsum('sqhd,skhd->shqk', queries.reshape(head_shape), keys_all.reshape(head_shape), precision=highest)
    logits = low_back(logits * 0.125)
    allowed = (groups[:, :, None] == groups[:, None, :]) & (usable[:, None, :] == 1)
    logits = jnp.where(allowed[:, None], logits, masked)
    probs = low(jax.nn.softmax(logits, axis=-1))
    attended = jnp.einsum('shqk,skhd->sqhd', probs, values_all.reshape(head_shape), precision=highest)
    attended = low_back(low(attended.reshape(-1, features)))
    branch = low_back(matmul(attended, out_weight) + out_bias)
    first = layer_norm(flattened + branch, gain_one, shift_one)
    inner = low_back(matmul(low(first), up_weight) + up_bias)
    active = low(jax.nn.gelu(inner, approximate=False))
    feed = low_back(matmul(active, down_weight) + down_bias)
    return layer_norm(first + feed, gain_two, shift_two).reshape(inputs.shape)

def reference(tokens, query_weight, query_bias, key_weight, value_weight, value_bias, out_weight, out_bias, gain_one, shift_one, up_weight, up_bias, down_weight, down_bias, gain_two, shift_two, group_ids, valid_mask, cotangent):
    params = tuple((member.astype(jnp.float32) for member in (query_weight, query_bias, key_weight, value_weight, value_bias, out_weight, out_bias, gain_one, shift_one, up_weight, up_bias, down_weight, down_bias, gain_two, shift_two)))
    pair_count = tokens.shape[0] // 2
    inputs = tokens.astype(jnp.float32).reshape(pair_count, 2, LEN, D)
    groups = group_ids.reshape(pair_count, 2, LEN)
    usable = valid_mask.reshape(pair_count, 2, LEN)
    cotangents = cotangent.astype(jnp.float32).reshape(pair_count, 2, LEN, D)

    def advance(running, sample):
        inputs_now, groups_now, usable_now, cotangent_now = sample

        def closed(values, weights):
            return forward(values, weights, groups_now, usable_now)
        result, pullback = jax.vjp(closed, inputs_now, params)
        input_gradient, weight_gradients = pullback(cotangent_now)
        running = tuple((earlier + addition for earlier, addition in zip(running, weight_gradients)))
        return (running, (result.astype(jnp.bfloat16), input_gradient.astype(jnp.bfloat16)))
    starting = tuple((jnp.zeros_like(member) for member in params))
    sums, (outputs, input_gradients) = lax.scan(advance, starting, (inputs, groups, usable, cotangents))
    return (outputs.reshape(tokens.shape), input_gradients.reshape(tokens.shape), sums[0], sums[1], sums[2], sums[3], sums[4], sums[5], sums[6], sums[7], sums[8], sums[9], sums[10], sums[11], sums[12], sums[13], sums[14])
```

```python
import functools
import math

import jax
import jax.numpy as jnp
from jax import lax
from jax.experimental import pallas as pl
from jax.experimental.pallas import tpu as pltpu
from jax.sharding import PartitionSpec as P

HEAD = 64
PAIR = 2 * HEAD
EPSILON = 1e-12
MASKED = -1e30
FLOOR = -3e38
SCALE = HEAD**-0.5
EXPO = SCALE * math.log2(math.e)
NN = (((1,), (0,)), ((), ()))
NT = (((1,), (1,)), ((), ()))
F32 = jnp.float32
BF16 = jnp.bfloat16
MIB = 1 << 20


def dot(left, right, dims=NN):
    return lax.dot_general(left, right, dims, preferred_element_type=F32)


def whole_spec(shape):
    return pl.BlockSpec(shape, lambda *_: (0,) * len(shape), pipeline_mode=pl.Buffered(1))


def params(limit):
    return pltpu.CompilerParams(vmem_limit_bytes=limit * MIB)


def cost(flops, touched, exps=0):
    return pl.CostEstimate(flops=int(flops), bytes_accessed=int(touched), transcendentals=int(exps))


def project_kernel(has_query, *refs):
    if has_query:
        x_ref, bias_ref, wq_ref, wk_ref, wv_ref, q_ref, k_ref, v_ref = refs
    else:
        x_ref, bias_ref, wk_ref, wv_ref, k_ref, v_ref = refs
    x = x_ref[0]
    if has_query:
        q_ref[0] = (dot(x, wq_ref[...]) + bias_ref[0:1]).astype(BF16)
    k_ref[0] = dot(x, wk_ref[...]).astype(BF16)
    v_ref[0] = (dot(x, wv_ref[...]) + bias_ref[1:2]).astype(BF16)


def project(x, bias, weights):
    seqs, length, features = x.shape
    tile = math.gcd(length, 512)
    grid = (seqs, length // tile)
    row_spec = pl.BlockSpec((1, tile, features), lambda s, i: (s, i, 0))
    return pl.pallas_call(
        functools.partial(project_kernel, len(weights) == 3),
        grid=grid,
        in_specs=[row_spec, whole_spec(bias.shape)] + [whole_spec(w.shape) for w in weights],
        out_specs=[row_spec] * len(weights),
        out_shape=[jax.ShapeDtypeStruct(x.shape, BF16)] * len(weights),
        compiler_params=params(40),
        cost_estimate=cost(
            2 * x.size * features * len(weights), 2 * x.size * (1 + len(weights))
        ),
        name="project",
    )(x, bias, *weights)


def sides(q_block, qm_block, k_block, km_block, head):
    lane = lax.broadcasted_iota(jnp.int32, (1, PAIR), 1)
    mine = (lane >= HEAD) if head else (lane < HEAD)
    return (
        mine,
        jnp.where(mine, q_block, qm_block),
        jnp.where(mine, k_block, km_block),
    )


def key_chunks(parts, chunk):
    found, start = [], 0
    for part, length in enumerate(parts):
        for row in range(0, length, chunk):
            found.append((part, row, start + row))
        start += length
    return found


def attend_kernel(sizes, active_ref, q_ref, qm_ref, ko_ref, kmo_ref, vo_ref, kr_ref, kmr_ref, vr_ref,
                  o_ref, lse_ref, top_ref, sum_ref):
    query_chunk, key_chunk = sizes
    s = pl.program_id(0)
    parts = ((ko_ref, kmo_ref, vo_ref), (kr_ref, kmr_ref, vr_ref))
    chunks = key_chunks([p[0].shape[1] for p in parts], key_chunk)
    for qb in range(q_ref.shape[1] // query_chunk):
        rows = pl.ds(qb * query_chunk, query_chunk)
        top_ref[...] = jnp.full_like(top_ref, FLOOR)
        sum_ref[...] = jnp.zeros_like(sum_ref)
        for c, (part, row, _) in enumerate(chunks):
            k_ref, km_ref, v_ref = parts[part]
            cols = pl.ds(row, key_chunk)

            @pl.when(active_ref[s, qb * len(chunks) + c] != 0)
            def _(k_ref=k_ref, km_ref=km_ref, v_ref=v_ref, cols=cols):
                q, qm = q_ref[0, rows], qm_ref[0, rows]
                k, km = k_ref[0, cols], km_ref[0, cols]
                v_t = v_ref[0, cols].T
                ones = jnp.ones((16, key_chunk), BF16)
                for head in range(2):
                    mine, q_side, k_side = sides(q, qm, k, km, head)
                    scores = dot(k_side, q_side, NT)
                    before = top_ref[head : head + 1]
                    top = jnp.maximum(before, jnp.max(scores, axis=0, keepdims=True))
                    weights = jnp.exp2((scores - top) * EXPO)
                    fading = jnp.exp2((before - top) * EXPO)
                    v_side = jnp.concatenate([v_t[head * HEAD : (head + 1) * HEAD], ones], axis=0)
                    sum_ref[head] = sum_ref[head] * fading + dot(v_side, weights.astype(BF16))
                    top_ref[head : head + 1] = top

        outs = []
        for head in range(2):
            total = sum_ref[head, HEAD : HEAD + 1]
            outs.append(sum_ref[head, :HEAD] / total)
            lse_ref[0, 0, head : head + 1, rows] = top_ref[head : head + 1] * EXPO + jnp.log2(total)
        o_ref[0, rows] = jnp.concatenate(outs, axis=0).T.astype(BF16)


def pair_spec(length):
    return pl.BlockSpec((1, length, PAIR), lambda s, h, *_: (s, 0, h))


def mask_spec(length):
    return pl.BlockSpec((1, length, PAIR), lambda s, h, *_: (s, 0, 0))


def attend(active, sizes, q, qm, own, rem):
    seqs, length, features = q.shape
    pairs = features // PAIR
    other = rem[0].shape[1]
    lse_spec = pl.BlockSpec((1, 1, 8, length), lambda s, h, *_: (s, h, 0, 0))
    return pl.pallas_call(
        functools.partial(attend_kernel, sizes),
        grid_spec=pltpu.PrefetchScalarGridSpec(
            num_scalar_prefetch=1,
            grid=(seqs, pairs),
            in_specs=[
                pair_spec(length),
                mask_spec(length),
                pair_spec(length),
                mask_spec(length),
                pair_spec(length),
                pair_spec(other),
                mask_spec(other),
                pair_spec(other),
            ],
            out_specs=[pair_spec(length), lse_spec],
            scratch_shapes=[
                pltpu.VMEM((8, sizes[0]), F32),
                pltpu.VMEM((2, HEAD + 16, sizes[0]), F32),
            ],
        ),
        out_shape=[
            jax.ShapeDtypeStruct(q.shape, BF16),
            jax.ShapeDtypeStruct((seqs, pairs, 8, length), F32),
        ],
        compiler_params=params(40),
        cost_estimate=cost(
            16 * q.size * (length + other), 2 * q.size * 6, q.size * (length + other) // HEAD
        ),
        name="attend",
    )(active, q, qm, *own, *rem)


def attend_back_kernel(sizes, active_ref, q_ref, qm_ref, o_ref, g_ref, lse_ref, ko_ref, kmo_ref, vo_ref,
                       kr_ref, kmr_ref, vr_ref, dq_ref, dko_ref, dvo_ref, dkr_ref, dvr_ref,
                       dq_sum, dk_sum, dv_sum):
    query_chunk, key_chunk = sizes
    s = pl.program_id(0)
    parts = ((ko_ref, kmo_ref, vo_ref), (kr_ref, kmr_ref, vr_ref))
    chunks = key_chunks([p[0].shape[1] for p in parts], key_chunk)
    dq_sum[...] = jnp.zeros_like(dq_sum)
    dk_sum[...] = jnp.zeros_like(dk_sum)
    dv_sum[...] = jnp.zeros_like(dv_sum)
    lane = lax.broadcasted_iota(jnp.int32, (8, PAIR), 1)
    for qb in range(q_ref.shape[1] // query_chunk):
        rows = pl.ds(qb * query_chunk, query_chunk)
        product = g_ref[0, rows].astype(F32) * o_ref[0, rows].astype(F32)
        deltas = [
            lax.dot_general(
                jnp.where((lane >= HEAD) == bool(head), 1.0, 0.0).astype(F32),
                product,
                NT,
                precision=lax.Precision.HIGHEST,
                preferred_element_type=F32,
            )[0:1]
            for head in range(2)
        ]
        for c, (part, row, start) in enumerate(chunks):
            k_ref, km_ref, v_ref = parts[part]
            cols = pl.ds(row, key_chunk)
            into = pl.ds(start, key_chunk)

            @pl.when(active_ref[s, qb * len(chunks) + c] != 0)
            def _(k_ref=k_ref, km_ref=km_ref, v_ref=v_ref, cols=cols, into=into):
                q, qm, g = q_ref[0, rows], qm_ref[0, rows], g_ref[0, rows]
                k, km, v = k_ref[0, cols], km_ref[0, cols], v_ref[0, cols]
                k_t = k.T
                none = jnp.zeros_like(q)
                dk = dk_sum[into]
                dv = dv_sum[into]
                for head in range(2):
                    mine, q_side, k_side = sides(q, qm, k, km, head)
                    scores = dot(k_side, q_side, NT)
                    probs = jnp.exp2(scores * EXPO - lse_ref[0, 0, head : head + 1, rows])
                    v_side = jnp.where(mine, v, jnp.zeros_like(v))
                    grads = probs * (dot(v_side, g, NT) - deltas[head])
                    grads = grads.astype(BF16)
                    dv += dot(probs.astype(BF16), jnp.where(mine, g, none))
                    dk += dot(grads, jnp.where(mine, q, none))
                    span = slice(head * HEAD, (head + 1) * HEAD)
                    dq_sum[span, rows] += dot(k_t[span], grads)
                dk_sum[into] = dk
                dv_sum[into] = dv

    dq_ref[0] = (dq_sum[...] * SCALE).T.astype(BF16)
    mid = dko_ref.shape[1]
    dko_ref[0] = (dk_sum[:mid] * SCALE).astype(BF16)
    dkr_ref[0] = (dk_sum[mid:] * SCALE).astype(BF16)
    dvo_ref[0] = dv_sum[:mid].astype(BF16)
    dvr_ref[0] = dv_sum[mid:].astype(BF16)


def attend_back(active, sizes, q, qm, o, g, lse, own, rem):
    seqs, length, features = q.shape
    pairs = features // PAIR
    other = rem[0].shape[1]
    lse_spec = pl.BlockSpec((1, 1, 8, length), lambda s, h, *_: (s, h, 0, 0))
    return pl.pallas_call(
        functools.partial(attend_back_kernel, sizes),
        grid_spec=pltpu.PrefetchScalarGridSpec(
            num_scalar_prefetch=1,
            grid=(seqs, pairs),
            in_specs=[
                pair_spec(length),
                mask_spec(length),
                pair_spec(length),
                pair_spec(length),
                lse_spec,
                pair_spec(length),
                mask_spec(length),
                pair_spec(length),
                pair_spec(other),
                mask_spec(other),
                pair_spec(other),
            ],
            out_specs=[pair_spec(length)] * 3 + [pair_spec(other)] * 2,
            scratch_shapes=[
                pltpu.VMEM((PAIR, length), F32),
                pltpu.VMEM((length + other, PAIR), F32),
                pltpu.VMEM((length + other, PAIR), F32),
            ],
        ),
        out_shape=[jax.ShapeDtypeStruct(q.shape, BF16)] * 3
        + [jax.ShapeDtypeStruct(rem[0].shape, BF16)] * 2,
        compiler_params=params(40),
        cost_estimate=cost(
            40 * q.size * (length + other), 2 * q.size * 14, q.size * (length + other) // HEAD
        ),
        name="attend_back",
    )(active, q, qm, o, g, lse, *own, *rem)


def gelu_and_slope(x):
    bell = jnp.exp2(x * x * (-0.5 * math.log2(math.e)))
    t = 1.0 / (1.0 + (0.3275911 / math.sqrt(2.0)) * jnp.abs(x))
    poly = 1.061405429 * t - 1.453152027
    poly = poly * t + 1.421413741
    poly = poly * t - 0.284496736
    poly = poly * t + 0.254829592
    tail = (0.5 * poly) * t * bell
    share = jnp.where(x >= 0.0, 1.0 - tail, tail)
    return x * share, share + x * bell * (1.0 / math.sqrt(2.0 * math.pi))


def mean(values):
    return jnp.sum(values, axis=-1, keepdims=True) * (1.0 / values.shape[-1])


def norm_parts(values):
    centred = values - mean(values)
    scale = lax.rsqrt(mean(centred * centred) + EPSILON)
    return centred * scale, scale


def norm_back(upper, normed, scale):
    return scale * (upper - mean(upper) - normed * mean(upper * normed))


def column_sum(values):
    return jnp.sum(values, axis=0, keepdims=True)


def feed_kernel(layout, tok_ref, att_ref, cot_ref, vec_ref, bu_ref, wo_ref, wu_ref, wd_ref,
                out_ref, bg_ref, ag_ref, vg_ref, dbu_ref, dwu_ref, dwd_ref, dwo_ref,
                act_s, din_s, slope_s, first_t, feed_t, att_t, bg_s):
    tiles, ff_steps, out_steps, chunk = layout
    step = pl.program_id(0)
    tile = tok_ref.shape[0]
    hidden = act_s.shape[1]
    vec = [vec_ref[i : i + 1] for i in range(6)]
    out_bias, gain_one, shift_one, down_bias, gain_two, shift_two = vec

    @pl.when(step == 0)
    def _():
        vg_ref[...] = jnp.zeros_like(vg_ref)
        dbu_ref[...] = jnp.zeros_like(dbu_ref)

    @pl.when(step < tiles)
    def _():
        start = pl.multiple_of(step * tile, tile)
        rows = pl.ds(start, tile)
        att = att_ref[...]
        normed_one, scale_one = norm_parts(
            tok_ref[...].astype(F32) + (dot(att, wo_ref[...]) + out_bias)
        )
        first = normed_one * gain_one + shift_one
        first_low = first.astype(BF16)
        first_t[:, rows] = first_low.T
        att_t[:, rows] = att.T
        feed = jnp.zeros_like(first) + down_bias
        for c in range(0, hidden, chunk):
            cols = slice(c, c + chunk)
            active, slope = gelu_and_slope(dot(first_low, wu_ref[:, cols]) + bu_ref[:, cols])
            active = active.astype(BF16)
            act_s[rows, cols] = active
            slope_s[:, cols] = slope
            feed += dot(active, wd_ref[cols])
        normed_two, scale_two = norm_parts(first + feed)
        out_ref[...] = (normed_two * gain_two + shift_two).astype(BF16)
        cot = cot_ref[...].astype(F32)
        second = norm_back(cot * gain_two, normed_two, scale_two)
        feed_low = second.astype(BF16)
        feed_t[:, rows] = feed_low.T
        back = second
        for c in range(0, hidden, chunk):
            cols = slice(c, c + chunk)
            inner = (dot(feed_low, wd_ref[cols], NT) * slope_s[:, cols]).astype(BF16)
            din_s[rows, cols] = inner
            dbu_ref[:, cols] += column_sum(inner.astype(F32))
            back += dot(inner, wu_ref[:, cols], NT)
        residual = norm_back(back * gain_one, normed_one, scale_one)
        branch_low = residual.astype(BF16)
        bg_ref[...] = branch_low
        bg_s[rows] = branch_low
        ag_ref[...] = dot(branch_low, wo_ref[...], NT).astype(BF16)
        for i, values in enumerate(
            (
                branch_low.astype(F32),
                back * normed_one,
                back,
                feed_low.astype(F32),
                cot * normed_two,
                cot,
            )
        ):
            vg_ref[i : i + 1] += column_sum(values)

    wide = dwu_ref.shape[1]

    @pl.when((step >= tiles) & (step < tiles + ff_steps))
    def _():
        cols = pl.ds(pl.multiple_of((step - tiles) * wide, wide), wide)
        dwu_ref[...] = dot(first_t[...], din_s[:, cols]).astype(BF16)
        dwd_ref[...] = dot(feed_t[...], act_s[:, cols]).astype(BF16).T

    narrow = dwo_ref.shape[1]

    @pl.when(step >= tiles + ff_steps)
    def _():
        cols = pl.ds(pl.multiple_of((step - tiles - ff_steps) * narrow, narrow), narrow)
        dwo_ref[...] = dot(att_t[...], bg_s[:, cols]).astype(BF16)


def feed_both_ways(tokens, attended, cotangent, vectors, up_bias, wo, wu, wd):
    rows, features = tokens.shape
    hidden = wu.shape[1]
    tile = math.gcd(rows, 256)
    tiles = rows // tile
    wide, narrow = math.gcd(hidden, 512), math.gcd(features, 384)
    ff_steps, out_steps = hidden // wide, features // narrow
    layout = (tiles, ff_steps, out_steps, math.gcd(hidden, 512))
    row_spec = pl.BlockSpec((tile, features), lambda i: (jnp.minimum(i, tiles - 1), 0))

    def ff_at(i):
        return jnp.clip(i - tiles, 0, ff_steps - 1)

    return pl.pallas_call(
        functools.partial(feed_kernel, layout),
        grid=(tiles + ff_steps + out_steps,),
        in_specs=[row_spec] * 3
        + [whole_spec(a.shape) for a in (vectors, up_bias, wo, wu, wd)],
        out_specs=[row_spec] * 3
        + [
            pl.BlockSpec((8, features), lambda i: (0, 0)),
            pl.BlockSpec((1, hidden), lambda i: (0, 0)),
            pl.BlockSpec((features, wide), lambda i: (0, ff_at(i))),
            pl.BlockSpec((wide, features), lambda i: (ff_at(i), 0)),
            pl.BlockSpec(
                (features, narrow),
                lambda i: (0, jnp.clip(i - tiles - ff_steps, 0, out_steps - 1)),
            ),
        ],
        out_shape=[jax.ShapeDtypeStruct(tokens.shape, BF16)] * 3
        + [
            jax.ShapeDtypeStruct((8, features), F32),
            jax.ShapeDtypeStruct((1, hidden), F32),
            jax.ShapeDtypeStruct(wu.shape, BF16),
            jax.ShapeDtypeStruct(wd.shape, BF16),
            jax.ShapeDtypeStruct(wo.shape, BF16),
        ],
        scratch_shapes=[
            pltpu.VMEM((rows, hidden), BF16),
            pltpu.VMEM((rows, hidden), BF16),
            pltpu.VMEM((tile, hidden), F32),
            pltpu.VMEM((features, rows), BF16),
            pltpu.VMEM((features, rows), BF16),
            pltpu.VMEM((features, rows), BF16),
            pltpu.VMEM((rows, features), BF16),
        ],
        compiler_params=params(60),
        cost_estimate=cost(
            6 * rows * features * (features + 2 * hidden),
            2 * (6 * rows * features + 4 * features * hidden + 2 * features * features),
            2 * rows * hidden,
        ),
        name="feed_both_ways",
    )(tokens, attended, cotangent, vectors, up_bias, wo, wu, wd)


def own_back_kernel(bg_ref, dq_ref, dk_ref, dv_ref, wq_ref, wk_ref, wv_ref, out_ref):
    total = bg_ref[0].astype(F32) + dot(dq_ref[0], wq_ref[...], NT)
    total += dot(dk_ref[0], wk_ref[...], NT)
    total += dot(dv_ref[0], wv_ref[...], NT)
    out_ref[0] = total.astype(BF16)


def rem_back_kernel(dk_ref, dv_ref, wk_ref, wv_ref, out_ref):
    total = dot(dk_ref[0], wk_ref[...], NT) + dot(dv_ref[0], wv_ref[...], NT)
    out_ref[0] = total.astype(BF16)


def tokens_back(kernel, rows, weights):
    seqs, length, features = rows[0].shape
    tile = math.gcd(length, 512)
    row_spec = pl.BlockSpec((1, tile, features), lambda s, i: (s, i, 0))
    size = rows[0].size
    return pl.pallas_call(
        kernel,
        grid=(seqs, length // tile),
        in_specs=[row_spec] * len(rows) + [whole_spec(w.shape) for w in weights],
        out_specs=row_spec,
        out_shape=jax.ShapeDtypeStruct(rows[0].shape, BF16),
        compiler_params=params(40),
        cost_estimate=cost(2 * size * features * len(weights), 2 * size * (1 + len(rows))),
        name="tokens_back",
    )(*rows, *weights)


def weights_back_kernel(tok_ref, rem_ref, dq_ref, dko_ref, dvo_ref, dkr_ref, dvr_ref,
                        wq_ref, wk_ref, wv_ref, bq_ref, bv_ref, tok_t, rem_t):
    @pl.when(pl.program_id(0) == 0)
    def _():
        tok_t[...] = tok_ref[...].T
        rem_t[...] = rem_ref[...].T

    wq_ref[...] = dot(tok_t[...], dq_ref[...]).astype(BF16)
    wk_ref[...] = (dot(tok_t[...], dko_ref[...]) + dot(rem_t[...], dkr_ref[...])).astype(BF16)
    wv_ref[...] = (dot(tok_t[...], dvo_ref[...]) + dot(rem_t[...], dvr_ref[...])).astype(BF16)
    bq_ref[...] = column_sum(dq_ref[...].astype(F32))
    bv_ref[...] = column_sum(dvo_ref[...].astype(F32)) + column_sum(dvr_ref[...].astype(F32))


def weights_back(tok, rem, dq, dko, dvo, dkr, dvr):
    rows, features = tok.shape
    others = rem.shape[0]
    wide = math.gcd(features, 256)
    own_spec = pl.BlockSpec((rows, wide), lambda j: (0, j))
    rem_spec = pl.BlockSpec((others, wide), lambda j: (0, j))
    bias_spec = pl.BlockSpec((1, wide), lambda j: (0, j))
    return pl.pallas_call(
        weights_back_kernel,
        grid=(features // wide,),
        in_specs=[
            whole_spec(tok.shape),
            whole_spec(rem.shape),
            own_spec,
            own_spec,
            own_spec,
            rem_spec,
            rem_spec,
        ],
        out_specs=[pl.BlockSpec((features, wide), lambda j: (0, j))] * 3 + [bias_spec] * 2,
        out_shape=[jax.ShapeDtypeStruct((features, features), BF16)] * 3
        + [jax.ShapeDtypeStruct((1, features), F32)] * 2,
        scratch_shapes=[
            pltpu.VMEM((features, rows), BF16),
            pltpu.VMEM((features, others), BF16),
        ],
        compiler_params=params(48),
        cost_estimate=cost(
            2 * features * features * (3 * rows + 2 * others),
            2 * (4 * tok.size + 3 * rem.size + 3 * features * features),
        ),
        name="weights_back",
    )(tok, rem, dq, dko, dvo, dkr, dvr)


def halve(value, axis, bit):
    size = lax.axis_size(axis)
    mine = (lax.axis_index(axis) >> bit) & 1
    pairs = value.reshape((value.shape[0] // 2, 2) + value.shape[1:])
    keep = lax.dynamic_index_in_dim(pairs, mine, 1, keepdims=False)
    send = lax.dynamic_index_in_dim(pairs, 1 - mine, 1, keepdims=False)
    came = lax.ppermute(send, axis, [(i, i ^ (1 << bit)) for i in range(size)])
    return keep.astype(F32) + came.astype(F32)


def scatter_sum(value, low=True):
    dp, blk = lax.axis_size("dp"), lax.axis_size("blk")
    if dp & (dp - 1) or blk & (blk - 1):
        return lax.psum_scatter(
            value.astype(F32), ("dp", "blk"), scatter_dimension=0, tiled=True
        )
    kept = value.dtype
    each = value.shape[0] // (dp * blk)
    value = value.reshape((dp, blk * each) + value.shape[1:])
    for bit in range(dp.bit_length() - 1):
        value = halve(value, "dp", bit).astype(kept)
    value = value.reshape((blk, each) + value.shape[2:])
    for bit in range(blk.bit_length() - 1):
        value = halve(value, "blk", bit)
        value = value if (2 << bit) == blk else value.astype(kept)
    return value.reshape(value.shape[1:]).astype(F32)


def scatter_vectors(vectors):
    shards = lax.axis_size("dp") * lax.axis_size("blk")
    widths = [v.size // shards for v in vectors]
    summed = scatter_sum(jnp.concatenate([v.reshape(shards, -1) for v in vectors], axis=1))
    found, at = [], 0
    for width in widths:
        found.append(summed[0, at : at + width])
        at += width
    return found


def body(
    tokens,
    query_weight,
    query_bias,
    key_weight,
    value_weight,
    value_bias,
    out_weight,
    out_bias,
    gain_one,
    shift_one,
    up_weight,
    up_bias,
    down_weight,
    down_bias,
    gain_two,
    shift_two,
    group_ids,
    valid_mask,
    cotangent,
):
    seqs, length, features = tokens.shape
    rows = seqs * length
    blk = lax.axis_size("blk")

    def from_others(value):
        found = [
            lax.ppermute(value, "blk", [(i, (i + r) % blk) for i in range(blk)])
            for r in range(1, blk)
        ]
        return found[0] if len(found) == 1 else jnp.concatenate(found, axis=1)

    codes = jnp.where(valid_mask == 1, group_ids, -1).astype(BF16)
    rem_tokens = from_others(tokens)
    rem_codes = from_others(codes).astype(jnp.int32)
    own_codes = codes.astype(jnp.int32)

    slot = jnp.arange(PAIR, dtype=jnp.int32) % HEAD

    def key_mask(code):
        return jnp.where(code[:, :, None] == slot, 0.0, MASKED).astype(BF16)

    query_mask = (group_ids[:, :, None] == slot).astype(BF16)
    chunk = math.gcd(length, 256)
    sizes = (chunk, chunk)
    query_groups = group_ids.reshape(seqs, length // chunk, chunk)
    all_codes = jnp.concatenate([own_codes, rem_codes], axis=1)
    all_codes = all_codes.reshape(seqs, -1, chunk)
    lowest = jnp.min(jnp.where(all_codes < 0, HEAD, all_codes), axis=-1)
    highest = jnp.max(all_codes, axis=-1)
    active = (lowest[:, None, :] <= jnp.max(query_groups, axis=-1)[:, :, None]) & (
        highest[:, None, :] >= jnp.min(query_groups, axis=-1)[:, :, None]
    )
    active = active.astype(jnp.int32).reshape(seqs, -1)

    biases = jnp.concatenate(
        [query_bias[None], value_bias[None], jnp.zeros((6, features), BF16)], axis=0
    ).astype(F32)
    queries, own_keys, own_values = project(
        tokens, biases, (query_weight, key_weight, value_weight)
    )
    rem_keys, rem_values = project(rem_tokens, biases, (key_weight, value_weight))
    own = (own_keys, key_mask(own_codes), own_values)
    rem = (rem_keys, key_mask(rem_codes), rem_values)
    attended, lse = attend(active, sizes, queries, query_mask, own, rem)

    vectors = jnp.stack(
        [out_bias, gain_one, shift_one, down_bias, gain_two, shift_two, out_bias, out_bias]
    ).astype(F32)
    block_out, branch_gradient, attended_gradient, vector_gradients, up_bias_gradient, dwu, dwd, dwo = (
        feed_both_ways(
            tokens.reshape(rows, features),
            attended.reshape(rows, features),
            cotangent.reshape(rows, features),
            vectors,
            up_bias.astype(F32)[None],
            out_weight,
            up_weight,
            down_weight,
        )
    )
    dwd, dwu, dwo = scatter_sum(dwd), scatter_sum(dwu), scatter_sum(dwo)

    dq, dko, dvo, dkr, dvr = attend_back(
        active,
        sizes,
        queries,
        query_mask,
        attended,
        attended_gradient.reshape(tokens.shape),
        lse,
        own,
        rem,
    )
    rem_gradient = tokens_back(rem_back_kernel, (dkr, dvr), (key_weight, value_weight))
    came = [
        lax.ppermute(part, "blk", [((i + r) % blk, i) for i in range(blk)])
        for r, part in enumerate(jnp.split(rem_gradient, blk - 1, axis=1), 1)
    ]

    def flat(value):
        return value.reshape(-1, features)

    dwq, dwk, dwv, dbq, dbv = weights_back(*map(flat, (tokens, rem_tokens, dq, dko, dvo, dkr, dvr)))
    dwq, dwk, dwv = scatter_sum(dwq), scatter_sum(dwk), scatter_sum(dwv)
    own_gradient = tokens_back(
        own_back_kernel,
        (branch_gradient.reshape(tokens.shape), dq, dko, dvo),
        (query_weight, key_weight, value_weight),
    )
    tokens_gradient = own_gradient.astype(F32)
    for part in came:
        tokens_gradient += part.astype(F32)
    summed = scatter_vectors(
        [dbq, dbv] + [vector_gradients[i] for i in range(6)] + [up_bias_gradient]
    )
    dbq, dbv, dbo, dg1, ds1, dbd, dg2, ds2, dbu = summed
    return (
        block_out.reshape(tokens.shape),
        tokens_gradient.astype(BF16),
        dwq,
        dbq,
        dwk,
        dwv,
        dbv,
        dwo,
        dbo,
        dg1,
        ds1,
        dwu,
        dbu,
        dwd,
        dbd,
        dg2,
        ds2,
    )


def solution(mesh):
    rows, shared, pair = P("dp", "blk", None), P(), P("dp", "blk")
    matrix, vector = P(("dp", "blk"), None), P(("dp", "blk"))
    return jax.shard_map(
        body,
        mesh=mesh,
        in_specs=(rows,) + (shared,) * 15 + (pair, pair, rows),
        out_specs=(
            rows,
            rows,
            matrix,
            vector,
            matrix,
            matrix,
            vector,
            matrix,
            vector,
            vector,
            vector,
            matrix,
            vector,
            matrix,
            vector,
            vector,
            vector,
        ),
        check_vma=False,
    )
```

```python
import functools
import math

import jax
import jax.numpy as jnp
from jax import lax
from jax.experimental import pallas as pl
from jax.experimental.pallas import tpu as pltpu
from jax.sharding import PartitionSpec as P

HEAD = 64
PAIR = 2 * HEAD
EPSILON = 1e-12
MASKED = -1e30
FLOOR = -3e38
SCALE = HEAD**-0.5
EXPO = SCALE * math.log2(math.e)
NN = (((1,), (0,)), ((), ()))
NT = (((1,), (1,)), ((), ()))
F32 = jnp.float32
BF16 = jnp.bfloat16
MIB = 1 << 20


def dot(left, right, dims=NN):
    return lax.dot_general(left, right, dims, preferred_element_type=F32)


def whole_spec(shape):
    return pl.BlockSpec(shape, lambda *_: (0,) * len(shape), pipeline_mode=pl.Buffered(1))


def params(limit):
    return pltpu.CompilerParams(vmem_limit_bytes=limit * MIB)


def cost(flops, touched, exps=0):
    return pl.CostEstimate(flops=int(flops), bytes_accessed=int(touched), transcendentals=int(exps))


def project_kernel(has_query, *refs):
    if has_query:
        x_ref, bias_ref, wq_ref, wk_ref, wv_ref, q_ref, k_ref, v_ref = refs
    else:
        x_ref, bias_ref, wk_ref, wv_ref, k_ref, v_ref = refs
    x = x_ref[0]
    if has_query:
        q_ref[0] = (dot(x, wq_ref[...]) + bias_ref[0:1]).astype(BF16)
    k_ref[0] = dot(x, wk_ref[...]).astype(BF16)
    v_ref[0] = (dot(x, wv_ref[...]) + bias_ref[1:2]).astype(BF16)


def project(x, bias, weights):
    seqs, length, features = x.shape
    tile = math.gcd(length, 512)
    grid = (seqs, length // tile)
    row_spec = pl.BlockSpec((1, tile, features), lambda s, i: (s, i, 0))
    return pl.pallas_call(
        functools.partial(project_kernel, len(weights) == 3),
        grid=grid,
        in_specs=[row_spec, whole_spec(bias.shape)] + [whole_spec(w.shape) for w in weights],
        out_specs=[row_spec] * len(weights),
        out_shape=[jax.ShapeDtypeStruct(x.shape, BF16)] * len(weights),
        compiler_params=params(40),
        cost_estimate=cost(
            2 * x.size * features * len(weights), 2 * x.size * (1 + len(weights))
        ),
        name="project",
    )(x, bias, *weights)


def low_lanes():
    return lax.broadcasted_iota(jnp.int32, (1, PAIR), 1) < HEAD


def attend_kernel(q_ref, qm_ref, ko_ref, kmo_ref, vo_ref, kr_ref, kmr_ref, vr_ref, o_ref, lse_ref):
    tile = math.gcd(q_ref.shape[1], 256)
    qm = qm_ref[0]
    low = low_lanes()
    for pair in range(q_ref.shape[2] // PAIR):
        lanes = slice(pair * PAIR, (pair + 1) * PAIR)
        keys, values = [], []
        for head in range(2):
            mine = ~low if head else low
            keys.append(
                [
                    jnp.where(mine, k_ref[0, :, lanes], km_ref[0])
                    for k_ref, km_ref in ((ko_ref, kmo_ref), (kr_ref, kmr_ref))
                ]
            )
            values.append(
                [
                    jnp.where(mine, v_ref[0, :, lanes], jnp.ones((1, PAIR), BF16))
                    for v_ref in (vo_ref, vr_ref)
                ]
            )
        for row in range(0, q_ref.shape[1], tile):
            rows = slice(row, row + tile)
            sums, tops = [], []
            for head in range(2):
                mine = ~low if head else low
                q_side = jnp.where(mine, q_ref[0, rows, lanes], qm[rows])
                scores = [dot(q_side, k, NT) for k in keys[head]]
                top = functools.reduce(
                    jnp.maximum, [jnp.max(part, axis=-1, keepdims=True) for part in scores]
                )
                weights = [jnp.exp2((part - top) * EXPO).astype(BF16) for part in scores]
                sums.append(sum(dot(w, v) for w, v in zip(weights, values[head])))
                tops.append(top)
            totals = pltpu.roll(jnp.where(low, sums[1], sums[0]), HEAD, 1)
            outs = jnp.where(low, sums[0], sums[1]) / totals
            o_ref[0, rows, lanes] = outs.astype(BF16)
            lse = (jnp.where(low, tops[0], tops[1]) * EXPO + jnp.log2(totals)).T
            lse_ref[0, pair, 0:1, rows] = lse[0:1]
            lse_ref[0, pair, 1:2, rows] = lse[HEAD : HEAD + 1]


def pair_spec(length, lanes):
    return pl.BlockSpec((1, length, lanes), lambda s, h: (s, 0, h))


def mask_spec(length):
    return pl.BlockSpec((1, length, PAIR), lambda s, h: (s, 0, 0))


def lse_spec(length, lanes):
    return pl.BlockSpec((1, lanes // PAIR, 8, length), lambda s, h: (s, h, 0, 0))


def attend(q, qm, own, rem):
    seqs, length, features = q.shape
    lanes = math.gcd(features, 2 * PAIR)
    other = rem[0].shape[1]
    own_spec, rem_spec = pair_spec(length, lanes), pair_spec(other, lanes)
    return pl.pallas_call(
        attend_kernel,
        grid=(seqs, features // lanes),
        in_specs=[own_spec, mask_spec(length)]
        + [own_spec, mask_spec(length), own_spec]
        + [rem_spec, mask_spec(other), rem_spec],
        out_specs=[own_spec, lse_spec(length, lanes)],
        out_shape=[
            jax.ShapeDtypeStruct(q.shape, BF16),
            jax.ShapeDtypeStruct((seqs, features // PAIR, 8, length), F32),
        ],
        compiler_params=params(48),
        cost_estimate=cost(
            16 * q.size * (length + other), 2 * q.size * 6, q.size * (length + other) // HEAD
        ),
        name="attend",
    )(q, qm, *own, *rem)


def attend_back_kernel(q_ref, qm_ref, o_ref, g_ref, lse_ref, ko_ref, kmo_ref, vo_ref, kr_ref, kmr_ref,
                       vr_ref, dq_ref, dko_ref, dvo_ref, dkr_ref, dvr_ref):
    low = low_lanes()
    parts = ((ko_ref, kmo_ref, vo_ref, dko_ref, dvo_ref), (kr_ref, kmr_ref, vr_ref, dkr_ref, dvr_ref))
    qm = qm_ref[0]
    for pair in range(q_ref.shape[2] // PAIR):
        lanes = slice(pair * PAIR, (pair + 1) * PAIR)
        q, g = q_ref[0, :, lanes], g_ref[0, :, lanes]
        none = jnp.zeros((1, PAIR), BF16)
        product = g.astype(F32) * o_ref[0, :, lanes].astype(F32)
        deltas, q_sides, q_zero, g_zero = [], [], [], []
        for head in range(2):
            mine = ~low if head else low
            deltas.append(
                lax.dot_general(
                    jnp.broadcast_to(jnp.where(mine, 1.0, 0.0).astype(F32), (8, PAIR)),
                    product,
                    NT,
                    precision=lax.Precision.HIGHEST,
                    preferred_element_type=F32,
                )[0:1]
            )
            q_sides.append(jnp.where(mine, q, qm))
            q_zero.append(jnp.where(mine, q, none))
            g_zero.append(jnp.where(mine, g, none))
        dq = [0.0, 0.0]
        for k_ref, km_ref, v_ref, dk_ref, dv_ref in parts:
            k, km, v = k_ref[0, :, lanes], km_ref[0], v_ref[0, :, lanes]
            k_t = k.T
            dk = dv = 0.0
            for head in range(2):
                mine = ~low if head else low
                scores = dot(jnp.where(mine, k, km), q_sides[head], NT)
                grads = dot(jnp.where(mine, v, none), g, NT)
                probs = jnp.exp2(scores * EXPO - lse_ref[0, pair, head : head + 1, :])
                grads = (probs * (grads - deltas[head])).astype(BF16)
                dv += dot(probs.astype(BF16), g_zero[head])
                dk += dot(grads, q_zero[head])
                dq[head] += dot(k_t[head * HEAD : (head + 1) * HEAD], grads)
            dk_ref[0, :, lanes] = (dk * SCALE).astype(BF16)
            dv_ref[0, :, lanes] = dv.astype(BF16)
        dq_ref[0, :, lanes] = (jnp.concatenate(dq, axis=0) * SCALE).T.astype(BF16)


def attend_back(q, qm, o, g, lse, own, rem):
    seqs, length, features = q.shape
    lanes = math.gcd(features, 2 * PAIR)
    other = rem[0].shape[1]
    own_spec, rem_spec = pair_spec(length, lanes), pair_spec(other, lanes)
    return pl.pallas_call(
        attend_back_kernel,
        grid=(seqs, features // lanes),
        in_specs=[own_spec, mask_spec(length), own_spec, own_spec, lse_spec(length, lanes)]
        + [own_spec, mask_spec(length), own_spec]
        + [rem_spec, mask_spec(other), rem_spec],
        out_specs=[own_spec] * 3 + [rem_spec] * 2,
        out_shape=[jax.ShapeDtypeStruct(q.shape, BF16)] * 3
        + [jax.ShapeDtypeStruct(rem[0].shape, BF16)] * 2,
        compiler_params=params(48),
        cost_estimate=cost(
            40 * q.size * (length + other), 2 * q.size * 14, q.size * (length + other) // HEAD
        ),
        name="attend_back",
    )(q, qm, o, g, lse, *own, *rem)


def gelu_and_slope(x):
    bell = jnp.exp2(x * x * (-0.5 * math.log2(math.e)))
    t = 1.0 / (1.0 + (0.3275911 / math.sqrt(2.0)) * jnp.abs(x))
    poly = 1.061405429 * t - 1.453152027
    poly = poly * t + 1.421413741
    poly = poly * t - 0.284496736
    poly = poly * t + 0.254829592
    tail = (0.5 * poly) * t * bell
    share = jnp.where(x >= 0.0, 1.0 - tail, tail)
    return x * share, share + x * bell * (1.0 / math.sqrt(2.0 * math.pi))


def mean(values):
    return jnp.sum(values, axis=-1, keepdims=True) * (1.0 / values.shape[-1])


def norm_parts(values):
    centred = values - mean(values)
    scale = lax.rsqrt(mean(centred * centred) + EPSILON)
    return centred * scale, scale


def norm_back(upper, normed, scale):
    return scale * (upper - mean(upper) - normed * mean(upper * normed))


def column_sum(values):
    return jnp.sum(values, axis=0, keepdims=True)


def feed_kernel(layout, tok_ref, att_ref, cot_ref, vec_ref, bu_ref, wo_ref, wu_ref, wd_ref,
                out_ref, bg_ref, ag_ref, vg_ref, dbu_ref, dwu_ref, dwd_ref, dwo_ref,
                act_s, din_s, first_t, feed_t, att_t, bg_s):
    tiles, ff_steps, chunk, wide, narrow = layout
    step = pl.program_id(0)
    tile = tok_ref.shape[0]
    hidden = act_s.shape[1]
    vec = [vec_ref[i : i + 1] for i in range(6)]
    out_bias, gain_one, shift_one, down_bias, gain_two, shift_two = vec

    @pl.when(step == 0)
    def _():
        vg_ref[...] = jnp.zeros_like(vg_ref)
        dbu_ref[...] = jnp.zeros_like(dbu_ref)

    @pl.when(step < tiles)
    def _():
        start = pl.multiple_of(step * tile, tile)
        rows = pl.ds(start, tile)
        att = att_ref[...]
        normed_one, scale_one = norm_parts(
            tok_ref[...].astype(F32) + (dot(att, wo_ref[...]) + out_bias)
        )
        first = normed_one * gain_one + shift_one
        first_low = first.astype(BF16)
        first_t[:, rows] = first_low.T
        att_t[:, rows] = att.T
        feed = jnp.zeros_like(first) + down_bias
        spans = [slice(c, c + chunk) for c in range(0, hidden, chunk)]
        ahead = dot(first_low, wu_ref[:, spans[0]])
        for i, cols in enumerate(spans):
            inner = ahead + bu_ref[:, cols]
            if i + 1 < len(spans):
                ahead = dot(first_low, wu_ref[:, spans[i + 1]])
            active, slope = gelu_and_slope(inner)
            active = active.astype(BF16)
            act_s[rows, cols] = active
            din_s[rows, cols] = slope.astype(BF16)
            feed += dot(active, wd_ref[cols])
        normed_two, scale_two = norm_parts(first + feed)
        out_ref[...] = (normed_two * gain_two + shift_two).astype(BF16)
        cot = cot_ref[...].astype(F32)
        second = norm_back(cot * gain_two, normed_two, scale_two)
        feed_low = second.astype(BF16)
        feed_t[:, rows] = feed_low.T
        back = second
        ahead = dot(feed_low, wd_ref[spans[0]], NT)
        for i, cols in enumerate(spans):
            inner = ahead
            if i + 1 < len(spans):
                ahead = dot(feed_low, wd_ref[spans[i + 1]], NT)
            inner = (inner * din_s[rows, cols].astype(F32)).astype(BF16)
            din_s[rows, cols] = inner
            dbu_ref[:, cols] += column_sum(inner.astype(F32))
            back += dot(inner, wu_ref[:, cols], NT)
        residual = norm_back(back * gain_one, normed_one, scale_one)
        branch_low = residual.astype(BF16)
        bg_ref[...] = branch_low
        bg_s[rows] = branch_low
        ag_ref[...] = dot(branch_low, wo_ref[...], NT).astype(BF16)
        for i, values in enumerate(
            (
                branch_low.astype(F32),
                back * normed_one,
                back,
                feed_low.astype(F32),
                cot * normed_two,
                cot,
            )
        ):
            vg_ref[i : i + 1] += column_sum(values)

    @pl.when((step >= tiles) & (step < tiles + ff_steps))
    def _():
        cols = pl.ds(pl.multiple_of((step - tiles) * wide, wide), wide)
        dwu = dot(first_t[...], din_s[:, cols]).astype(BF16)
        dwu_ref[...] = dwu.reshape(dwu_ref.shape)
        dwd_ref[...] = dot(feed_t[...], act_s[:, cols]).astype(BF16).T

    @pl.when(step >= tiles + ff_steps)
    def _():
        cols = pl.ds(pl.multiple_of((step - tiles - ff_steps) * narrow, narrow), narrow)
        dwo_ref[...] = dot(att_t[...], bg_s[:, cols]).astype(BF16)


def feed_both_ways(tokens, attended, cotangent, vectors, up_bias, wo, wu, wd, groups):
    rows, features = tokens.shape
    hidden = wu.shape[1]
    tile = math.gcd(rows, 256)
    tiles = rows // tile
    wide, narrow = features, math.gcd(features, 384)
    ff_steps, out_steps = hidden // wide, features // narrow
    layout = (tiles, ff_steps, math.gcd(hidden, 512), wide, narrow)
    blocked = (groups, ff_steps, features // groups, wide)
    row_spec = pl.BlockSpec((tile, features), lambda i: (jnp.minimum(i, tiles - 1), 0))

    def ff_at(i):
        return jnp.clip(i - tiles, 0, ff_steps - 1)

    return pl.pallas_call(
        functools.partial(feed_kernel, layout),
        grid=(tiles + ff_steps + out_steps,),
        in_specs=[row_spec] * 3
        + [whole_spec(a.shape) for a in (vectors, up_bias, wo, wu, wd)],
        out_specs=[row_spec] * 3
        + [
            pl.BlockSpec((8, features), lambda i: (0, 0)),
            pl.BlockSpec((1, hidden), lambda i: (0, 0)),
            pl.BlockSpec((groups, 1) + blocked[2:], lambda i: (0, ff_at(i), 0, 0)),
            pl.BlockSpec((wide, features), lambda i: (ff_at(i), 0)),
            pl.BlockSpec(
                (features, narrow),
                lambda i: (0, jnp.clip(i - tiles - ff_steps, 0, out_steps - 1)),
            ),
        ],
        out_shape=[jax.ShapeDtypeStruct(tokens.shape, BF16)] * 3
        + [
            jax.ShapeDtypeStruct((8, features), F32),
            jax.ShapeDtypeStruct((1, hidden), F32),
            jax.ShapeDtypeStruct(blocked, BF16),
            jax.ShapeDtypeStruct(wd.shape, BF16),
            jax.ShapeDtypeStruct(wo.shape, BF16),
        ],
        scratch_shapes=[
            pltpu.VMEM((rows, hidden), BF16),
            pltpu.VMEM((rows, hidden), BF16),
            pltpu.VMEM((features, rows), BF16),
            pltpu.VMEM((features, rows), BF16),
            pltpu.VMEM((features, rows), BF16),
            pltpu.VMEM((rows, features), BF16),
        ],
        compiler_params=params(60),
        cost_estimate=cost(
            6 * rows * features * (features + 2 * hidden),
            2 * (6 * rows * features + 4 * features * hidden + 2 * features * features),
            2 * rows * hidden,
        ),
        name="feed_both_ways",
    )(tokens, attended, cotangent, vectors, up_bias, wo, wu, wd)


def own_back_kernel(bg_ref, dq_ref, dk_ref, dv_ref, wq_ref, wk_ref, wv_ref, out_ref):
    total = bg_ref[0].astype(F32) + dot(dq_ref[0], wq_ref[...], NT)
    total += dot(dk_ref[0], wk_ref[...], NT)
    total += dot(dv_ref[0], wv_ref[...], NT)
    out_ref[0] = total.astype(BF16)


def rem_back_kernel(dk_ref, dv_ref, wk_ref, wv_ref, out_ref):
    total = dot(dk_ref[0], wk_ref[...], NT) + dot(dv_ref[0], wv_ref[...], NT)
    out_ref[0] = total.astype(BF16)


def tokens_back(kernel, rows, weights):
    seqs, length, features = rows[0].shape
    tile = math.gcd(length, 512)
    row_spec = pl.BlockSpec((1, tile, features), lambda s, i: (s, i, 0))
    size = rows[0].size
    return pl.pallas_call(
        kernel,
        grid=(seqs, length // tile),
        in_specs=[row_spec] * len(rows) + [whole_spec(w.shape) for w in weights],
        out_specs=row_spec,
        out_shape=jax.ShapeDtypeStruct(rows[0].shape, BF16),
        compiler_params=params(40),
        cost_estimate=cost(2 * size * features * len(weights), 2 * size * (1 + len(rows))),
        name="tokens_back",
    )(*rows, *weights)


def weights_back_kernel(tok_ref, rem_ref, dq_ref, dko_ref, dvo_ref, dkr_ref, dvr_ref,
                        wq_ref, wk_ref, wv_ref, bq_ref, bv_ref, tok_t, rem_t):
    @pl.when(pl.program_id(0) == 0)
    def _():
        tok_t[...] = tok_ref[...].T
        rem_t[...] = rem_ref[...].T

    wq_ref[...] = dot(tok_t[...], dq_ref[...]).astype(BF16)
    wk_ref[...] = (dot(tok_t[...], dko_ref[...]) + dot(rem_t[...], dkr_ref[...])).astype(BF16)
    wv_ref[...] = (dot(tok_t[...], dvo_ref[...]) + dot(rem_t[...], dvr_ref[...])).astype(BF16)
    bq_ref[...] = column_sum(dq_ref[...].astype(F32))
    bv_ref[...] = column_sum(dvo_ref[...].astype(F32)) + column_sum(dvr_ref[...].astype(F32))


def weights_back(tok, rem, dq, dko, dvo, dkr, dvr):
    rows, features = tok.shape
    others = rem.shape[0]
    wide = math.gcd(features, 256)
    own_spec = pl.BlockSpec((rows, wide), lambda j: (0, j))
    rem_spec = pl.BlockSpec((others, wide), lambda j: (0, j))
    bias_spec = pl.BlockSpec((1, wide), lambda j: (0, j))
    return pl.pallas_call(
        weights_back_kernel,
        grid=(features // wide,),
        in_specs=[
            whole_spec(tok.shape),
            whole_spec(rem.shape),
            own_spec,
            own_spec,
            own_spec,
            rem_spec,
            rem_spec,
        ],
        out_specs=[pl.BlockSpec((features, wide), lambda j: (0, j))] * 3 + [bias_spec] * 2,
        out_shape=[jax.ShapeDtypeStruct((features, features), BF16)] * 3
        + [jax.ShapeDtypeStruct((1, features), F32)] * 2,
        scratch_shapes=[
            pltpu.VMEM((features, rows), BF16),
            pltpu.VMEM((features, others), BF16),
        ],
        compiler_params=params(48),
        cost_estimate=cost(
            2 * features * features * (3 * rows + 2 * others),
            2 * (4 * tok.size + 3 * rem.size + 3 * features * features),
        ),
        name="weights_back",
    )(tok, rem, dq, dko, dvo, dkr, dvr)


def halve(value, axis, bit):
    size = lax.axis_size(axis)
    mine = (lax.axis_index(axis) >> bit) & 1
    pairs = value.reshape((value.shape[0] // 2, 2) + value.shape[1:])
    keep = lax.dynamic_index_in_dim(pairs, mine, 1, keepdims=False)
    send = lax.dynamic_index_in_dim(pairs, 1 - mine, 1, keepdims=False)
    came = lax.ppermute(send, axis, [(i, i ^ (1 << bit)) for i in range(size)])
    return keep.astype(F32) + came.astype(F32)


def scatter_sum(value, low=True):
    dp, blk = lax.axis_size("dp"), lax.axis_size("blk")
    if dp & (dp - 1) or blk & (blk - 1):
        return lax.psum_scatter(
            value.astype(F32), ("dp", "blk"), scatter_dimension=0, tiled=True
        )
    kept = value.dtype
    each = value.shape[0] // (dp * blk)
    value = value.reshape((dp, blk * each) + value.shape[1:])
    for bit in range(dp.bit_length() - 1):
        value = halve(value, "dp", bit).astype(kept)
    value = value.reshape((blk, each) + value.shape[2:])
    for bit in range(blk.bit_length() - 1):
        value = halve(value, "blk", bit)
        value = value if (2 << bit) == blk else value.astype(kept)
    return value.reshape(value.shape[1:]).astype(F32)


def pack_vectors(vectors, dp, blk):
    lanes = [v.reshape(dp, blk, 1, -1) for v in vectors]
    lanes = [jnp.pad(v, ((0, 0),) * 3 + ((0, PAIR - v.shape[-1]),)) for v in lanes]
    lanes.append(jnp.zeros((dp, blk, -len(vectors) % 8, PAIR), F32))
    return jnp.concatenate(lanes, axis=2)


class Unit:
    def __init__(self, parts, halves, order, columns, dtype):
        self.parts, self.halves, self.order = parts, halves, order
        self.rows = sum(p[2] for p in parts)
        self.columns, self.dtype = columns, dtype


def plan(units, bits):
    free, events = {}, []
    done = [0.0] * len(units)
    for step in range(bits + 1):
        for u, unit in enumerate(units):
            bit = unit.order[step] if step < bits else "blk"
            size = unit.rows * unit.columns * (1 << (bits - 1 - min(step, bits - 1))) * 4e-5
            size *= {0: 1 / 6, "blk": 0.5}.get(bit, 1.0)
            start = max(done[u], free.get(bit, 0.0))
            done[u] = free[bit] = start + size + 1e-3
            events.append((done[u], u, step))
    return [(u, step) for _, u, step in sorted(events)]


def scatter_kernel(units, bits, n_in, n_out, *refs):
    sources, outs = refs[:n_in], refs[n_in : n_in + n_out]
    refs = list(refs[n_in + n_out :])
    kept = [refs.pop(0) for _ in units]
    landed = [[refs.pop(0) for _ in range(bits)] for _ in units]
    wide = [refs.pop(0) for _ in units]
    parting = [refs.pop(0) for _ in units]
    last = [refs.pop(0) for _ in units]
    send_sem, recv_sem, local_sem = refs
    me, side = lax.axis_index("dp"), lax.axis_index("blk")
    own = [(me // (1 << bit)) % 2 for bit in range(bits)]
    partner = [{"dp": me + (1 << bit) * (1 - 2 * own[bit])} for bit in range(bits)]
    partner.append({"blk": 1 - side})

    barrier = pltpu.get_barrier_semaphore()
    for other in partner:
        pl.semaphore_signal(barrier, inc=1, device_id=other, device_id_type=pl.DeviceIdType.MESH)
    pl.semaphore_wait(barrier, bits + 1)

    sems = {}

    def sem(*key):
        return sems.setdefault(key, len(sems))

    def send(src, dst, device, key):
        at = sem(*key)
        copy = pltpu.make_async_remote_copy(
            src_ref=src,
            dst_ref=dst,
            send_sem=send_sem.at[at],
            recv_sem=recv_sem.at[at],
            device_id=device,
            device_id_type=pl.DeviceIdType.MESH,
        )
        copy.start()
        return copy

    def index(unit, step, bit_value):
        found = []
        for bit in range(bits - 1, 0, -1):
            at = unit.order.index(bit)
            found.append(own[bit] if at < step else bit_value if at == step else slice(None))
        return tuple(found)

    waiting, locals_ = {}, {}
    for u, unit in enumerate(units):
        found, near, row = [], [], 0
        for p, (source, first, rows) in enumerate(unit.parts):
            from_rows, to_rows = pl.ds(first, rows), pl.ds(row, rows)
            lead = (slice(None),) * (bits - 1)
            ref = sources[source]
            copy = pltpu.make_async_copy(
                ref.at[lead + (own[0], from_rows)],
                kept[u].at[lead + (to_rows,)],
                local_sem.at[sem(u, 0, p)],
            )
            copy.start()
            near.append(copy)
            found.append(
                send(
                    ref.at[lead + (1 - own[0], from_rows)],
                    landed[u][0].at[lead + (to_rows,)],
                    partner[0],
                    (u, 0, p),
                )
            )
            row += rows
        waiting[u, 0], locals_[u] = found, near

    for u, step in plan(units, bits):
        unit = units[u]
        for copy in waiting[u, step]:
            copy.wait_recv()
        if step == 0:
            for copy in locals_[u]:
                copy.wait()
        if step < bits:
            into, came = kept[u], landed[u][step]
            spot = index(unit, step, own[unit.order[step]])
            open_at = [i for i, s in enumerate(spot) if isinstance(s, slice)]

            def add(n, _, spot=spot, open_at=open_at, into=into, came=came, final=step == bits - 1, u=u):
                at, where = list(spot), []
                for place, i in enumerate(open_at):
                    digit = (n // (1 << (len(open_at) - 1 - place))) % 2
                    at[i] = digit
                    where.append(digit)
                total = into[tuple(at)].astype(F32) + came[tuple(where)].astype(F32)
                if final:
                    wide[u][...] = total
                else:
                    into[tuple(at)] = total.astype(into.dtype)
                return _

            count = 1 << len(open_at)
            if count == 1:
                add(0, 0)
            else:
                lax.fori_loop(0, count, add, 0)
        if step < bits - 1:
            bit = unit.order[step + 1]
            waiting[u, step + 1] = [
                send(
                    kept[u].at[index(unit, step + 1, 1 - own[bit])],
                    landed[u][step + 1],
                    partner[bit],
                    (u, step + 1, 0),
                )
            ]
        elif step == bits - 1:
            half = unit.rows // (2 * unit.halves)
            pieces = [
                wide[u][pl.ds(pl.multiple_of(h * 2 * half + (1 - side) * half, 8), half)]
                for h in range(unit.halves)
            ]
            pieces = pieces[0] if len(pieces) == 1 else jnp.concatenate(pieces, axis=0)
            parting[u][...] = pieces.astype(unit.dtype)
            waiting[u, bits] = [send(parting[u], last[u], partner[bits], (u, bits, 0))]
        else:
            half = unit.rows // (2 * unit.halves)
            for h, (out, rows, columns) in enumerate(unit.outs):
                mine = wide[u][pl.ds(pl.multiple_of(h * 2 * half + side * half, 8), half)]
                outs[out][rows, columns] = mine + last[u][...].astype(F32)[h * half : (h + 1) * half]
    for copies in waiting.values():
        for copy in copies:
            copy.wait_send()


def scatter_all(dwd, dwu, dwo, dwq, dwk, dwv, vectors):
    dp, blk = lax.axis_size("dp"), lax.axis_size("blk")
    bits = dp.bit_length() - 1
    features = dwo.shape[0]
    low, deep = features // dp, dwd.shape[0] // dp
    lead = (2,) * bits
    sources = [
        dwd.reshape(lead + (deep, features)),
        dwu.reshape(lead + (-1, features)),
        *(w.reshape(lead + (low, features)) for w in (dwo, dwq, dwk, dwv)),
        vectors.reshape(lead + (-1, PAIR)),
    ]
    inner = tuple(range(bits))
    outer = (0,) + tuple(range(2, bits)) + (1,) if bits > 1 else inner
    quarter, half = deep // 4, low // 2
    units = []

    def add(parts, outs, order, halves, columns=features, dtype=BF16):
        unit = Unit(parts, halves, order, columns, dtype)
        unit.outs = outs
        units.append(unit)

    everything = slice(None)
    for i, order in enumerate((inner, outer)):
        rows = slice(i * quarter, (i + 1) * quarter)
        add(
            [(0, i * quarter, quarter), (0, (2 + i) * quarter, quarter)],
            [(0, rows, everything)],
            order,
            1,
        )
    blocks = dwu.shape[1]
    for i, order in enumerate((inner, outer)):
        found = range(i * blocks // 2, (i + 1) * blocks // 2)
        add(
            [(1, b * low, low) for b in found],
            [(1, everything, slice(b * features, (b + 1) * features)) for b in found],
            order,
            len(found),
        )
    whole = (everything, everything)
    add([(2, 0, low), (3, 0, low)], [(2,) + whole, (3,) + whole], outer, 2)
    add([(4, 0, low), (5, 0, low)], [(4,) + whole, (5,) + whole], inner, 2)
    depth = vectors.shape[-2] * blk
    add([(6, 0, depth)], [(6,) + whole], inner, 1, PAIR, F32)

    out_shape = [
        jax.ShapeDtypeStruct((deep // 2, features), F32),
        jax.ShapeDtypeStruct((half, blocks * features), F32),
        *(jax.ShapeDtypeStruct((half, features), F32) for _ in range(4)),
        jax.ShapeDtypeStruct((depth // 2, PAIR), F32),
    ]
    scratch = [
        pltpu.VMEM(lead[1:] + (u.rows, u.columns), u.dtype) for u in units
    ]
    for u in units:
        scratch += [
            pltpu.VMEM(lead[1 + step :] + (u.rows, u.columns), u.dtype) for step in range(bits)
        ]
    scratch += [pltpu.VMEM((u.rows, u.columns), F32) for u in units]
    scratch += [pltpu.VMEM((u.rows // 2, u.columns), u.dtype) for u in units] * 2
    count = sum(len(u.parts) + bits for u in units)
    scratch += [pltpu.SemaphoreType.DMA((count,))] * 3
    return pl.pallas_call(
        functools.partial(scatter_kernel, units, bits, len(sources), len(out_shape)),
        in_specs=[pl.BlockSpec(memory_space=pl.ANY)] * len(sources),
        out_specs=[pl.BlockSpec(memory_space=pltpu.VMEM)] * len(out_shape),
        out_shape=out_shape,
        scratch_shapes=scratch,
        compiler_params=pltpu.CompilerParams(
            collective_id=1, has_side_effects=True, vmem_limit_bytes=48 * MIB
        ),
        cost_estimate=cost(0, 2 * 12 * features * features * 3),
        name="scatter_all",
    )(*sources)


def scatter_plainly(dwd, dwu, dwo, dwq, dwk, dwv, vectors):
    dwu = jnp.moveaxis(dwu[0], 0, 1).reshape(dwo.shape[0], -1)
    vectors = vectors.reshape((-1,) + vectors.shape[2:])
    return [scatter_sum(w) for w in (dwd, dwu, dwo, dwq, dwk, dwv)] + [
        scatter_sum(vectors.reshape(vectors.shape[0], -1)).reshape(vectors.shape[1:])
    ]


def body(
    tokens,
    query_weight,
    query_bias,
    key_weight,
    value_weight,
    value_bias,
    out_weight,
    out_bias,
    gain_one,
    shift_one,
    up_weight,
    up_bias,
    down_weight,
    down_bias,
    gain_two,
    shift_two,
    group_ids,
    valid_mask,
    cotangent,
):
    seqs, length, features = tokens.shape
    rows = seqs * length
    blk = lax.axis_size("blk")

    def from_others(value):
        found = [
            lax.ppermute(value, "blk", [(i, (i + r) % blk) for i in range(blk)])
            for r in range(1, blk)
        ]
        return found[0] if len(found) == 1 else jnp.concatenate(found, axis=1)

    codes = jnp.where(valid_mask == 1, group_ids, -1).astype(BF16)
    rem_tokens = from_others(tokens)
    rem_codes = from_others(codes).astype(jnp.int32)
    own_codes = codes.astype(jnp.int32)

    slot = jnp.arange(PAIR, dtype=jnp.int32) % HEAD

    def key_mask(code):
        return jnp.where(code[:, :, None] == slot, 0.0, MASKED).astype(BF16)

    query_mask = (group_ids[:, :, None] == slot).astype(BF16)
    dp = lax.axis_size("dp")
    by_kernel = blk == 2 and dp & (dp - 1) == 0 and dp > 1 and (features // dp) % 16 == 0

    biases = jnp.concatenate(
        [query_bias[None], value_bias[None], jnp.zeros((6, features), BF16)], axis=0
    ).astype(F32)
    queries, own_keys, own_values = project(
        tokens, biases, (query_weight, key_weight, value_weight)
    )
    rem_keys, rem_values = project(rem_tokens, biases, (key_weight, value_weight))
    own = (own_keys, key_mask(own_codes), own_values)
    rem = (rem_keys, key_mask(rem_codes), rem_values)
    attended, lse = attend(queries, query_mask, own, rem)

    vectors = jnp.stack(
        [out_bias, gain_one, shift_one, down_bias, gain_two, shift_two, out_bias, out_bias]
    ).astype(F32)
    block_out, branch_gradient, attended_gradient, vector_gradients, up_bias_gradient, dwu, dwd, dwo = (
        feed_both_ways(
            tokens.reshape(rows, features),
            attended.reshape(rows, features),
            cotangent.reshape(rows, features),
            vectors,
            up_bias.astype(F32)[None],
            out_weight,
            up_weight,
            down_weight,
            dp if by_kernel else 1,
        )
    )

    dq, dko, dvo, dkr, dvr = attend_back(
        queries,
        query_mask,
        attended,
        attended_gradient.reshape(tokens.shape),
        lse,
        own,
        rem,
    )
    rem_gradient = tokens_back(rem_back_kernel, (dkr, dvr), (key_weight, value_weight))
    came = [
        lax.ppermute(part, "blk", [((i + r) % blk, i) for i in range(blk)])
        for r, part in enumerate(jnp.split(rem_gradient, blk - 1, axis=1), 1)
    ]

    def flat(value):
        return value.reshape(-1, features)

    dwq, dwk, dwv, dbq, dbv = weights_back(*map(flat, (tokens, rem_tokens, dq, dko, dvo, dkr, dvr)))
    vectors = pack_vectors(
        [dbq, dbv] + [vector_gradients[i] for i in range(6)] + [up_bias_gradient], dp, blk
    )
    scatter = scatter_all if by_kernel else scatter_plainly
    dwd, dwu, dwo, dwq, dwk, dwv, vectors = scatter(dwd, dwu, dwo, dwq, dwk, dwv, vectors)
    share = features // (dp * blk)
    dbq, dbv, dbo, dg1, ds1, dbd, dg2, ds2 = [vectors[i, :share] for i in range(8)]
    dbu = vectors[8, : up_bias.size // (dp * blk)]
    own_gradient = tokens_back(
        own_back_kernel,
        (branch_gradient.reshape(tokens.shape), dq, dko, dvo),
        (query_weight, key_weight, value_weight),
    )
    tokens_gradient = own_gradient.astype(F32)
    for part in came:
        tokens_gradient += part.astype(F32)
    return (
        block_out.reshape(tokens.shape),
        tokens_gradient.astype(BF16),
        dwq,
        dbq,
        dwk,
        dwv,
        dbv,
        dwo,
        dbo,
        dg1,
        ds1,
        dwu,
        dbu,
        dwd,
        dbd,
        dg2,
        ds2,
    )


def solution(mesh):
    rows, shared, pair = P("dp", "blk", None), P(), P("dp", "blk")
    matrix, vector = P(("dp", "blk"), None), P(("dp", "blk"))
    return jax.shard_map(
        body,
        mesh=mesh,
        in_specs=(rows,) + (shared,) * 15 + (pair, pair, rows),
        out_specs=(
            rows,
            rows,
            matrix,
            vector,
            matrix,
            matrix,
            vector,
            matrix,
            vector,
            vector,
            vector,
            matrix,
            vector,
            matrix,
            vector,
            vector,
            vector,
        ),
        check_vma=False,
    )
```

```python
import functools
import math

import jax
import jax.numpy as jnp
from jax import lax
from jax.experimental import pallas as pl
from jax.experimental.pallas import tpu as pltpu
from jax.sharding import PartitionSpec as P

HEAD = 64
PAIR = 2 * HEAD
EPSILON = 1e-12
MASKED = -1e30
FLOOR = -3e38
SCALE = HEAD**-0.5
EXPO = SCALE * math.log2(math.e)
NN = (((1,), (0,)), ((), ()))
NT = (((1,), (1,)), ((), ()))
F32 = jnp.float32
BF16 = jnp.bfloat16
MIB = 1 << 20


def dot(left, right, dims=NN):
    return lax.dot_general(left, right, dims, preferred_element_type=F32)


def whole_spec(shape):
    return pl.BlockSpec(shape, lambda *_: (0,) * len(shape), pipeline_mode=pl.Buffered(1))


def params(limit):
    return pltpu.CompilerParams(vmem_limit_bytes=limit * MIB)


def cost(flops, touched, exps=0):
    return pl.CostEstimate(flops=int(flops), bytes_accessed=int(touched), transcendentals=int(exps))


def project_kernel(has_query, *refs):
    if has_query:
        x_ref, bias_ref, wq_ref, wk_ref, wv_ref, q_ref, k_ref, v_ref = refs
    else:
        x_ref, bias_ref, wk_ref, wv_ref, k_ref, v_ref = refs
    x = x_ref[0]
    if has_query:
        q_ref[0] = (dot(x, wq_ref[...]) + bias_ref[0:1]).astype(BF16)
    k_ref[0] = dot(x, wk_ref[...]).astype(BF16)
    v_ref[0] = (dot(x, wv_ref[...]) + bias_ref[1:2]).astype(BF16)


def project(x, bias, weights):
    seqs, length, features = x.shape
    tile = math.gcd(length, 512)
    grid = (seqs, length // tile)
    row_spec = pl.BlockSpec((1, tile, features), lambda s, i: (s, i, 0))
    return pl.pallas_call(
        functools.partial(project_kernel, len(weights) == 3),
        grid=grid,
        in_specs=[row_spec, whole_spec(bias.shape)] + [whole_spec(w.shape) for w in weights],
        out_specs=[row_spec] * len(weights),
        out_shape=[jax.ShapeDtypeStruct(x.shape, BF16)] * len(weights),
        compiler_params=params(60),
        cost_estimate=cost(
            2 * x.size * features * len(weights), 2 * x.size * (1 + len(weights))
        ),
        name="project",
    )(x, bias, *weights)


def low_lanes():
    return lax.broadcasted_iota(jnp.int32, (1, PAIR), 1) < HEAD


def attend_kernel(q_ref, qm_ref, ko_ref, kmo_ref, vo_ref, kr_ref, kmr_ref, vr_ref, o_ref, lse_ref):
    tile = math.gcd(q_ref.shape[1], 256)
    qm = qm_ref[0]
    low = low_lanes()
    for pair in range(q_ref.shape[2] // PAIR):
        lanes = slice(pair * PAIR, (pair + 1) * PAIR)
        keys, values = [], []
        for head in range(2):
            mine = ~low if head else low
            keys.append(
                [
                    jnp.where(mine, k_ref[0, :, lanes], km_ref[0])
                    for k_ref, km_ref in ((ko_ref, kmo_ref), (kr_ref, kmr_ref))
                ]
            )
            values.append(
                [
                    jnp.where(mine, v_ref[0, :, lanes], jnp.ones((1, PAIR), BF16))
                    for v_ref in (vo_ref, vr_ref)
                ]
            )
        for row in range(0, q_ref.shape[1], tile):
            rows = slice(row, row + tile)
            sums, tops = [], []
            for head in range(2):
                mine = ~low if head else low
                q_side = jnp.where(mine, q_ref[0, rows, lanes], qm[rows])
                scores = [dot(q_side, k, NT) for k in keys[head]]
                top = functools.reduce(
                    jnp.maximum, [jnp.max(part, axis=-1, keepdims=True) for part in scores]
                )
                weights = [jnp.exp2((part - top) * EXPO).astype(BF16) for part in scores]
                sums.append(sum(dot(w, v) for w, v in zip(weights, values[head])))
                tops.append(top)
            totals = pltpu.roll(jnp.where(low, sums[1], sums[0]), HEAD, 1)
            outs = jnp.where(low, sums[0], sums[1]) / totals
            o_ref[0, rows, lanes] = outs.astype(BF16)
            lse = (jnp.where(low, tops[0], tops[1]) * EXPO + jnp.log2(totals)).T
            lse_ref[0, pair, 0:1, rows] = lse[0:1]
            lse_ref[0, pair, 1:2, rows] = lse[HEAD : HEAD + 1]


def pair_spec(length, lanes):
    return pl.BlockSpec((1, length, lanes), lambda s, h: (s, 0, h))


def mask_spec(length):
    return pl.BlockSpec((1, length, PAIR), lambda s, h: (s, 0, 0))


def lse_spec(length, lanes):
    return pl.BlockSpec((1, lanes // PAIR, 8, length), lambda s, h: (s, h, 0, 0))


def attend(q, qm, own, rem):
    seqs, length, features = q.shape
    lanes = math.gcd(features, 2 * PAIR)
    other = rem[0].shape[1]
    own_spec, rem_spec = pair_spec(length, lanes), pair_spec(other, lanes)
    return pl.pallas_call(
        attend_kernel,
        grid=(seqs, features // lanes),
        in_specs=[own_spec, mask_spec(length)]
        + [own_spec, mask_spec(length), own_spec]
        + [rem_spec, mask_spec(other), rem_spec],
        out_specs=[own_spec, lse_spec(length, lanes)],
        out_shape=[
            jax.ShapeDtypeStruct(q.shape, BF16),
            jax.ShapeDtypeStruct((seqs, features // PAIR, 8, length), F32),
        ],
        compiler_params=params(60),
        cost_estimate=cost(
            16 * q.size * (length + other), 2 * q.size * 6, q.size * (length + other) // HEAD
        ),
        name="attend",
    )(q, qm, *own, *rem)


def attend_back_pair(pair, low, parts, q_ref, qm_ref, o_ref, g_ref, lse_ref, dq_ref):
    def of(ref):
        return ref.at[0] if len(ref.shape) == 3 else ref

    lanes = slice(pair * PAIR, (pair + 1) * PAIR)
    q, g, qm = q_ref[0, :, lanes], g_ref[0, :, lanes], qm_ref[0]
    none = jnp.zeros((1, PAIR), BF16)
    product = g.astype(F32) * o_ref[0, :, lanes].astype(F32)
    deltas, q_sides, q_zero, g_zero = [], [], [], []
    for head in range(2):
        mine = ~low if head else low
        deltas.append(
            lax.dot_general(
                jnp.broadcast_to(jnp.where(mine, 1.0, 0.0).astype(F32), (8, PAIR)),
                product,
                NT,
                precision=lax.Precision.HIGHEST,
                preferred_element_type=F32,
            )[0:1]
        )
        q_sides.append(jnp.where(mine, q, qm))
        q_zero.append(jnp.where(mine, q, none))
        g_zero.append(jnp.where(mine, g, none))
    dq = [0.0, 0.0]
    for k_ref, km_ref, v_ref, dk_ref, dv_ref in parts:
        k, km, v = k_ref[0, :, lanes], km_ref[0], v_ref[0, :, lanes]
        k_t = k.T
        dk = dv = 0.0
        for head in range(2):
            mine = ~low if head else low
            scores = dot(jnp.where(mine, k, km), q_sides[head], NT)
            grads = dot(jnp.where(mine, v, none), g, NT)
            probs = jnp.exp2(scores * EXPO - lse_ref[0, pair, head : head + 1, :])
            grads = (probs * (grads - deltas[head])).astype(BF16)
            dv += dot(probs.astype(BF16), g_zero[head])
            dk += dot(grads, q_zero[head])
            dq[head] += dot(k_t[head * HEAD : (head + 1) * HEAD], grads)
        of(dk_ref)[:, lanes] = (dk * SCALE).astype(BF16)
        of(dv_ref)[:, lanes] = dv.astype(BF16)
    of(dq_ref)[:, lanes] = (jnp.concatenate(dq, axis=0) * SCALE).T.astype(BF16)


def attend_back_kernel(q_ref, qm_ref, o_ref, g_ref, lse_ref, ko_ref, kmo_ref, vo_ref, kr_ref, kmr_ref,
                       vr_ref, dq_ref, dko_ref, dvo_ref, dkr_ref, dvr_ref):
    parts = ((ko_ref, kmo_ref, vo_ref, dko_ref, dvo_ref), (kr_ref, kmr_ref, vr_ref, dkr_ref, dvr_ref))
    for pair in range(q_ref.shape[2] // PAIR):
        attend_back_pair(pair, low_lanes(), parts, q_ref, qm_ref, o_ref, g_ref, lse_ref, dq_ref)


def attend_back(q, qm, o, g, lse, own, rem):
    seqs, length, features = q.shape
    lanes = math.gcd(features, 2 * PAIR)
    other = rem[0].shape[1]
    own_spec, rem_spec = pair_spec(length, lanes), pair_spec(other, lanes)
    return pl.pallas_call(
        attend_back_kernel,
        grid=(seqs, features // lanes),
        in_specs=[own_spec, mask_spec(length), own_spec, own_spec, lse_spec(length, lanes)]
        + [own_spec, mask_spec(length), own_spec]
        + [rem_spec, mask_spec(other), rem_spec],
        out_specs=[own_spec] * 3 + [rem_spec] * 2,
        out_shape=[jax.ShapeDtypeStruct(q.shape, BF16)] * 3
        + [jax.ShapeDtypeStruct(rem[0].shape, BF16)] * 2,
        compiler_params=params(60),
        cost_estimate=cost(
            40 * q.size * (length + other), 2 * q.size * 14, q.size * (length + other) // HEAD
        ),
        name="attend_back",
    )(q, qm, o, g, lse, *own, *rem)


def gelu_and_slope(x):
    bell = jnp.exp2(x * x * (-0.5 * math.log2(math.e)))
    t = 1.0 / (1.0 + (0.3275911 / math.sqrt(2.0)) * jnp.abs(x))
    poly = 1.061405429 * t - 1.453152027
    poly = poly * t + 1.421413741
    poly = poly * t - 0.284496736
    poly = poly * t + 0.254829592
    tail = (0.5 * poly) * t * bell
    share = jnp.where(x >= 0.0, 1.0 - tail, tail)
    return x * share, share + x * bell * (1.0 / math.sqrt(2.0 * math.pi))


def mean(values):
    return jnp.sum(values, axis=-1, keepdims=True) * (1.0 / values.shape[-1])


def norm_parts(values):
    centred = values - mean(values)
    scale = lax.rsqrt(mean(centred * centred) + EPSILON)
    return centred * scale, scale


def norm_back(upper, normed, scale):
    return scale * (upper - mean(upper) - normed * mean(upper * normed))


def column_sum(values):
    return jnp.sum(values, axis=0, keepdims=True)


def feed_kernel(layout, tok_ref, att_ref, cot_ref, vec_ref, bu_ref, wo_ref, wu_ref, wd_ref,
                out_ref, bg_ref, ag_ref, vg_ref, dbu_ref, dwu_ref, dwd_ref, dwo_ref,
                act_s, din_s, first_t, feed_t, att_t, bg_s):
    tiles, ff_steps, chunk, wide, narrow = layout
    step = pl.program_id(0)
    tile = tok_ref.shape[0]
    hidden = act_s.shape[1]
    vec = [vec_ref[i : i + 1] for i in range(6)]
    out_bias, gain_one, shift_one, down_bias, gain_two, shift_two = vec

    @pl.when(step == 0)
    def _():
        vg_ref[...] = jnp.zeros_like(vg_ref)
        dbu_ref[...] = jnp.zeros_like(dbu_ref)

    @pl.when(step < tiles)
    def _():
        start = pl.multiple_of(step * tile, tile)
        rows = pl.ds(start, tile)
        att = att_ref[...]
        normed_one, scale_one = norm_parts(
            tok_ref[...].astype(F32) + (dot(att, wo_ref[...]) + out_bias)
        )
        first = normed_one * gain_one + shift_one
        first_low = first.astype(BF16)
        first_t[:, rows] = first_low.T
        att_t[:, rows] = att.T
        feed = jnp.zeros_like(first) + down_bias
        spans = [slice(c, c + chunk) for c in range(0, hidden, chunk)]
        ahead = dot(first_low, wu_ref[:, spans[0]])
        for i, cols in enumerate(spans):
            inner = ahead + bu_ref[:, cols]
            if i + 1 < len(spans):
                ahead = dot(first_low, wu_ref[:, spans[i + 1]])
            active, slope = gelu_and_slope(inner)
            active = active.astype(BF16)
            act_s[rows, cols] = active
            din_s[rows, cols] = slope.astype(BF16)
            feed += dot(active, wd_ref[cols])
        normed_two, scale_two = norm_parts(first + feed)
        out_ref[...] = (normed_two * gain_two + shift_two).astype(BF16)
        cot = cot_ref[...].astype(F32)
        second = norm_back(cot * gain_two, normed_two, scale_two)
        feed_low = second.astype(BF16)
        feed_t[:, rows] = feed_low.T
        back = second
        ahead = dot(feed_low, wd_ref[spans[0]], NT)
        for i, cols in enumerate(spans):
            inner = ahead
            if i + 1 < len(spans):
                ahead = dot(feed_low, wd_ref[spans[i + 1]], NT)
            inner = (inner * din_s[rows, cols].astype(F32)).astype(BF16)
            din_s[rows, cols] = inner
            dbu_ref[:, cols] += column_sum(inner.astype(F32))
            back += dot(inner, wu_ref[:, cols], NT)
        residual = norm_back(back * gain_one, normed_one, scale_one)
        branch_low = residual.astype(BF16)
        bg_ref[...] = branch_low
        bg_s[rows] = branch_low
        ag_ref[...] = dot(branch_low, wo_ref[...], NT).astype(BF16)
        for i, values in enumerate(
            (
                branch_low.astype(F32),
                back * normed_one,
                back,
                feed_low.astype(F32),
                cot * normed_two,
                cot,
            )
        ):
            vg_ref[i : i + 1] += column_sum(values)

    @pl.when((step >= tiles) & (step < tiles + ff_steps))
    def _():
        cols = pl.ds(pl.multiple_of((step - tiles) * wide, wide), wide)
        dwu = dot(first_t[...], din_s[:, cols]).astype(BF16)
        dwu_ref[...] = dwu.reshape(dwu_ref.shape)
        dwd_ref[...] = dot(feed_t[...], act_s[:, cols]).astype(BF16).T

    @pl.when(step >= tiles + ff_steps)
    def _():
        cols = pl.ds(pl.multiple_of((step - tiles - ff_steps) * narrow, narrow), narrow)
        dwo_ref[...] = dot(att_t[...], bg_s[:, cols]).astype(BF16)


def feed_both_ways(tokens, attended, cotangent, vectors, up_bias, wo, wu, wd, groups):
    rows, features = tokens.shape
    hidden = wu.shape[1]
    tile = math.gcd(rows, 256)
    tiles = rows // tile
    wide, narrow = features, math.gcd(features, 384)
    ff_steps, out_steps = hidden // wide, features // narrow
    layout = (tiles, ff_steps, math.gcd(hidden, 512), wide, narrow)
    blocked = (groups, ff_steps, features // groups, wide)
    row_spec = pl.BlockSpec((tile, features), lambda i: (jnp.minimum(i, tiles - 1), 0))

    def ff_at(i):
        return jnp.clip(i - tiles, 0, ff_steps - 1)

    return pl.pallas_call(
        functools.partial(feed_kernel, layout),
        grid=(tiles + ff_steps + out_steps,),
        in_specs=[row_spec] * 3
        + [whole_spec(a.shape) for a in (vectors, up_bias, wo, wu, wd)],
        out_specs=[row_spec] * 3
        + [
            pl.BlockSpec((8, features), lambda i: (0, 0)),
            pl.BlockSpec((1, hidden), lambda i: (0, 0)),
            pl.BlockSpec((groups, 1) + blocked[2:], lambda i: (0, ff_at(i), 0, 0)),
            pl.BlockSpec((wide, features), lambda i: (ff_at(i), 0)),
            pl.BlockSpec(
                (features, narrow),
                lambda i: (0, jnp.clip(i - tiles - ff_steps, 0, out_steps - 1)),
            ),
        ],
        out_shape=[jax.ShapeDtypeStruct(tokens.shape, BF16)] * 3
        + [
            jax.ShapeDtypeStruct((8, features), F32),
            jax.ShapeDtypeStruct((1, hidden), F32),
            jax.ShapeDtypeStruct(blocked, BF16),
            jax.ShapeDtypeStruct(wd.shape, BF16),
            jax.ShapeDtypeStruct(wo.shape, BF16),
        ],
        scratch_shapes=[
            pltpu.VMEM((rows, hidden), BF16),
            pltpu.VMEM((rows, hidden), BF16),
            pltpu.VMEM((features, rows), BF16),
            pltpu.VMEM((features, rows), BF16),
            pltpu.VMEM((features, rows), BF16),
            pltpu.VMEM((rows, features), BF16),
        ],
        compiler_params=params(60),
        cost_estimate=cost(
            6 * rows * features * (features + 2 * hidden),
            2 * (6 * rows * features + 4 * features * hidden + 2 * features * features),
            2 * rows * hidden,
        ),
        name="feed_both_ways",
    )(tokens, attended, cotangent, vectors, up_bias, wo, wu, wd)


def own_back_kernel(bg_ref, dq_ref, dk_ref, dv_ref, wq_ref, wk_ref, wv_ref, out_ref):
    total = bg_ref[0].astype(F32) + dot(dq_ref[0], wq_ref[...], NT)
    total += dot(dk_ref[0], wk_ref[...], NT)
    total += dot(dv_ref[0], wv_ref[...], NT)
    out_ref[0] = total.astype(BF16)


def rem_back_kernel(dk_ref, dv_ref, wk_ref, wv_ref, out_ref):
    total = dot(dk_ref[0], wk_ref[...], NT) + dot(dv_ref[0], wv_ref[...], NT)
    out_ref[0] = total.astype(BF16)


def tokens_back(kernel, rows, weights):
    seqs, length, features = rows[0].shape
    tile = math.gcd(length, 512)
    row_spec = pl.BlockSpec((1, tile, features), lambda s, i: (s, i, 0))
    size = rows[0].size
    return pl.pallas_call(
        kernel,
        grid=(seqs, length // tile),
        in_specs=[row_spec] * len(rows) + [whole_spec(w.shape) for w in weights],
        out_specs=row_spec,
        out_shape=jax.ShapeDtypeStruct(rows[0].shape, BF16),
        compiler_params=params(60),
        cost_estimate=cost(2 * size * features * len(weights), 2 * size * (1 + len(rows))),
        name="tokens_back",
    )(*rows, *weights)


def weights_back_kernel(tok_ref, rem_ref, dq_ref, dko_ref, dvo_ref, dkr_ref, dvr_ref,
                        wq_ref, wk_ref, wv_ref, bq_ref, bv_ref, tok_t, rem_t):
    @pl.when(pl.program_id(0) == 0)
    def _():
        tok_t[...] = tok_ref[...].T
        rem_t[...] = rem_ref[...].T

    wq_ref[...] = dot(tok_t[...], dq_ref[...]).astype(BF16)
    wk_ref[...] = (dot(tok_t[...], dko_ref[...]) + dot(rem_t[...], dkr_ref[...])).astype(BF16)
    wv_ref[...] = (dot(tok_t[...], dvo_ref[...]) + dot(rem_t[...], dvr_ref[...])).astype(BF16)
    bq_ref[...] = column_sum(dq_ref[...].astype(F32))
    bv_ref[...] = column_sum(dvo_ref[...].astype(F32)) + column_sum(dvr_ref[...].astype(F32))


def weights_back(tok, rem, dq, dko, dvo, dkr, dvr):
    rows, features = tok.shape
    others = rem.shape[0]
    wide = math.gcd(features, 256)
    own_spec = pl.BlockSpec((rows, wide), lambda j: (0, j))
    rem_spec = pl.BlockSpec((others, wide), lambda j: (0, j))
    bias_spec = pl.BlockSpec((1, wide), lambda j: (0, j))
    return pl.pallas_call(
        weights_back_kernel,
        grid=(features // wide,),
        in_specs=[
            whole_spec(tok.shape),
            whole_spec(rem.shape),
            own_spec,
            own_spec,
            own_spec,
            rem_spec,
            rem_spec,
        ],
        out_specs=[pl.BlockSpec((features, wide), lambda j: (0, j))] * 3 + [bias_spec] * 2,
        out_shape=[jax.ShapeDtypeStruct((features, features), BF16)] * 3
        + [jax.ShapeDtypeStruct((1, features), F32)] * 2,
        scratch_shapes=[
            pltpu.VMEM((features, rows), BF16),
            pltpu.VMEM((features, others), BF16),
        ],
        compiler_params=params(60),
        cost_estimate=cost(
            2 * features * features * (3 * rows + 2 * others),
            2 * (4 * tok.size + 3 * rem.size + 3 * features * features),
        ),
        name="weights_back",
    )(tok, rem, dq, dko, dvo, dkr, dvr)


def halve(value, axis, bit):
    size = lax.axis_size(axis)
    mine = (lax.axis_index(axis) >> bit) & 1
    pairs = value.reshape((value.shape[0] // 2, 2) + value.shape[1:])
    keep = lax.dynamic_index_in_dim(pairs, mine, 1, keepdims=False)
    send = lax.dynamic_index_in_dim(pairs, 1 - mine, 1, keepdims=False)
    came = lax.ppermute(send, axis, [(i, i ^ (1 << bit)) for i in range(size)])
    return keep.astype(F32) + came.astype(F32)


def scatter_sum(value, low=True):
    dp, blk = lax.axis_size("dp"), lax.axis_size("blk")
    if dp & (dp - 1) or blk & (blk - 1):
        return lax.psum_scatter(
            value.astype(F32), ("dp", "blk"), scatter_dimension=0, tiled=True
        )
    kept = value.dtype
    each = value.shape[0] // (dp * blk)
    value = value.reshape((dp, blk * each) + value.shape[1:])
    for bit in range(dp.bit_length() - 1):
        value = halve(value, "dp", bit).astype(kept)
    value = value.reshape((blk, each) + value.shape[2:])
    for bit in range(blk.bit_length() - 1):
        value = halve(value, "blk", bit)
        value = value if (2 << bit) == blk else value.astype(kept)
    return value.reshape(value.shape[1:]).astype(F32)


class Unit:
    def __init__(self, parts, rows, columns, halves, order, outs):
        self.parts, self.rows, self.columns = parts, rows, columns
        self.halves, self.order, self.outs = halves, order, outs
        self.half = rows // (2 * halves)
        self.last_type = BF16 if (rows // 2) % 16 == 0 else F32


def timetable(units, bits, seqs, groups, slots_each, slot_us, token_us):
    free, pending, table = {}, [], []
    slots = seqs * groups * slots_each

    def launch(key, now):
        kind, which, step = key
        if kind == "tokens":
            link, us = "blk", token_us
        elif kind == "vectors":
            link, us = None, 1.0
        else:
            unit = units[which]
            bit = unit.order[step] if step < bits else "blk"
            size = unit.rows * unit.columns * (1 << max(bits - 1 - step, 0)) * 2e-5
            size = size * 0.5 if step == bits else size
            link = {0: "core", 1: "y"}.get(bit, bit if bit == "blk" else "z")
            us = size * 2 * (1.0 if bit == "blk" or bit < 3 else 2.0)
            us = us / 8 if bit == 0 else us
        start = max(now, free.get(link, 0.0))
        if link:
            free[link] = start + us
        pending.append((start + us + 1.5, key))

    for u, unit in enumerate(units):
        if unit.parts:
            launch(("unit", u, 0), 0.0)
    first_group = sum(1 for unit in units if unit.parts)
    now = 0.0
    while len(table) < slots or pending:
        slot = len(table)
        if slot < slots:
            now = (slot + 1) * slot_us
            step, within = divmod(slot, slots_each)
            if within == slots_each - 1:
                s, h = divmod(step, groups)
                if h == groups - 1:
                    launch(("tokens", s, 0), now)
                if s == seqs - 1:
                    launch(("unit", first_group + h, 0), now)
                if step == seqs * groups - 1:
                    launch(("vectors", 0, 0), now)
            due = sorted(p for p in pending if p[0] <= now)
        else:
            due = [min(pending)]
            now = max(now + 0.3, due[0][0])
        table.append([key for _, key in due])
        for found in due:
            pending.remove(found)
            kind, which, step = found[1]
            if kind != "tokens" and step < bits:
                launch((kind, which, step + 1), now)
    return table[:slots], [key for keys in table[slots:] for key in keys]


def back_kernel(units, bits, groups, table, tail, n_out, *refs):
    (q_ref, qm_ref, o_ref, g_ref, lse_ref, ko_ref, kmo_ref, vo_ref, kr_ref, kmr_ref, vr_ref,
     bg_ref, tok_ref, rem_ref, wq_ref, wk_ref, wv_ref, vg_ref, vu_ref) = refs[:19]
    sources, refs = refs[19:22], list(refs[22:])
    tokens_out, *outs = refs[:n_out]
    refs = refs[n_out:]
    kept = [refs.pop(0) for _ in units]
    landed = [[refs.pop(0) for _ in range(bits)] for _ in units]
    wide = [refs.pop(0) for _ in units]
    parting = [refs.pop(0) for _ in units]
    last = [refs.pop(0) for _ in units]
    (weight_sum, group_src, own_sum, rem_sum, tok_t, rem_t, dq_s, dko_s, dvo_s, dkr_s, dvr_s,
     rem_out, rem_in, vec, vec_in, bias_sum, send_sem, recv_sem, local_sem) = refs
    step = pl.program_id(0)
    steps = pl.num_programs(0)
    s, h = step // groups, step % groups
    seqs = tokens_out.shape[0]
    features = tok_ref.shape[2]
    me, side = lax.axis_index("dp"), lax.axis_index("blk")
    own = [(me // (1 << bit)) % 2 for bit in range(bits)]
    partner = [{"dp": me + (1 << bit) * (1 - 2 * own[bit])} for bit in range(bits)]
    partner.append({"blk": 1 - side})
    first_group = sum(1 for unit in units if unit.parts)
    lead = (slice(None),) * (bits - 1)

    sems = {}
    for u, unit in enumerate(units):
        for k in range(bits + 1):
            for p in range(len(unit.parts) if unit.parts and k == 0 else 1):
                sems["unit", u, k, p] = len(sems)
    for k in range(bits + 1):
        sems["vectors", 0, k, 0] = len(sems)
    for k in range(seqs):
        sems["tokens", k, 0, 0] = len(sems)

    def remote(source, target, device, key):
        return pltpu.make_async_remote_copy(
            src_ref=source,
            dst_ref=target,
            send_sem=send_sem.at[sems[key]],
            recv_sem=recv_sem.at[sems[key]],
            device_id=device,
            device_id_type=pl.DeviceIdType.MESH,
        )

    def spot(unit, k, value):
        found = []
        for bit in range(bits - 1, 0, -1):
            at = unit.order.index(bit)
            found.append(own[bit] if at < k else value if at == k else slice(None))
        return tuple(found)

    def copies(kind, which, k):
        if kind == "tokens":
            return [remote(rem_out.at[which], rem_in.at[which], partner[bits], (kind, which, 0, 0))]
        if kind == "vectors":
            return [remote(vec.at[k], vec_in.at[k], partner[k], (kind, 0, k, 0))]
        u, unit = which, units[which]
        if k == bits:
            return [remote(parting[u], last[u], partner[bits], (kind, u, k, 0))]
        if k:
            bit = unit.order[k]
            source = kept[u].at[spot(unit, k, 1 - own[bit])]
            return [remote(source, landed[u][k], partner[bit], (kind, u, k, 0))]
        if not unit.parts:
            source = group_src.at[(u - first_group,) + lead + (1 - own[0],)]
            return [remote(source, landed[u][0], partner[0], (kind, u, 0, 0))]
        found, row = [], 0
        for p, (source, first, rows) in enumerate(unit.parts):
            found.append(
                remote(
                    sources[source].at[lead + (1 - own[0], pl.ds(first, rows))],
                    landed[u][0].at[lead + (pl.ds(row, rows),)],
                    partner[0],
                    (kind, u, 0, p),
                )
            )
            row += rows
        return found

    def near_copies(u):
        found, row = [], 0
        for p, (source, first, rows) in enumerate(units[u].parts):
            found.append(
                pltpu.make_async_copy(
                    sources[source].at[lead + (own[0], pl.ds(first, rows))],
                    kept[u].at[lead + (pl.ds(row, rows),)],
                    local_sem.at[sems["unit", u, 0, p]],
                )
            )
            row += rows
        return found

    def launch(*key):
        for copy in copies(*key):
            copy.start()

    def halves_of(u, which):
        unit = units[u]
        return [
            wide[u][pl.ds(pl.multiple_of(i * 2 * unit.half + which * unit.half, 8), unit.half)]
            for i in range(unit.halves)
        ]

    def receive(kind, which, k):
        for copy in copies(kind, which, k):
            copy.wait_recv()
        if kind == "tokens":
            total = tokens_out[which].astype(F32) + rem_in[which].astype(F32)
            tokens_out[which] = total.astype(BF16)
            return
        if kind == "vectors":
            vec[k + 1] = vec[k] + vec_in[k]
            if k < bits:
                launch(kind, 0, k + 1)
            return
        u, unit = which, units[which]
        if k == bits:
            for i, (mine, (out, rows, columns)) in enumerate(zip(halves_of(u, side), unit.outs)):
                came = last[u][...].astype(F32)[i * unit.half : (i + 1) * unit.half]
                outs[out][rows, columns] = mine + came
            return
        if unit.parts and k == 0:
            for copy in near_copies(u):
                copy.wait()
        place = spot(unit, k, own[unit.order[k]])
        open_at = [i for i, at in enumerate(place) if isinstance(at, slice)]

        def add(n, carry):
            at, where = list(place), []
            for digit, i in enumerate(open_at):
                at[i] = (n // (1 << (len(open_at) - 1 - digit))) % 2
                where.append(at[i])
            at = tuple(at)
            if unit.parts or k:
                mine = kept[u][at]
            else:
                mine = group_src[(u - first_group,) + at + (own[0],)]
            total = mine.astype(F32) + landed[u][k][tuple(where)].astype(F32)
            if k == bits - 1:
                wide[u][...] = total
            else:
                kept[u][at] = total.astype(BF16)
            return carry

        if open_at:
            lax.fori_loop(0, 1 << len(open_at), add, 0)
        else:
            add(0, 0)
        if k == bits - 1:
            pieces = halves_of(u, 1 - side)
            pieces = pieces[0] if len(pieces) == 1 else jnp.concatenate(pieces, axis=0)
            parting[u][...] = pieces.astype(unit.last_type)
        launch(kind, u, k + 1)

    @pl.when(step == 0)
    def _():
        barrier = pltpu.get_barrier_semaphore()
        for other in partner:
            pl.semaphore_signal(barrier, inc=1, device_id=other, device_id_type=pl.DeviceIdType.MESH)
        pl.semaphore_wait(barrier, bits + 1)
        for u, unit in enumerate(units):
            if unit.parts:
                launch("unit", u, 0)
                for copy in near_copies(u):
                    copy.start()
        weight_sum[...] = jnp.zeros_like(weight_sum)
        bias_sum[...] = jnp.zeros_like(bias_sum)

    @pl.when(h == 0)
    def _():
        tok_t[...] = tok_ref[0].T
        rem_t[...] = rem_ref[0].T
        own_sum[...] = bg_ref[0].astype(F32)
        rem_sum[...] = jnp.zeros_like(rem_sum)

    low = low_lanes()
    parts = ((ko_ref, kmo_ref, vo_ref, dko_s, dvo_s), (kr_ref, kmr_ref, vr_ref, dkr_s, dvr_s))
    pairs = q_ref.shape[2] // PAIR
    for pair in range(pairs):
        attend_back_pair(pair, low, parts, q_ref, qm_ref, o_ref, g_ref, lse_ref, dq_s)
        if pair == pairs - 1:
            width = q_ref.shape[2]
            columns = pl.ds(pl.multiple_of(h * width, width), width)
            wq, wk, wv = wq_ref[:, columns], wk_ref[:, columns], wv_ref[:, columns]
            dq, dko, dvo, dkr, dvr = dq_s[...], dko_s[...], dvo_s[...], dkr_s[...], dvr_s[...]
            own_sum[...] += dot(dq, wq, NT) + dot(dko, wk, NT) + dot(dvo, wv, NT)
            rem_sum[...] += dot(dkr, wk, NT) + dot(dvr, wv, NT)
            weight_sum[h, 0] += dot(tok_t[...], dq)
            weight_sum[h, 1] += dot(tok_t[...], dko) + dot(rem_t[...], dkr)
            weight_sum[h, 2] += dot(tok_t[...], dvo) + dot(rem_t[...], dvr)
            bias_sum[h, 0:1] += column_sum(dq.astype(F32))
            bias_sum[h, 1:2] += column_sum(dvo.astype(F32)) + column_sum(dvr.astype(F32))

            for at in range(seqs):

                @pl.when((h == groups - 1) & (s == at))
                def _(at=at):
                    tokens_out[at] = own_sum[...].astype(BF16)
                    rem_out[at] = rem_sum[...].astype(BF16)
                    launch("tokens", at, 0)

            for at in range(groups):

                @pl.when((s == seqs - 1) & (h == at))
                def _(at=at):
                    rows = features // (1 << bits)
                    for i in range(3):
                        piece = weight_sum[at, i].astype(BF16)
                        piece = piece.reshape((2,) * bits + (rows, piece.shape[1]))
                        group_src[(at,) + (slice(None),) * bits + (slice(i * rows, (i + 1) * rows),)] = piece
                    launch("unit", first_group + at, 0)

            @pl.when(step == steps - 1)
            def _():
                vec[0] = jnp.zeros_like(vec[0])
                vec[0, 0:6] = vg_ref[0:6]
                for at in range(groups):
                    vec[0, 6:8, at * width : (at + 1) * width] = bias_sum[at, 0:2]
                blocks = vu_ref.shape[1] // features
                for at in range(blocks):
                    vec[0, 8 + at : 9 + at] = vu_ref[:, at * features : (at + 1) * features]
                launch("vectors", 0, 0)

        for at in range(seqs * groups):
            keys = table[at * pairs + pair]
            if keys:

                @pl.when(step == at)
                def _(keys=keys):
                    for key in keys:
                        receive(*key)

    @pl.when(step == steps - 1)
    def _():
        for key in tail:
            receive(*key)
        shards = (1 << bits) * 2
        place = me * 2 + side
        share = features // shards
        rows = pltpu.roll(vec[bits + 1, 0:8], (shards - place) * share % features, 1)
        outs[-1][0:8] = rows[:, :PAIR]
        share = vu_ref.shape[1] // shards
        each = features // share
        row = vec[bits + 1, pl.ds(8 + place // each, 1)]
        rows = pltpu.roll(jnp.broadcast_to(row, (8, features)), (each - place % each) * share % features, 1)
        outs[-1][8:16] = rows[:, :PAIR]
        for u in range(len(units)):
            for k in range(bits + 1):
                for copy in copies("unit", u, k):
                    copy.wait_send()
        for k in range(bits + 1):
            copies("vectors", 0, k)[0].wait_send()
        for k in range(seqs):
            copies("tokens", k, 0)[0].wait_send()


def back_and_sum(q, qm, o, g, lse, own, rem, bg, tokens, rem_tokens, weights, dwd, dwu, dwo, vg, vu):
    dp = lax.axis_size("dp")
    bits = dp.bit_length() - 1
    seqs, length, features = q.shape
    other = rem[0].shape[1]
    width = math.gcd(features, 2 * PAIR)
    groups, pairs = features // width, width // PAIR
    low, deep, blocks = features // dp, dwd.shape[0] // dp, dwu.shape[1]
    lead = (2,) * bits
    sources = [
        dwd.reshape(lead + (deep, features)),
        dwu.reshape(lead + (-1, features)),
        dwo.reshape(lead + (low, features)),
    ]
    order = tuple(range(bits))
    every = slice(None)
    units = []
    for i in range(2):
        at, quarter = slice(i * deep // 4, (i + 1) * deep // 4), deep // 4
        parts = [(0, i * quarter, quarter), (0, (2 + i) * quarter, quarter)]
        units.append(Unit(parts, 2 * quarter, features, 1, order, [(0, at, every)]))
    for i in range(2):
        found = range(i * blocks // 2, (i + 1) * blocks // 2)
        units.append(
            Unit(
                [(1, b * low, low) for b in found],
                len(found) * low,
                features,
                len(found),
                order,
                [(1, every, slice(b * features, (b + 1) * features)) for b in found],
            )
        )
    units.append(Unit([(2, 0, low)], low, features, 1, order, [(2, every, every)]))
    for h in range(groups):
        columns = slice(h * width, (h + 1) * width)
        units.append(Unit(None, 3 * low, width, 3, order, [(3 + i, every, columns) for i in range(3)]))
    table, tail = timetable(units, bits, seqs, groups, pairs, 4.3, length * features * 4e-5)

    half = low // 2
    out_shape = [
        jax.ShapeDtypeStruct(q.shape, BF16),
        jax.ShapeDtypeStruct((deep // 2, features), F32),
        jax.ShapeDtypeStruct((half, blocks * features), F32),
        *(jax.ShapeDtypeStruct((half, features), F32) for _ in range(4)),
        jax.ShapeDtypeStruct((16, PAIR), F32),
    ]
    tops = lead[1:]
    scratch = [pltpu.VMEM(tops + (u.rows, u.columns), BF16) for u in units]
    for u in units:
        scratch += [pltpu.VMEM(tops[k:] + (u.rows, u.columns), BF16) for k in range(bits)]
    scratch += [pltpu.VMEM((u.rows, u.columns), F32) for u in units]
    scratch += [pltpu.VMEM((u.rows // 2, u.columns), u.last_type) for u in units] * 2
    count = sum((len(u.parts) if u.parts else 1) + bits for u in units) + bits + 1 + seqs
    scratch += [
        pltpu.VMEM((groups, 3, features, width), F32),
        pltpu.VMEM((groups,) + lead + (3 * low, width), BF16),
        pltpu.VMEM((length, features), F32),
        pltpu.VMEM((other, features), F32),
        pltpu.VMEM((features, length), BF16),
        pltpu.VMEM((features, other), BF16),
        *(pltpu.VMEM((length, width), BF16) for _ in range(3)),
        *(pltpu.VMEM((other, width), BF16) for _ in range(2)),
        pltpu.VMEM((seqs, other, features), BF16),
        pltpu.VMEM((seqs, other, features), BF16),
        pltpu.VMEM((bits + 2, 16, features), F32),
        pltpu.VMEM((bits + 1, 16, features), F32),
        pltpu.VMEM((groups, 8, width), F32),
        *(pltpu.SemaphoreType.DMA((count,)) for _ in range(3)),
    ]

    def pair_at(rows):
        return pl.BlockSpec((1, rows, width), lambda i: (i // groups, 0, i % groups))

    def mask_at(rows):
        return pl.BlockSpec((1, rows, PAIR), lambda i: (i // groups, 0, 0))

    def rows_at(rows):
        return pl.BlockSpec(
            (1, rows, features), lambda i: (i // groups, 0, 0), pipeline_mode=pl.Buffered(1)
        )

    return pl.pallas_call(
        functools.partial(back_kernel, units, bits, groups, table, tail, len(out_shape)),
        grid=(seqs * groups,),
        in_specs=[
            pair_at(length),
            mask_at(length),
            pair_at(length),
            pair_at(length),
            pl.BlockSpec((1, pairs, 8, length), lambda i: (i // groups, i % groups, 0, 0)),
            pair_at(length),
            mask_at(length),
            pair_at(length),
            pair_at(other),
            mask_at(other),
            pair_at(other),
            rows_at(length),
            rows_at(length),
            rows_at(other),
        ]
        + [whole_spec(w.shape) for w in weights + (vg, vu)]
        + [pl.BlockSpec(memory_space=pl.ANY)] * 3,
        out_specs=[pl.BlockSpec(s.shape, lambda i, n=len(s.shape): (0,) * n, pipeline_mode=pl.Buffered(1)) for s in out_shape],
        out_shape=out_shape,
        scratch_shapes=scratch,
        compiler_params=pltpu.CompilerParams(
            collective_id=1, has_side_effects=True, vmem_limit_bytes=63 * MIB
        ),
        cost_estimate=cost(
            40 * q.size * (length + other), 2 * q.size * 14, q.size * (length + other) // HEAD
        ),
        name="back_and_sum",
    )(q, qm, o, g, lse, *own, *rem, bg, tokens, rem_tokens, *weights, vg, vu, *sources)


def back_plainly(q, qm, o, g, lse, own, rem, bg, tokens, rem_tokens, weights, dwd, dwu, dwo, vg, vu):
    seqs, length, features = q.shape
    dp, blk = lax.axis_size("dp"), lax.axis_size("blk")
    dq, dko, dvo, dkr, dvr = attend_back(q, qm, o, g, lse, own, rem)
    rem_gradient = tokens_back(rem_back_kernel, (dkr, dvr), weights[1:])
    came = [
        lax.ppermute(part, "blk", [((i + r) % blk, i) for i in range(blk)])
        for r, part in enumerate(jnp.split(rem_gradient, blk - 1, axis=1), 1)
    ]
    flat = [v.reshape(-1, features) for v in (tokens, rem_tokens, dq, dko, dvo, dkr, dvr)]
    dwq, dwk, dwv, dbq, dbv = weights_back(*flat)
    total = tokens_back(own_back_kernel, (bg, dq, dko, dvo), weights).astype(F32)
    for part in came:
        total += part.astype(F32)
    dwu = jnp.moveaxis(dwu[0], 0, 1).reshape(features, -1)
    summed = [scatter_sum(w) for w in (dwd, dwu, dwo, dwq, dwk, dwv)]
    rows = [vg[i] for i in range(6)] + [dbq, dbv, vu]
    rows = [scatter_sum(v.reshape(dp * blk, -1)) for v in rows]
    return [total.astype(BF16)] + summed + [[v[0] for v in rows]]


def body(
    tokens,
    query_weight,
    query_bias,
    key_weight,
    value_weight,
    value_bias,
    out_weight,
    out_bias,
    gain_one,
    shift_one,
    up_weight,
    up_bias,
    down_weight,
    down_bias,
    gain_two,
    shift_two,
    group_ids,
    valid_mask,
    cotangent,
):
    seqs, length, features = tokens.shape
    rows = seqs * length
    blk = lax.axis_size("blk")

    def from_others(value):
        found = [
            lax.ppermute(value, "blk", [(i, (i + r) % blk) for i in range(blk)])
            for r in range(1, blk)
        ]
        return found[0] if len(found) == 1 else jnp.concatenate(found, axis=1)

    codes = jnp.where(valid_mask == 1, group_ids, -1).astype(BF16)
    rem_tokens = from_others(tokens)
    rem_codes = from_others(codes).astype(jnp.int32)
    own_codes = codes.astype(jnp.int32)

    slot = jnp.arange(PAIR, dtype=jnp.int32) % HEAD

    def key_mask(code):
        return jnp.where(code[:, :, None] == slot, 0.0, MASKED).astype(BF16)

    query_mask = (group_ids[:, :, None] == slot).astype(BF16)
    dp = lax.axis_size("dp")
    by_kernel = blk == 2 and dp & (dp - 1) == 0 and dp > 1 and (features // dp) % 16 == 0

    biases = jnp.concatenate(
        [query_bias[None], value_bias[None], jnp.zeros((6, features), BF16)], axis=0
    ).astype(F32)
    queries, own_keys, own_values = project(
        tokens, biases, (query_weight, key_weight, value_weight)
    )
    rem_keys, rem_values = project(rem_tokens, biases, (key_weight, value_weight))
    own = (own_keys, key_mask(own_codes), own_values)
    rem = (rem_keys, key_mask(rem_codes), rem_values)
    attended, lse = attend(queries, query_mask, own, rem)

    vectors = jnp.stack(
        [out_bias, gain_one, shift_one, down_bias, gain_two, shift_two, out_bias, out_bias]
    ).astype(F32)
    block_out, branch_gradient, attended_gradient, vector_gradients, up_bias_gradient, dwu, dwd, dwo = (
        feed_both_ways(
            tokens.reshape(rows, features),
            attended.reshape(rows, features),
            cotangent.reshape(rows, features),
            vectors,
            up_bias.astype(F32)[None],
            out_weight,
            up_weight,
            down_weight,
            dp if by_kernel else 1,
        )
    )

    finish = back_and_sum if by_kernel else back_plainly
    tokens_gradient, dwd, dwu, dwo, dwq, dwk, dwv, rows_left = finish(
        queries,
        query_mask,
        attended,
        attended_gradient.reshape(tokens.shape),
        lse,
        own,
        rem,
        branch_gradient.reshape(tokens.shape),
        tokens,
        rem_tokens,
        (query_weight, key_weight, value_weight),
        dwd,
        dwu,
        dwo,
        vector_gradients,
        up_bias_gradient,
    )
    if by_kernel:
        share, wide = features // (dp * blk), up_bias.size // (dp * blk)
        rows_left = [rows_left[i, :share] for i in range(8)] + [rows_left[8, :wide]]
    dbo, dg1, ds1, dbd, dg2, ds2, dbq, dbv, dbu = rows_left
    return (
        block_out.reshape(tokens.shape),
        tokens_gradient,
        dwq,
        dbq,
        dwk,
        dwv,
        dbv,
        dwo,
        dbo,
        dg1,
        ds1,
        dwu,
        dbu,
        dwd,
        dbd,
        dg2,
        ds2,
    )


def solution(mesh):
    rows, shared, pair = P("dp", "blk", None), P(), P("dp", "blk")
    matrix, vector = P(("dp", "blk"), None), P(("dp", "blk"))
    return jax.shard_map(
        body,
        mesh=mesh,
        in_specs=(rows,) + (shared,) * 15 + (pair, pair, rows),
        out_specs=(
            rows,
            rows,
            matrix,
            vector,
            matrix,
            matrix,
            vector,
            matrix,
            vector,
            vector,
            vector,
            matrix,
            vector,
            matrix,
            vector,
            vector,
            vector,
        ),
        check_vma=False,
    )
```

```python
import functools
import math

import jax
import jax.numpy as jnp
from jax import lax
from jax.experimental import pallas as pl
from jax.experimental.pallas import tpu as pltpu
from jax.sharding import PartitionSpec as P

HEAD = 64
PAIR = 2 * HEAD
EPSILON = 1e-12
MASKED = -1e30
FLOOR = -3e38
SCALE = HEAD**-0.5
EXPO = SCALE * math.log2(math.e)
NN = (((1,), (0,)), ((), ()))
NT = (((1,), (1,)), ((), ()))
F32 = jnp.float32
BF16 = jnp.bfloat16
MIB = 1 << 20


def dot(left, right, dims=NN):
    return lax.dot_general(left, right, dims, preferred_element_type=F32)


def whole_spec(shape):
    return pl.BlockSpec(shape, lambda *_: (0,) * len(shape), pipeline_mode=pl.Buffered(1))


def params(limit):
    return pltpu.CompilerParams(vmem_limit_bytes=limit * MIB)


def cost(flops, touched, exps=0):
    return pl.CostEstimate(flops=int(flops), bytes_accessed=int(touched), transcendentals=int(exps))


def project_kernel(has_query, *refs):
    if has_query:
        x_ref, bias_ref, wq_ref, wk_ref, wv_ref, q_ref, k_ref, v_ref = refs
    else:
        x_ref, bias_ref, wk_ref, wv_ref, k_ref, v_ref = refs
    x = x_ref[0]
    if has_query:
        q_ref[0] = (dot(x, wq_ref[...]) + bias_ref[0:1]).astype(BF16)
    k_ref[0] = dot(x, wk_ref[...]).astype(BF16)
    v_ref[0] = (dot(x, wv_ref[...]) + bias_ref[1:2]).astype(BF16)


def project(x, bias, weights):
    seqs, length, features = x.shape
    tile = math.gcd(length, 512)
    grid = (seqs, length // tile)
    row_spec = pl.BlockSpec((1, tile, features), lambda s, i: (s, i, 0))
    return pl.pallas_call(
        functools.partial(project_kernel, len(weights) == 3),
        grid=grid,
        in_specs=[row_spec, whole_spec(bias.shape)] + [whole_spec(w.shape) for w in weights],
        out_specs=[row_spec] * len(weights),
        out_shape=[jax.ShapeDtypeStruct(x.shape, BF16)] * len(weights),
        compiler_params=params(60),
        cost_estimate=cost(
            2 * x.size * features * len(weights), 2 * x.size * (1 + len(weights))
        ),
        name="project",
    )(x, bias, *weights)


def low_lanes():
    return lax.broadcasted_iota(jnp.int32, (1, PAIR), 1) < HEAD


def attend_group(q, qm, sources, o_ref, lse_ref):
    length = q.shape[0]
    tile = math.gcd(length, 256)
    low = low_lanes()
    one = jnp.ones((1, PAIR), BF16)
    todo = [
        (pair, row, head)
        for pair in range(q.shape[1] // PAIR)
        for row in range(0, length, tile)
        for head in range(2)
    ]

    def lanes_of(pair):
        return slice(pair * PAIR, (pair + 1) * PAIR)

    def mine_of(head):
        return ~low if head else low

    def scores_of(pair, row, head):
        mine, lanes = mine_of(head), lanes_of(pair)
        q_side = jnp.where(mine, q[row : row + tile, lanes], qm[row : row + tile])
        return [dot(q_side, jnp.where(mine, k[:, lanes], km), NT) for k, km, _ in sources]

    ahead = scores_of(*todo[0])
    for i, (pair, row, head) in enumerate(todo):
        scores = ahead
        if i + 1 < len(todo):
            ahead = scores_of(*todo[i + 1])
        top = functools.reduce(
            jnp.maximum, [jnp.max(part, axis=-1, keepdims=True) for part in scores]
        )
        weights = [jnp.exp2((part - top) * EXPO).astype(BF16) for part in scores]
        total = sum(
            dot(w, jnp.where(mine_of(head), v[:, lanes_of(pair)], one))
            for w, (_, _, v) in zip(weights, sources)
        )
        if head == 0:
            earlier, earlier_top = total, top
            continue
        totals = pltpu.roll(jnp.where(low, total, earlier), HEAD, 1)
        rows = slice(row, row + tile)
        o_ref[rows, lanes_of(pair)] = (jnp.where(low, earlier, total) / totals).astype(BF16)
        lse = (jnp.where(low, earlier_top, top) * EXPO + jnp.log2(totals)).T
        lse_ref[pair, 0:1, rows] = lse[0:1]
        lse_ref[pair, 1:2, rows] = lse[HEAD : HEAD + 1]


def attend_kernel(q_ref, qm_ref, ko_ref, kmo_ref, vo_ref, kr_ref, kmr_ref, vr_ref, o_ref, lse_ref):
    sources = [(ko_ref[0], kmo_ref[0], vo_ref[0]), (kr_ref[0], kmr_ref[0], vr_ref[0])]
    attend_group(q_ref[0], qm_ref[0], sources, o_ref.at[0], lse_ref.at[0])


def pair_spec(length, lanes):
    return pl.BlockSpec((1, length, lanes), lambda s, h: (s, 0, h))


def mask_spec(length):
    return pl.BlockSpec((1, length, PAIR), lambda s, h: (s, 0, 0))


def lse_spec(length, lanes):
    return pl.BlockSpec((1, lanes // PAIR, 8, length), lambda s, h: (s, h, 0, 0))


def attend(q, qm, own, rem):
    seqs, length, features = q.shape
    lanes = math.gcd(features, 2 * PAIR)
    other = rem[0].shape[1]
    own_spec, rem_spec = pair_spec(length, lanes), pair_spec(other, lanes)
    return pl.pallas_call(
        attend_kernel,
        grid=(seqs, features // lanes),
        in_specs=[own_spec, mask_spec(length)]
        + [own_spec, mask_spec(length), own_spec]
        + [rem_spec, mask_spec(other), rem_spec],
        out_specs=[own_spec, lse_spec(length, lanes)],
        out_shape=[
            jax.ShapeDtypeStruct(q.shape, BF16),
            jax.ShapeDtypeStruct((seqs, features // PAIR, 8, length), F32),
        ],
        compiler_params=params(60),
        cost_estimate=cost(
            16 * q.size * (length + other), 2 * q.size * 6, q.size * (length + other) // HEAD
        ),
        name="attend",
    )(q, qm, *own, *rem)


def attend_back_pair(pair, low, parts, q_ref, qm_ref, o_ref, g_ref, lse_ref, dq_ref):
    def of(ref):
        return ref.at[0] if len(ref.shape) == 3 else ref

    lanes = slice(pair * PAIR, (pair + 1) * PAIR)
    q, g, qm = q_ref[0, :, lanes], g_ref[0, :, lanes], qm_ref[0]
    none = jnp.zeros((1, PAIR), BF16)
    product = g.astype(F32) * o_ref[0, :, lanes].astype(F32)
    deltas, q_sides, q_zero, g_zero = [], [], [], []
    for head in range(2):
        mine = ~low if head else low
        deltas.append(
            lax.dot_general(
                jnp.broadcast_to(jnp.where(mine, 1.0, 0.0).astype(F32), (8, PAIR)),
                product,
                NT,
                precision=lax.Precision.HIGHEST,
                preferred_element_type=F32,
            )[0:1]
        )
        q_sides.append(jnp.where(mine, q, qm))
        q_zero.append(jnp.where(mine, q, none))
        g_zero.append(jnp.where(mine, g, none))
    keys = [(k_ref[0, :, lanes], km_ref[0], v_ref[0, :, lanes]) for k_ref, km_ref, v_ref, _, _ in parts]
    todo = [(part, head) for part in range(len(parts)) for head in range(2)]

    def products(part, head):
        mine = ~low if head else low
        k, km, v = keys[part]
        return (
            dot(jnp.where(mine, k, km), q_sides[head], NT),
            dot(jnp.where(mine, v, none), g, NT),
        )

    dq = [0.0, 0.0]
    ahead = products(*todo[0])
    for i, (part, head) in enumerate(todo):
        scores, grads = ahead
        if i + 1 < len(todo):
            ahead = products(*todo[i + 1])
        if head == 0:
            k_t = keys[part][0].T
            dk = dv = 0.0
        probs = jnp.exp2(scores * EXPO - lse_ref[0, pair, head : head + 1, :])
        grads = (probs * (grads - deltas[head])).astype(BF16)
        dv += dot(probs.astype(BF16), g_zero[head])
        dk += dot(grads, q_zero[head])
        dq[head] += dot(k_t[head * HEAD : (head + 1) * HEAD], grads)
        if head == 1:
            of(parts[part][3])[:, lanes] = (dk * SCALE).astype(BF16)
            of(parts[part][4])[:, lanes] = dv.astype(BF16)
    of(dq_ref)[:, lanes] = (jnp.concatenate(dq, axis=0) * SCALE).T.astype(BF16)


def attend_back_kernel(q_ref, qm_ref, o_ref, g_ref, lse_ref, ko_ref, kmo_ref, vo_ref, kr_ref, kmr_ref,
                       vr_ref, dq_ref, dko_ref, dvo_ref, dkr_ref, dvr_ref):
    parts = ((ko_ref, kmo_ref, vo_ref, dko_ref, dvo_ref), (kr_ref, kmr_ref, vr_ref, dkr_ref, dvr_ref))
    for pair in range(q_ref.shape[2] // PAIR):
        attend_back_pair(pair, low_lanes(), parts, q_ref, qm_ref, o_ref, g_ref, lse_ref, dq_ref)


def attend_back(q, qm, o, g, lse, own, rem):
    seqs, length, features = q.shape
    lanes = math.gcd(features, 2 * PAIR)
    other = rem[0].shape[1]
    own_spec, rem_spec = pair_spec(length, lanes), pair_spec(other, lanes)
    return pl.pallas_call(
        attend_back_kernel,
        grid=(seqs, features // lanes),
        in_specs=[own_spec, mask_spec(length), own_spec, own_spec, lse_spec(length, lanes)]
        + [own_spec, mask_spec(length), own_spec]
        + [rem_spec, mask_spec(other), rem_spec],
        out_specs=[own_spec] * 3 + [rem_spec] * 2,
        out_shape=[jax.ShapeDtypeStruct(q.shape, BF16)] * 3
        + [jax.ShapeDtypeStruct(rem[0].shape, BF16)] * 2,
        compiler_params=params(60),
        cost_estimate=cost(
            40 * q.size * (length + other), 2 * q.size * 14, q.size * (length + other) // HEAD
        ),
        name="attend_back",
    )(q, qm, o, g, lse, *own, *rem)


def gelu_and_slope(x):
    bell = jnp.exp2(x * x * (-0.5 * math.log2(math.e)))
    t = 1.0 / (1.0 + (0.3275911 / math.sqrt(2.0)) * jnp.abs(x))
    poly = 1.061405429 * t - 1.453152027
    poly = poly * t + 1.421413741
    poly = poly * t - 0.284496736
    poly = poly * t + 0.254829592
    tail = (0.5 * poly) * t * bell
    share = jnp.where(x >= 0.0, 1.0 - tail, tail)
    return x * share, share + x * bell * (1.0 / math.sqrt(2.0 * math.pi))


def mean(values):
    return jnp.sum(values, axis=-1, keepdims=True) * (1.0 / values.shape[-1])


def norm_parts(values):
    centred = values - mean(values)
    scale = lax.rsqrt(mean(centred * centred) + EPSILON)
    return centred * scale, scale


def norm_back(upper, normed, scale):
    return scale * (upper - mean(upper) - normed * mean(upper * normed))


def column_sum(values):
    return jnp.sum(values, axis=0, keepdims=True)


def feed_kernel(layout, tok_ref, att_ref, cot_ref, vec_ref, bu_ref, wo_ref, wu_ref, wd_ref,
                out_ref, bg_ref, ag_ref, vg_ref, dbu_ref, dwu_ref, dwd_ref, dwo_ref,
                act_s, din_s, first_t, feed_t, att_t, bg_s):
    tiles, ff_steps, chunk, wide, narrow = layout
    step = pl.program_id(0)
    tile = tok_ref.shape[0]
    hidden = act_s.shape[1]
    vec = [vec_ref[i : i + 1] for i in range(6)]
    out_bias, gain_one, shift_one, down_bias, gain_two, shift_two = vec

    @pl.when(step == 0)
    def _():
        vg_ref[...] = jnp.zeros_like(vg_ref)
        dbu_ref[...] = jnp.zeros_like(dbu_ref)

    @pl.when(step < tiles)
    def _():
        start = pl.multiple_of(step * tile, tile)
        rows = pl.ds(start, tile)
        att = att_ref[...]
        normed_one, scale_one = norm_parts(
            tok_ref[...].astype(F32) + (dot(att, wo_ref[...]) + out_bias)
        )
        first = normed_one * gain_one + shift_one
        first_low = first.astype(BF16)
        first_t[:, rows] = first_low.T
        att_t[:, rows] = att.T
        feed = jnp.zeros_like(first) + down_bias
        spans = [slice(c, c + chunk) for c in range(0, hidden, chunk)]
        ahead = dot(first_low, wu_ref[:, spans[0]])
        for i, cols in enumerate(spans):
            inner = ahead + bu_ref[:, cols]
            if i + 1 < len(spans):
                ahead = dot(first_low, wu_ref[:, spans[i + 1]])
            active, slope = gelu_and_slope(inner)
            active = active.astype(BF16)
            act_s[rows, cols] = active
            din_s[rows, cols] = slope.astype(BF16)
            feed += dot(active, wd_ref[cols])
        normed_two, scale_two = norm_parts(first + feed)
        out_ref[...] = (normed_two * gain_two + shift_two).astype(BF16)
        cot = cot_ref[...].astype(F32)
        second = norm_back(cot * gain_two, normed_two, scale_two)
        feed_low = second.astype(BF16)
        feed_t[:, rows] = feed_low.T
        back = second
        ahead = dot(feed_low, wd_ref[spans[0]], NT)
        for i, cols in enumerate(spans):
            inner = ahead
            if i + 1 < len(spans):
                ahead = dot(feed_low, wd_ref[spans[i + 1]], NT)
            inner = (inner * din_s[rows, cols].astype(F32)).astype(BF16)
            din_s[rows, cols] = inner
            dbu_ref[:, cols] += column_sum(inner.astype(F32))
            back += dot(inner, wu_ref[:, cols], NT)
        residual = norm_back(back * gain_one, normed_one, scale_one)
        branch_low = residual.astype(BF16)
        bg_ref[...] = branch_low
        bg_s[rows] = branch_low
        ag_ref[...] = dot(branch_low, wo_ref[...], NT).astype(BF16)
        for i, values in enumerate(
            (
                branch_low.astype(F32),
                back * normed_one,
                back,
                feed_low.astype(F32),
                cot * normed_two,
                cot,
            )
        ):
            vg_ref[i : i + 1] += column_sum(values)

    @pl.when((step >= tiles) & (step < tiles + ff_steps))
    def _():
        cols = pl.ds(pl.multiple_of((step - tiles) * wide, wide), wide)
        dwu = dot(first_t[...], din_s[:, cols]).astype(BF16)
        dwu_ref[...] = dwu.reshape(dwu_ref.shape)
        dwd_ref[...] = dot(feed_t[...], act_s[:, cols]).astype(BF16).T

    @pl.when(step >= tiles + ff_steps)
    def _():
        cols = pl.ds(pl.multiple_of((step - tiles - ff_steps) * narrow, narrow), narrow)
        dwo_ref[...] = dot(att_t[...], bg_s[:, cols]).astype(BF16)


def feed_both_ways(tokens, attended, cotangent, vectors, up_bias, wo, wu, wd, groups):
    rows, features = tokens.shape
    hidden = wu.shape[1]
    tile = math.gcd(rows, 256)
    tiles = rows // tile
    wide, narrow = features, math.gcd(features, 384)
    ff_steps, out_steps = hidden // wide, features // narrow
    layout = (tiles, ff_steps, math.gcd(hidden, 512), wide, narrow)
    blocked = (groups, ff_steps, features // groups, wide)
    row_spec = pl.BlockSpec((tile, features), lambda i: (jnp.minimum(i, tiles - 1), 0))

    def ff_at(i):
        return jnp.clip(i - tiles, 0, ff_steps - 1)

    return pl.pallas_call(
        functools.partial(feed_kernel, layout),
        grid=(tiles + ff_steps + out_steps,),
        in_specs=[row_spec] * 3
        + [whole_spec(a.shape) for a in (vectors, up_bias, wo, wu, wd)],
        out_specs=[row_spec] * 3
        + [
            pl.BlockSpec((8, features), lambda i: (0, 0)),
            pl.BlockSpec((1, hidden), lambda i: (0, 0)),
            pl.BlockSpec((groups, 1) + blocked[2:], lambda i: (0, ff_at(i), 0, 0)),
            pl.BlockSpec((wide, features), lambda i: (ff_at(i), 0)),
            pl.BlockSpec(
                (features, narrow),
                lambda i: (0, jnp.clip(i - tiles - ff_steps, 0, out_steps - 1)),
            ),
        ],
        out_shape=[jax.ShapeDtypeStruct(tokens.shape, BF16)] * 3
        + [
            jax.ShapeDtypeStruct((8, features), F32),
            jax.ShapeDtypeStruct((1, hidden), F32),
            jax.ShapeDtypeStruct(blocked, BF16),
            jax.ShapeDtypeStruct(wd.shape, BF16),
            jax.ShapeDtypeStruct(wo.shape, BF16),
        ],
        scratch_shapes=[
            pltpu.VMEM((rows, hidden), BF16),
            pltpu.VMEM((rows, hidden), BF16),
            pltpu.VMEM((features, rows), BF16),
            pltpu.VMEM((features, rows), BF16),
            pltpu.VMEM((features, rows), BF16),
            pltpu.VMEM((rows, features), BF16),
        ],
        compiler_params=params(60),
        cost_estimate=cost(
            6 * rows * features * (features + 2 * hidden),
            2 * (6 * rows * features + 4 * features * hidden + 2 * features * features),
            2 * rows * hidden,
        ),
        name="feed_both_ways",
    )(tokens, attended, cotangent, vectors, up_bias, wo, wu, wd)


def spread(row):
    return jnp.broadcast_to(row, (PAIR, row.shape[1])).T


def front_kernel(tokens_ref, codes_ref, group_ref, cot_ref, vec_ref, bu_ref, wq_any, wk_any, wv_any, wo_any,
                 wu_any, wd_any, code_any, out_ref, bg_ref, ag_ref, att_ref, lse_ref, qm_ref, kmo_ref, kmr_ref,
                 first_t, feed_t, vg_ref, dbu_ref, q_any, k_any, v_any, kr_any, vr_any, rem_any, act_any, din_any,
                 wq, wk, wv, wo, wu, wd, tok_s, q_s, k_s, v_s, kr_s, vr_s, rem_s, code_s, act_s, din_s,
                 weight_sem, out_sem, send_sem, recv_sem):
    s = pl.program_id(0)
    seqs = tok_s.shape[0]
    length, features = tok_s.shape[1:]
    hidden = act_s.shape[1]
    side = lax.axis_index("blk")
    other = {"blk": 1 - side}
    query_bias, value_bias, out_bias, gain_one, shift_one, down_bias, gain_two, shift_two = [
        vec_ref[i : i + 1] for i in range(8)
    ]
    pairs_of = [(wq_any, wq), (wk_any, wk), (wv_any, wv), (wo_any, wo), (wu_any, wu), (wd_any, wd)]

    def weight(i):
        return pltpu.make_async_copy(*pairs_of[i], weight_sem.at[i])

    def remote(source, target, at):
        return pltpu.make_async_remote_copy(
            src_ref=source,
            dst_ref=target,
            send_sem=send_sem.at[at],
            recv_sem=recv_sem.at[at],
            device_id=other,
            device_id_type=pl.DeviceIdType.MESH,
        )

    def exchange(at):
        return remote(tokens_ref.at[at], rem_s.at[at], at)

    def code_exchange():
        return remote(code_any, code_s, seqs)

    def whole_out(i):
        source, target = ((q_s, q_any), (k_s, k_any), (v_s, v_any))[i]
        return pltpu.make_async_copy(source, target, out_sem.at[i])

    def part_out(i, at):
        source, target = (
            (kr_s, kr_any.at[at]),
            (vr_s, vr_any.at[at]),
            (rem_s.at[at], rem_any.at[at]),
            (act_s, act_any.at[at]),
            (din_s, din_any.at[at]),
        )[i]
        return pltpu.make_async_copy(source, target, out_sem.at[3 + i])

    @pl.when(s == 0)
    def _():
        barrier = pltpu.get_barrier_semaphore()
        pl.semaphore_signal(barrier, inc=1, device_id=other, device_id_type=pl.DeviceIdType.MESH)
        load = pltpu.make_async_copy(tokens_ref, tok_s, weight_sem.at[len(pairs_of)])
        load.start()
        for i in range(3):
            weight(i).start()
        pl.semaphore_wait(barrier, 1)
        exchange(0).start()
        code_exchange().start()
        for i in range(3, len(pairs_of)):
            weight(i).start()
        vg_ref[...] = jnp.zeros_like(vg_ref)
        dbu_ref[...] = jnp.zeros_like(dbu_ref)
        load.wait()
        for i in range(3):
            weight(i).wait()

        def project_own(at, carry):
            x = tok_s[at]
            q_s[at] = (dot(x, wq[...]) + query_bias).astype(BF16)
            k_s[at] = dot(x, wk[...]).astype(BF16)
            v_s[at] = (dot(x, wv[...]) + value_bias).astype(BF16)
            return carry

        lax.fori_loop(0, seqs, project_own, 0)
        for i in range(3):
            whole_out(i).start()
        for i in range(3, len(pairs_of)):
            weight(i).wait()
        code_exchange().wait_recv()
        exchange(0).wait_send()
        if seqs > 1:
            exchange(1).start()

    for at in range(seqs):

        @pl.when(s == at)
        def _(at=at):
            exchange(at).wait_recv()
            if at:
                for i in range(3):
                    part_out(i, at - 1).wait()

    x = rem_s[s]
    kr_s[...] = dot(x, wk[...]).astype(BF16)
    vr_s[...] = (dot(x, wv[...]) + value_bias).astype(BF16)
    slot = lax.broadcasted_iota(jnp.int32, (1, PAIR), 1) % HEAD
    slot = slot.astype(F32)
    qm_ref[0] = jnp.where(spread(group_ref[pl.ds(s, 1)]) == slot, 1.0, 0.0).astype(BF16)
    kmo_ref[0] = jnp.where(spread(codes_ref[pl.ds(s, 1)]) == slot, 0.0, MASKED).astype(BF16)
    kmr_ref[0] = jnp.where(spread(code_s[pl.ds(s, 1)]) == slot, 0.0, MASKED).astype(BF16)
    for at in range(seqs):

        @pl.when(s == at)
        def _(at=at):
            for i in range(3):
                part_out(i, at).start()

    groups = features // (2 * PAIR)

    def heads(group, carry):
        lanes = pl.ds(pl.multiple_of(group * 2 * PAIR, 2 * PAIR), 2 * PAIR)
        attend_group(
            q_s[s, :, lanes],
            qm_ref[0],
            [(k_s[s, :, lanes], kmo_ref[0], v_s[s, :, lanes]), (kr_s[:, lanes], kmr_ref[0], vr_s[:, lanes])],
            att_ref.at[0, :, lanes],
            lse_ref.at[0, pl.ds(group * 2, 2)],
        )
        return carry

    lax.fori_loop(0, groups, heads, 0)

    for at in range(1, seqs):

        @pl.when(s == at)
        def _(at=at):
            for i in range(3, 5):
                part_out(i, at - 1).wait()

    tile = math.gcd(length, 256)
    chunk = math.gcd(hidden, 512)
    spans = [slice(c, c + chunk) for c in range(0, hidden, chunk)]

    def feed_rows(t, carry):
        rows = pl.ds(pl.multiple_of(t * tile, tile), tile)
        att = att_ref[0, rows]
        normed_one, scale_one = norm_parts(
            tok_s[s, rows].astype(F32) + (dot(att, wo[...]) + out_bias)
        )
        first = normed_one * gain_one + shift_one
        first_low = first.astype(BF16)
        first_t[0, :, rows] = first_low.T
        feed = jnp.zeros_like(first) + down_bias
        ahead = dot(first_low, wu[:, spans[0]])
        for i, cols in enumerate(spans):
            inner = ahead + bu_ref[:, cols]
            if i + 1 < len(spans):
                ahead = dot(first_low, wu[:, spans[i + 1]])
            active, slope = gelu_and_slope(inner)
            active = active.astype(BF16)
            act_s[rows, cols] = active
            din_s[rows, cols] = slope.astype(BF16)
            feed += dot(active, wd[cols])
        normed_two, scale_two = norm_parts(first + feed)
        out_ref[0, rows] = (normed_two * gain_two + shift_two).astype(BF16)
        cot = cot_ref[0, rows].astype(F32)
        second = norm_back(cot * gain_two, normed_two, scale_two)
        feed_low = second.astype(BF16)
        feed_t[0, :, rows] = feed_low.T
        back = second
        ahead = dot(feed_low, wd[spans[0]], NT)
        for i, cols in enumerate(spans):
            inner = ahead
            if i + 1 < len(spans):
                ahead = dot(feed_low, wd[spans[i + 1]], NT)
            inner = (inner * din_s[rows, cols].astype(F32)).astype(BF16)
            din_s[rows, cols] = inner
            dbu_ref[:, cols] += column_sum(inner.astype(F32))
            back += dot(inner, wu[:, cols], NT)
        residual = norm_back(back * gain_one, normed_one, scale_one)
        branch_low = residual.astype(BF16)
        bg_ref[0, rows] = branch_low
        ag_ref[0, rows] = dot(branch_low, wo[...], NT).astype(BF16)
        for i, values in enumerate(
            (
                branch_low.astype(F32),
                back * normed_one,
                back,
                feed_low.astype(F32),
                cot * normed_two,
                cot,
            )
        ):
            vg_ref[i : i + 1] += column_sum(values)
        return carry

    lax.fori_loop(0, length // tile, feed_rows, 0)

    for at in range(seqs):

        @pl.when(s == at)
        def _(at=at):
            for i in range(3, 5):
                part_out(i, at).start()
            if at < seqs - 1:
                exchange(at + 1).wait_send()
            if at + 2 < seqs:
                exchange(at + 2).start()
            if at == seqs - 1:
                for i in range(3):
                    whole_out(i).wait()
                for i in range(5):
                    part_out(i, at).wait()
                code_exchange().wait_send()


def front(tokens, codes, group_rows, cotangent, vectors, up_bias, wq, wk, wv, wo, wu, wd):
    seqs, length, features = tokens.shape
    hidden = wu.shape[1]
    pairs = features // PAIR
    anywhere = pl.BlockSpec(memory_space=pl.ANY)

    def at_seq(*shape):
        return pl.BlockSpec((1,) + shape, lambda s: (s,) + (0,) * len(shape))

    def of_seqs(*shape, dtype=BF16):
        return jax.ShapeDtypeStruct((seqs,) + shape, dtype)

    def fixed(*shape):
        return pl.BlockSpec(shape, lambda s: (0,) * len(shape))

    rows, mask, lses = (length, features), (length, PAIR), (pairs, 8, length)
    turned, wide = (features, length), (length, hidden)
    return pl.pallas_call(
        front_kernel,
        grid=(seqs,),
        in_specs=[anywhere, whole_spec(codes.shape), whole_spec(group_rows.shape), at_seq(*rows)]
        + [whole_spec(vectors.shape), whole_spec(up_bias.shape)]
        + [anywhere] * 7,
        out_specs=[at_seq(*rows)] * 4
        + [at_seq(*lses)]
        + [at_seq(*mask)] * 3
        + [at_seq(*turned)] * 2
        + [fixed(8, features), fixed(1, hidden)]
        + [anywhere] * 8,
        out_shape=[of_seqs(*rows)] * 4
        + [of_seqs(*lses, dtype=F32)]
        + [of_seqs(*mask)] * 3
        + [of_seqs(*turned)] * 2
        + [jax.ShapeDtypeStruct((8, features), F32), jax.ShapeDtypeStruct((1, hidden), F32)]
        + [of_seqs(*rows)] * 6
        + [of_seqs(*wide)] * 2,
        scratch_shapes=[pltpu.VMEM(w.shape, BF16) for w in (wq, wk, wv, wo, wu, wd)]
        + [pltpu.VMEM(tokens.shape, BF16)] * 4
        + [pltpu.VMEM(rows, BF16)] * 2
        + [pltpu.VMEM(tokens.shape, BF16), pltpu.VMEM(codes.shape, F32)]
        + [pltpu.VMEM(wide, BF16)] * 2
        + [pltpu.SemaphoreType.DMA((7,)), pltpu.SemaphoreType.DMA((8,))]
        + [pltpu.SemaphoreType.DMA((seqs + 1,))] * 2,
        compiler_params=pltpu.CompilerParams(
            collective_id=2, has_side_effects=True, vmem_limit_bytes=63 * MIB
        ),
        cost_estimate=cost(
            2 * tokens.size * (9 * features + 4 * hidden + 8 * length), 2 * 20 * tokens.size, tokens.size * 24
        ),
        name="front",
    )(tokens, codes, group_rows, cotangent, vectors, up_bias, wq, wk, wv, wo, wu, wd, codes)


def feed_weights_kernel(steps, first_ref, din_ref, feed_ref, act_ref, att_ref, bg_ref, dwu_ref, dwd_ref, dwo_ref):
    seqs = first_ref.shape[0]

    @pl.when(pl.program_id(0) < steps)
    def _():
        dwu = sum(dot(first_ref[s], din_ref[s]) for s in range(seqs)).astype(BF16)
        dwu_ref[...] = dwu.reshape(dwu_ref.shape)
        dwd_ref[...] = sum(dot(feed_ref[s], act_ref[s]) for s in range(seqs)).astype(BF16).T

    @pl.when(pl.program_id(0) == steps)
    def _():
        dwo_ref[...] = sum(dot(att_ref[s].T, bg_ref[s]) for s in range(seqs)).astype(BF16)


def feed_weights(first_t, din, feed_t, act, att, bg, groups):
    seqs, features, length = first_t.shape
    hidden = act.shape[2]
    steps = hidden // features
    wide_spec = pl.BlockSpec((seqs, length, features), lambda i: (0, 0, jnp.minimum(i, steps - 1)))
    blocked = (groups, steps, features // groups, features)
    size = seqs * length
    return pl.pallas_call(
        functools.partial(feed_weights_kernel, steps),
        grid=(steps + 1,),
        in_specs=[
            whole_spec(first_t.shape),
            wide_spec,
            whole_spec(feed_t.shape),
            wide_spec,
            whole_spec(att.shape),
            whole_spec(bg.shape),
        ],
        out_specs=[
            pl.BlockSpec((groups, 1) + blocked[2:], lambda i: (0, jnp.minimum(i, steps - 1), 0, 0)),
            pl.BlockSpec((features, features), lambda i: (jnp.minimum(i, steps - 1), 0)),
            pl.BlockSpec((features, features), lambda i: (0, 0)),
        ],
        out_shape=[
            jax.ShapeDtypeStruct(blocked, BF16),
            jax.ShapeDtypeStruct((hidden, features), BF16),
            jax.ShapeDtypeStruct((features, features), BF16),
        ],
        compiler_params=params(60),
        cost_estimate=cost(
            2 * size * features * (2 * hidden + features), 4 * size * (hidden + 2 * features)
        ),
        name="feed_weights",
    )(first_t, din, feed_t, act, att, bg)


def own_back_kernel(bg_ref, dq_ref, dk_ref, dv_ref, wq_ref, wk_ref, wv_ref, out_ref):
    total = bg_ref[0].astype(F32) + dot(dq_ref[0], wq_ref[...], NT)
    total += dot(dk_ref[0], wk_ref[...], NT)
    total += dot(dv_ref[0], wv_ref[...], NT)
    out_ref[0] = total.astype(BF16)


def rem_back_kernel(dk_ref, dv_ref, wk_ref, wv_ref, out_ref):
    total = dot(dk_ref[0], wk_ref[...], NT) + dot(dv_ref[0], wv_ref[...], NT)
    out_ref[0] = total.astype(BF16)


def tokens_back(kernel, rows, weights):
    seqs, length, features = rows[0].shape
    tile = math.gcd(length, 512)
    row_spec = pl.BlockSpec((1, tile, features), lambda s, i: (s, i, 0))
    size = rows[0].size
    return pl.pallas_call(
        kernel,
        grid=(seqs, length // tile),
        in_specs=[row_spec] * len(rows) + [whole_spec(w.shape) for w in weights],
        out_specs=row_spec,
        out_shape=jax.ShapeDtypeStruct(rows[0].shape, BF16),
        compiler_params=params(60),
        cost_estimate=cost(2 * size * features * len(weights), 2 * size * (1 + len(rows))),
        name="tokens_back",
    )(*rows, *weights)


def weights_back_kernel(tok_ref, rem_ref, dq_ref, dko_ref, dvo_ref, dkr_ref, dvr_ref,
                        wq_ref, wk_ref, wv_ref, bq_ref, bv_ref, tok_t, rem_t):
    @pl.when(pl.program_id(0) == 0)
    def _():
        tok_t[...] = tok_ref[...].T
        rem_t[...] = rem_ref[...].T

    wq_ref[...] = dot(tok_t[...], dq_ref[...]).astype(BF16)
    wk_ref[...] = (dot(tok_t[...], dko_ref[...]) + dot(rem_t[...], dkr_ref[...])).astype(BF16)
    wv_ref[...] = (dot(tok_t[...], dvo_ref[...]) + dot(rem_t[...], dvr_ref[...])).astype(BF16)
    bq_ref[...] = column_sum(dq_ref[...].astype(F32))
    bv_ref[...] = column_sum(dvo_ref[...].astype(F32)) + column_sum(dvr_ref[...].astype(F32))


def weights_back(tok, rem, dq, dko, dvo, dkr, dvr):
    rows, features = tok.shape
    others = rem.shape[0]
    wide = math.gcd(features, 256)
    own_spec = pl.BlockSpec((rows, wide), lambda j: (0, j))
    rem_spec = pl.BlockSpec((others, wide), lambda j: (0, j))
    bias_spec = pl.BlockSpec((1, wide), lambda j: (0, j))
    return pl.pallas_call(
        weights_back_kernel,
        grid=(features // wide,),
        in_specs=[
            whole_spec(tok.shape),
            whole_spec(rem.shape),
            own_spec,
            own_spec,
            own_spec,
            rem_spec,
            rem_spec,
        ],
        out_specs=[pl.BlockSpec((features, wide), lambda j: (0, j))] * 3 + [bias_spec] * 2,
        out_shape=[jax.ShapeDtypeStruct((features, features), BF16)] * 3
        + [jax.ShapeDtypeStruct((1, features), F32)] * 2,
        scratch_shapes=[
            pltpu.VMEM((features, rows), BF16),
            pltpu.VMEM((features, others), BF16),
        ],
        compiler_params=params(60),
        cost_estimate=cost(
            2 * features * features * (3 * rows + 2 * others),
            2 * (4 * tok.size + 3 * rem.size + 3 * features * features),
        ),
        name="weights_back",
    )(tok, rem, dq, dko, dvo, dkr, dvr)


def halve(value, axis, bit):
    size = lax.axis_size(axis)
    mine = (lax.axis_index(axis) >> bit) & 1
    pairs = value.reshape((value.shape[0] // 2, 2) + value.shape[1:])
    keep = lax.dynamic_index_in_dim(pairs, mine, 1, keepdims=False)
    send = lax.dynamic_index_in_dim(pairs, 1 - mine, 1, keepdims=False)
    came = lax.ppermute(send, axis, [(i, i ^ (1 << bit)) for i in range(size)])
    return keep.astype(F32) + came.astype(F32)


def scatter_sum(value, low=True):
    dp, blk = lax.axis_size("dp"), lax.axis_size("blk")
    if dp & (dp - 1) or blk & (blk - 1):
        return lax.psum_scatter(
            value.astype(F32), ("dp", "blk"), scatter_dimension=0, tiled=True
        )
    kept = value.dtype
    each = value.shape[0] // (dp * blk)
    value = value.reshape((dp, blk * each) + value.shape[1:])
    for bit in range(dp.bit_length() - 1):
        value = halve(value, "dp", bit).astype(kept)
    value = value.reshape((blk, each) + value.shape[2:])
    for bit in range(blk.bit_length() - 1):
        value = halve(value, "blk", bit)
        value = value if (2 << bit) == blk else value.astype(kept)
    return value.reshape(value.shape[1:]).astype(F32)


class Unit:
    def __init__(self, parts, rows, columns, halves, order, outs):
        self.parts, self.rows, self.columns = parts, rows, columns
        self.halves, self.order, self.outs = halves, order, outs
        self.half = rows // (2 * halves)
        self.last_type = BF16 if (rows // 2) % 16 == 0 else F32


def timetable(units, bits, seqs, groups, slots_each, slot_us, token_us):
    free, pending, table = {}, [], []
    slots = seqs * groups * slots_each

    def launch(key, now):
        kind, which, step = key
        if kind == "tokens":
            link, us = "blk", token_us
        elif kind == "vectors":
            link, us = None, 1.0
        else:
            unit = units[which]
            bit = unit.order[step] if step < bits else "blk"
            size = unit.rows * unit.columns * (1 << max(bits - 1 - step, 0)) * 2e-5
            size = size * 0.5 if step == bits else size
            link = {0: "core", 1: "y"}.get(bit, bit if bit == "blk" else "z")
            us = size * 2 * (1.0 if bit == "blk" or bit < 3 else 2.0)
            us = us / 8 if bit == 0 else us
        start = max(now, free.get(link, 0.0))
        if link:
            free[link] = start + us
        pending.append((start + us + 1.5, key))

    for u, unit in enumerate(units):
        if unit.parts:
            launch(("unit", u, 0), 0.0)
    first_group = sum(1 for unit in units if unit.parts)
    now = 0.0
    while len(table) < slots or pending:
        slot = len(table)
        if slot < slots:
            now = (slot + 1) * slot_us
            step, within = divmod(slot, slots_each)
            if within == slots_each - 1:
                s, h = divmod(step, groups)
                if h == groups - 1:
                    launch(("tokens", s, 0), now)
                if s == seqs - 1:
                    launch(("unit", first_group + h, 0), now)
                if step == seqs * groups - 1:
                    launch(("vectors", 0, 0), now)
            due = sorted(p for p in pending if p[0] <= now)
        else:
            due = [min(pending)]
            now = max(now + 0.3, due[0][0])
        table.append([key for _, key in due])
        for found in due:
            pending.remove(found)
            kind, which, step = found[1]
            if kind != "tokens" and step < bits:
                launch((kind, which, step + 1), now)
    return table[:slots], [key for keys in table[slots:] for key in keys]


def back_kernel(units, bits, groups, table, tail, n_out, *refs):
    (q_ref, qm_ref, o_ref, g_ref, lse_ref, ko_ref, kmo_ref, vo_ref, kr_ref, kmr_ref, vr_ref,
     bg_ref, tok_ref, rem_ref, wq_ref, wk_ref, wv_ref, vg_ref, vu_ref) = refs[:19]
    sources, refs = refs[19:22], list(refs[22:])
    tokens_out, *outs = refs[:n_out]
    refs = refs[n_out:]
    kept = [refs.pop(0) for _ in units]
    landed = [[refs.pop(0) for _ in range(bits)] for _ in units]
    wide = [refs.pop(0) for _ in units]
    parting = [refs.pop(0) for _ in units]
    last = [refs.pop(0) for _ in units]
    (weight_sum, group_src, own_sum, rem_sum, tok_t, rem_t, dq_s, dko_s, dvo_s, dkr_s, dvr_s,
     rem_out, rem_in, vec, vec_in, bias_sum, send_sem, recv_sem, local_sem) = refs
    step = pl.program_id(0)
    steps = pl.num_programs(0)
    s, h = step // groups, step % groups
    seqs = tokens_out.shape[0]
    features = tok_ref.shape[2]
    me, side = lax.axis_index("dp"), lax.axis_index("blk")
    own = [(me // (1 << bit)) % 2 for bit in range(bits)]
    partner = [{"dp": me + (1 << bit) * (1 - 2 * own[bit])} for bit in range(bits)]
    partner.append({"blk": 1 - side})
    first_group = sum(1 for unit in units if unit.parts)
    lead = (slice(None),) * (bits - 1)

    sems = {}
    for u, unit in enumerate(units):
        for k in range(bits + 1):
            for p in range(len(unit.parts) if unit.parts and k == 0 else 1):
                sems["unit", u, k, p] = len(sems)
    for k in range(bits + 1):
        sems["vectors", 0, k, 0] = len(sems)
    for k in range(seqs):
        sems["tokens", k, 0, 0] = len(sems)

    def remote(source, target, device, key):
        return pltpu.make_async_remote_copy(
            src_ref=source,
            dst_ref=target,
            send_sem=send_sem.at[sems[key]],
            recv_sem=recv_sem.at[sems[key]],
            device_id=device,
            device_id_type=pl.DeviceIdType.MESH,
        )

    def spot(unit, k, value):
        found = []
        for bit in range(bits - 1, 0, -1):
            at = unit.order.index(bit)
            found.append(own[bit] if at < k else value if at == k else slice(None))
        return tuple(found)

    def copies(kind, which, k):
        if kind == "tokens":
            return [remote(rem_out.at[which], rem_in.at[which], partner[bits], (kind, which, 0, 0))]
        if kind == "vectors":
            return [remote(vec.at[k], vec_in.at[k], partner[k], (kind, 0, k, 0))]
        u, unit = which, units[which]
        if k == bits:
            return [remote(parting[u], last[u], partner[bits], (kind, u, k, 0))]
        if k:
            bit = unit.order[k]
            source = kept[u].at[spot(unit, k, 1 - own[bit])]
            return [remote(source, landed[u][k], partner[bit], (kind, u, k, 0))]
        if not unit.parts:
            source = group_src.at[(u - first_group,) + lead + (1 - own[0],)]
            return [remote(source, landed[u][0], partner[0], (kind, u, 0, 0))]
        found, row = [], 0
        for p, (source, first, rows) in enumerate(unit.parts):
            found.append(
                remote(
                    sources[source].at[lead + (1 - own[0], pl.ds(first, rows))],
                    landed[u][0].at[lead + (pl.ds(row, rows),)],
                    partner[0],
                    (kind, u, 0, p),
                )
            )
            row += rows
        return found

    def near_copies(u):
        found, row = [], 0
        for p, (source, first, rows) in enumerate(units[u].parts):
            found.append(
                pltpu.make_async_copy(
                    sources[source].at[lead + (own[0], pl.ds(first, rows))],
                    kept[u].at[lead + (pl.ds(row, rows),)],
                    local_sem.at[sems["unit", u, 0, p]],
                )
            )
            row += rows
        return found

    def launch(*key):
        for copy in copies(*key):
            copy.start()

    def halves_of(u, which):
        unit = units[u]
        return [
            wide[u][pl.ds(pl.multiple_of(i * 2 * unit.half + which * unit.half, 8), unit.half)]
            for i in range(unit.halves)
        ]

    def receive(kind, which, k):
        for copy in copies(kind, which, k):
            copy.wait_recv()
        if kind == "tokens":
            total = tokens_out[which].astype(F32) + rem_in[which].astype(F32)
            tokens_out[which] = total.astype(BF16)
            return
        if kind == "vectors":
            vec[k + 1] = vec[k] + vec_in[k]
            if k < bits:
                launch(kind, 0, k + 1)
            return
        u, unit = which, units[which]
        if k == bits:
            for i, (mine, (out, rows, columns)) in enumerate(zip(halves_of(u, side), unit.outs)):
                came = last[u][...].astype(F32)[i * unit.half : (i + 1) * unit.half]
                outs[out][rows, columns] = mine + came
            return
        if unit.parts and k == 0:
            for copy in near_copies(u):
                copy.wait()
        place = spot(unit, k, own[unit.order[k]])
        open_at = [i for i, at in enumerate(place) if isinstance(at, slice)]

        def add(n, carry):
            at, where = list(place), []
            for digit, i in enumerate(open_at):
                at[i] = (n // (1 << (len(open_at) - 1 - digit))) % 2
                where.append(at[i])
            at = tuple(at)
            if unit.parts or k:
                mine = kept[u][at]
            else:
                mine = group_src[(u - first_group,) + at + (own[0],)]
            total = mine.astype(F32) + landed[u][k][tuple(where)].astype(F32)
            if k == bits - 1:
                wide[u][...] = total
            else:
                kept[u][at] = total.astype(BF16)
            return carry

        if open_at:
            lax.fori_loop(0, 1 << len(open_at), add, 0)
        else:
            add(0, 0)
        if k == bits - 1:
            pieces = halves_of(u, 1 - side)
            pieces = pieces[0] if len(pieces) == 1 else jnp.concatenate(pieces, axis=0)
            parting[u][...] = pieces.astype(unit.last_type)
        launch(kind, u, k + 1)

    @pl.when(step == 0)
    def _():
        barrier = pltpu.get_barrier_semaphore()
        for other in partner:
            pl.semaphore_signal(barrier, inc=1, device_id=other, device_id_type=pl.DeviceIdType.MESH)
        pl.semaphore_wait(barrier, bits + 1)
        for u, unit in enumerate(units):
            if unit.parts:
                launch("unit", u, 0)
                for copy in near_copies(u):
                    copy.start()
        weight_sum[...] = jnp.zeros_like(weight_sum)
        bias_sum[...] = jnp.zeros_like(bias_sum)

    @pl.when(h == 0)
    def _():
        tok_t[...] = tok_ref[0].T
        rem_t[...] = rem_ref[0].T
        own_sum[...] = bg_ref[0].astype(F32)
        rem_sum[...] = jnp.zeros_like(rem_sum)

    low = low_lanes()
    parts = ((ko_ref, kmo_ref, vo_ref, dko_s, dvo_s), (kr_ref, kmr_ref, vr_ref, dkr_s, dvr_s))
    pairs = q_ref.shape[2] // PAIR
    for pair in range(pairs):
        attend_back_pair(pair, low, parts, q_ref, qm_ref, o_ref, g_ref, lse_ref, dq_s)
        if pair == pairs - 1:
            width = q_ref.shape[2]
            columns = pl.ds(pl.multiple_of(h * width, width), width)
            wq, wk, wv = wq_ref[:, columns], wk_ref[:, columns], wv_ref[:, columns]
            dq, dko, dvo, dkr, dvr = dq_s[...], dko_s[...], dvo_s[...], dkr_s[...], dvr_s[...]
            own_sum[...] += dot(dq, wq, NT) + dot(dko, wk, NT) + dot(dvo, wv, NT)
            rem_sum[...] += dot(dkr, wk, NT) + dot(dvr, wv, NT)
            weight_sum[h, 0] += dot(tok_t[...], dq)
            weight_sum[h, 1] += dot(tok_t[...], dko) + dot(rem_t[...], dkr)
            weight_sum[h, 2] += dot(tok_t[...], dvo) + dot(rem_t[...], dvr)
            bias_sum[h, 0:1] += column_sum(dq.astype(F32))
            bias_sum[h, 1:2] += column_sum(dvo.astype(F32)) + column_sum(dvr.astype(F32))

            for at in range(seqs):

                @pl.when((h == groups - 1) & (s == at))
                def _(at=at):
                    tokens_out[at] = own_sum[...].astype(BF16)
                    rem_out[at] = rem_sum[...].astype(BF16)
                    launch("tokens", at, 0)

            for at in range(groups):

                @pl.when((s == seqs - 1) & (h == at))
                def _(at=at):
                    rows = features // (1 << bits)
                    for i in range(3):
                        piece = weight_sum[at, i].astype(BF16)
                        piece = piece.reshape((2,) * bits + (rows, piece.shape[1]))
                        group_src[(at,) + (slice(None),) * bits + (slice(i * rows, (i + 1) * rows),)] = piece
                    launch("unit", first_group + at, 0)

            @pl.when(step == steps - 1)
            def _():
                vec[0] = jnp.zeros_like(vec[0])
                vec[0, 0:6] = vg_ref[0:6]
                for at in range(groups):
                    vec[0, 6:8, at * width : (at + 1) * width] = bias_sum[at, 0:2]
                blocks = vu_ref.shape[1] // features
                for at in range(blocks):
                    vec[0, 8 + at : 9 + at] = vu_ref[:, at * features : (at + 1) * features]
                launch("vectors", 0, 0)

        for at in range(seqs * groups):
            keys = table[at * pairs + pair]
            if keys:

                @pl.when(step == at)
                def _(keys=keys):
                    for key in keys:
                        receive(*key)

    @pl.when(step == steps - 1)
    def _():
        for key in tail:
            receive(*key)
        shards = (1 << bits) * 2
        place = me * 2 + side
        share = features // shards
        rows = pltpu.roll(vec[bits + 1, 0:8], (shards - place) * share % features, 1)
        outs[-1][0:8] = rows[:, :PAIR]
        share = vu_ref.shape[1] // shards
        each = features // share
        row = vec[bits + 1, pl.ds(8 + place // each, 1)]
        rows = pltpu.roll(jnp.broadcast_to(row, (8, features)), (each - place % each) * share % features, 1)
        outs[-1][8:16] = rows[:, :PAIR]
        for u in range(len(units)):
            for k in range(bits + 1):
                for copy in copies("unit", u, k):
                    copy.wait_send()
        for k in range(bits + 1):
            copies("vectors", 0, k)[0].wait_send()
        for k in range(seqs):
            copies("tokens", k, 0)[0].wait_send()


def back_and_sum(q, qm, o, g, lse, own, rem, bg, tokens, rem_tokens, weights, dwd, dwu, dwo, vg, vu):
    dp = lax.axis_size("dp")
    bits = dp.bit_length() - 1
    seqs, length, features = q.shape
    other = rem[0].shape[1]
    width = math.gcd(features, 2 * PAIR)
    groups, pairs = features // width, width // PAIR
    low, deep, blocks = features // dp, dwd.shape[0] // dp, dwu.shape[1]
    lead = (2,) * bits
    sources = [
        dwd.reshape(lead + (deep, features)),
        dwu.reshape(lead + (-1, features)),
        dwo.reshape(lead + (low, features)),
    ]
    order = tuple(range(bits))
    every = slice(None)
    units = []
    for i in range(2):
        at, quarter = slice(i * deep // 4, (i + 1) * deep // 4), deep // 4
        parts = [(0, i * quarter, quarter), (0, (2 + i) * quarter, quarter)]
        units.append(Unit(parts, 2 * quarter, features, 1, order, [(0, at, every)]))
    for i in range(2):
        found = range(i * blocks // 2, (i + 1) * blocks // 2)
        units.append(
            Unit(
                [(1, b * low, low) for b in found],
                len(found) * low,
                features,
                len(found),
                order,
                [(1, every, slice(b * features, (b + 1) * features)) for b in found],
            )
        )
    units.append(Unit([(2, 0, low)], low, features, 1, order, [(2, every, every)]))
    for h in range(groups):
        columns = slice(h * width, (h + 1) * width)
        units.append(Unit(None, 3 * low, width, 3, order, [(3 + i, every, columns) for i in range(3)]))
    table, tail = timetable(units, bits, seqs, groups, pairs, 4.3, length * features * 4e-5)

    half = low // 2
    out_shape = [
        jax.ShapeDtypeStruct(q.shape, BF16),
        jax.ShapeDtypeStruct((deep // 2, features), F32),
        jax.ShapeDtypeStruct((half, blocks * features), F32),
        *(jax.ShapeDtypeStruct((half, features), F32) for _ in range(4)),
        jax.ShapeDtypeStruct((16, PAIR), F32),
    ]
    tops = lead[1:]
    scratch = [pltpu.VMEM(tops + (u.rows, u.columns), BF16) for u in units]
    for u in units:
        scratch += [pltpu.VMEM(tops[k:] + (u.rows, u.columns), BF16) for k in range(bits)]
    scratch += [pltpu.VMEM((u.rows, u.columns), F32) for u in units]
    scratch += [pltpu.VMEM((u.rows // 2, u.columns), u.last_type) for u in units] * 2
    count = sum((len(u.parts) if u.parts else 1) + bits for u in units) + bits + 1 + seqs
    scratch += [
        pltpu.VMEM((groups, 3, features, width), F32),
        pltpu.VMEM((groups,) + lead + (3 * low, width), BF16),
        pltpu.VMEM((length, features), F32),
        pltpu.VMEM((other, features), F32),
        pltpu.VMEM((features, length), BF16),
        pltpu.VMEM((features, other), BF16),
        *(pltpu.VMEM((length, width), BF16) for _ in range(3)),
        *(pltpu.VMEM((other, width), BF16) for _ in range(2)),
        pltpu.VMEM((seqs, other, features), BF16),
        pltpu.VMEM((seqs, other, features), BF16),
        pltpu.VMEM((bits + 2, 16, features), F32),
        pltpu.VMEM((bits + 1, 16, features), F32),
        pltpu.VMEM((groups, 8, width), F32),
        *(pltpu.SemaphoreType.DMA((count,)) for _ in range(3)),
    ]

    def pair_at(rows):
        return pl.BlockSpec((1, rows, width), lambda i: (i // groups, 0, i % groups))

    def mask_at(rows):
        return pl.BlockSpec((1, rows, PAIR), lambda i: (i // groups, 0, 0))

    def rows_at(rows):
        return pl.BlockSpec(
            (1, rows, features), lambda i: (i // groups, 0, 0), pipeline_mode=pl.Buffered(1)
        )

    return pl.pallas_call(
        functools.partial(back_kernel, units, bits, groups, table, tail, len(out_shape)),
        grid=(seqs * groups,),
        in_specs=[
            pair_at(length),
            mask_at(length),
            pair_at(length),
            pair_at(length),
            pl.BlockSpec((1, pairs, 8, length), lambda i: (i // groups, i % groups, 0, 0)),
            pair_at(length),
            mask_at(length),
            pair_at(length),
            pair_at(other),
            mask_at(other),
            pair_at(other),
            rows_at(length),
            rows_at(length),
            rows_at(other),
        ]
        + [whole_spec(w.shape) for w in weights + (vg, vu)]
        + [pl.BlockSpec(memory_space=pl.ANY)] * 3,
        out_specs=[pl.BlockSpec(s.shape, lambda i, n=len(s.shape): (0,) * n, pipeline_mode=pl.Buffered(1)) for s in out_shape],
        out_shape=out_shape,
        scratch_shapes=scratch,
        compiler_params=pltpu.CompilerParams(
            collective_id=1, has_side_effects=True, vmem_limit_bytes=63 * MIB
        ),
        cost_estimate=cost(
            40 * q.size * (length + other), 2 * q.size * 14, q.size * (length + other) // HEAD
        ),
        name="back_and_sum",
    )(q, qm, o, g, lse, *own, *rem, bg, tokens, rem_tokens, *weights, vg, vu, *sources)


def back_plainly(q, qm, o, g, lse, own, rem, bg, tokens, rem_tokens, weights, dwd, dwu, dwo, vg, vu):
    seqs, length, features = q.shape
    dp, blk = lax.axis_size("dp"), lax.axis_size("blk")
    dq, dko, dvo, dkr, dvr = attend_back(q, qm, o, g, lse, own, rem)
    rem_gradient = tokens_back(rem_back_kernel, (dkr, dvr), weights[1:])
    came = [
        lax.ppermute(part, "blk", [((i + r) % blk, i) for i in range(blk)])
        for r, part in enumerate(jnp.split(rem_gradient, blk - 1, axis=1), 1)
    ]
    flat = [v.reshape(-1, features) for v in (tokens, rem_tokens, dq, dko, dvo, dkr, dvr)]
    dwq, dwk, dwv, dbq, dbv = weights_back(*flat)
    total = tokens_back(own_back_kernel, (bg, dq, dko, dvo), weights).astype(F32)
    for part in came:
        total += part.astype(F32)
    dwu = jnp.moveaxis(dwu[0], 0, 1).reshape(features, -1)
    summed = [scatter_sum(w) for w in (dwd, dwu, dwo, dwq, dwk, dwv)]
    rows = [vg[i] for i in range(6)] + [dbq, dbv, vu]
    rows = [scatter_sum(v.reshape(dp * blk, -1)) for v in rows]
    return [total.astype(BF16)] + summed + [[v[0] for v in rows]]


def body(
    tokens,
    query_weight,
    query_bias,
    key_weight,
    value_weight,
    value_bias,
    out_weight,
    out_bias,
    gain_one,
    shift_one,
    up_weight,
    up_bias,
    down_weight,
    down_bias,
    gain_two,
    shift_two,
    group_ids,
    valid_mask,
    cotangent,
):
    seqs, length, features = tokens.shape
    rows = seqs * length
    blk = lax.axis_size("blk")

    def from_others(value):
        found = [
            lax.ppermute(value, "blk", [(i, (i + r) % blk) for i in range(blk)])
            for r in range(1, blk)
        ]
        return found[0] if len(found) == 1 else jnp.concatenate(found, axis=1)

    codes = jnp.where(valid_mask == 1, group_ids, -1)
    dp = lax.axis_size("dp")
    by_kernel = blk == 2 and dp & (dp - 1) == 0 and dp > 1 and (features // dp) % 16 == 0
    projections = (query_weight, key_weight, value_weight)
    vectors = jnp.stack(
        [query_bias, value_bias, out_bias, gain_one, shift_one, down_bias, gain_two, shift_two]
    ).astype(F32)
    wide_bias = up_bias.astype(F32)[None]

    if by_kernel:
        def as_rows(values):
            return jnp.pad(values.astype(F32), ((0, -seqs % 8), (0, 0)))

        (block_out, branch_gradient, attended_gradient, attended, lse, query_mask, own_mask, rem_mask,
         first_t, feed_t, vector_gradients, up_bias_gradient, queries, own_keys, own_values, rem_keys,
         rem_values, rem_tokens, active, inner_gradient) = front(
            tokens,
            as_rows(codes),
            as_rows(group_ids),
            cotangent,
            vectors,
            wide_bias,
            *projections,
            out_weight,
            up_weight,
            down_weight,
        )
        dwu, dwd, dwo = feed_weights(
            first_t, inner_gradient, feed_t, active, attended, branch_gradient, dp
        )
        own = (own_keys, own_mask, own_values)
        rem = (rem_keys, rem_mask, rem_values)
    else:
        rem_tokens = from_others(tokens)
        rem_codes = from_others(codes.astype(BF16)).astype(jnp.int32)
        slot = jnp.arange(PAIR, dtype=jnp.int32) % HEAD

        def key_mask(code):
            return jnp.where(code[:, :, None] == slot, 0.0, MASKED).astype(BF16)

        query_mask = (group_ids[:, :, None] == slot).astype(BF16)
        queries, own_keys, own_values = project(tokens, vectors, projections)
        rem_keys, rem_values = project(rem_tokens, vectors, projections[1:])
        own = (own_keys, key_mask(codes), own_values)
        rem = (rem_keys, key_mask(rem_codes), rem_values)
        attended, lse = attend(queries, query_mask, own, rem)
        (block_out, branch_gradient, attended_gradient, vector_gradients, up_bias_gradient,
         dwu, dwd, dwo) = feed_both_ways(
            tokens.reshape(rows, features),
            attended.reshape(rows, features),
            cotangent.reshape(rows, features),
            vectors[2:],
            wide_bias,
            out_weight,
            up_weight,
            down_weight,
            1,
        )
    finish = back_and_sum if by_kernel else back_plainly
    tokens_gradient, dwd, dwu, dwo, dwq, dwk, dwv, rows_left = finish(
        queries,
        query_mask,
        attended,
        attended_gradient.reshape(tokens.shape),
        lse,
        own,
        rem,
        branch_gradient.reshape(tokens.shape),
        tokens,
        rem_tokens,
        projections,
        dwd,
        dwu,
        dwo,
        vector_gradients,
        up_bias_gradient,
    )
    if by_kernel:
        share, wide = features // (dp * blk), up_bias.size // (dp * blk)
        rows_left = [rows_left[i, :share] for i in range(8)] + [rows_left[8, :wide]]
    dbo, dg1, ds1, dbd, dg2, ds2, dbq, dbv, dbu = rows_left
    return (
        block_out.reshape(tokens.shape),
        tokens_gradient,
        dwq,
        dbq,
        dwk,
        dwv,
        dbv,
        dwo,
        dbo,
        dg1,
        ds1,
        dwu,
        dbu,
        dwd,
        dbd,
        dg2,
        ds2,
    )


def solution(mesh):
    rows, shared, pair = P("dp", "blk", None), P(), P("dp", "blk")
    matrix, vector = P(("dp", "blk"), None), P(("dp", "blk"))
    return jax.shard_map(
        body,
        mesh=mesh,
        in_specs=(rows,) + (shared,) * 15 + (pair, pair, rows),
        out_specs=(
            rows,
            rows,
            matrix,
            vector,
            matrix,
            matrix,
            vector,
            matrix,
            vector,
            vector,
            vector,
            matrix,
            vector,
            matrix,
            vector,
            vector,
            vector,
        ),
        check_vma=False,
    )
```

```python
import functools
import math

import jax
import jax.numpy as jnp
from jax import lax
from jax.experimental import pallas as pl
from jax.experimental.pallas import tpu as pltpu
from jax.sharding import PartitionSpec as P

HEAD = 64
PAIR = 2 * HEAD
EPSILON = 1e-12
MASKED = -1e30
FLOOR = -3e38
SCALE = HEAD**-0.5
EXPO = SCALE * math.log2(math.e)
NN = (((1,), (0,)), ((), ()))
NT = (((1,), (1,)), ((), ()))
F32 = jnp.float32
BF16 = jnp.bfloat16
MIB = 1 << 20
FEED_ROWS = 512


def dot(left, right, dims=NN):
    return lax.dot_general(left, right, dims, preferred_element_type=F32)


def whole_spec(shape):
    return pl.BlockSpec(shape, lambda *_: (0,) * len(shape), pipeline_mode=pl.Buffered(1))


def params(limit):
    return pltpu.CompilerParams(vmem_limit_bytes=limit * MIB)


def cost(flops, touched, exps=0):
    return pl.CostEstimate(flops=int(flops), bytes_accessed=int(touched), transcendentals=int(exps))


def project_kernel(has_query, *refs):
    if has_query:
        x_ref, bias_ref, wq_ref, wk_ref, wv_ref, q_ref, k_ref, v_ref = refs
    else:
        x_ref, bias_ref, wk_ref, wv_ref, k_ref, v_ref = refs
    x = x_ref[0]
    if has_query:
        q_ref[0] = (dot(x, wq_ref[...]) + bias_ref[0:1]).astype(BF16)
    k_ref[0] = dot(x, wk_ref[...]).astype(BF16)
    v_ref[0] = (dot(x, wv_ref[...]) + bias_ref[1:2]).astype(BF16)


def project(x, bias, weights):
    seqs, length, features = x.shape
    tile = math.gcd(length, 512)
    grid = (seqs, length // tile)
    row_spec = pl.BlockSpec((1, tile, features), lambda s, i: (s, i, 0))
    return pl.pallas_call(
        functools.partial(project_kernel, len(weights) == 3),
        grid=grid,
        in_specs=[row_spec, whole_spec(bias.shape)] + [whole_spec(w.shape) for w in weights],
        out_specs=[row_spec] * len(weights),
        out_shape=[jax.ShapeDtypeStruct(x.shape, BF16)] * len(weights),
        compiler_params=params(60),
        cost_estimate=cost(
            2 * x.size * features * len(weights), 2 * x.size * (1 + len(weights))
        ),
        name="project",
    )(x, bias, *weights)


def low_lanes():
    return lax.broadcasted_iota(jnp.int32, (1, PAIR), 1) < HEAD


def attend_group(q, qm, sources, o_ref, lse_ref):
    length = q.shape[0]
    tile = math.gcd(length, 256)
    low = low_lanes()
    one = jnp.ones((1, PAIR), BF16)
    todo = [
        (pair, row, head)
        for pair in range(q.shape[1] // PAIR)
        for row in range(0, length, tile)
        for head in range(2)
    ]

    def lanes_of(pair):
        return slice(pair * PAIR, (pair + 1) * PAIR)

    def mine_of(head):
        return ~low if head else low

    def scores_of(pair, row, head):
        mine, lanes = mine_of(head), lanes_of(pair)
        q_side = jnp.where(mine, q[row : row + tile, lanes], qm[row : row + tile])
        return [dot(q_side, jnp.where(mine, k[:, lanes], km), NT) for k, km, _ in sources]

    ahead = scores_of(*todo[0])
    for i, (pair, row, head) in enumerate(todo):
        scores = ahead
        if i + 1 < len(todo):
            ahead = scores_of(*todo[i + 1])
        top = functools.reduce(
            jnp.maximum, [jnp.max(part, axis=-1, keepdims=True) for part in scores]
        )
        weights = [jnp.exp2((part - top) * EXPO).astype(BF16) for part in scores]
        total = sum(
            dot(w, jnp.where(mine_of(head), v[:, lanes_of(pair)], one))
            for w, (_, _, v) in zip(weights, sources)
        )
        if head == 0:
            earlier, earlier_top = total, top
            continue
        totals = pltpu.roll(jnp.where(low, total, earlier), HEAD, 1)
        rows = slice(row, row + tile)
        o_ref[rows, lanes_of(pair)] = (jnp.where(low, earlier, total) / totals).astype(BF16)
        lse = (jnp.where(low, earlier_top, top) * EXPO + jnp.log2(totals)).T
        lse_ref[pair, 0:1, rows] = lse[0:1]
        lse_ref[pair, 1:2, rows] = lse[HEAD : HEAD + 1]


def attend_kernel(q_ref, qm_ref, ko_ref, kmo_ref, vo_ref, kr_ref, kmr_ref, vr_ref, o_ref, lse_ref):
    sources = [(ko_ref[0], kmo_ref[0], vo_ref[0]), (kr_ref[0], kmr_ref[0], vr_ref[0])]
    attend_group(q_ref[0], qm_ref[0], sources, o_ref.at[0], lse_ref.at[0])


def pair_spec(length, lanes):
    return pl.BlockSpec((1, length, lanes), lambda s, h: (s, 0, h))


def mask_spec(length):
    return pl.BlockSpec((1, length, PAIR), lambda s, h: (s, 0, 0))


def lse_spec(length, lanes):
    return pl.BlockSpec((1, lanes // PAIR, 8, length), lambda s, h: (s, h, 0, 0))


def attend(q, qm, own, rem):
    seqs, length, features = q.shape
    lanes = math.gcd(features, 2 * PAIR)
    other = rem[0].shape[1]
    own_spec, rem_spec = pair_spec(length, lanes), pair_spec(other, lanes)
    return pl.pallas_call(
        attend_kernel,
        grid=(seqs, features // lanes),
        in_specs=[own_spec, mask_spec(length)]
        + [own_spec, mask_spec(length), own_spec]
        + [rem_spec, mask_spec(other), rem_spec],
        out_specs=[own_spec, lse_spec(length, lanes)],
        out_shape=[
            jax.ShapeDtypeStruct(q.shape, BF16),
            jax.ShapeDtypeStruct((seqs, features // PAIR, 8, length), F32),
        ],
        compiler_params=params(60),
        cost_estimate=cost(
            16 * q.size * (length + other), 2 * q.size * 6, q.size * (length + other) // HEAD
        ),
        name="attend",
    )(q, qm, *own, *rem)


def attend_back_part(q, qm, o, g, lse_ref, k, km, v, dk_ref, dv_ref):
    low = low_lanes()
    none = jnp.zeros((1, PAIR), BF16)
    pairs = q.shape[1] // PAIR
    todo = [(pair, head) for pair in range(pairs) for head in range(2)]

    def lanes_of(pair):
        return slice(pair * PAIR, (pair + 1) * PAIR)

    def mine_of(head):
        return ~low if head else low

    def products(pair, head):
        mine, lanes = mine_of(head), lanes_of(pair)
        return (
            dot(jnp.where(mine, k[:, lanes], km), jnp.where(mine, q[:, lanes], qm), NT),
            dot(jnp.where(mine, v[:, lanes], none), g[:, lanes], NT),
        )

    def delta_of(pair, head):
        product = g[:, lanes_of(pair)].astype(F32) * o[:, lanes_of(pair)].astype(F32)
        return lax.dot_general(
            jnp.broadcast_to(jnp.where(mine_of(head), 1.0, 0.0).astype(F32), (8, PAIR)),
            product,
            NT,
            precision=lax.Precision.HIGHEST,
            preferred_element_type=F32,
        )[0:1]

    found = []
    ahead = products(*todo[0])
    for i, (pair, head) in enumerate(todo):
        scores, grads = ahead
        if i + 1 < len(todo):
            ahead = products(*todo[i + 1])
        lanes, mine = lanes_of(pair), mine_of(head)
        if head == 0:
            k_t = k[:, lanes].T
            dk = dv = 0.0
            dq = []
        probs = jnp.exp2(scores * EXPO - lse_ref[pair, head : head + 1, :])
        grads = (probs * (grads - delta_of(pair, head))).astype(BF16)
        dv += dot(probs.astype(BF16), jnp.where(mine, g[:, lanes], none))
        dk += dot(grads, jnp.where(mine, q[:, lanes], none))
        dq.append(dot(k_t[head * HEAD : (head + 1) * HEAD], grads))
        if head == 1:
            dk_ref[:, lanes] = (dk * SCALE).astype(BF16)
            dv_ref[:, lanes] = dv.astype(BF16)
            found.append(jnp.concatenate(dq, axis=0))
    return found


def attend_back_kernel(q_ref, qm_ref, o_ref, g_ref, lse_ref, ko_ref, kmo_ref, vo_ref, kr_ref, kmr_ref,
                       vr_ref, dq_ref, dko_ref, dvo_ref, dkr_ref, dvr_ref):
    parts = ((ko_ref, kmo_ref, vo_ref, dko_ref, dvo_ref), (kr_ref, kmr_ref, vr_ref, dkr_ref, dvr_ref))
    found = [
        attend_back_part(
            q_ref[0], qm_ref[0], o_ref[0], g_ref[0], lse_ref.at[0], k[0], km[0], v[0], dk.at[0], dv.at[0]
        )
        for k, km, v, dk, dv in parts
    ]
    for pair, both in enumerate(zip(*found)):
        dq_ref[0, :, pair * PAIR : (pair + 1) * PAIR] = (sum(both) * SCALE).T.astype(BF16)


def attend_back(q, qm, o, g, lse, own, rem):
    seqs, length, features = q.shape
    lanes = math.gcd(features, 2 * PAIR)
    other = rem[0].shape[1]
    own_spec, rem_spec = pair_spec(length, lanes), pair_spec(other, lanes)
    return pl.pallas_call(
        attend_back_kernel,
        grid=(seqs, features // lanes),
        in_specs=[own_spec, mask_spec(length), own_spec, own_spec, lse_spec(length, lanes)]
        + [own_spec, mask_spec(length), own_spec]
        + [rem_spec, mask_spec(other), rem_spec],
        out_specs=[own_spec] * 3 + [rem_spec] * 2,
        out_shape=[jax.ShapeDtypeStruct(q.shape, BF16)] * 3
        + [jax.ShapeDtypeStruct(rem[0].shape, BF16)] * 2,
        compiler_params=params(60),
        cost_estimate=cost(
            40 * q.size * (length + other), 2 * q.size * 14, q.size * (length + other) // HEAD
        ),
        name="attend_back",
    )(q, qm, o, g, lse, *own, *rem)


def gelu_and_slope(x):
    bell = jnp.exp2(x * x * (-0.5 * math.log2(math.e)))
    below = 1.0 + (0.3275911 / math.sqrt(2.0)) * jnp.abs(x)
    t = pl.reciprocal(below, approx=True)
    t = t * (2.0 - below * t)
    poly = 1.061405429 * t - 1.453152027
    poly = poly * t + 1.421413741
    poly = poly * t - 0.284496736
    poly = poly * t + 0.254829592
    tail = (0.5 * poly) * t * bell
    share = jnp.where(x >= 0.0, 1.0 - tail, tail)
    return x * share, share + x * bell * (1.0 / math.sqrt(2.0 * math.pi))


def mean(values):
    return jnp.sum(values, axis=-1, keepdims=True) * (1.0 / values.shape[-1])


def norm_parts(values):
    centred = values - mean(values)
    scale = lax.rsqrt(mean(centred * centred) + EPSILON)
    return centred * scale, scale


def norm_back(upper, normed, scale):
    return scale * (upper - mean(upper) - normed * mean(upper * normed))


def column_sum(values):
    return jnp.sum(values, axis=0, keepdims=True)


def feed_kernel(layout, tok_ref, att_ref, cot_ref, vec_ref, bu_ref, wo_ref, wu_ref, wd_ref,
                out_ref, bg_ref, ag_ref, vg_ref, dbu_ref, dwu_ref, dwd_ref, dwo_ref,
                act_s, din_s, first_t, feed_t, att_t, bg_s):
    tiles, ff_steps, chunk, wide, narrow = layout
    step = pl.program_id(0)
    tile = tok_ref.shape[0]
    hidden = act_s.shape[1]
    vec = [vec_ref[i : i + 1] for i in range(6)]
    out_bias, gain_one, shift_one, down_bias, gain_two, shift_two = vec

    @pl.when(step == 0)
    def _():
        vg_ref[...] = jnp.zeros_like(vg_ref)
        dbu_ref[...] = jnp.zeros_like(dbu_ref)

    @pl.when(step < tiles)
    def _():
        start = pl.multiple_of(step * tile, tile)
        rows = pl.ds(start, tile)
        att = att_ref[...]
        normed_one, scale_one = norm_parts(
            tok_ref[...].astype(F32) + (dot(att, wo_ref[...]) + out_bias)
        )
        first = normed_one * gain_one + shift_one
        first_low = first.astype(BF16)
        first_t[:, rows] = first_low.T
        att_t[:, rows] = att.T
        feed = jnp.zeros_like(first) + down_bias
        spans = [slice(c, c + chunk) for c in range(0, hidden, chunk)]
        ahead = dot(first_low, wu_ref[:, spans[0]])
        for i, cols in enumerate(spans):
            inner = ahead + bu_ref[:, cols]
            if i + 1 < len(spans):
                ahead = dot(first_low, wu_ref[:, spans[i + 1]])
            active, slope = gelu_and_slope(inner)
            active = active.astype(BF16)
            act_s[rows, cols] = active
            din_s[rows, cols] = slope.astype(BF16)
            feed += dot(active, wd_ref[cols])
        normed_two, scale_two = norm_parts(first + feed)
        out_ref[...] = (normed_two * gain_two + shift_two).astype(BF16)
        cot = cot_ref[...].astype(F32)
        second = norm_back(cot * gain_two, normed_two, scale_two)
        feed_low = second.astype(BF16)
        feed_t[:, rows] = feed_low.T
        back = second
        ahead = dot(feed_low, wd_ref[spans[0]], NT)
        for i, cols in enumerate(spans):
            inner = ahead
            if i + 1 < len(spans):
                ahead = dot(feed_low, wd_ref[spans[i + 1]], NT)
            inner = (inner * din_s[rows, cols].astype(F32)).astype(BF16)
            din_s[rows, cols] = inner
            dbu_ref[:, cols] += column_sum(inner.astype(F32))
            back += dot(inner, wu_ref[:, cols], NT)
        residual = norm_back(back * gain_one, normed_one, scale_one)
        branch_low = residual.astype(BF16)
        bg_ref[...] = branch_low
        bg_s[rows] = branch_low
        ag_ref[...] = dot(branch_low, wo_ref[...], NT).astype(BF16)
        for i, values in enumerate(
            (
                branch_low.astype(F32),
                back * normed_one,
                back,
                feed_low.astype(F32),
                cot * normed_two,
                cot,
            )
        ):
            vg_ref[i : i + 1] += column_sum(values)

    @pl.when((step >= tiles) & (step < tiles + ff_steps))
    def _():
        cols = pl.ds(pl.multiple_of((step - tiles) * wide, wide), wide)
        dwu = dot(first_t[...], din_s[:, cols]).astype(BF16)
        dwu_ref[...] = dwu.reshape(dwu_ref.shape)
        dwd_ref[...] = dot(feed_t[...], act_s[:, cols]).astype(BF16).T

    @pl.when(step >= tiles + ff_steps)
    def _():
        cols = pl.ds(pl.multiple_of((step - tiles - ff_steps) * narrow, narrow), narrow)
        dwo_ref[...] = dot(att_t[...], bg_s[:, cols]).astype(BF16)


def feed_both_ways(tokens, attended, cotangent, vectors, up_bias, wo, wu, wd, groups):
    rows, features = tokens.shape
    hidden = wu.shape[1]
    tile = math.gcd(rows, 256)
    tiles = rows // tile
    wide, narrow = features, math.gcd(features, 384)
    ff_steps, out_steps = hidden // wide, features // narrow
    layout = (tiles, ff_steps, math.gcd(hidden, 512), wide, narrow)
    blocked = (groups, ff_steps, features // groups, wide)
    row_spec = pl.BlockSpec((tile, features), lambda i: (jnp.minimum(i, tiles - 1), 0))

    def ff_at(i):
        return jnp.clip(i - tiles, 0, ff_steps - 1)

    return pl.pallas_call(
        functools.partial(feed_kernel, layout),
        grid=(tiles + ff_steps + out_steps,),
        in_specs=[row_spec] * 3
        + [whole_spec(a.shape) for a in (vectors, up_bias, wo, wu, wd)],
        out_specs=[row_spec] * 3
        + [
            pl.BlockSpec((8, features), lambda i: (0, 0)),
            pl.BlockSpec((1, hidden), lambda i: (0, 0)),
            pl.BlockSpec((groups, 1) + blocked[2:], lambda i: (0, ff_at(i), 0, 0)),
            pl.BlockSpec((wide, features), lambda i: (ff_at(i), 0)),
            pl.BlockSpec(
                (features, narrow),
                lambda i: (0, jnp.clip(i - tiles - ff_steps, 0, out_steps - 1)),
            ),
        ],
        out_shape=[jax.ShapeDtypeStruct(tokens.shape, BF16)] * 3
        + [
            jax.ShapeDtypeStruct((8, features), F32),
            jax.ShapeDtypeStruct((1, hidden), F32),
            jax.ShapeDtypeStruct(blocked, BF16),
            jax.ShapeDtypeStruct(wd.shape, BF16),
            jax.ShapeDtypeStruct(wo.shape, BF16),
        ],
        scratch_shapes=[
            pltpu.VMEM((rows, hidden), BF16),
            pltpu.VMEM((rows, hidden), BF16),
            pltpu.VMEM((features, rows), BF16),
            pltpu.VMEM((features, rows), BF16),
            pltpu.VMEM((features, rows), BF16),
            pltpu.VMEM((rows, features), BF16),
        ],
        compiler_params=params(60),
        cost_estimate=cost(
            6 * rows * features * (features + 2 * hidden),
            2 * (6 * rows * features + 4 * features * hidden + 2 * features * features),
            2 * rows * hidden,
        ),
        name="feed_both_ways",
    )(tokens, attended, cotangent, vectors, up_bias, wo, wu, wd)


def spread(row):
    return jnp.broadcast_to(row, (PAIR, row.shape[1])).T


def as_row(ref):
    return ref[...].astype(F32).reshape(1, ref.shape[0])


def front_kernel(tokens_ref, group_ref, valid_ref, cot_ref, bq_ref, bv_ref, bo_ref, g1_ref, s1_ref, bd_ref,
                 g2_ref, s2_ref, bu_in, wq_any, wk_any, wv_any, wo_any, wu_any, wd_any,
                 out_ref, bg_ref, ag_ref, att_ref, lse_ref, qm_ref, km_ref,
                 first_t, feed_t, vg_ref, dbu_ref, q_any, k_any, v_any, rem_any, act_any, din_any,
                 wq, wk, wv, wo, wu, wd, tok_s, q_s, k_s, v_s, kr_s, vr_s, rem_s, own_codes, code_s, act_s, din_s,
                 bu_ref, weight_sem, out_sem, send_sem, recv_sem):
    s = pl.program_id(0)
    seqs = tok_s.shape[0]
    length, features = tok_s.shape[1:]
    hidden = act_s.shape[1]
    side = lax.axis_index("blk")
    other = {"blk": 1 - side}
    query_bias, value_bias, out_bias, gain_one, shift_one, down_bias, gain_two, shift_two = [
        as_row(ref) for ref in (bq_ref, bv_ref, bo_ref, g1_ref, s1_ref, bd_ref, g2_ref, s2_ref)
    ]
    pairs_of = [(wq_any, wq), (wk_any, wk), (wv_any, wv), (wo_any, wo), (wu_any, wu), (wd_any, wd)]

    def weight(i):
        return pltpu.make_async_copy(*pairs_of[i], weight_sem.at[i])

    def remote(source, target, at):
        return pltpu.make_async_remote_copy(
            src_ref=source,
            dst_ref=target,
            send_sem=send_sem.at[at],
            recv_sem=recv_sem.at[at],
            device_id=other,
            device_id_type=pl.DeviceIdType.MESH,
        )

    def exchange(at):
        return remote(tokens_ref.at[at], rem_s.at[at], at)

    def code_exchange():
        return remote(own_codes, code_s, seqs)

    def whole_out(i):
        source, target = ((q_s, q_any), (k_s, k_any.at[0]), (v_s, v_any.at[0]))[i]
        return pltpu.make_async_copy(source, target, out_sem.at[i])

    def part_out(i, at):
        source, target = (
            (kr_s, k_any.at[1, at]),
            (vr_s, v_any.at[1, at]),
            (rem_s.at[at], rem_any.at[at]),
            (act_s, act_any.at[at]),
            (din_s, din_any.at[at]),
        )[i]
        return pltpu.make_async_copy(source, target, out_sem.at[3 + i])

    @pl.when(s == 0)
    def _():
        barrier = pltpu.get_barrier_semaphore()
        pl.semaphore_signal(barrier, inc=1, device_id=other, device_id_type=pl.DeviceIdType.MESH)
        load = pltpu.make_async_copy(tokens_ref, tok_s, weight_sem.at[len(pairs_of)])
        load.start()
        for i in range(3):
            weight(i).start()
        codes = jnp.where(valid_ref[...] == 1, group_ref[...], -1).astype(F32)
        own_codes[...] = jnp.zeros_like(own_codes)
        own_codes[0:seqs] = codes
        pl.semaphore_wait(barrier, 1)
        exchange(0).start()
        code_exchange().start()
        for i in range(3, len(pairs_of)):
            weight(i).start()
        vg_ref[...] = jnp.zeros_like(vg_ref)
        dbu_ref[...] = jnp.zeros_like(dbu_ref)
        bu_ref[...] = as_row(bu_in)
        load.wait()
        for i in range(3):
            weight(i).wait()

        def project_own(at, carry):
            x = tok_s[at]
            q_s[at] = (dot(x, wq[...]) + query_bias).astype(BF16)
            k_s[at] = dot(x, wk[...]).astype(BF16)
            v_s[at] = (dot(x, wv[...]) + value_bias).astype(BF16)
            return carry

        lax.fori_loop(0, seqs, project_own, 0)
        for i in range(3):
            whole_out(i).start()
        for i in range(3, len(pairs_of)):
            weight(i).wait()
        code_exchange().wait_recv()
        exchange(0).wait_send()
        if seqs > 1:
            exchange(1).start()

    for at in range(seqs):

        @pl.when(s == at)
        def _(at=at):
            exchange(at).wait_recv()
            if at:
                for i in range(3):
                    part_out(i, at - 1).wait()

    x = rem_s[s]
    kr_s[...] = dot(x, wk[...]).astype(BF16)
    vr_s[...] = (dot(x, wv[...]) + value_bias).astype(BF16)
    slot = lax.broadcasted_iota(jnp.int32, (1, PAIR), 1) % HEAD
    slot = slot.astype(F32)
    groups_row = group_ref[pl.ds(s, 1)].astype(F32)
    qm_ref[0] = jnp.where(spread(groups_row) == slot, 1.0, 0.0).astype(BF16)
    km_ref[0, 0] = jnp.where(spread(own_codes[pl.ds(s, 1)]) == slot, 0.0, MASKED).astype(BF16)
    km_ref[1, 0] = jnp.where(spread(code_s[pl.ds(s, 1)]) == slot, 0.0, MASKED).astype(BF16)
    for at in range(seqs):

        @pl.when(s == at)
        def _(at=at):
            for i in range(3):
                part_out(i, at).start()

    groups = features // (2 * PAIR)

    def heads(group, carry):
        lanes = pl.ds(pl.multiple_of(group * 2 * PAIR, 2 * PAIR), 2 * PAIR)
        attend_group(
            q_s[s, :, lanes],
            qm_ref[0],
            [(k_s[s, :, lanes], km_ref[0, 0], v_s[s, :, lanes]), (kr_s[:, lanes], km_ref[1, 0], vr_s[:, lanes])],
            att_ref.at[0, :, lanes],
            lse_ref.at[0, pl.ds(group * 2, 2)],
        )
        return carry

    lax.fori_loop(0, groups, heads, 0)

    for at in range(1, seqs):

        @pl.when(s == at)
        def _(at=at):
            for i in range(3, 5):
                part_out(i, at - 1).wait()

    tile = math.gcd(length, FEED_ROWS)
    chunk = math.gcd(hidden, 512)
    spans = [slice(c, c + chunk) for c in range(0, hidden, chunk)]

    def feed_rows(t, carry):
        rows = pl.ds(pl.multiple_of(t * tile, tile), tile)
        att = att_ref[0, rows]
        normed_one, scale_one = norm_parts(
            tok_s[s, rows].astype(F32) + (dot(att, wo[...]) + out_bias)
        )
        first = normed_one * gain_one + shift_one
        first_low = first.astype(BF16)
        first_t[:, rows] = first_low.T
        feed = jnp.zeros_like(first) + down_bias
        ahead = dot(first_low, wu[:, spans[0]])
        for i, cols in enumerate(spans):
            inner = ahead + bu_ref[:, cols]
            if i + 1 < len(spans):
                ahead = dot(first_low, wu[:, spans[i + 1]])
            active, slope = gelu_and_slope(inner)
            active = active.astype(BF16)
            act_s[rows, cols] = active
            din_s[rows, cols] = slope.astype(BF16)
            feed += dot(active, wd[cols])
        normed_two, scale_two = norm_parts(first + feed)
        out_ref[0, rows] = (normed_two * gain_two + shift_two).astype(BF16)
        cot = cot_ref[0, rows].astype(F32)
        second = norm_back(cot * gain_two, normed_two, scale_two)
        feed_low = second.astype(BF16)
        feed_t[:, rows] = feed_low.T
        back = second
        ahead = dot(feed_low, wd[spans[0]], NT)
        for i, cols in enumerate(spans):
            inner = ahead
            if i + 1 < len(spans):
                ahead = dot(feed_low, wd[spans[i + 1]], NT)
            inner = (inner * din_s[rows, cols].astype(F32)).astype(BF16)
            din_s[rows, cols] = inner
            dbu_ref[:, cols] += column_sum(inner.astype(F32))
            back += dot(inner, wu[:, cols], NT)
        residual = norm_back(back * gain_one, normed_one, scale_one)
        branch_low = residual.astype(BF16)
        bg_ref[0, rows] = branch_low
        ag_ref[0, rows] = dot(branch_low, wo[...], NT).astype(BF16)
        for i, values in enumerate(
            (
                branch_low.astype(F32),
                back * normed_one,
                back,
                feed_low.astype(F32),
                cot * normed_two,
                cot,
            )
        ):
            vg_ref[i : i + 1] += column_sum(values)
        return carry

    lax.fori_loop(0, length // tile, feed_rows, 0)

    for at in range(seqs):

        @pl.when(s == at)
        def _(at=at):
            for i in range(3, 5):
                part_out(i, at).start()
            if at < seqs - 1:
                exchange(at + 1).wait_send()
            if at + 2 < seqs:
                exchange(at + 2).start()
            if at == seqs - 1:
                for i in range(3):
                    whole_out(i).wait()
                for i in range(5):
                    part_out(i, at).wait()
                code_exchange().wait_send()


def front(tokens, group_ids, valid, cotangent, vectors, up_bias, weights):
    seqs, length, features = tokens.shape
    hidden = up_bias.shape[0]
    pairs = features // PAIR
    anywhere = pl.BlockSpec(memory_space=pl.ANY)

    def at_seq(*shape):
        return pl.BlockSpec((1,) + shape, lambda s: (s,) + (0,) * len(shape))

    def of_seqs(*shape, dtype=BF16):
        return jax.ShapeDtypeStruct((seqs,) + shape, dtype)

    def fixed(*shape):
        return pl.BlockSpec(shape, lambda s: (0,) * len(shape))

    rows, mask, lses, wide = (length, features), (length, PAIR), (pairs, 8, length), (length, hidden)
    turned = pl.BlockSpec((features, length), lambda s: (0, s))
    return pl.pallas_call(
        front_kernel,
        grid=(seqs,),
        in_specs=[anywhere, whole_spec(group_ids.shape), whole_spec(valid.shape), at_seq(*rows)]
        + [whole_spec(v.shape) for v in vectors + (up_bias,)]
        + [anywhere] * 6,
        out_specs=[at_seq(*rows)] * 4
        + [at_seq(*lses), at_seq(*mask)]
        + [pl.BlockSpec((2, 1) + mask, lambda s: (0, s, 0, 0))]
        + [turned] * 2
        + [fixed(8, features), fixed(1, hidden)]
        + [anywhere] * 6,
        out_shape=[of_seqs(*rows)] * 4
        + [of_seqs(*lses, dtype=F32), of_seqs(*mask)]
        + [jax.ShapeDtypeStruct((2, seqs) + mask, BF16)]
        + [jax.ShapeDtypeStruct((features, seqs * length), BF16)] * 2
        + [jax.ShapeDtypeStruct((8, features), F32), jax.ShapeDtypeStruct((1, hidden), F32)]
        + [of_seqs(*rows)]
        + [jax.ShapeDtypeStruct((2, seqs) + rows, BF16)] * 2
        + [of_seqs(*rows)]
        + [of_seqs(*wide)] * 2,
        scratch_shapes=[pltpu.VMEM(w.shape, BF16) for w in weights]
        + [pltpu.VMEM(tokens.shape, BF16)] * 4
        + [pltpu.VMEM(rows, BF16)] * 2
        + [pltpu.VMEM(tokens.shape, BF16)]
        + [pltpu.VMEM((seqs + -seqs % 8, length), F32)] * 2
        + [pltpu.VMEM(wide, BF16)] * 2
        + [pltpu.VMEM((1, hidden), F32)]
        + [pltpu.SemaphoreType.DMA((7,)), pltpu.SemaphoreType.DMA((8,))]
        + [pltpu.SemaphoreType.DMA((seqs + 1,))] * 2,
        compiler_params=pltpu.CompilerParams(
            collective_id=2, has_side_effects=True, vmem_limit_bytes=63 * MIB
        ),
        cost_estimate=cost(
            2 * tokens.size * (9 * features + 4 * hidden + 8 * length), 2 * 20 * tokens.size, tokens.size * 24
        ),
        name="front",
    )(tokens, group_ids, valid, cotangent, *vectors, up_bias, *weights)


def feed_weights_kernel(blocks, first_ref, din_ref, feed_ref, act_ref, att_any, bg_any,
                        dwu_ref, dwd_ref, dwo_ref, up_s, up_in, down_s, down_in, out_s, out_in,
                        att_s, bg_s, near_sem, send_sem, recv_sem):
    step = pl.program_id(0)
    features = first_ref.shape[0]
    me = lax.axis_index("dp")
    core = me % 2
    other = {"dp": me + 1 - 2 * core}

    def loads():
        return [
            pltpu.make_async_copy(att_any, att_s, near_sem.at[0]),
            pltpu.make_async_copy(bg_any, bg_s, near_sem.at[1]),
        ]

    def swaps(block):
        if block == blocks:
            pairs = [(out_s.at[:, 1 - core], out_in)]
        else:
            pairs = [
                (up_s.at[block % 2, :, 1 - core], up_in.at[block]),
                (down_s.at[block % 2, :, 1 - core], down_in.at[block]),
            ]
        return [
            pltpu.make_async_remote_copy(
                src_ref=source,
                dst_ref=target,
                send_sem=send_sem.at[2 * block + i],
                recv_sem=recv_sem.at[2 * block + i],
                device_id=other,
                device_id_type=pl.DeviceIdType.MESH,
            )
            for i, (source, target) in enumerate(pairs)
        ]

    @pl.when(step == 0)
    def _():
        for load in loads():
            load.start()
        barrier = pltpu.get_barrier_semaphore()
        pl.semaphore_signal(barrier, inc=1, device_id=other, device_id_type=pl.DeviceIdType.MESH)
        pl.semaphore_wait(barrier, 1)

    @pl.when(step < blocks)
    def _():
        slot = step % 2
        up_s[slot] = dot(first_ref[...], din_ref[...]).astype(BF16).reshape(up_s.shape[1:])
        down_s[slot] = dot(feed_ref[...], act_ref[...]).astype(BF16).T.reshape(down_s.shape[1:])

    for block in range(blocks):

        @pl.when(step == block)
        def _(block=block):
            for swap in swaps(block):
                swap.start()

    @pl.when(step == blocks)
    def _():
        for load in loads():
            load.wait()
        out_s[...] = dot(att_s[...].T, bg_s[...]).astype(BF16).reshape(out_s.shape)
        for swap in swaps(blocks):
            swap.start()

    for block in range(blocks):

        @pl.when(step == block + 1)
        def _(block=block):
            for swap in swaps(block):
                swap.wait()
            dwu_ref[:, 0] = (up_s[block % 2, :, core].astype(F32) + up_in[block].astype(F32)).astype(BF16)
            dwd_ref[...] = (down_s[block % 2, :, core].astype(F32) + down_in[block].astype(F32)).astype(BF16)

    @pl.when(step == blocks + 1)
    def _():
        for swap in swaps(blocks):
            swap.wait()
        dwo_ref[...] = (out_s[:, core].astype(F32) + out_in[...].astype(F32)).astype(BF16)


def feed_weights(first_t, din, feed_t, act, att, bg):
    dp = lax.axis_size("dp")
    features, rows = first_t.shape
    hidden = act.shape[1]
    blocks, half, low, deep = hidden // features, dp // 2, features // dp, hidden // dp
    each = half // blocks
    wide_spec = pl.BlockSpec((rows, features), lambda i: (0, jnp.minimum(i, blocks - 1)))
    anywhere = pl.BlockSpec(memory_space=pl.ANY)

    def behind(i):
        return jnp.clip(i - 1, 0, blocks - 1)

    return pl.pallas_call(
        functools.partial(feed_weights_kernel, blocks),
        grid=(blocks + 2,),
        in_specs=[
            whole_spec(first_t.shape),
            wide_spec,
            whole_spec(feed_t.shape),
            wide_spec,
            anywhere,
            anywhere,
        ],
        out_specs=[
            pl.BlockSpec((half, 1, low, features), lambda i: (0, behind(i), 0, 0)),
            pl.BlockSpec((each, deep, features), lambda i: (behind(i), 0, 0)),
            pl.BlockSpec((half, low, features), lambda i: (0, 0, 0)),
        ],
        out_shape=[
            jax.ShapeDtypeStruct((half, blocks, low, features), BF16),
            jax.ShapeDtypeStruct((half, deep, features), BF16),
            jax.ShapeDtypeStruct((half, low, features), BF16),
        ],
        scratch_shapes=[
            pltpu.VMEM((2, half, 2, low, features), BF16),
            pltpu.VMEM((blocks, half, low, features), BF16),
            pltpu.VMEM((2, each, 2, deep, features), BF16),
            pltpu.VMEM((blocks, each, deep, features), BF16),
            pltpu.VMEM((half, 2, low, features), BF16),
            pltpu.VMEM((half, low, features), BF16),
            pltpu.VMEM(att.shape, BF16),
            pltpu.VMEM(bg.shape, BF16),
            pltpu.SemaphoreType.DMA((2,)),
            pltpu.SemaphoreType.DMA((2 * blocks + 2,)),
            pltpu.SemaphoreType.DMA((2 * blocks + 2,)),
        ],
        compiler_params=pltpu.CompilerParams(
            collective_id=3, has_side_effects=True, vmem_limit_bytes=63 * MIB
        ),
        cost_estimate=cost(
            2 * rows * features * (2 * hidden + features), 4 * rows * (hidden + 2 * features)
        ),
        name="feed_weights",
    )(first_t, din, feed_t, act, att, bg)


def own_back_kernel(bg_ref, dq_ref, dk_ref, dv_ref, wq_ref, wk_ref, wv_ref, out_ref):
    total = bg_ref[0].astype(F32) + dot(dq_ref[0], wq_ref[...], NT)
    total += dot(dk_ref[0], wk_ref[...], NT)
    total += dot(dv_ref[0], wv_ref[...], NT)
    out_ref[0] = total.astype(BF16)


def rem_back_kernel(dk_ref, dv_ref, wk_ref, wv_ref, out_ref):
    total = dot(dk_ref[0], wk_ref[...], NT) + dot(dv_ref[0], wv_ref[...], NT)
    out_ref[0] = total.astype(BF16)


def tokens_back(kernel, rows, weights):
    seqs, length, features = rows[0].shape
    tile = math.gcd(length, 512)
    row_spec = pl.BlockSpec((1, tile, features), lambda s, i: (s, i, 0))
    size = rows[0].size
    return pl.pallas_call(
        kernel,
        grid=(seqs, length // tile),
        in_specs=[row_spec] * len(rows) + [whole_spec(w.shape) for w in weights],
        out_specs=row_spec,
        out_shape=jax.ShapeDtypeStruct(rows[0].shape, BF16),
        compiler_params=params(60),
        cost_estimate=cost(2 * size * features * len(weights), 2 * size * (1 + len(rows))),
        name="tokens_back",
    )(*rows, *weights)


def weights_back_kernel(tok_ref, rem_ref, dq_ref, dko_ref, dvo_ref, dkr_ref, dvr_ref,
                        wq_ref, wk_ref, wv_ref, bq_ref, bv_ref, tok_t, rem_t):
    @pl.when(pl.program_id(0) == 0)
    def _():
        tok_t[...] = tok_ref[...].T
        rem_t[...] = rem_ref[...].T

    wq_ref[...] = dot(tok_t[...], dq_ref[...]).astype(BF16)
    wk_ref[...] = (dot(tok_t[...], dko_ref[...]) + dot(rem_t[...], dkr_ref[...])).astype(BF16)
    wv_ref[...] = (dot(tok_t[...], dvo_ref[...]) + dot(rem_t[...], dvr_ref[...])).astype(BF16)
    bq_ref[...] = column_sum(dq_ref[...].astype(F32))
    bv_ref[...] = column_sum(dvo_ref[...].astype(F32)) + column_sum(dvr_ref[...].astype(F32))


def weights_back(tok, rem, dq, dko, dvo, dkr, dvr):
    rows, features = tok.shape
    others = rem.shape[0]
    wide = math.gcd(features, 256)
    own_spec = pl.BlockSpec((rows, wide), lambda j: (0, j))
    rem_spec = pl.BlockSpec((others, wide), lambda j: (0, j))
    bias_spec = pl.BlockSpec((1, wide), lambda j: (0, j))
    return pl.pallas_call(
        weights_back_kernel,
        grid=(features // wide,),
        in_specs=[
            whole_spec(tok.shape),
            whole_spec(rem.shape),
            own_spec,
            own_spec,
            own_spec,
            rem_spec,
            rem_spec,
        ],
        out_specs=[pl.BlockSpec((features, wide), lambda j: (0, j))] * 3 + [bias_spec] * 2,
        out_shape=[jax.ShapeDtypeStruct((features, features), BF16)] * 3
        + [jax.ShapeDtypeStruct((1, features), F32)] * 2,
        scratch_shapes=[
            pltpu.VMEM((features, rows), BF16),
            pltpu.VMEM((features, others), BF16),
        ],
        compiler_params=params(60),
        cost_estimate=cost(
            2 * features * features * (3 * rows + 2 * others),
            2 * (4 * tok.size + 3 * rem.size + 3 * features * features),
        ),
        name="weights_back",
    )(tok, rem, dq, dko, dvo, dkr, dvr)


def halve(value, axis, bit):
    size = lax.axis_size(axis)
    mine = (lax.axis_index(axis) >> bit) & 1
    pairs = value.reshape((value.shape[0] // 2, 2) + value.shape[1:])
    keep = lax.dynamic_index_in_dim(pairs, mine, 1, keepdims=False)
    send = lax.dynamic_index_in_dim(pairs, 1 - mine, 1, keepdims=False)
    came = lax.ppermute(send, axis, [(i, i ^ (1 << bit)) for i in range(size)])
    return keep.astype(F32) + came.astype(F32)


def scatter_sum(value, low=True):
    dp, blk = lax.axis_size("dp"), lax.axis_size("blk")
    if dp & (dp - 1) or blk & (blk - 1):
        return lax.psum_scatter(
            value.astype(F32), ("dp", "blk"), scatter_dimension=0, tiled=True
        )
    kept = value.dtype
    each = value.shape[0] // (dp * blk)
    value = value.reshape((dp, blk * each) + value.shape[1:])
    for bit in range(dp.bit_length() - 1):
        value = halve(value, "dp", bit).astype(kept)
    value = value.reshape((blk, each) + value.shape[2:])
    for bit in range(blk.bit_length() - 1):
        value = halve(value, "blk", bit)
        value = value if (2 << bit) == blk else value.astype(kept)
    return value.reshape(value.shape[1:]).astype(F32)


class Unit:
    def __init__(self, parts, rows, columns, halves, order, outs):
        self.parts, self.rows, self.columns = parts, rows, columns
        self.halves, self.order, self.outs = halves, order, outs
        self.first = 1 if parts else 0
        self.half = rows // (2 * halves)
        self.last_type = BF16 if (rows // 2) % 16 == 0 else F32


def timetable(units, bits, seqs, groups, slot_us, token_us):
    free, pending, table = {}, [], []
    slots = seqs * groups * 2

    def launch(key, now):
        kind, which, step = key
        if kind == "tokens":
            link, us = "blk", token_us
        elif kind == "vectors":
            link, us = None, 1.0
        else:
            unit = units[which]
            bit = unit.order[step] if step < bits else "blk"
            size = unit.rows * unit.columns * (1 << max(bits - 1 - step, 0)) * 2e-5
            size = size * 0.5 if step == bits else size
            link = {0: "core", 1: "y"}.get(bit, bit if bit == "blk" else "z")
            us = size * 2 * (1.0 if bit == "blk" or bit < 3 else 2.0)
            us = us / 8 if bit == 0 else us
        start = max(now, free.get(link, 0.0))
        if link:
            free[link] = start + us
        pending.append((start + us + 1.5, key))

    for u, unit in enumerate(units):
        if unit.parts:
            launch(("unit", u, 1), 0.0)
    first_group = sum(1 for unit in units if unit.parts)
    now = 0.0
    while len(table) < slots or pending:
        slot = len(table)
        if slot < slots:
            now = (slot + 1) * slot_us
            s, part, h = slot // (2 * groups), slot // groups % 2, slot % groups
            if part == 0 and h == groups - 1:
                launch(("tokens", s, 0), now)
            if part == 1 and s == seqs - 1:
                launch(("unit", first_group + h, 0), now)
            if slot == slots - 1:
                launch(("vectors", 0, 0), now)
            due = sorted(p for p in pending if p[0] <= now)
        else:
            due = [min(pending)]
            now = max(now + 0.3, due[0][0])
        table.append([key for _, key in due])
        for found in due:
            pending.remove(found)
            kind, which, step = found[1]
            if kind != "tokens" and step < bits:
                launch((kind, which, step + 1), now)
    return table[:slots], [key for keys in table[slots:] for key in keys]


def back_kernel(units, bits, groups, table, tail, n_out, *refs):
    (q_ref, qm_ref, o_ref, g_ref, lse_ref, k_ref, km_ref, v_ref,
     bg_ref, tok_ref, rem_ref, wq_ref, wk_ref, wv_ref, vg_ref, vu_ref) = refs[:16]
    sources, refs = refs[16:19], list(refs[19:])
    tokens_out, rem_in, *outs = refs[:n_out]
    refs = refs[n_out:]
    kept = [refs.pop(0) for _ in units]
    landed = [
        [refs.pop(0) if k >= unit.first else None for k in range(bits)] for unit in units
    ]
    wide = [refs.pop(0) for _ in units]
    parting = [refs.pop(0) for _ in units]
    last = [refs.pop(0) for _ in units]
    (weight_sum, group_src, total_s, turned, dq_part, dq_s, dk_s, dv_s,
     rem_out, vec, vec_in, bias_sum, send_sem, recv_sem, local_sem) = refs
    step = pl.program_id(0)
    steps = pl.num_programs(0)
    s, part, h = step // (2 * groups), step // groups % 2, step % groups
    seqs = rem_out.shape[0]
    features = tok_ref.shape[2]
    me, side = lax.axis_index("dp"), lax.axis_index("blk")
    own = [(me // (1 << bit)) % 2 for bit in range(bits)]
    partner = [{"dp": me + (1 << bit) * (1 - 2 * own[bit])} for bit in range(bits)]
    partner.append({"blk": 1 - side})
    first_group = sum(1 for unit in units if unit.parts)
    lead = (slice(None),) * (bits - 1)

    sems = {}
    for u, unit in enumerate(units):
        for k in range(unit.first, bits + 1):
            for p in range(len(unit.parts) if unit.parts and k == unit.first else 1):
                sems["unit", u, k, p] = len(sems)
    for k in range(bits + 1):
        sems["vectors", 0, k, 0] = len(sems)
    for k in range(seqs):
        sems["tokens", k, 0, 0] = len(sems)

    def remote(source, target, device, key):
        return pltpu.make_async_remote_copy(
            src_ref=source,
            dst_ref=target,
            send_sem=send_sem.at[sems[key]],
            recv_sem=recv_sem.at[sems[key]],
            device_id=device,
            device_id_type=pl.DeviceIdType.MESH,
        )

    def spot(unit, k, value):
        found = []
        for bit in range(bits - 1, 0, -1):
            at = unit.order.index(bit)
            found.append(own[bit] if at < k else value if at == k else slice(None))
        return tuple(found)

    def copies(kind, which, k):
        if kind == "tokens":
            return [remote(rem_out.at[which], rem_in.at[which], partner[bits], (kind, which, 0, 0))]
        if kind == "vectors":
            return [remote(vec.at[k], vec_in.at[k], partner[k], (kind, 0, k, 0))]
        u, unit = which, units[which]
        if k == bits:
            return [remote(parting[u], last[u], partner[bits], (kind, u, k, 0))]
        if unit.parts and k == 1:
            found, row = [], 0
            place = spot(unit, k, 1 - own[unit.order[k]])
            open_at = (slice(None),) * (bits - 2)
            for p, (source, first, rows) in enumerate(unit.parts):
                found.append(
                    remote(
                        sources[source].at[place + (pl.ds(first, rows),)],
                        landed[u][k].at[open_at + (pl.ds(row, rows),)],
                        partner[unit.order[k]],
                        (kind, u, k, p),
                    )
                )
                row += rows
            return found
        if k:
            bit = unit.order[k]
            source = kept[u].at[spot(unit, k, 1 - own[bit])]
            return [remote(source, landed[u][k], partner[bit], (kind, u, k, 0))]
        source = group_src.at[(u - first_group,) + lead + (1 - own[0],)]
        return [remote(source, landed[u][0], partner[0], (kind, u, 0, 0))]

    def near_copies(u):
        found, row = [], 0
        for p, (source, first, rows) in enumerate(units[u].parts):
            found.append(
                pltpu.make_async_copy(
                    sources[source].at[lead + (pl.ds(first, rows),)],
                    kept[u].at[lead + (pl.ds(row, rows),)],
                    local_sem.at[sems["unit", u, 1, p]],
                )
            )
            row += rows
        return found

    def launch(*key):
        for copy in copies(*key):
            copy.start()

    def halves_of(u, which):
        unit = units[u]
        return [
            wide[u][pl.ds(pl.multiple_of(i * 2 * unit.half + which * unit.half, 8), unit.half)]
            for i in range(unit.halves)
        ]

    def receive(kind, which, k):
        for copy in copies(kind, which, k):
            copy.wait_recv()
        if kind == "tokens":
            return
        if kind == "vectors":
            vec[k + 1] = vec[k] + vec_in[k]
            if k < bits:
                launch(kind, 0, k + 1)
            return
        u, unit = which, units[which]
        if k == bits:
            for i, (mine, (out, rows, columns)) in enumerate(zip(halves_of(u, side), unit.outs)):
                came = last[u][...].astype(F32)[i * unit.half : (i + 1) * unit.half]
                outs[out][rows, columns] = mine + came
            return
        if unit.parts and k == 1:
            for copy in near_copies(u):
                copy.wait()
        place = spot(unit, k, own[unit.order[k]])
        open_at = [i for i, at in enumerate(place) if isinstance(at, slice)]

        def add(n, carry):
            at, where = list(place), []
            for digit, i in enumerate(open_at):
                at[i] = (n // (1 << (len(open_at) - 1 - digit))) % 2
                where.append(at[i])
            at = tuple(at)
            if unit.parts or k:
                mine = kept[u][at]
            else:
                mine = group_src[(u - first_group,) + at + (own[0],)]
            total = mine.astype(F32) + landed[u][k][tuple(where)].astype(F32)
            if k == bits - 1:
                wide[u][...] = total
            else:
                kept[u][at] = total.astype(BF16)
            return carry

        if open_at:
            lax.fori_loop(0, 1 << len(open_at), add, 0)
        else:
            add(0, 0)
        if k == bits - 1:
            pieces = halves_of(u, 1 - side)
            pieces = pieces[0] if len(pieces) == 1 else jnp.concatenate(pieces, axis=0)
            parting[u][...] = pieces.astype(unit.last_type)
        launch(kind, u, k + 1)

    @pl.when(step == 0)
    def _():
        barrier = pltpu.get_barrier_semaphore()
        for other in partner:
            pl.semaphore_signal(barrier, inc=1, device_id=other, device_id_type=pl.DeviceIdType.MESH)
        pl.semaphore_wait(barrier, bits + 1)
        for u, unit in enumerate(units):
            if unit.parts:
                launch("unit", u, 1)
                for copy in near_copies(u):
                    copy.start()
        weight_sum[...] = jnp.zeros_like(weight_sum)
        bias_sum[...] = jnp.zeros_like(bias_sum)

    @pl.when(step % (2 * groups) == 0)
    def _():
        turned[...] = rem_ref[0].T
        total_s[...] = jnp.zeros_like(total_s)

    @pl.when(step % (2 * groups) == groups)
    def _():
        turned[...] = tok_ref[0].T
        total_s[...] = bg_ref[0].astype(F32)

    found = attend_back_part(
        q_ref[0], qm_ref[0], o_ref[0], g_ref[0], lse_ref.at[0], k_ref[0, 0], km_ref[0, 0], v_ref[0, 0], dk_s, dv_s
    )
    width = q_ref.shape[2]
    columns = pl.ds(pl.multiple_of(h * width, width), width)
    dk, dv = dk_s[...], dv_s[...]
    more = dot(dk, wk_ref[:, columns], NT) + dot(dv, wv_ref[:, columns], NT)
    weight_sum[h, 1] += dot(turned[...], dk)
    weight_sum[h, 2] += dot(turned[...], dv)
    bias_sum[h, 1:2] += column_sum(dv.astype(F32))

    @pl.when(part == 0)
    def _():
        total_s[...] += more
        for pair, value in enumerate(found):
            dq_part[h, pair] = value

    @pl.when(part == 1)
    def _():
        for pair, value in enumerate(found):
            value = (value + dq_part[h, pair]) * SCALE
            dq_s[:, pair * PAIR : (pair + 1) * PAIR] = value.T.astype(BF16)
        dq = dq_s[...]
        total_s[...] += more + dot(dq, wq_ref[:, columns], NT)
        weight_sum[h, 0] += dot(turned[...], dq)
        bias_sum[h, 0:1] += column_sum(dq.astype(F32))

    for at in range(seqs):

        @pl.when(step == at * 2 * groups + groups - 1)
        def _(at=at):
            rem_out[at] = total_s[...].astype(BF16)
            launch("tokens", at, 0)

    @pl.when(step % (2 * groups) == 2 * groups - 1)
    def _():
        tokens_out[0] = total_s[...].astype(BF16)

    for at in range(groups):

        @pl.when(step == steps - groups + at)
        def _(at=at):
            rows = features // (1 << bits)
            for i in range(3):
                piece = weight_sum[at, i].astype(BF16)
                piece = piece.reshape((2,) * bits + (rows, piece.shape[1]))
                group_src[(at,) + (slice(None),) * bits + (slice(i * rows, (i + 1) * rows),)] = piece
            launch("unit", first_group + at, 0)

    @pl.when(step == steps - 1)
    def _():
        vec[0] = jnp.zeros_like(vec[0])
        vec[0, 0:6] = vg_ref[0:6]
        for at in range(groups):
            vec[0, 6:8, at * width : (at + 1) * width] = bias_sum[at, 0:2]
        blocks = vu_ref.shape[1] // features
        for at in range(blocks):
            vec[0, 8 + at : 9 + at] = vu_ref[:, at * features : (at + 1) * features]
        launch("vectors", 0, 0)

    for at, keys in enumerate(table):
        if keys:

            @pl.when(step == at)
            def _(keys=keys):
                for key in keys:
                    receive(*key)

    @pl.when(step == steps - 1)
    def _():
        for key in tail:
            receive(*key)
        shards = (1 << bits) * 2
        place = me * 2 + side
        share = features // shards
        rows = pltpu.roll(vec[bits + 1, 0:8], (shards - place) * share % features, 1)
        outs[-1][0:8] = rows[:, :PAIR]
        share = vu_ref.shape[1] // shards
        each = features // share
        row = vec[bits + 1, pl.ds(8 + place // each, 1)]
        rows = pltpu.roll(jnp.broadcast_to(row, (8, features)), (each - place % each) * share % features, 1)
        outs[-1][8:16] = rows[:, :PAIR]
        for u, unit in enumerate(units):
            for k in range(unit.first, bits + 1):
                for copy in copies("unit", u, k):
                    copy.wait_send()
        for k in range(bits + 1):
            copies("vectors", 0, k)[0].wait_send()
        for k in range(seqs):
            copies("tokens", k, 0)[0].wait_send()


def back_and_sum(q, qm, o, g, lse, k, km, v, bg, tokens, rem_tokens, weights, dwd, dwu, dwo, vg, vu):
    bits = lax.axis_size("dp").bit_length() - 1
    seqs, length, features = q.shape
    width = math.gcd(features, 2 * PAIR)
    groups, pairs = features // width, width // PAIR
    low, deep, blocks = dwo.shape[1], dwd.shape[1], dwu.shape[1]
    lead = (2,) * bits
    sources = [x.reshape(lead[1:] + (-1, features)) for x in (dwd, dwu, dwo)]
    order = tuple(range(bits))
    every = slice(None)
    units = []
    quarter = deep // 4
    for i in range(2):
        at = slice(i * quarter, (i + 1) * quarter)
        parts = [(0, i * quarter, quarter), (0, (2 + i) * quarter, quarter)]
        units.append(Unit(parts, 2 * quarter, features, 1, order, [(0, at, every)]))
    for i in range(2):
        found = range(i * blocks // 2, (i + 1) * blocks // 2)
        units.append(
            Unit(
                [(1, found[0] * low, len(found) * low)],
                len(found) * low,
                features,
                len(found),
                order,
                [(1, every, slice(b * features, (b + 1) * features)) for b in found],
            )
        )
    units.append(Unit([(2, 0, low)], low, features, 1, order, [(2, every, every)]))
    for h in range(groups):
        columns = slice(h * width, (h + 1) * width)
        units.append(Unit(None, 3 * low, width, 3, order, [(3 + i, every, columns) for i in range(3)]))
    table, tail = timetable(units, bits, seqs, groups, 5.0, length * features * 4e-5)

    half = low // 2
    out_shape = [
        jax.ShapeDtypeStruct(q.shape, BF16),
        jax.ShapeDtypeStruct(q.shape, BF16),
        jax.ShapeDtypeStruct((deep // 2, features), F32),
        jax.ShapeDtypeStruct((half, blocks * features), F32),
        *(jax.ShapeDtypeStruct((half, features), F32) for _ in range(4)),
        jax.ShapeDtypeStruct((16, PAIR), F32),
    ]
    tops = lead[1:]
    scratch = [pltpu.VMEM(tops + (u.rows, u.columns), BF16) for u in units]
    for u in units:
        scratch += [pltpu.VMEM(tops[k:] + (u.rows, u.columns), BF16) for k in range(u.first, bits)]
    scratch += [pltpu.VMEM((u.rows, u.columns), F32) for u in units]
    scratch += [pltpu.VMEM((u.rows // 2, u.columns), u.last_type) for u in units] * 2
    count = sum((len(u.parts) if u.parts else 1) + bits for u in units) + bits + 1 + seqs
    scratch += [
        pltpu.VMEM((groups, 3, features, width), F32),
        pltpu.VMEM((groups,) + lead + (3 * low, width), BF16),
        pltpu.VMEM((length, features), F32),
        pltpu.VMEM((features, length), BF16),
        pltpu.VMEM((groups, pairs, PAIR, length), F32),
        *(pltpu.VMEM((length, width), BF16) for _ in range(3)),
        pltpu.VMEM((seqs, length, features), BF16),
        pltpu.VMEM((bits + 2, 16, features), F32),
        pltpu.VMEM((bits + 1, 16, features), F32),
        pltpu.VMEM((groups, 8, width), F32),
        *(pltpu.SemaphoreType.DMA((count,)) for _ in range(3)),
    ]
    turn = 2 * groups
    heads_at = pl.BlockSpec((1, length, width), lambda i: (i // turn, 0, i % groups))
    keys_at = pl.BlockSpec(
        (1, 1, length, width), lambda i: (1 - i // groups % 2, i // turn, 0, i % groups)
    )
    rows_at = pl.BlockSpec((1, length, features), lambda i: (i // turn, 0, 0), pipeline_mode=pl.Buffered(1))

    def fixed(shape):
        return pl.BlockSpec(shape, lambda i: (0,) * len(shape), pipeline_mode=pl.Buffered(1))

    return pl.pallas_call(
        functools.partial(back_kernel, units, bits, groups, table, tail, len(out_shape)),
        grid=(seqs * turn,),
        in_specs=[
            heads_at,
            pl.BlockSpec((1, length, PAIR), lambda i: (i // turn, 0, 0)),
            heads_at,
            heads_at,
            pl.BlockSpec((1, pairs, 8, length), lambda i: (i // turn, i % groups, 0, 0)),
            keys_at,
            pl.BlockSpec((1, 1, length, PAIR), lambda i: (1 - i // groups % 2, i // turn, 0, 0)),
            keys_at,
            rows_at,
            rows_at,
            rows_at,
        ]
        + [whole_spec(w.shape) for w in weights + (vg, vu)]
        + [pl.BlockSpec(memory_space=pl.ANY)] * 3,
        out_specs=[
            pl.BlockSpec((1, length, features), lambda i: (i // turn, 0, 0)),
            pl.BlockSpec(memory_space=pl.ANY),
        ]
        + [fixed(s.shape) for s in out_shape[2:]],
        out_shape=out_shape,
        scratch_shapes=scratch,
        compiler_params=pltpu.CompilerParams(
            collective_id=1, has_side_effects=True, vmem_limit_bytes=63 * MIB
        ),
        cost_estimate=cost(80 * q.size * length, 2 * q.size * 14, 2 * q.size * length // HEAD),
        name="back_and_sum",
    )(q, qm, o, g, lse, k, km, v, bg, tokens, rem_tokens, *weights, vg, vu, *sources)


def finish_kernel(own_ref, rem_ref, *refs):
    ins, outs = refs[:7], refs[7:]
    outs[0][...] = (own_ref[...].astype(F32) + rem_ref[...].astype(F32)).astype(BF16)

    @pl.when(pl.program_id(0) == 0)
    def _():
        for source, target in zip(ins[:6], outs[1:7]):
            target[...] = source[...]
        for i, target in enumerate(outs[7:]):
            target[...] = ins[6][i, : target.shape[0]]


def finish(own, rem, matrices, vectors, shares):
    seqs, length, features = own.shape
    row_spec = pl.BlockSpec((1, length, features), lambda s: (s, 0, 0))

    def fixed(shape):
        return pl.BlockSpec(shape, lambda s: (0,) * len(shape))

    shapes = [m.shape for m in matrices] + [(n,) for n in shares]
    return pl.pallas_call(
        finish_kernel,
        grid=(seqs,),
        in_specs=[row_spec] * 2 + [fixed(m.shape) for m in matrices] + [fixed(vectors.shape)],
        out_specs=[row_spec] + [fixed(s) for s in shapes],
        out_shape=[jax.ShapeDtypeStruct(own.shape, BF16)] + [jax.ShapeDtypeStruct(s, F32) for s in shapes],
        compiler_params=params(60),
        cost_estimate=cost(own.size, 6 * own.size),
        name="finish",
    )(own, rem, *matrices, vectors)


def back_plainly(q, qm, o, g, lse, own, rem, bg, tokens, rem_tokens, weights, dwd, dwu, dwo, vg, vu):
    seqs, length, features = q.shape
    dp, blk = lax.axis_size("dp"), lax.axis_size("blk")
    dq, dko, dvo, dkr, dvr = attend_back(q, qm, o, g, lse, own, rem)
    rem_gradient = tokens_back(rem_back_kernel, (dkr, dvr), weights[1:])
    came = [
        lax.ppermute(part, "blk", [((i + r) % blk, i) for i in range(blk)])
        for r, part in enumerate(jnp.split(rem_gradient, blk - 1, axis=1), 1)
    ]
    flat = [v.reshape(-1, features) for v in (tokens, rem_tokens, dq, dko, dvo, dkr, dvr)]
    dwq, dwk, dwv, dbq, dbv = weights_back(*flat)
    total = tokens_back(own_back_kernel, (bg, dq, dko, dvo), weights).astype(F32)
    for part in came:
        total += part.astype(F32)
    dwu = jnp.moveaxis(dwu[0], 0, 1).reshape(features, -1)
    summed = [scatter_sum(w) for w in (dwd, dwu, dwo, dwq, dwk, dwv)]
    rows = [vg[i] for i in range(6)] + [dbq, dbv, vu]
    rows = [scatter_sum(v.reshape(dp * blk, -1)) for v in rows]
    return [total.astype(BF16)] + summed + [[v[0] for v in rows]]


def body(
    tokens,
    query_weight,
    query_bias,
    key_weight,
    value_weight,
    value_bias,
    out_weight,
    out_bias,
    gain_one,
    shift_one,
    up_weight,
    up_bias,
    down_weight,
    down_bias,
    gain_two,
    shift_two,
    group_ids,
    valid_mask,
    cotangent,
):
    seqs, length, features = tokens.shape
    rows = seqs * length
    blk = lax.axis_size("blk")

    def from_others(value):
        found = [
            lax.ppermute(value, "blk", [(i, (i + r) % blk) for i in range(blk)])
            for r in range(1, blk)
        ]
        return found[0] if len(found) == 1 else jnp.concatenate(found, axis=1)

    codes = jnp.where(valid_mask == 1, group_ids, -1)
    dp = lax.axis_size("dp")
    by_kernel = blk == 2 and dp & (dp - 1) == 0 and dp > 1 and (features // dp) % 16 == 0
    projections = (query_weight, key_weight, value_weight)
    vectors = (
        query_bias,
        value_bias,
        out_bias,
        gain_one,
        shift_one,
        down_bias,
        gain_two,
        shift_two,
    )

    if by_kernel:
        (block_out, branch_gradient, attended_gradient, attended, lse, query_mask, key_masks,
         first_t, feed_t, vector_gradients, up_bias_gradient, queries, keys, values,
         rem_tokens, active, inner_gradient) = front(
            tokens,
            group_ids,
            valid_mask,
            cotangent,
            vectors,
            up_bias,
            projections + (out_weight, up_weight, down_weight),
        )
        dwu, dwd, dwo = feed_weights(
            first_t,
            inner_gradient.reshape(rows, -1),
            feed_t,
            active.reshape(rows, -1),
            attended.reshape(rows, features),
            branch_gradient.reshape(rows, features),
        )
        own_gradient, rem_gradient, *matrices, vectors = back_and_sum(
            queries,
            query_mask,
            attended,
            attended_gradient,
            lse,
            keys,
            key_masks,
            values,
            branch_gradient,
            tokens,
            rem_tokens,
            projections,
            dwd,
            dwu,
            dwo,
            vector_gradients,
            up_bias_gradient,
        )
        shares = [features // (dp * blk)] * 8 + [up_bias.size // (dp * blk)]
        found = finish(own_gradient, rem_gradient, matrices, vectors, shares)
        tokens_gradient, dwd, dwu, dwo, dwq, dwk, dwv, *rows_left = found
    else:
        rem_tokens = from_others(tokens)
        rem_codes = from_others(codes.astype(BF16)).astype(jnp.int32)
        slot = jnp.arange(PAIR, dtype=jnp.int32) % HEAD

        def key_mask(code):
            return jnp.where(code[:, :, None] == slot, 0.0, MASKED).astype(BF16)

        query_mask = (group_ids[:, :, None] == slot).astype(BF16)
        vectors = jnp.stack(vectors).astype(F32)
        queries, own_keys, own_values = project(tokens, vectors, projections)
        rem_keys, rem_values = project(rem_tokens, vectors, projections[1:])
        own = (own_keys, key_mask(codes), own_values)
        rem = (rem_keys, key_mask(rem_codes), rem_values)
        attended, lse = attend(queries, query_mask, own, rem)
        (block_out, branch_gradient, attended_gradient, vector_gradients, up_bias_gradient,
         dwu, dwd, dwo) = feed_both_ways(
            tokens.reshape(rows, features),
            attended.reshape(rows, features),
            cotangent.reshape(rows, features),
            vectors[2:],
            up_bias.astype(F32)[None],
            out_weight,
            up_weight,
            down_weight,
            1,
        )
        tokens_gradient, dwd, dwu, dwo, dwq, dwk, dwv, rows_left = back_plainly(
            queries,
            query_mask,
            attended,
            attended_gradient.reshape(tokens.shape),
            lse,
            own,
            rem,
            branch_gradient.reshape(tokens.shape),
            tokens,
            rem_tokens,
            projections,
            dwd,
            dwu,
            dwo,
            vector_gradients,
            up_bias_gradient,
        )
    dbo, dg1, ds1, dbd, dg2, ds2, dbq, dbv, dbu = rows_left
    return (
        block_out.reshape(tokens.shape),
        tokens_gradient,
        dwq,
        dbq,
        dwk,
        dwv,
        dbv,
        dwo,
        dbo,
        dg1,
        ds1,
        dwu,
        dbu,
        dwd,
        dbd,
        dg2,
        ds2,
    )


def solution(mesh):
    rows, shared, pair = P("dp", "blk", None), P(), P("dp", "blk")
    matrix, vector = P(("dp", "blk"), None), P(("dp", "blk"))
    return jax.shard_map(
        body,
        mesh=mesh,
        in_specs=(rows,) + (shared,) * 15 + (pair, pair, rows),
        out_specs=(
            rows,
            rows,
            matrix,
            vector,
            matrix,
            matrix,
            vector,
            matrix,
            vector,
            vector,
            vector,
            matrix,
            vector,
            matrix,
            vector,
            vector,
            vector,
        ),
        check_vma=False,
    )
```

```python
import functools
import math

import jax
import jax.numpy as jnp
from jax import lax
from jax.experimental import pallas as pl
from jax.experimental.pallas import tpu as pltpu
from jax.sharding import PartitionSpec as P

HEAD = 64
PAIR = 2 * HEAD
EPSILON = 1e-12
MASKED = -1e30
FLOOR = -3e38
SCALE = HEAD**-0.5
EXPO = SCALE * math.log2(math.e)
NN = (((1,), (0,)), ((), ()))
NT = (((1,), (1,)), ((), ()))
F32 = jnp.float32
BF16 = jnp.bfloat16
MIB = 1 << 20
FEED_ROWS = 512


def dot(left, right, dims=NN):
    return lax.dot_general(left, right, dims, preferred_element_type=F32)


def whole_spec(shape):
    return pl.BlockSpec(shape, lambda *_: (0,) * len(shape), pipeline_mode=pl.Buffered(1))


def params(limit):
    return pltpu.CompilerParams(vmem_limit_bytes=limit * MIB)


def cost(flops, touched, exps=0):
    return pl.CostEstimate(flops=int(flops), bytes_accessed=int(touched), transcendentals=int(exps))


def project_kernel(has_query, *refs):
    if has_query:
        x_ref, bias_ref, wq_ref, wk_ref, wv_ref, q_ref, k_ref, v_ref = refs
    else:
        x_ref, bias_ref, wk_ref, wv_ref, k_ref, v_ref = refs
    x = x_ref[0]
    if has_query:
        q_ref[0] = (dot(x, wq_ref[...]) + bias_ref[0:1]).astype(BF16)
    k_ref[0] = dot(x, wk_ref[...]).astype(BF16)
    v_ref[0] = (dot(x, wv_ref[...]) + bias_ref[1:2]).astype(BF16)


def project(x, bias, weights):
    seqs, length, features = x.shape
    tile = math.gcd(length, 512)
    grid = (seqs, length // tile)
    row_spec = pl.BlockSpec((1, tile, features), lambda s, i: (s, i, 0))
    return pl.pallas_call(
        functools.partial(project_kernel, len(weights) == 3),
        grid=grid,
        in_specs=[row_spec, whole_spec(bias.shape)] + [whole_spec(w.shape) for w in weights],
        out_specs=[row_spec] * len(weights),
        out_shape=[jax.ShapeDtypeStruct(x.shape, BF16)] * len(weights),
        compiler_params=params(60),
        cost_estimate=cost(
            2 * x.size * features * len(weights), 2 * x.size * (1 + len(weights))
        ),
        name="project",
    )(x, bias, *weights)


def low_lanes():
    return lax.broadcasted_iota(jnp.int32, (1, PAIR), 1) < HEAD


def attend_group(q, qm, sources, o_ref, lse_ref):
    length = q.shape[0]
    tile = math.gcd(length, 256)
    low = low_lanes()
    one = jnp.ones((1, PAIR), BF16)
    todo = [
        (pair, row, head)
        for pair in range(q.shape[1] // PAIR)
        for row in range(0, length, tile)
        for head in range(2)
    ]

    def lanes_of(pair):
        return slice(pair * PAIR, (pair + 1) * PAIR)

    def mine_of(head):
        return ~low if head else low

    def scores_of(pair, row, head):
        mine, lanes = mine_of(head), lanes_of(pair)
        q_side = jnp.where(mine, q[row : row + tile, lanes], qm[row : row + tile])
        return [dot(q_side, jnp.where(mine, k[:, lanes], km), NT) for k, km, _ in sources]

    ahead = scores_of(*todo[0])
    for i, (pair, row, head) in enumerate(todo):
        scores = ahead
        if i + 1 < len(todo):
            ahead = scores_of(*todo[i + 1])
        top = functools.reduce(
            jnp.maximum, [jnp.max(part, axis=-1, keepdims=True) for part in scores]
        )
        weights = [jnp.exp2((part - top) * EXPO).astype(BF16) for part in scores]
        total = sum(
            dot(w, jnp.where(mine_of(head), v[:, lanes_of(pair)], one))
            for w, (_, _, v) in zip(weights, sources)
        )
        if head == 0:
            earlier, earlier_top = total, top
            continue
        totals = pltpu.roll(jnp.where(low, total, earlier), HEAD, 1)
        rows = slice(row, row + tile)
        o_ref[rows, lanes_of(pair)] = (jnp.where(low, earlier, total) / totals).astype(BF16)
        lse = (jnp.where(low, earlier_top, top) * EXPO + jnp.log2(totals)).T
        lse_ref[pair, 0:1, rows] = lse[0:1]
        lse_ref[pair, 1:2, rows] = lse[HEAD : HEAD + 1]


def attend_kernel(q_ref, qm_ref, ko_ref, kmo_ref, vo_ref, kr_ref, kmr_ref, vr_ref, o_ref, lse_ref):
    sources = [(ko_ref[0], kmo_ref[0], vo_ref[0]), (kr_ref[0], kmr_ref[0], vr_ref[0])]
    attend_group(q_ref[0], qm_ref[0], sources, o_ref.at[0], lse_ref.at[0])


def pair_spec(length, lanes):
    return pl.BlockSpec((1, length, lanes), lambda s, h: (s, 0, h))


def mask_spec(length):
    return pl.BlockSpec((1, length, PAIR), lambda s, h: (s, 0, 0))


def lse_spec(length, lanes):
    return pl.BlockSpec((1, lanes // PAIR, 8, length), lambda s, h: (s, h, 0, 0))


def attend(q, qm, own, rem):
    seqs, length, features = q.shape
    lanes = math.gcd(features, 2 * PAIR)
    other = rem[0].shape[1]
    own_spec, rem_spec = pair_spec(length, lanes), pair_spec(other, lanes)
    return pl.pallas_call(
        attend_kernel,
        grid=(seqs, features // lanes),
        in_specs=[own_spec, mask_spec(length)]
        + [own_spec, mask_spec(length), own_spec]
        + [rem_spec, mask_spec(other), rem_spec],
        out_specs=[own_spec, lse_spec(length, lanes)],
        out_shape=[
            jax.ShapeDtypeStruct(q.shape, BF16),
            jax.ShapeDtypeStruct((seqs, features // PAIR, 8, length), F32),
        ],
        compiler_params=params(60),
        cost_estimate=cost(
            16 * q.size * (length + other), 2 * q.size * 6, q.size * (length + other) // HEAD
        ),
        name="attend",
    )(q, qm, *own, *rem)


def attend_back_part(q, qm, o, g, lse_ref, k, km, v, dk_ref, dv_ref):
    low = low_lanes()
    none = jnp.zeros((1, PAIR), BF16)
    pairs = q.shape[1] // PAIR
    todo = [(pair, head) for pair in range(pairs) for head in range(2)]

    def lanes_of(pair):
        return slice(pair * PAIR, (pair + 1) * PAIR)

    def mine_of(head):
        return ~low if head else low

    def products(pair, head):
        mine, lanes = mine_of(head), lanes_of(pair)
        return (
            dot(jnp.where(mine, k[:, lanes], km), jnp.where(mine, q[:, lanes], qm), NT),
            dot(jnp.where(mine, v[:, lanes], none), g[:, lanes], NT),
        )

    def delta_of(pair, head):
        product = g[:, lanes_of(pair)].astype(F32) * o[:, lanes_of(pair)].astype(F32)
        return lax.dot_general(
            jnp.broadcast_to(jnp.where(mine_of(head), 1.0, 0.0).astype(F32), (8, PAIR)),
            product,
            NT,
            precision=lax.Precision.HIGHEST,
            preferred_element_type=F32,
        )[0:1]

    found = []
    ahead = products(*todo[0])
    for i, (pair, head) in enumerate(todo):
        scores, grads = ahead
        if i + 1 < len(todo):
            ahead = products(*todo[i + 1])
        lanes, mine = lanes_of(pair), mine_of(head)
        if head == 0:
            k_t = k[:, lanes].T
            dk = dv = 0.0
            dq = []
        probs = jnp.exp2(scores * EXPO - lse_ref[pair, head : head + 1, :])
        grads = (probs * (grads - delta_of(pair, head))).astype(BF16)
        dv += dot(probs.astype(BF16), jnp.where(mine, g[:, lanes], none))
        dk += dot(grads, jnp.where(mine, q[:, lanes], none))
        dq.append(dot(k_t[head * HEAD : (head + 1) * HEAD], grads))
        if head == 1:
            dk_ref[:, lanes] = (dk * SCALE).astype(BF16)
            dv_ref[:, lanes] = dv.astype(BF16)
            found.append(jnp.concatenate(dq, axis=0))
    return found


def attend_back_kernel(q_ref, qm_ref, o_ref, g_ref, lse_ref, ko_ref, kmo_ref, vo_ref, kr_ref, kmr_ref,
                       vr_ref, dq_ref, dko_ref, dvo_ref, dkr_ref, dvr_ref):
    parts = ((ko_ref, kmo_ref, vo_ref, dko_ref, dvo_ref), (kr_ref, kmr_ref, vr_ref, dkr_ref, dvr_ref))
    found = [
        attend_back_part(
            q_ref[0], qm_ref[0], o_ref[0], g_ref[0], lse_ref.at[0], k[0], km[0], v[0], dk.at[0], dv.at[0]
        )
        for k, km, v, dk, dv in parts
    ]
    for pair, both in enumerate(zip(*found)):
        dq_ref[0, :, pair * PAIR : (pair + 1) * PAIR] = (sum(both) * SCALE).T.astype(BF16)


def attend_back(q, qm, o, g, lse, own, rem):
    seqs, length, features = q.shape
    lanes = math.gcd(features, 2 * PAIR)
    other = rem[0].shape[1]
    own_spec, rem_spec = pair_spec(length, lanes), pair_spec(other, lanes)
    return pl.pallas_call(
        attend_back_kernel,
        grid=(seqs, features // lanes),
        in_specs=[own_spec, mask_spec(length), own_spec, own_spec, lse_spec(length, lanes)]
        + [own_spec, mask_spec(length), own_spec]
        + [rem_spec, mask_spec(other), rem_spec],
        out_specs=[own_spec] * 3 + [rem_spec] * 2,
        out_shape=[jax.ShapeDtypeStruct(q.shape, BF16)] * 3
        + [jax.ShapeDtypeStruct(rem[0].shape, BF16)] * 2,
        compiler_params=params(60),
        cost_estimate=cost(
            40 * q.size * (length + other), 2 * q.size * 14, q.size * (length + other) // HEAD
        ),
        name="attend_back",
    )(q, qm, o, g, lse, *own, *rem)


def gelu_and_slope(x):
    bell = jnp.exp2(x * x * (-0.5 * math.log2(math.e)))
    below = 1.0 + (0.3275911 / math.sqrt(2.0)) * jnp.abs(x)
    t = pl.reciprocal(below, approx=True)
    t = t * (2.0 - below * t)
    poly = 1.061405429 * t - 1.453152027
    poly = poly * t + 1.421413741
    poly = poly * t - 0.284496736
    poly = poly * t + 0.254829592
    tail = (0.5 * poly) * t * bell
    share = jnp.where(x >= 0.0, 1.0 - tail, tail)
    return x * share, share + x * bell * (1.0 / math.sqrt(2.0 * math.pi))


def mean(values):
    return jnp.sum(values, axis=-1, keepdims=True) * (1.0 / values.shape[-1])


def norm_parts(values):
    centred = values - mean(values)
    scale = lax.rsqrt(mean(centred * centred) + EPSILON)
    return centred * scale, scale


def norm_back(upper, normed, scale):
    return scale * (upper - mean(upper) - normed * mean(upper * normed))


def column_sum(values):
    return jnp.sum(values, axis=0, keepdims=True)


def feed_kernel(layout, tok_ref, att_ref, cot_ref, vec_ref, bu_ref, wo_ref, wu_ref, wd_ref,
                out_ref, bg_ref, ag_ref, vg_ref, dbu_ref, dwu_ref, dwd_ref, dwo_ref,
                act_s, din_s, first_t, feed_t, att_t, bg_s):
    tiles, ff_steps, chunk, wide, narrow = layout
    step = pl.program_id(0)
    tile = tok_ref.shape[0]
    hidden = act_s.shape[1]
    vec = [vec_ref[i : i + 1] for i in range(6)]
    out_bias, gain_one, shift_one, down_bias, gain_two, shift_two = vec

    @pl.when(step == 0)
    def _():
        vg_ref[...] = jnp.zeros_like(vg_ref)
        dbu_ref[...] = jnp.zeros_like(dbu_ref)

    @pl.when(step < tiles)
    def _():
        start = pl.multiple_of(step * tile, tile)
        rows = pl.ds(start, tile)
        att = att_ref[...]
        normed_one, scale_one = norm_parts(
            tok_ref[...].astype(F32) + (dot(att, wo_ref[...]) + out_bias)
        )
        first = normed_one * gain_one + shift_one
        first_low = first.astype(BF16)
        first_t[:, rows] = first_low.T
        att_t[:, rows] = att.T
        feed = jnp.zeros_like(first) + down_bias
        spans = [slice(c, c + chunk) for c in range(0, hidden, chunk)]
        ahead = dot(first_low, wu_ref[:, spans[0]])
        for i, cols in enumerate(spans):
            inner = ahead + bu_ref[:, cols]
            if i + 1 < len(spans):
                ahead = dot(first_low, wu_ref[:, spans[i + 1]])
            active, slope = gelu_and_slope(inner)
            active = active.astype(BF16)
            act_s[rows, cols] = active
            din_s[rows, cols] = slope.astype(BF16)
            feed += dot(active, wd_ref[cols])
        normed_two, scale_two = norm_parts(first + feed)
        out_ref[...] = (normed_two * gain_two + shift_two).astype(BF16)
        cot = cot_ref[...].astype(F32)
        second = norm_back(cot * gain_two, normed_two, scale_two)
        feed_low = second.astype(BF16)
        feed_t[:, rows] = feed_low.T
        back = second
        ahead = dot(feed_low, wd_ref[spans[0]], NT)
        for i, cols in enumerate(spans):
            inner = ahead
            if i + 1 < len(spans):
                ahead = dot(feed_low, wd_ref[spans[i + 1]], NT)
            inner = (inner * din_s[rows, cols].astype(F32)).astype(BF16)
            din_s[rows, cols] = inner
            dbu_ref[:, cols] += column_sum(inner.astype(F32))
            back += dot(inner, wu_ref[:, cols], NT)
        residual = norm_back(back * gain_one, normed_one, scale_one)
        branch_low = residual.astype(BF16)
        bg_ref[...] = branch_low
        bg_s[rows] = branch_low
        ag_ref[...] = dot(branch_low, wo_ref[...], NT).astype(BF16)
        for i, values in enumerate(
            (
                branch_low.astype(F32),
                back * normed_one,
                back,
                feed_low.astype(F32),
                cot * normed_two,
                cot,
            )
        ):
            vg_ref[i : i + 1] += column_sum(values)

    @pl.when((step >= tiles) & (step < tiles + ff_steps))
    def _():
        cols = pl.ds(pl.multiple_of((step - tiles) * wide, wide), wide)
        dwu = dot(first_t[...], din_s[:, cols]).astype(BF16)
        dwu_ref[...] = dwu.reshape(dwu_ref.shape)
        dwd_ref[...] = dot(feed_t[...], act_s[:, cols]).astype(BF16).T

    @pl.when(step >= tiles + ff_steps)
    def _():
        cols = pl.ds(pl.multiple_of((step - tiles - ff_steps) * narrow, narrow), narrow)
        dwo_ref[...] = dot(att_t[...], bg_s[:, cols]).astype(BF16)


def feed_both_ways(tokens, attended, cotangent, vectors, up_bias, wo, wu, wd, groups):
    rows, features = tokens.shape
    hidden = wu.shape[1]
    tile = math.gcd(rows, 256)
    tiles = rows // tile
    wide, narrow = features, math.gcd(features, 384)
    ff_steps, out_steps = hidden // wide, features // narrow
    layout = (tiles, ff_steps, math.gcd(hidden, 512), wide, narrow)
    blocked = (groups, ff_steps, features // groups, wide)
    row_spec = pl.BlockSpec((tile, features), lambda i: (jnp.minimum(i, tiles - 1), 0))

    def ff_at(i):
        return jnp.clip(i - tiles, 0, ff_steps - 1)

    return pl.pallas_call(
        functools.partial(feed_kernel, layout),
        grid=(tiles + ff_steps + out_steps,),
        in_specs=[row_spec] * 3
        + [whole_spec(a.shape) for a in (vectors, up_bias, wo, wu, wd)],
        out_specs=[row_spec] * 3
        + [
            pl.BlockSpec((8, features), lambda i: (0, 0)),
            pl.BlockSpec((1, hidden), lambda i: (0, 0)),
            pl.BlockSpec((groups, 1) + blocked[2:], lambda i: (0, ff_at(i), 0, 0)),
            pl.BlockSpec((wide, features), lambda i: (ff_at(i), 0)),
            pl.BlockSpec(
                (features, narrow),
                lambda i: (0, jnp.clip(i - tiles - ff_steps, 0, out_steps - 1)),
            ),
        ],
        out_shape=[jax.ShapeDtypeStruct(tokens.shape, BF16)] * 3
        + [
            jax.ShapeDtypeStruct((8, features), F32),
            jax.ShapeDtypeStruct((1, hidden), F32),
            jax.ShapeDtypeStruct(blocked, BF16),
            jax.ShapeDtypeStruct(wd.shape, BF16),
            jax.ShapeDtypeStruct(wo.shape, BF16),
        ],
        scratch_shapes=[
            pltpu.VMEM((rows, hidden), BF16),
            pltpu.VMEM((rows, hidden), BF16),
            pltpu.VMEM((features, rows), BF16),
            pltpu.VMEM((features, rows), BF16),
            pltpu.VMEM((features, rows), BF16),
            pltpu.VMEM((rows, features), BF16),
        ],
        compiler_params=params(60),
        cost_estimate=cost(
            6 * rows * features * (features + 2 * hidden),
            2 * (6 * rows * features + 4 * features * hidden + 2 * features * features),
            2 * rows * hidden,
        ),
        name="feed_both_ways",
    )(tokens, attended, cotangent, vectors, up_bias, wo, wu, wd)


def spread(row):
    return jnp.broadcast_to(row, (PAIR, row.shape[1])).T


def as_row(ref):
    return ref[...].astype(F32).reshape(1, ref.shape[0])


def front_kernel(tokens_ref, group_ref, valid_ref, cot_ref, bq_ref, bv_ref, bo_ref, g1_ref, s1_ref, bd_ref,
                 g2_ref, s2_ref, bu_in, wq_any, wk_any, wv_any, wo_any, wu_any, wd_any,
                 out_ref, bg_ref, ag_ref, att_ref, lse_ref, qm_ref, km_ref,
                 first_t, feed_t, vg_ref, dbu_ref, q_any, k_any, v_any, rem_any, act_any, din_any,
                 wq, wk, wv, wo, wu, wd, tok_s, q_s, k_s, v_s, kr_s, vr_s, rem_s, own_codes, code_s, act_s, din_s,
                 bu_ref, weight_sem, out_sem, send_sem, recv_sem):
    s = pl.program_id(0)
    seqs = tok_s.shape[0]
    length, features = tok_s.shape[1:]
    hidden = act_s.shape[1]
    side = lax.axis_index("blk")
    other = {"blk": 1 - side}
    query_bias, value_bias, out_bias, gain_one, shift_one, down_bias, gain_two, shift_two = [
        as_row(ref) for ref in (bq_ref, bv_ref, bo_ref, g1_ref, s1_ref, bd_ref, g2_ref, s2_ref)
    ]
    pairs_of = [(wq_any, wq), (wk_any, wk), (wv_any, wv), (wo_any, wo), (wu_any, wu), (wd_any, wd)]

    def weight(i):
        return pltpu.make_async_copy(*pairs_of[i], weight_sem.at[i])

    def remote(source, target, at):
        return pltpu.make_async_remote_copy(
            src_ref=source,
            dst_ref=target,
            send_sem=send_sem.at[at],
            recv_sem=recv_sem.at[at],
            device_id=other,
            device_id_type=pl.DeviceIdType.MESH,
        )

    def exchange(at):
        return remote(tokens_ref.at[at], rem_s.at[at], at)

    def code_exchange():
        return remote(own_codes, code_s, seqs)

    def whole_out(i):
        source, target = ((q_s, q_any), (k_s, k_any.at[0]), (v_s, v_any.at[0]))[i]
        return pltpu.make_async_copy(source, target, out_sem.at[i])

    def part_out(i, at):
        source, target = (
            (kr_s, k_any.at[1, at]),
            (vr_s, v_any.at[1, at]),
            (rem_s.at[at], rem_any.at[at]),
            (act_s, act_any.at[at]),
            (din_s, din_any.at[at]),
        )[i]
        return pltpu.make_async_copy(source, target, out_sem.at[3 + i])

    @pl.when(s == 0)
    def _():
        barrier = pltpu.get_barrier_semaphore()
        pl.semaphore_signal(barrier, inc=1, device_id=other, device_id_type=pl.DeviceIdType.MESH)
        load = pltpu.make_async_copy(tokens_ref, tok_s, weight_sem.at[len(pairs_of)])
        load.start()
        for i in range(3):
            weight(i).start()
        codes = jnp.where(valid_ref[...] == 1, group_ref[...], -1).astype(F32)
        own_codes[...] = jnp.zeros_like(own_codes)
        own_codes[0:seqs] = codes
        pl.semaphore_wait(barrier, 1)
        exchange(0).start()
        code_exchange().start()
        for i in range(3, len(pairs_of)):
            weight(i).start()
        vg_ref[...] = jnp.zeros_like(vg_ref)
        dbu_ref[...] = jnp.zeros_like(dbu_ref)
        bu_ref[...] = as_row(bu_in)
        load.wait()
        for i in range(3):
            weight(i).wait()

        def project_own(at, carry):
            x = tok_s[at]
            q_s[at] = (dot(x, wq[...]) + query_bias).astype(BF16)
            k_s[at] = dot(x, wk[...]).astype(BF16)
            v_s[at] = (dot(x, wv[...]) + value_bias).astype(BF16)
            return carry

        lax.fori_loop(0, seqs, project_own, 0)
        for i in range(3):
            whole_out(i).start()
        for i in range(3, len(pairs_of)):
            weight(i).wait()
        code_exchange().wait_recv()
        exchange(0).wait_send()
        if seqs > 1:
            exchange(1).start()

    for at in range(seqs):

        @pl.when(s == at)
        def _(at=at):
            exchange(at).wait_recv()
            if at:
                for i in range(3):
                    part_out(i, at - 1).wait()

    x = rem_s[s]
    kr_s[...] = dot(x, wk[...]).astype(BF16)
    vr_s[...] = (dot(x, wv[...]) + value_bias).astype(BF16)
    slot = lax.broadcasted_iota(jnp.int32, (1, PAIR), 1) % HEAD
    slot = slot.astype(F32)
    groups_row = group_ref[pl.ds(s, 1)].astype(F32)
    qm_ref[0] = jnp.where(spread(groups_row) == slot, 1.0, 0.0).astype(BF16)
    km_ref[0, 0] = jnp.where(spread(own_codes[pl.ds(s, 1)]) == slot, 0.0, MASKED).astype(BF16)
    km_ref[1, 0] = jnp.where(spread(code_s[pl.ds(s, 1)]) == slot, 0.0, MASKED).astype(BF16)
    for at in range(seqs):

        @pl.when(s == at)
        def _(at=at):
            for i in range(3):
                part_out(i, at).start()

    groups = features // (2 * PAIR)

    def heads(group, carry):
        lanes = pl.ds(pl.multiple_of(group * 2 * PAIR, 2 * PAIR), 2 * PAIR)
        attend_group(
            q_s[s, :, lanes],
            qm_ref[0],
            [(k_s[s, :, lanes], km_ref[0, 0], v_s[s, :, lanes]), (kr_s[:, lanes], km_ref[1, 0], vr_s[:, lanes])],
            att_ref.at[0, :, lanes],
            lse_ref.at[0, pl.ds(group * 2, 2)],
        )
        return carry

    lax.fori_loop(0, groups, heads, 0)

    for at in range(1, seqs):

        @pl.when(s == at)
        def _(at=at):
            for i in range(3, 5):
                part_out(i, at - 1).wait()

    tile = math.gcd(length, FEED_ROWS)
    chunk = math.gcd(hidden, 512)
    spans = [slice(c, c + chunk) for c in range(0, hidden, chunk)]

    def feed_rows(t, carry):
        rows = pl.ds(pl.multiple_of(t * tile, tile), tile)
        att = att_ref[0, rows]
        normed_one, scale_one = norm_parts(
            tok_s[s, rows].astype(F32) + (dot(att, wo[...]) + out_bias)
        )
        first = normed_one * gain_one + shift_one
        first_low = first.astype(BF16)
        first_t[:, rows] = first_low.T
        feed = jnp.zeros_like(first) + down_bias
        ahead = dot(first_low, wu[:, spans[0]])
        for i, cols in enumerate(spans):
            inner = ahead + bu_ref[:, cols]
            if i + 1 < len(spans):
                ahead = dot(first_low, wu[:, spans[i + 1]])
            active, slope = gelu_and_slope(inner)
            active = active.astype(BF16)
            act_s[rows, cols] = active
            din_s[rows, cols] = slope.astype(BF16)
            feed += dot(active, wd[cols])
        normed_two, scale_two = norm_parts(first + feed)
        out_ref[0, rows] = (normed_two * gain_two + shift_two).astype(BF16)
        cot = cot_ref[0, rows].astype(F32)
        second = norm_back(cot * gain_two, normed_two, scale_two)
        feed_low = second.astype(BF16)
        feed_t[:, rows] = feed_low.T
        back = second
        ahead = dot(feed_low, wd[spans[0]], NT)
        for i, cols in enumerate(spans):
            inner = ahead
            if i + 1 < len(spans):
                ahead = dot(feed_low, wd[spans[i + 1]], NT)
            inner = (inner * din_s[rows, cols].astype(F32)).astype(BF16)
            din_s[rows, cols] = inner
            dbu_ref[:, cols] += column_sum(inner.astype(F32))
            back += dot(inner, wu[:, cols], NT)
        residual = norm_back(back * gain_one, normed_one, scale_one)
        branch_low = residual.astype(BF16)
        bg_ref[0, rows] = branch_low
        ag_ref[0, rows] = dot(branch_low, wo[...], NT).astype(BF16)
        for i, values in enumerate(
            (
                branch_low.astype(F32),
                back * normed_one,
                back,
                feed_low.astype(F32),
                cot * normed_two,
                cot,
            )
        ):
            vg_ref[i : i + 1] += column_sum(values)
        return carry

    lax.fori_loop(0, length // tile, feed_rows, 0)

    for at in range(seqs):

        @pl.when(s == at)
        def _(at=at):
            for i in range(3, 5):
                part_out(i, at).start()
            if at < seqs - 1:
                exchange(at + 1).wait_send()
            if at + 2 < seqs:
                exchange(at + 2).start()
            if at == seqs - 1:
                for i in range(3):
                    whole_out(i).wait()
                for i in range(5):
                    part_out(i, at).wait()
                code_exchange().wait_send()


def front(tokens, group_ids, valid, cotangent, vectors, up_bias, weights):
    seqs, length, features = tokens.shape
    hidden = up_bias.shape[0]
    pairs = features // PAIR
    anywhere = pl.BlockSpec(memory_space=pl.ANY)

    def at_seq(*shape):
        return pl.BlockSpec((1,) + shape, lambda s: (s,) + (0,) * len(shape))

    def of_seqs(*shape, dtype=BF16):
        return jax.ShapeDtypeStruct((seqs,) + shape, dtype)

    def fixed(*shape):
        return pl.BlockSpec(shape, lambda s: (0,) * len(shape))

    rows, mask, lses, wide = (length, features), (length, PAIR), (pairs, 8, length), (length, hidden)
    turned = pl.BlockSpec((features, length), lambda s: (0, s))
    return pl.pallas_call(
        front_kernel,
        grid=(seqs,),
        in_specs=[anywhere, whole_spec(group_ids.shape), whole_spec(valid.shape), at_seq(*rows)]
        + [whole_spec(v.shape) for v in vectors + (up_bias,)]
        + [anywhere] * 6,
        out_specs=[at_seq(*rows)] * 4
        + [at_seq(*lses), at_seq(*mask)]
        + [pl.BlockSpec((2, 1) + mask, lambda s: (0, s, 0, 0))]
        + [turned] * 2
        + [fixed(8, features), fixed(1, hidden)]
        + [anywhere] * 6,
        out_shape=[of_seqs(*rows)] * 4
        + [of_seqs(*lses, dtype=F32), of_seqs(*mask)]
        + [jax.ShapeDtypeStruct((2, seqs) + mask, BF16)]
        + [jax.ShapeDtypeStruct((features, seqs * length), BF16)] * 2
        + [jax.ShapeDtypeStruct((8, features), F32), jax.ShapeDtypeStruct((1, hidden), F32)]
        + [of_seqs(*rows)]
        + [jax.ShapeDtypeStruct((2, seqs) + rows, BF16)] * 2
        + [of_seqs(*rows)]
        + [of_seqs(*wide)] * 2,
        scratch_shapes=[pltpu.VMEM(w.shape, BF16) for w in weights]
        + [pltpu.VMEM(tokens.shape, BF16)] * 4
        + [pltpu.VMEM(rows, BF16)] * 2
        + [pltpu.VMEM(tokens.shape, BF16)]
        + [pltpu.VMEM((seqs + -seqs % 8, length), F32)] * 2
        + [pltpu.VMEM(wide, BF16)] * 2
        + [pltpu.VMEM((1, hidden), F32)]
        + [pltpu.SemaphoreType.DMA((7,)), pltpu.SemaphoreType.DMA((8,))]
        + [pltpu.SemaphoreType.DMA((seqs + 1,))] * 2,
        compiler_params=pltpu.CompilerParams(
            collective_id=2, has_side_effects=True, vmem_limit_bytes=63 * MIB
        ),
        cost_estimate=cost(
            2 * tokens.size * (9 * features + 4 * hidden + 8 * length), 2 * 20 * tokens.size, tokens.size * 24
        ),
        name="front",
    )(tokens, group_ids, valid, cotangent, *vectors, up_bias, *weights)


def feed_weights_kernel(blocks, first_ref, din_ref, feed_ref, act_ref, att_any, bg_any,
                        dwu_ref, dwd_ref, dwo_ref, up_s, up_in, down_s, down_in, out_s, out_in,
                        att_s, bg_s, near_sem, send_sem, recv_sem):
    step = pl.program_id(0)
    features = first_ref.shape[0]
    me = lax.axis_index("dp")
    core = me % 2
    other = {"dp": me + 1 - 2 * core}

    def loads():
        return [
            pltpu.make_async_copy(att_any, att_s, near_sem.at[0]),
            pltpu.make_async_copy(bg_any, bg_s, near_sem.at[1]),
        ]

    def swaps(block):
        if block == blocks:
            pairs = [(out_s.at[:, 1 - core], out_in)]
        else:
            pairs = [
                (up_s.at[block % 2, :, 1 - core], up_in.at[block]),
                (down_s.at[block % 2, :, 1 - core], down_in.at[block]),
            ]
        return [
            pltpu.make_async_remote_copy(
                src_ref=source,
                dst_ref=target,
                send_sem=send_sem.at[2 * block + i],
                recv_sem=recv_sem.at[2 * block + i],
                device_id=other,
                device_id_type=pl.DeviceIdType.MESH,
            )
            for i, (source, target) in enumerate(pairs)
        ]

    @pl.when(step == 0)
    def _():
        for load in loads():
            load.start()
        barrier = pltpu.get_barrier_semaphore()
        pl.semaphore_signal(barrier, inc=1, device_id=other, device_id_type=pl.DeviceIdType.MESH)
        pl.semaphore_wait(barrier, 1)

    @pl.when(step < blocks)
    def _():
        slot = step % 2
        up_s[slot] = dot(first_ref[...], din_ref[...]).astype(BF16).reshape(up_s.shape[1:])
        down_s[slot] = dot(feed_ref[...], act_ref[...]).astype(BF16).T.reshape(down_s.shape[1:])

    for block in range(blocks):

        @pl.when(step == block)
        def _(block=block):
            for swap in swaps(block):
                swap.start()

    @pl.when(step == blocks)
    def _():
        for load in loads():
            load.wait()
        out_s[...] = dot(att_s[...].T, bg_s[...]).astype(BF16).reshape(out_s.shape)
        for swap in swaps(blocks):
            swap.start()

    for block in range(blocks):

        @pl.when(step == block + 1)
        def _(block=block):
            for swap in swaps(block):
                swap.wait()
            dwu_ref[:, 0] = (up_s[block % 2, :, core].astype(F32) + up_in[block].astype(F32)).astype(BF16)
            dwd_ref[...] = (down_s[block % 2, :, core].astype(F32) + down_in[block].astype(F32)).astype(BF16)

    @pl.when(step == blocks + 1)
    def _():
        for swap in swaps(blocks):
            swap.wait()
        dwo_ref[...] = (out_s[:, core].astype(F32) + out_in[...].astype(F32)).astype(BF16)


def feed_weights(first_t, din, feed_t, act, att, bg):
    dp = lax.axis_size("dp")
    features, rows = first_t.shape
    hidden = act.shape[1]
    blocks, half, low, deep = hidden // features, dp // 2, features // dp, hidden // dp
    each = half // blocks
    wide_spec = pl.BlockSpec((rows, features), lambda i: (0, jnp.minimum(i, blocks - 1)))
    anywhere = pl.BlockSpec(memory_space=pl.ANY)

    def behind(i):
        return jnp.clip(i - 1, 0, blocks - 1)

    return pl.pallas_call(
        functools.partial(feed_weights_kernel, blocks),
        grid=(blocks + 2,),
        in_specs=[
            whole_spec(first_t.shape),
            wide_spec,
            whole_spec(feed_t.shape),
            wide_spec,
            anywhere,
            anywhere,
        ],
        out_specs=[
            pl.BlockSpec((half, 1, low, features), lambda i: (0, behind(i), 0, 0)),
            pl.BlockSpec((each, deep, features), lambda i: (behind(i), 0, 0)),
            pl.BlockSpec((half, low, features), lambda i: (0, 0, 0)),
        ],
        out_shape=[
            jax.ShapeDtypeStruct((half, blocks, low, features), BF16),
            jax.ShapeDtypeStruct((half, deep, features), BF16),
            jax.ShapeDtypeStruct((half, low, features), BF16),
        ],
        scratch_shapes=[
            pltpu.VMEM((2, half, 2, low, features), BF16),
            pltpu.VMEM((blocks, half, low, features), BF16),
            pltpu.VMEM((2, each, 2, deep, features), BF16),
            pltpu.VMEM((blocks, each, deep, features), BF16),
            pltpu.VMEM((half, 2, low, features), BF16),
            pltpu.VMEM((half, low, features), BF16),
            pltpu.VMEM(att.shape, BF16),
            pltpu.VMEM(bg.shape, BF16),
            pltpu.SemaphoreType.DMA((2,)),
            pltpu.SemaphoreType.DMA((2 * blocks + 2,)),
            pltpu.SemaphoreType.DMA((2 * blocks + 2,)),
        ],
        compiler_params=pltpu.CompilerParams(
            collective_id=3, has_side_effects=True, vmem_limit_bytes=63 * MIB
        ),
        cost_estimate=cost(
            2 * rows * features * (2 * hidden + features), 4 * rows * (hidden + 2 * features)
        ),
        name="feed_weights",
    )(first_t, din, feed_t, act, att, bg)


def own_back_kernel(bg_ref, dq_ref, dk_ref, dv_ref, wq_ref, wk_ref, wv_ref, out_ref):
    total = bg_ref[0].astype(F32) + dot(dq_ref[0], wq_ref[...], NT)
    total += dot(dk_ref[0], wk_ref[...], NT)
    total += dot(dv_ref[0], wv_ref[...], NT)
    out_ref[0] = total.astype(BF16)


def rem_back_kernel(dk_ref, dv_ref, wk_ref, wv_ref, out_ref):
    total = dot(dk_ref[0], wk_ref[...], NT) + dot(dv_ref[0], wv_ref[...], NT)
    out_ref[0] = total.astype(BF16)


def tokens_back(kernel, rows, weights):
    seqs, length, features = rows[0].shape
    tile = math.gcd(length, 512)
    row_spec = pl.BlockSpec((1, tile, features), lambda s, i: (s, i, 0))
    size = rows[0].size
    return pl.pallas_call(
        kernel,
        grid=(seqs, length // tile),
        in_specs=[row_spec] * len(rows) + [whole_spec(w.shape) for w in weights],
        out_specs=row_spec,
        out_shape=jax.ShapeDtypeStruct(rows[0].shape, BF16),
        compiler_params=params(60),
        cost_estimate=cost(2 * size * features * len(weights), 2 * size * (1 + len(rows))),
        name="tokens_back",
    )(*rows, *weights)


def weights_back_kernel(tok_ref, rem_ref, dq_ref, dko_ref, dvo_ref, dkr_ref, dvr_ref,
                        wq_ref, wk_ref, wv_ref, bq_ref, bv_ref, tok_t, rem_t):
    @pl.when(pl.program_id(0) == 0)
    def _():
        tok_t[...] = tok_ref[...].T
        rem_t[...] = rem_ref[...].T

    wq_ref[...] = dot(tok_t[...], dq_ref[...]).astype(BF16)
    wk_ref[...] = (dot(tok_t[...], dko_ref[...]) + dot(rem_t[...], dkr_ref[...])).astype(BF16)
    wv_ref[...] = (dot(tok_t[...], dvo_ref[...]) + dot(rem_t[...], dvr_ref[...])).astype(BF16)
    bq_ref[...] = column_sum(dq_ref[...].astype(F32))
    bv_ref[...] = column_sum(dvo_ref[...].astype(F32)) + column_sum(dvr_ref[...].astype(F32))


def weights_back(tok, rem, dq, dko, dvo, dkr, dvr):
    rows, features = tok.shape
    others = rem.shape[0]
    wide = math.gcd(features, 256)
    own_spec = pl.BlockSpec((rows, wide), lambda j: (0, j))
    rem_spec = pl.BlockSpec((others, wide), lambda j: (0, j))
    bias_spec = pl.BlockSpec((1, wide), lambda j: (0, j))
    return pl.pallas_call(
        weights_back_kernel,
        grid=(features // wide,),
        in_specs=[
            whole_spec(tok.shape),
            whole_spec(rem.shape),
            own_spec,
            own_spec,
            own_spec,
            rem_spec,
            rem_spec,
        ],
        out_specs=[pl.BlockSpec((features, wide), lambda j: (0, j))] * 3 + [bias_spec] * 2,
        out_shape=[jax.ShapeDtypeStruct((features, features), BF16)] * 3
        + [jax.ShapeDtypeStruct((1, features), F32)] * 2,
        scratch_shapes=[
            pltpu.VMEM((features, rows), BF16),
            pltpu.VMEM((features, others), BF16),
        ],
        compiler_params=params(60),
        cost_estimate=cost(
            2 * features * features * (3 * rows + 2 * others),
            2 * (4 * tok.size + 3 * rem.size + 3 * features * features),
        ),
        name="weights_back",
    )(tok, rem, dq, dko, dvo, dkr, dvr)


def halve(value, axis, bit):
    size = lax.axis_size(axis)
    mine = (lax.axis_index(axis) >> bit) & 1
    pairs = value.reshape((value.shape[0] // 2, 2) + value.shape[1:])
    keep = lax.dynamic_index_in_dim(pairs, mine, 1, keepdims=False)
    send = lax.dynamic_index_in_dim(pairs, 1 - mine, 1, keepdims=False)
    came = lax.ppermute(send, axis, [(i, i ^ (1 << bit)) for i in range(size)])
    return keep.astype(F32) + came.astype(F32)


def scatter_sum(value, low=True):
    dp, blk = lax.axis_size("dp"), lax.axis_size("blk")
    if dp & (dp - 1) or blk & (blk - 1):
        return lax.psum_scatter(
            value.astype(F32), ("dp", "blk"), scatter_dimension=0, tiled=True
        )
    kept = value.dtype
    each = value.shape[0] // (dp * blk)
    value = value.reshape((dp, blk * each) + value.shape[1:])
    for bit in range(dp.bit_length() - 1):
        value = halve(value, "dp", bit).astype(kept)
    value = value.reshape((blk, each) + value.shape[2:])
    for bit in range(blk.bit_length() - 1):
        value = halve(value, "blk", bit)
        value = value if (2 << bit) == blk else value.astype(kept)
    return value.reshape(value.shape[1:]).astype(F32)


class Unit:
    def __init__(self, parts, rows, columns, halves, outs):
        self.parts, self.rows, self.columns = parts, rows, columns
        self.halves, self.outs = halves, outs
        self.first = 1 if parts else 0
        self.half = rows // (2 * halves)
        self.last_type = BF16 if (rows // 2) % 16 == 0 else F32


def timetable(units, bits, seqs, groups, slot_us, token_us):
    pending, table = [], []
    free = 0.0
    slots = seqs * groups * 2

    def launch(key, now):
        nonlocal free
        kind, which, step = key
        if kind == "tokens":
            us = token_us
        elif kind == "vectors":
            us = 0.5
        else:
            piece = units[which].rows * units[which].columns * 2e-5
            us = piece * (1 << max(bits - 1 - step, 0))
            us *= {0: 0.25, bits - 1: 3.0}.get(step, 1.0)
        free = max(now, free) + us
        if kind != "tokens":
            pending.append((free + 1.5, key))

    for u, unit in enumerate(units):
        if unit.parts:
            launch(("unit", u, 1), 2.0)
    first_group = sum(1 for unit in units if unit.parts)
    now = 0.0
    while len(table) < slots or pending:
        slot = len(table)
        if slot < slots:
            now = (slot + 1) * slot_us
            s, part, h = slot // (2 * groups), slot // groups % 2, slot % groups
            if part == 0 and h == groups - 1:
                launch(("tokens", s, 0), now)
            if part == 1 and s == seqs - 1:
                launch(("unit", first_group + h, 0), now)
            if slot == slots - 1:
                launch(("vectors", 0, 0), now)
            due = sorted(p for p in pending if p[0] <= now)
        else:
            due = [min(pending)]
            now = max(now + 0.3, due[0][0])
        table.append([key for _, key in due])
        for found in due:
            pending.remove(found)
            kind, which, step = found[1]
            if step < bits:
                launch((kind, which, step + 1), now)
    tail = [key for keys in table[slots:] for key in keys]
    return table[:slots], tail + [("tokens", s, 0) for s in range(seqs)]


def back_kernel(units, bits, groups, table, tail, n_out, *refs):
    (q_ref, qm_ref, o_ref, g_ref, lse_ref, k_ref, km_ref, v_ref,
     bg_ref, tok_ref, rem_ref, wq_ref, wk_ref, wv_ref, vg_ref, vu_ref) = refs[:16]
    sources, refs = refs[16:19], list(refs[19:])
    tokens_out, rem_in, *outs = refs[:n_out]
    refs = refs[n_out:]
    kept = [refs.pop(0) for _ in units]
    landed = [
        [refs.pop(0) if k >= unit.first else None for k in range(bits)] for unit in units
    ]
    wide = [refs.pop(0) for _ in units]
    parting = [refs.pop(0) for _ in units]
    last = [refs.pop(0) for _ in units]
    (weight_sum, group_src, total_s, turned, dq_part, dq_s, dk_s, dv_s,
     rem_out, vec, vec_in, bias_sum, send_sem, recv_sem, local_sem) = refs
    step = pl.program_id(0)
    steps = pl.num_programs(0)
    s, part, h = step // (2 * groups), step // groups % 2, step % groups
    seqs = rem_out.shape[0]
    features = tok_ref.shape[2]
    me, side = lax.axis_index("dp"), lax.axis_index("blk")
    core = me % 2

    def swapped(k):
        return {1: 2, 2: 1}.get(k, k) if bits > 2 else k

    def pick(values, k):
        return values[k] + (values[swapped(k)] - values[k]) * core

    bit_own = [(me // (1 << bit)) % 2 for bit in range(bits)]
    across = [me + (1 << bit) * (1 - 2 * bit_own[bit]) for bit in range(bits)]
    own = [pick(bit_own, k) for k in range(bits)]
    partner = [{"dp": pick(across, k)} for k in range(bits)] + [{"blk": 1 - side}]
    first_group = sum(1 for unit in units if unit.parts)
    lead = (slice(None),) * (bits - 1)

    def natural(digits):
        by_step = [None] + list(digits[::-1])
        return tuple(pick(by_step, bit) for bit in range(bits - 1, 0, -1))

    def digits_of(n, count):
        return [(n // (1 << (count - 1 - i))) % 2 for i in range(count)]

    sems = {}
    for u, unit in enumerate(units):
        for k in range(unit.first, bits + 1):
            sems["unit", u, k, 0] = len(sems)
    for k in range(bits + 1):
        sems["vectors", 0, k, 0] = len(sems)
    for k in range(seqs):
        sems["tokens", k, 0, 0] = len(sems)

    def remote(source, target, device, key):
        return pltpu.make_async_remote_copy(
            src_ref=source,
            dst_ref=target,
            send_sem=send_sem.at[sems[key]],
            recv_sem=recv_sem.at[sems[key]],
            device_id=device,
            device_id_type=pl.DeviceIdType.MESH,
        )

    near_sems = {}
    for u, unit in enumerate(units):
        for p in range(len(unit.parts or ())):
            for n in range(1 << (bits - 1)):
                near_sems[u, p, n] = len(near_sems)

    def spot(k, value):
        return tuple(
            own[at] if at < k else value if at == k else slice(None) for at in range(bits - 1, 0, -1)
        )

    def copies(kind, which, k):
        if kind == "tokens":
            return [remote(rem_out.at[which], rem_in.at[which], partner[bits], (kind, which, 0, 0))]
        if kind == "vectors":
            return [remote(vec.at[k], vec_in.at[k], partner[k], (kind, 0, k, 0))]
        u, unit = which, units[which]
        if k == bits:
            return [remote(parting[u], last[u], partner[bits], (kind, u, k, 0))]
        if k:
            source = kept[u].at[spot(k, 1 - own[k])]
            return [remote(source, landed[u][k], partner[k], (kind, u, k, 0))]
        source = group_src.at[(u - first_group,) + lead + (1 - core,)]
        return [remote(source, landed[u][0], partner[0], (kind, u, 0, 0))]

    def near_copies(u):
        found, row = [], 0
        for p, (source, first, rows) in enumerate(units[u].parts):
            for n in range(1 << (bits - 1)):
                digits = digits_of(n, bits - 1)
                found.append(
                    pltpu.make_async_copy(
                        sources[source].at[natural(digits) + (pl.ds(first, rows),)],
                        kept[u].at[tuple(digits) + (pl.ds(row, rows),)],
                        local_sem.at[near_sems[u, p, n]],
                    )
                )
            row += rows
        return found

    def launch(*key):
        for copy in copies(*key):
            copy.start()

    def halves_of(u, which):
        unit = units[u]
        return [
            wide[u][pl.ds(pl.multiple_of(i * 2 * unit.half + which * unit.half, 8), unit.half)]
            for i in range(unit.halves)
        ]

    def receive(kind, which, k):
        for copy in copies(kind, which, k):
            copy.wait_recv()
        if kind == "tokens":
            return
        if kind == "vectors":
            vec[k + 1] = vec[k] + vec_in[k]
            if k < bits:
                launch(kind, 0, k + 1)
            return
        u, unit = which, units[which]
        if k == bits:
            for i, (mine, (out, rows, columns)) in enumerate(zip(halves_of(u, side), unit.outs)):
                came = last[u][...].astype(F32)[i * unit.half : (i + 1) * unit.half]
                outs[out][rows, columns] = mine + came
            return
        place = spot(k, own[k]) if k else lead
        open_at = [i for i, at in enumerate(place) if isinstance(at, slice)]

        def add(n, carry):
            at, where = list(place), digits_of(n, len(open_at))
            for i, digit in zip(open_at, where):
                at[i] = digit
            at = tuple(at)
            if k:
                mine, came = kept[u][at], landed[u][k][tuple(where)]
            else:
                mine = group_src[(u - first_group,) + natural(at) + (core,)]
                came = landed[u][0][natural(at)]
            total = mine.astype(F32) + came.astype(F32)
            if k == bits - 1:
                wide[u][...] = total
            else:
                kept[u][at] = total.astype(BF16)
            return carry

        if open_at:
            lax.fori_loop(0, 1 << len(open_at), add, 0)
        else:
            add(0, 0)
        if k == bits - 1:
            pieces = halves_of(u, 1 - side)
            pieces = pieces[0] if len(pieces) == 1 else jnp.concatenate(pieces, axis=0)
            parting[u][...] = pieces.astype(unit.last_type)
        launch(kind, u, k + 1)

    @pl.when(step == 0)
    def _():
        barrier = pltpu.get_barrier_semaphore()
        for other in partner:
            pl.semaphore_signal(barrier, inc=1, device_id=other, device_id_type=pl.DeviceIdType.MESH)
        pl.semaphore_wait(barrier, bits + 1)
        for u, unit in enumerate(units):
            if unit.parts:
                for copy in near_copies(u):
                    copy.start()
        for u, unit in enumerate(units):
            if unit.parts:
                for copy in near_copies(u):
                    copy.wait()
                launch("unit", u, 1)
        weight_sum[...] = jnp.zeros_like(weight_sum)
        bias_sum[...] = jnp.zeros_like(bias_sum)

    @pl.when(step % (2 * groups) == 0)
    def _():
        turned[...] = rem_ref[0].T
        total_s[...] = jnp.zeros_like(total_s)

    @pl.when(step % (2 * groups) == groups)
    def _():
        turned[...] = tok_ref[0].T
        total_s[...] = bg_ref[0].astype(F32)

    found = attend_back_part(
        q_ref[0], qm_ref[0], o_ref[0], g_ref[0], lse_ref.at[0], k_ref[0, 0], km_ref[0, 0], v_ref[0, 0], dk_s, dv_s
    )
    width = q_ref.shape[2]
    columns = pl.ds(pl.multiple_of(h * width, width), width)
    dk, dv = dk_s[...], dv_s[...]
    more = dot(dk, wk_ref[:, columns], NT) + dot(dv, wv_ref[:, columns], NT)
    weight_sum[h, 1] += dot(turned[...], dk)
    weight_sum[h, 2] += dot(turned[...], dv)
    bias_sum[h, 1:2] += column_sum(dv.astype(F32))

    @pl.when(part == 0)
    def _():
        total_s[...] += more
        for pair, value in enumerate(found):
            dq_part[h, pair] = value

    @pl.when(part == 1)
    def _():
        for pair, value in enumerate(found):
            value = (value + dq_part[h, pair]) * SCALE
            dq_s[:, pair * PAIR : (pair + 1) * PAIR] = value.T.astype(BF16)
        dq = dq_s[...]
        total_s[...] += more + dot(dq, wq_ref[:, columns], NT)
        weight_sum[h, 0] += dot(turned[...], dq)
        bias_sum[h, 0:1] += column_sum(dq.astype(F32))

    for at in range(seqs):

        @pl.when(step == at * 2 * groups + groups - 1)
        def _(at=at):
            rem_out[at] = total_s[...].astype(BF16)
            launch("tokens", at, 0)

    @pl.when(step % (2 * groups) == 2 * groups - 1)
    def _():
        tokens_out[0] = total_s[...].astype(BF16)

    for at in range(groups):

        @pl.when(step == steps - groups + at)
        def _(at=at):
            rows = features // (1 << bits)
            for i in range(3):
                piece = weight_sum[at, i].astype(BF16)
                piece = piece.reshape((2,) * bits + (rows, piece.shape[1]))
                group_src[(at,) + (slice(None),) * bits + (slice(i * rows, (i + 1) * rows),)] = piece
            launch("unit", first_group + at, 0)

    @pl.when(step == steps - 1)
    def _():
        vec[0] = jnp.zeros_like(vec[0])
        vec[0, 0:6] = vg_ref[0:6]
        for at in range(groups):
            vec[0, 6:8, at * width : (at + 1) * width] = bias_sum[at, 0:2]
        blocks = vu_ref.shape[1] // features
        for at in range(blocks):
            vec[0, 8 + at : 9 + at] = vu_ref[:, at * features : (at + 1) * features]
        launch("vectors", 0, 0)

    for at, keys in enumerate(table):
        if keys:

            @pl.when(step == at)
            def _(keys=keys):
                for key in keys:
                    receive(*key)

    @pl.when(step == steps - 1)
    def _():
        for key in tail:
            receive(*key)
        shards = (1 << bits) * 2
        place = me * 2 + side
        share = features // shards
        rows = pltpu.roll(vec[bits + 1, 0:8], (shards - place) * share % features, 1)
        outs[-1][0:8] = rows[:, :PAIR]
        share = vu_ref.shape[1] // shards
        each = features // share
        row = vec[bits + 1, pl.ds(8 + place // each, 1)]
        rows = pltpu.roll(jnp.broadcast_to(row, (8, features)), (each - place % each) * share % features, 1)
        outs[-1][8:16] = rows[:, :PAIR]
        for u, unit in enumerate(units):
            for k in range(unit.first, bits + 1):
                for copy in copies("unit", u, k):
                    copy.wait_send()
        for k in range(bits + 1):
            copies("vectors", 0, k)[0].wait_send()
        for k in range(seqs):
            copies("tokens", k, 0)[0].wait_send()


def back_and_sum(q, qm, o, g, lse, k, km, v, bg, tokens, rem_tokens, weights, dwd, dwu, dwo, vg, vu):
    bits = lax.axis_size("dp").bit_length() - 1
    seqs, length, features = q.shape
    width = math.gcd(features, 2 * PAIR)
    groups, pairs = features // width, width // PAIR
    low, deep, blocks = dwo.shape[1], dwd.shape[1], dwu.shape[1]
    lead = (2,) * bits
    sources = [x.reshape(lead[1:] + (-1, features)) for x in (dwd, dwu, dwo)]
    every = slice(None)
    units = []
    quarter = deep // 4
    for i in range(2):
        at = slice(i * quarter, (i + 1) * quarter)
        parts = [(0, i * quarter, quarter), (0, (2 + i) * quarter, quarter)]
        units.append(Unit(parts, 2 * quarter, features, 1, [(0, at, every)]))
    for i in range(2):
        found = range(i * blocks // 2, (i + 1) * blocks // 2)
        units.append(
            Unit(
                [(1, found[0] * low, len(found) * low)],
                len(found) * low,
                features,
                len(found),
                [(1, every, slice(b * features, (b + 1) * features)) for b in found],
            )
        )
    units.append(Unit([(2, 0, low)], low, features, 1, [(2, every, every)]))
    for h in range(groups):
        columns = slice(h * width, (h + 1) * width)
        units.append(Unit(None, 3 * low, width, 3, [(3 + i, every, columns) for i in range(3)]))
    table, tail = timetable(units, bits, seqs, groups, 5.3, length * features * 3e-5)

    half = low // 2
    out_shape = [
        jax.ShapeDtypeStruct(q.shape, BF16),
        jax.ShapeDtypeStruct(q.shape, BF16),
        jax.ShapeDtypeStruct((deep // 2, features), F32),
        jax.ShapeDtypeStruct((half, blocks * features), F32),
        *(jax.ShapeDtypeStruct((half, features), F32) for _ in range(4)),
        jax.ShapeDtypeStruct((16, PAIR), F32),
    ]
    tops = lead[1:]
    scratch = [pltpu.VMEM(tops + (u.rows, u.columns), BF16) for u in units]
    for u in units:
        scratch += [pltpu.VMEM(tops[k:] + (u.rows, u.columns), BF16) for k in range(u.first, bits)]
    scratch += [pltpu.VMEM((u.rows, u.columns), F32) for u in units]
    scratch += [pltpu.VMEM((u.rows // 2, u.columns), u.last_type) for u in units] * 2
    count = len(units) * (bits + 1) + bits + 1 + seqs
    near = sum(len(u.parts) << (bits - 1) for u in units if u.parts)
    scratch += [
        pltpu.VMEM((groups, 3, features, width), F32),
        pltpu.VMEM((groups,) + lead + (3 * low, width), BF16),
        pltpu.VMEM((length, features), F32),
        pltpu.VMEM((features, length), BF16),
        pltpu.VMEM((groups, pairs, PAIR, length), F32),
        *(pltpu.VMEM((length, width), BF16) for _ in range(3)),
        pltpu.VMEM((seqs, length, features), BF16),
        pltpu.VMEM((bits + 2, 16, features), F32),
        pltpu.VMEM((bits + 1, 16, features), F32),
        pltpu.VMEM((groups, 8, width), F32),
        pltpu.SemaphoreType.DMA((count,)),
        pltpu.SemaphoreType.DMA((count,)),
        pltpu.SemaphoreType.DMA((near,)),
    ]
    turn = 2 * groups
    heads_at = pl.BlockSpec((1, length, width), lambda i: (i // turn, 0, i % groups))
    keys_at = pl.BlockSpec(
        (1, 1, length, width), lambda i: (1 - i // groups % 2, i // turn, 0, i % groups)
    )
    rows_at = pl.BlockSpec((1, length, features), lambda i: (i // turn, 0, 0), pipeline_mode=pl.Buffered(1))

    def fixed(shape):
        return pl.BlockSpec(shape, lambda i: (0,) * len(shape), pipeline_mode=pl.Buffered(1))

    return pl.pallas_call(
        functools.partial(back_kernel, units, bits, groups, table, tail, len(out_shape)),
        grid=(seqs * turn,),
        in_specs=[
            heads_at,
            pl.BlockSpec((1, length, PAIR), lambda i: (i // turn, 0, 0)),
            heads_at,
            heads_at,
            pl.BlockSpec((1, pairs, 8, length), lambda i: (i // turn, i % groups, 0, 0)),
            keys_at,
            pl.BlockSpec((1, 1, length, PAIR), lambda i: (1 - i // groups % 2, i // turn, 0, 0)),
            keys_at,
            rows_at,
            rows_at,
            rows_at,
        ]
        + [whole_spec(w.shape) for w in weights + (vg, vu)]
        + [pl.BlockSpec(memory_space=pl.ANY)] * 3,
        out_specs=[
            pl.BlockSpec((1, length, features), lambda i: (i // turn, 0, 0)),
            pl.BlockSpec(memory_space=pl.ANY),
        ]
        + [fixed(s.shape) for s in out_shape[2:]],
        out_shape=out_shape,
        scratch_shapes=scratch,
        compiler_params=pltpu.CompilerParams(
            collective_id=1, has_side_effects=True, vmem_limit_bytes=63 * MIB
        ),
        cost_estimate=cost(80 * q.size * length, 2 * q.size * 14, 2 * q.size * length // HEAD),
        name="back_and_sum",
    )(q, qm, o, g, lse, k, km, v, bg, tokens, rem_tokens, *weights, vg, vu, *sources)


def finish_kernel(own_ref, rem_ref, *refs):
    ins, outs = refs[:7], refs[7:]
    outs[0][...] = (own_ref[...].astype(F32) + rem_ref[...].astype(F32)).astype(BF16)

    @pl.when(pl.program_id(0) == 0)
    def _():
        for source, target in zip(ins[:6], outs[1:7]):
            target[...] = source[...]
        for i, target in enumerate(outs[7:]):
            target[...] = ins[6][i, : target.shape[0]]


def finish(own, rem, matrices, vectors, shares):
    seqs, length, features = own.shape
    row_spec = pl.BlockSpec((1, length, features), lambda s: (s, 0, 0))

    def fixed(shape):
        return pl.BlockSpec(shape, lambda s: (0,) * len(shape))

    shapes = [m.shape for m in matrices] + [(n,) for n in shares]
    return pl.pallas_call(
        finish_kernel,
        grid=(seqs,),
        in_specs=[row_spec] * 2 + [fixed(m.shape) for m in matrices] + [fixed(vectors.shape)],
        out_specs=[row_spec] + [fixed(s) for s in shapes],
        out_shape=[jax.ShapeDtypeStruct(own.shape, BF16)] + [jax.ShapeDtypeStruct(s, F32) for s in shapes],
        compiler_params=params(60),
        cost_estimate=cost(own.size, 6 * own.size),
        name="finish",
    )(own, rem, *matrices, vectors)


def back_plainly(q, qm, o, g, lse, own, rem, bg, tokens, rem_tokens, weights, dwd, dwu, dwo, vg, vu):
    seqs, length, features = q.shape
    dp, blk = lax.axis_size("dp"), lax.axis_size("blk")
    dq, dko, dvo, dkr, dvr = attend_back(q, qm, o, g, lse, own, rem)
    rem_gradient = tokens_back(rem_back_kernel, (dkr, dvr), weights[1:])
    came = [
        lax.ppermute(part, "blk", [((i + r) % blk, i) for i in range(blk)])
        for r, part in enumerate(jnp.split(rem_gradient, blk - 1, axis=1), 1)
    ]
    flat = [v.reshape(-1, features) for v in (tokens, rem_tokens, dq, dko, dvo, dkr, dvr)]
    dwq, dwk, dwv, dbq, dbv = weights_back(*flat)
    total = tokens_back(own_back_kernel, (bg, dq, dko, dvo), weights).astype(F32)
    for part in came:
        total += part.astype(F32)
    dwu = jnp.moveaxis(dwu[0], 0, 1).reshape(features, -1)
    summed = [scatter_sum(w) for w in (dwd, dwu, dwo, dwq, dwk, dwv)]
    rows = [vg[i] for i in range(6)] + [dbq, dbv, vu]
    rows = [scatter_sum(v.reshape(dp * blk, -1)) for v in rows]
    return [total.astype(BF16)] + summed + [[v[0] for v in rows]]


def body(
    tokens,
    query_weight,
    query_bias,
    key_weight,
    value_weight,
    value_bias,
    out_weight,
    out_bias,
    gain_one,
    shift_one,
    up_weight,
    up_bias,
    down_weight,
    down_bias,
    gain_two,
    shift_two,
    group_ids,
    valid_mask,
    cotangent,
):
    seqs, length, features = tokens.shape
    rows = seqs * length
    blk = lax.axis_size("blk")

    def from_others(value):
        found = [
            lax.ppermute(value, "blk", [(i, (i + r) % blk) for i in range(blk)])
            for r in range(1, blk)
        ]
        return found[0] if len(found) == 1 else jnp.concatenate(found, axis=1)

    codes = jnp.where(valid_mask == 1, group_ids, -1)
    dp = lax.axis_size("dp")
    by_kernel = blk == 2 and dp & (dp - 1) == 0 and dp > 1 and (features // dp) % 16 == 0
    projections = (query_weight, key_weight, value_weight)
    vectors = (
        query_bias,
        value_bias,
        out_bias,
        gain_one,
        shift_one,
        down_bias,
        gain_two,
        shift_two,
    )

    if by_kernel:
        (block_out, branch_gradient, attended_gradient, attended, lse, query_mask, key_masks,
         first_t, feed_t, vector_gradients, up_bias_gradient, queries, keys, values,
         rem_tokens, active, inner_gradient) = front(
            tokens,
            group_ids,
            valid_mask,
            cotangent,
            vectors,
            up_bias,
            projections + (out_weight, up_weight, down_weight),
        )
        dwu, dwd, dwo = feed_weights(
            first_t,
            inner_gradient.reshape(rows, -1),
            feed_t,
            active.reshape(rows, -1),
            attended.reshape(rows, features),
            branch_gradient.reshape(rows, features),
        )
        own_gradient, rem_gradient, *matrices, vectors = back_and_sum(
            queries,
            query_mask,
            attended,
            attended_gradient,
            lse,
            keys,
            key_masks,
            values,
            branch_gradient,
            tokens,
            rem_tokens,
            projections,
            dwd,
            dwu,
            dwo,
            vector_gradients,
            up_bias_gradient,
        )
        shares = [features // (dp * blk)] * 8 + [up_bias.size // (dp * blk)]
        found = finish(own_gradient, rem_gradient, matrices, vectors, shares)
        tokens_gradient, dwd, dwu, dwo, dwq, dwk, dwv, *rows_left = found
    else:
        rem_tokens = from_others(tokens)
        rem_codes = from_others(codes.astype(BF16)).astype(jnp.int32)
        slot = jnp.arange(PAIR, dtype=jnp.int32) % HEAD

        def key_mask(code):
            return jnp.where(code[:, :, None] == slot, 0.0, MASKED).astype(BF16)

        query_mask = (group_ids[:, :, None] == slot).astype(BF16)
        vectors = jnp.stack(vectors).astype(F32)
        queries, own_keys, own_values = project(tokens, vectors, projections)
        rem_keys, rem_values = project(rem_tokens, vectors, projections[1:])
        own = (own_keys, key_mask(codes), own_values)
        rem = (rem_keys, key_mask(rem_codes), rem_values)
        attended, lse = attend(queries, query_mask, own, rem)
        (block_out, branch_gradient, attended_gradient, vector_gradients, up_bias_gradient,
         dwu, dwd, dwo) = feed_both_ways(
            tokens.reshape(rows, features),
            attended.reshape(rows, features),
            cotangent.reshape(rows, features),
            vectors[2:],
            up_bias.astype(F32)[None],
            out_weight,
            up_weight,
            down_weight,
            1,
        )
        tokens_gradient, dwd, dwu, dwo, dwq, dwk, dwv, rows_left = back_plainly(
            queries,
            query_mask,
            attended,
            attended_gradient.reshape(tokens.shape),
            lse,
            own,
            rem,
            branch_gradient.reshape(tokens.shape),
            tokens,
            rem_tokens,
            projections,
            dwd,
            dwu,
            dwo,
            vector_gradients,
            up_bias_gradient,
        )
    dbo, dg1, ds1, dbd, dg2, ds2, dbq, dbv, dbu = rows_left
    return (
        block_out.reshape(tokens.shape),
        tokens_gradient,
        dwq,
        dbq,
        dwk,
        dwv,
        dbv,
        dwo,
        dbo,
        dg1,
        ds1,
        dwu,
        dbu,
        dwd,
        dbd,
        dg2,
        ds2,
    )


def solution(mesh):
    rows, shared, pair = P("dp", "blk", None), P(), P("dp", "blk")
    matrix, vector = P(("dp", "blk"), None), P(("dp", "blk"))
    return jax.shard_map(
        body,
        mesh=mesh,
        in_specs=(rows,) + (shared,) * 15 + (pair, pair, rows),
        out_specs=(
            rows,
            rows,
            matrix,
            vector,
            matrix,
            matrix,
            vector,
            matrix,
            vector,
            vector,
            vector,
            matrix,
            vector,
            matrix,
            vector,
            vector,
            vector,
        ),
        check_vma=False,
    )
```

```python
import functools
import math

import jax
import jax.numpy as jnp
from jax import lax
from jax.experimental import pallas as pl
from jax.experimental.pallas import tpu as pltpu
from jax.sharding import PartitionSpec as P

HEAD = 64
PAIR = 2 * HEAD
EPSILON = 1e-12
MASKED = -1e30
FLOOR = -3e38
SCALE = HEAD**-0.5
EXPO = SCALE * math.log2(math.e)
NN = (((1,), (0,)), ((), ()))
NT = (((1,), (1,)), ((), ()))
F32 = jnp.float32
BF16 = jnp.bfloat16
MIB = 1 << 20
FEED_ROWS = 512


def dot(left, right, dims=NN):
    return lax.dot_general(left, right, dims, preferred_element_type=F32)


def whole_spec(shape):
    return pl.BlockSpec(shape, lambda *_: (0,) * len(shape), pipeline_mode=pl.Buffered(1))


def params(limit):
    return pltpu.CompilerParams(vmem_limit_bytes=limit * MIB)


def cost(flops, touched, exps=0):
    return pl.CostEstimate(flops=int(flops), bytes_accessed=int(touched), transcendentals=int(exps))


def project_kernel(has_query, *refs):
    if has_query:
        x_ref, bias_ref, wq_ref, wk_ref, wv_ref, q_ref, k_ref, v_ref = refs
    else:
        x_ref, bias_ref, wk_ref, wv_ref, k_ref, v_ref = refs
    x = x_ref[0]
    if has_query:
        q_ref[0] = (dot(x, wq_ref[...]) + bias_ref[0:1]).astype(BF16)
    k_ref[0] = dot(x, wk_ref[...]).astype(BF16)
    v_ref[0] = (dot(x, wv_ref[...]) + bias_ref[1:2]).astype(BF16)


def project(x, bias, weights):
    seqs, length, features = x.shape
    tile = math.gcd(length, 512)
    grid = (seqs, length // tile)
    row_spec = pl.BlockSpec((1, tile, features), lambda s, i: (s, i, 0))
    return pl.pallas_call(
        functools.partial(project_kernel, len(weights) == 3),
        grid=grid,
        in_specs=[row_spec, whole_spec(bias.shape)] + [whole_spec(w.shape) for w in weights],
        out_specs=[row_spec] * len(weights),
        out_shape=[jax.ShapeDtypeStruct(x.shape, BF16)] * len(weights),
        compiler_params=params(60),
        cost_estimate=cost(
            2 * x.size * features * len(weights), 2 * x.size * (1 + len(weights))
        ),
        name="project",
    )(x, bias, *weights)


def low_lanes():
    return lax.broadcasted_iota(jnp.int32, (1, PAIR), 1) < HEAD


def attend_group(q, qm, sources, o_ref, lse_ref):
    length = q.shape[0]
    tile = math.gcd(length, 256)
    low = low_lanes()
    one = jnp.ones((1, PAIR), BF16)
    todo = [
        (pair, row, head)
        for pair in range(q.shape[1] // PAIR)
        for row in range(0, length, tile)
        for head in range(2)
    ]

    def lanes_of(pair):
        return slice(pair * PAIR, (pair + 1) * PAIR)

    def mine_of(head):
        return ~low if head else low

    def scores_of(pair, row, head):
        mine, lanes = mine_of(head), lanes_of(pair)
        q_side = jnp.where(mine, q[row : row + tile, lanes], qm[row : row + tile])
        return [dot(q_side, jnp.where(mine, k[:, lanes], km), NT) for k, km, _ in sources]

    ahead = scores_of(*todo[0])
    for i, (pair, row, head) in enumerate(todo):
        scores = ahead
        if i + 1 < len(todo):
            ahead = scores_of(*todo[i + 1])
        top = functools.reduce(
            jnp.maximum, [jnp.max(part, axis=-1, keepdims=True) for part in scores]
        )
        weights = [jnp.exp2((part - top) * EXPO).astype(BF16) for part in scores]
        total = sum(
            dot(w, jnp.where(mine_of(head), v[:, lanes_of(pair)], one))
            for w, (_, _, v) in zip(weights, sources)
        )
        if head == 0:
            earlier, earlier_top = total, top
            continue
        totals = pltpu.roll(jnp.where(low, total, earlier), HEAD, 1)
        rows = slice(row, row + tile)
        o_ref[rows, lanes_of(pair)] = (jnp.where(low, earlier, total) / totals).astype(BF16)
        lse = (jnp.where(low, earlier_top, top) * EXPO + jnp.log2(totals)).T
        lse_ref[pair, 0:1, rows] = lse[0:1]
        lse_ref[pair, 1:2, rows] = lse[HEAD : HEAD + 1]


def attend_kernel(q_ref, qm_ref, ko_ref, kmo_ref, vo_ref, kr_ref, kmr_ref, vr_ref, o_ref, lse_ref):
    sources = [(ko_ref[0], kmo_ref[0], vo_ref[0]), (kr_ref[0], kmr_ref[0], vr_ref[0])]
    attend_group(q_ref[0], qm_ref[0], sources, o_ref.at[0], lse_ref.at[0])


def pair_spec(length, lanes):
    return pl.BlockSpec((1, length, lanes), lambda s, h: (s, 0, h))


def mask_spec(length):
    return pl.BlockSpec((1, length, PAIR), lambda s, h: (s, 0, 0))


def lse_spec(length, lanes):
    return pl.BlockSpec((1, lanes // PAIR, 8, length), lambda s, h: (s, h, 0, 0))


def attend(q, qm, own, rem):
    seqs, length, features = q.shape
    lanes = math.gcd(features, 2 * PAIR)
    other = rem[0].shape[1]
    own_spec, rem_spec = pair_spec(length, lanes), pair_spec(other, lanes)
    return pl.pallas_call(
        attend_kernel,
        grid=(seqs, features // lanes),
        in_specs=[own_spec, mask_spec(length)]
        + [own_spec, mask_spec(length), own_spec]
        + [rem_spec, mask_spec(other), rem_spec],
        out_specs=[own_spec, lse_spec(length, lanes)],
        out_shape=[
            jax.ShapeDtypeStruct(q.shape, BF16),
            jax.ShapeDtypeStruct((seqs, features // PAIR, 8, length), F32),
        ],
        compiler_params=params(60),
        cost_estimate=cost(
            16 * q.size * (length + other), 2 * q.size * 6, q.size * (length + other) // HEAD
        ),
        name="attend",
    )(q, qm, *own, *rem)


def attend_back_part(q, qm, g, lse_ref, k, km, v, dk_ref, dv_ref):
    low = low_lanes()
    none = jnp.zeros((1, PAIR), BF16)
    pairs = q.shape[1] // PAIR
    todo = [(pair, head) for pair in range(pairs) for head in range(2)]

    def lanes_of(pair):
        return slice(pair * PAIR, (pair + 1) * PAIR)

    def mine_of(head):
        return ~low if head else low

    def products(pair, head):
        mine, lanes = mine_of(head), lanes_of(pair)
        return (
            dot(jnp.where(mine, k[:, lanes], km), jnp.where(mine, q[:, lanes], qm), NT),
            dot(jnp.where(mine, v[:, lanes], none), g[:, lanes], NT),
        )

    found = []
    ahead = products(*todo[0])
    for i, (pair, head) in enumerate(todo):
        scores, grads = ahead
        if i + 1 < len(todo):
            ahead = products(*todo[i + 1])
        lanes, mine = lanes_of(pair), mine_of(head)
        if head == 0:
            k_t = k[:, lanes].T
            dk = dv = 0.0
            dq = []
        probs = jnp.exp2(scores * EXPO - lse_ref[pair, head : head + 1, :])
        grads = (probs * (grads - lse_ref[pair, 2 + head : 3 + head, :])).astype(BF16)
        dv += dot(probs.astype(BF16), jnp.where(mine, g[:, lanes], none))
        dk += dot(grads, jnp.where(mine, q[:, lanes], none))
        dq.append(dot(k_t[head * HEAD : (head + 1) * HEAD], grads))
        if head == 1:
            dk_ref[:, lanes] = (dk * SCALE).astype(BF16)
            dv_ref[:, lanes] = dv.astype(BF16)
            found.append(jnp.concatenate(dq, axis=0))
    return found


def attend_back_kernel(q_ref, qm_ref, g_ref, lse_ref, ko_ref, kmo_ref, vo_ref, kr_ref, kmr_ref,
                       vr_ref, dq_ref, dko_ref, dvo_ref, dkr_ref, dvr_ref):
    parts = ((ko_ref, kmo_ref, vo_ref, dko_ref, dvo_ref), (kr_ref, kmr_ref, vr_ref, dkr_ref, dvr_ref))
    found = [
        attend_back_part(
            q_ref[0], qm_ref[0], g_ref[0], lse_ref.at[0], k[0], km[0], v[0], dk.at[0], dv.at[0]
        )
        for k, km, v, dk, dv in parts
    ]
    for pair, both in enumerate(zip(*found)):
        dq_ref[0, :, pair * PAIR : (pair + 1) * PAIR] = (sum(both) * SCALE).T.astype(BF16)


def attend_back(q, qm, o, g, lse, own, rem):
    seqs, length, features = q.shape
    delta = (g.astype(F32) * o.astype(F32)).reshape(seqs, length, features // PAIR, 2, HEAD).sum(-1)
    lse = lax.dynamic_update_slice(lse, jnp.transpose(delta, (0, 2, 3, 1)), (0, 0, 2, 0))
    lanes = math.gcd(features, 2 * PAIR)
    other = rem[0].shape[1]
    own_spec, rem_spec = pair_spec(length, lanes), pair_spec(other, lanes)
    return pl.pallas_call(
        attend_back_kernel,
        grid=(seqs, features // lanes),
        in_specs=[own_spec, mask_spec(length), own_spec, lse_spec(length, lanes)]
        + [own_spec, mask_spec(length), own_spec]
        + [rem_spec, mask_spec(other), rem_spec],
        out_specs=[own_spec] * 3 + [rem_spec] * 2,
        out_shape=[jax.ShapeDtypeStruct(q.shape, BF16)] * 3
        + [jax.ShapeDtypeStruct(rem[0].shape, BF16)] * 2,
        compiler_params=params(60),
        cost_estimate=cost(
            40 * q.size * (length + other), 2 * q.size * 14, q.size * (length + other) // HEAD
        ),
        name="attend_back",
    )(q, qm, g, lse, *own, *rem)


def gelu_and_slope(x):
    bell = jnp.exp2(x * x * (-0.5 * math.log2(math.e)))
    below = 1.0 + (0.3275911 / math.sqrt(2.0)) * jnp.abs(x)
    t = pl.reciprocal(below, approx=True)
    t = t * (2.0 - below * t)
    poly = 1.061405429 * t - 1.453152027
    poly = poly * t + 1.421413741
    poly = poly * t - 0.284496736
    poly = poly * t + 0.254829592
    tail = (0.5 * poly) * t * bell
    share = jnp.where(x >= 0.0, 1.0 - tail, tail)
    return x * share, share + x * bell * (1.0 / math.sqrt(2.0 * math.pi))


def mean(values):
    return jnp.sum(values, axis=-1, keepdims=True) * (1.0 / values.shape[-1])


def norm_parts(values):
    centred = values - mean(values)
    scale = lax.rsqrt(mean(centred * centred) + EPSILON)
    return centred * scale, scale


def norm_back(upper, normed, scale):
    return scale * (upper - mean(upper) - normed * mean(upper * normed))


def column_sum(values):
    return jnp.sum(values, axis=0, keepdims=True)


def feed_kernel(layout, tok_ref, att_ref, cot_ref, vec_ref, bu_ref, wo_ref, wu_ref, wd_ref,
                out_ref, bg_ref, ag_ref, vg_ref, dbu_ref, dwu_ref, dwd_ref, dwo_ref,
                act_s, din_s, first_t, feed_t, att_t, bg_s):
    tiles, ff_steps, chunk, wide, narrow = layout
    step = pl.program_id(0)
    tile = tok_ref.shape[0]
    hidden = act_s.shape[1]
    vec = [vec_ref[i : i + 1] for i in range(6)]
    out_bias, gain_one, shift_one, down_bias, gain_two, shift_two = vec

    @pl.when(step == 0)
    def _():
        vg_ref[...] = jnp.zeros_like(vg_ref)
        dbu_ref[...] = jnp.zeros_like(dbu_ref)

    @pl.when(step < tiles)
    def _():
        start = pl.multiple_of(step * tile, tile)
        rows = pl.ds(start, tile)
        att = att_ref[...]
        normed_one, scale_one = norm_parts(
            tok_ref[...].astype(F32) + (dot(att, wo_ref[...]) + out_bias)
        )
        first = normed_one * gain_one + shift_one
        first_low = first.astype(BF16)
        first_t[:, rows] = first_low.T
        att_t[:, rows] = att.T
        feed = jnp.zeros_like(first) + down_bias
        spans = [slice(c, c + chunk) for c in range(0, hidden, chunk)]
        ahead = dot(first_low, wu_ref[:, spans[0]])
        for i, cols in enumerate(spans):
            inner = ahead + bu_ref[:, cols]
            if i + 1 < len(spans):
                ahead = dot(first_low, wu_ref[:, spans[i + 1]])
            active, slope = gelu_and_slope(inner)
            active = active.astype(BF16)
            act_s[rows, cols] = active
            din_s[rows, cols] = slope.astype(BF16)
            feed += dot(active, wd_ref[cols])
        normed_two, scale_two = norm_parts(first + feed)
        out_ref[...] = (normed_two * gain_two + shift_two).astype(BF16)
        cot = cot_ref[...].astype(F32)
        second = norm_back(cot * gain_two, normed_two, scale_two)
        feed_low = second.astype(BF16)
        feed_t[:, rows] = feed_low.T
        back = second
        ahead = dot(feed_low, wd_ref[spans[0]], NT)
        for i, cols in enumerate(spans):
            inner = ahead
            if i + 1 < len(spans):
                ahead = dot(feed_low, wd_ref[spans[i + 1]], NT)
            inner = (inner * din_s[rows, cols].astype(F32)).astype(BF16)
            din_s[rows, cols] = inner
            dbu_ref[:, cols] += column_sum(inner.astype(F32))
            back += dot(inner, wu_ref[:, cols], NT)
        residual = norm_back(back * gain_one, normed_one, scale_one)
        branch_low = residual.astype(BF16)
        bg_ref[...] = branch_low
        bg_s[rows] = branch_low
        ag_ref[...] = dot(branch_low, wo_ref[...], NT).astype(BF16)
        for i, values in enumerate(
            (
                branch_low.astype(F32),
                back * normed_one,
                back,
                feed_low.astype(F32),
                cot * normed_two,
                cot,
            )
        ):
            vg_ref[i : i + 1] += column_sum(values)

    @pl.when((step >= tiles) & (step < tiles + ff_steps))
    def _():
        cols = pl.ds(pl.multiple_of((step - tiles) * wide, wide), wide)
        dwu = dot(first_t[...], din_s[:, cols]).astype(BF16)
        dwu_ref[...] = dwu.reshape(dwu_ref.shape)
        dwd_ref[...] = dot(feed_t[...], act_s[:, cols]).astype(BF16).T

    @pl.when(step >= tiles + ff_steps)
    def _():
        cols = pl.ds(pl.multiple_of((step - tiles - ff_steps) * narrow, narrow), narrow)
        dwo_ref[...] = dot(att_t[...], bg_s[:, cols]).astype(BF16)


def feed_both_ways(tokens, attended, cotangent, vectors, up_bias, wo, wu, wd, groups):
    rows, features = tokens.shape
    hidden = wu.shape[1]
    tile = math.gcd(rows, 256)
    tiles = rows // tile
    wide, narrow = features, math.gcd(features, 384)
    ff_steps, out_steps = hidden // wide, features // narrow
    layout = (tiles, ff_steps, math.gcd(hidden, 512), wide, narrow)
    blocked = (groups, ff_steps, features // groups, wide)
    row_spec = pl.BlockSpec((tile, features), lambda i: (jnp.minimum(i, tiles - 1), 0))

    def ff_at(i):
        return jnp.clip(i - tiles, 0, ff_steps - 1)

    return pl.pallas_call(
        functools.partial(feed_kernel, layout),
        grid=(tiles + ff_steps + out_steps,),
        in_specs=[row_spec] * 3
        + [whole_spec(a.shape) for a in (vectors, up_bias, wo, wu, wd)],
        out_specs=[row_spec] * 3
        + [
            pl.BlockSpec((8, features), lambda i: (0, 0)),
            pl.BlockSpec((1, hidden), lambda i: (0, 0)),
            pl.BlockSpec((groups, 1) + blocked[2:], lambda i: (0, ff_at(i), 0, 0)),
            pl.BlockSpec((wide, features), lambda i: (ff_at(i), 0)),
            pl.BlockSpec(
                (features, narrow),
                lambda i: (0, jnp.clip(i - tiles - ff_steps, 0, out_steps - 1)),
            ),
        ],
        out_shape=[jax.ShapeDtypeStruct(tokens.shape, BF16)] * 3
        + [
            jax.ShapeDtypeStruct((8, features), F32),
            jax.ShapeDtypeStruct((1, hidden), F32),
            jax.ShapeDtypeStruct(blocked, BF16),
            jax.ShapeDtypeStruct(wd.shape, BF16),
            jax.ShapeDtypeStruct(wo.shape, BF16),
        ],
        scratch_shapes=[
            pltpu.VMEM((rows, hidden), BF16),
            pltpu.VMEM((rows, hidden), BF16),
            pltpu.VMEM((features, rows), BF16),
            pltpu.VMEM((features, rows), BF16),
            pltpu.VMEM((features, rows), BF16),
            pltpu.VMEM((rows, features), BF16),
        ],
        compiler_params=params(60),
        cost_estimate=cost(
            6 * rows * features * (features + 2 * hidden),
            2 * (6 * rows * features + 4 * features * hidden + 2 * features * features),
            2 * rows * hidden,
        ),
        name="feed_both_ways",
    )(tokens, attended, cotangent, vectors, up_bias, wo, wu, wd)


def spread(row):
    return jnp.broadcast_to(row, (PAIR, row.shape[1])).T


def as_row(ref):
    return ref[...].astype(F32).reshape(1, ref.shape[0])


def front_kernel(tokens_ref, group_ref, valid_ref, cot_ref, bq_ref, bv_ref, bo_ref, g1_ref, s1_ref, bd_ref,
                 g2_ref, s2_ref, bu_in, wq_any, wk_any, wv_any, wo_any, wu_any, wd_any,
                 out_ref, bg_ref, ag_ref, att_ref, lse_ref, qm_ref, km_ref,
                 first_t, feed_t, vg_ref, dbu_ref, q_any, k_any, v_any, rem_any, act_any, din_any,
                 wq, wk, wv, wo, wu, wd, tok_s, q_s, k_s, v_s, kr_s, vr_s, rem_s, own_codes, code_s, act_s, din_s,
                 bu_ref, weight_sem, out_sem, send_sem, recv_sem):
    s = pl.program_id(0)
    seqs = tok_s.shape[0]
    length, features = tok_s.shape[1:]
    hidden = act_s.shape[1]
    side = lax.axis_index("blk")
    other = {"blk": 1 - side}
    query_bias, value_bias, out_bias, gain_one, shift_one, down_bias, gain_two, shift_two = [
        as_row(ref) for ref in (bq_ref, bv_ref, bo_ref, g1_ref, s1_ref, bd_ref, g2_ref, s2_ref)
    ]
    pairs_of = [(wq_any, wq), (wk_any, wk), (wv_any, wv), (wo_any, wo), (wu_any, wu), (wd_any, wd)]

    def weight(i):
        return pltpu.make_async_copy(*pairs_of[i], weight_sem.at[i])

    def remote(source, target, at):
        return pltpu.make_async_remote_copy(
            src_ref=source,
            dst_ref=target,
            send_sem=send_sem.at[at],
            recv_sem=recv_sem.at[at],
            device_id=other,
            device_id_type=pl.DeviceIdType.MESH,
        )

    def exchange(at):
        return remote(tokens_ref.at[at], rem_s.at[at], at)

    def code_exchange():
        return remote(own_codes, code_s, seqs)

    def whole_out(i):
        source, target = ((q_s, q_any), (k_s, k_any.at[0]), (v_s, v_any.at[0]))[i]
        return pltpu.make_async_copy(source, target, out_sem.at[i])

    def part_out(i, at):
        source, target = (
            (kr_s, k_any.at[1, at]),
            (vr_s, v_any.at[1, at]),
            (rem_s.at[at], rem_any.at[at]),
            (act_s, act_any.at[at]),
            (din_s, din_any.at[at]),
        )[i]
        return pltpu.make_async_copy(source, target, out_sem.at[3 + i])

    @pl.when(s == 0)
    def _():
        barrier = pltpu.get_barrier_semaphore()
        pl.semaphore_signal(barrier, inc=1, device_id=other, device_id_type=pl.DeviceIdType.MESH)
        load = pltpu.make_async_copy(tokens_ref, tok_s, weight_sem.at[len(pairs_of)])
        load.start()
        for i in range(3):
            weight(i).start()
        codes = jnp.where(valid_ref[...] == 1, group_ref[...], -1).astype(F32)
        own_codes[...] = jnp.zeros_like(own_codes)
        own_codes[0:seqs] = codes
        pl.semaphore_wait(barrier, 1)
        exchange(0).start()
        code_exchange().start()
        for i in range(3, len(pairs_of)):
            weight(i).start()
        vg_ref[...] = jnp.zeros_like(vg_ref)
        dbu_ref[...] = jnp.zeros_like(dbu_ref)
        bu_ref[...] = as_row(bu_in)
        load.wait()
        for i in range(3):
            weight(i).wait()

        def project_own(at, carry):
            x = tok_s[at]
            q_s[at] = (dot(x, wq[...]) + query_bias).astype(BF16)
            k_s[at] = dot(x, wk[...]).astype(BF16)
            v_s[at] = (dot(x, wv[...]) + value_bias).astype(BF16)
            return carry

        lax.fori_loop(0, seqs, project_own, 0)
        for i in range(3):
            whole_out(i).start()
        for i in range(3, len(pairs_of)):
            weight(i).wait()
        code_exchange().wait_recv()
        exchange(0).wait_send()
        if seqs > 1:
            exchange(1).start()

    for at in range(seqs):

        @pl.when(s == at)
        def _(at=at):
            exchange(at).wait_recv()
            if at:
                for i in range(3):
                    part_out(i, at - 1).wait()

    x = rem_s[s]
    kr_s[...] = dot(x, wk[...]).astype(BF16)
    vr_s[...] = (dot(x, wv[...]) + value_bias).astype(BF16)
    slot = lax.broadcasted_iota(jnp.int32, (1, PAIR), 1) % HEAD
    slot = slot.astype(F32)
    groups_row = group_ref[pl.ds(s, 1)].astype(F32)
    qm_ref[0] = jnp.where(spread(groups_row) == slot, 1.0, 0.0).astype(BF16)
    km_ref[0, 0] = jnp.where(spread(own_codes[pl.ds(s, 1)]) == slot, 0.0, MASKED).astype(BF16)
    km_ref[1, 0] = jnp.where(spread(code_s[pl.ds(s, 1)]) == slot, 0.0, MASKED).astype(BF16)
    for at in range(seqs):

        @pl.when(s == at)
        def _(at=at):
            for i in range(3):
                part_out(i, at).start()

    groups = features // (2 * PAIR)

    def heads(group, carry):
        lanes = pl.ds(pl.multiple_of(group * 2 * PAIR, 2 * PAIR), 2 * PAIR)
        attend_group(
            q_s[s, :, lanes],
            qm_ref[0],
            [(k_s[s, :, lanes], km_ref[0, 0], v_s[s, :, lanes]), (kr_s[:, lanes], km_ref[1, 0], vr_s[:, lanes])],
            att_ref.at[0, :, lanes],
            lse_ref.at[0, pl.ds(group * 2, 2)],
        )
        return carry

    lax.fori_loop(0, groups, heads, 0)

    for at in range(1, seqs):

        @pl.when(s == at)
        def _(at=at):
            for i in range(3, 5):
                part_out(i, at - 1).wait()

    tile = math.gcd(length, FEED_ROWS)
    chunk = math.gcd(hidden, 512)
    spans = [slice(c, c + chunk) for c in range(0, hidden, chunk)]

    def feed_rows(t, carry):
        rows = pl.ds(pl.multiple_of(t * tile, tile), tile)
        att = att_ref[0, rows]
        normed_one, scale_one = norm_parts(
            tok_s[s, rows].astype(F32) + (dot(att, wo[...]) + out_bias)
        )
        first = normed_one * gain_one + shift_one
        first_low = first.astype(BF16)
        first_t[:, rows] = first_low.T
        feed = jnp.zeros_like(first) + down_bias
        ahead = dot(first_low, wu[:, spans[0]])
        for i, cols in enumerate(spans):
            inner = ahead + bu_ref[:, cols]
            if i + 1 < len(spans):
                ahead = dot(first_low, wu[:, spans[i + 1]])
            active, slope = gelu_and_slope(inner)
            active = active.astype(BF16)
            act_s[rows, cols] = active
            din_s[rows, cols] = slope.astype(BF16)
            feed += dot(active, wd[cols])
        normed_two, scale_two = norm_parts(first + feed)
        out_ref[0, rows] = (normed_two * gain_two + shift_two).astype(BF16)
        cot = cot_ref[0, rows].astype(F32)
        second = norm_back(cot * gain_two, normed_two, scale_two)
        feed_low = second.astype(BF16)
        feed_t[:, rows] = feed_low.T
        back = second
        ahead = dot(feed_low, wd[spans[0]], NT)
        for i, cols in enumerate(spans):
            inner = ahead
            if i + 1 < len(spans):
                ahead = dot(feed_low, wd[spans[i + 1]], NT)
            inner = (inner * din_s[rows, cols].astype(F32)).astype(BF16)
            din_s[rows, cols] = inner
            dbu_ref[:, cols] += column_sum(inner.astype(F32))
            back += dot(inner, wu[:, cols], NT)
        residual = norm_back(back * gain_one, normed_one, scale_one)
        branch_low = residual.astype(BF16)
        bg_ref[0, rows] = branch_low
        att_grad = dot(branch_low, wo[...], NT).astype(BF16)
        ag_ref[0, rows] = att_grad
        product = att_grad.astype(F32) * att.astype(F32)
        coarse = product.astype(BF16)
        fine = (product - coarse.astype(F32)).astype(BF16)
        heads_count = features // HEAD
        of_head = lax.broadcasted_iota(jnp.int32, (heads_count, features), 1) // HEAD
        selector = (of_head == lax.broadcasted_iota(jnp.int32, of_head.shape, 0)).astype(F32)
        selector = selector.astype(BF16)
        delta = dot(selector, coarse, NT) + dot(selector, fine, NT)
        for pair in range(features // PAIR):
            lse_ref[0, pair, 2:4, rows] = delta[2 * pair : 2 * pair + 2]
        for i, values in enumerate(
            (
                branch_low.astype(F32),
                back * normed_one,
                back,
                feed_low.astype(F32),
                cot * normed_two,
                cot,
            )
        ):
            vg_ref[i : i + 1] += column_sum(values)
        return carry

    lax.fori_loop(0, length // tile, feed_rows, 0)

    for at in range(seqs):

        @pl.when(s == at)
        def _(at=at):
            for i in range(3, 5):
                part_out(i, at).start()
            if at < seqs - 1:
                exchange(at + 1).wait_send()
            if at + 2 < seqs:
                exchange(at + 2).start()
            if at == seqs - 1:
                for i in range(3):
                    whole_out(i).wait()
                for i in range(5):
                    part_out(i, at).wait()
                code_exchange().wait_send()


def front(tokens, group_ids, valid, cotangent, vectors, up_bias, weights):
    seqs, length, features = tokens.shape
    hidden = up_bias.shape[0]
    pairs = features // PAIR
    anywhere = pl.BlockSpec(memory_space=pl.ANY)

    def at_seq(*shape):
        return pl.BlockSpec((1,) + shape, lambda s: (s,) + (0,) * len(shape))

    def of_seqs(*shape, dtype=BF16):
        return jax.ShapeDtypeStruct((seqs,) + shape, dtype)

    def fixed(*shape):
        return pl.BlockSpec(shape, lambda s: (0,) * len(shape))

    rows, mask, lses, wide = (length, features), (length, PAIR), (pairs, 8, length), (length, hidden)
    turned = pl.BlockSpec((features, length), lambda s: (0, s))
    return pl.pallas_call(
        front_kernel,
        grid=(seqs,),
        in_specs=[anywhere, whole_spec(group_ids.shape), whole_spec(valid.shape), at_seq(*rows)]
        + [whole_spec(v.shape) for v in vectors + (up_bias,)]
        + [anywhere] * 6,
        out_specs=[at_seq(*rows)] * 4
        + [at_seq(*lses), at_seq(*mask)]
        + [pl.BlockSpec((2, 1) + mask, lambda s: (0, s, 0, 0))]
        + [turned] * 2
        + [fixed(8, features), fixed(1, hidden)]
        + [anywhere] * 6,
        out_shape=[of_seqs(*rows)] * 4
        + [of_seqs(*lses, dtype=F32), of_seqs(*mask)]
        + [jax.ShapeDtypeStruct((2, seqs) + mask, BF16)]
        + [jax.ShapeDtypeStruct((features, seqs * length), BF16)] * 2
        + [jax.ShapeDtypeStruct((8, features), F32), jax.ShapeDtypeStruct((1, hidden), F32)]
        + [of_seqs(*rows)]
        + [jax.ShapeDtypeStruct((2, seqs) + rows, BF16)] * 2
        + [of_seqs(*rows)]
        + [of_seqs(*wide)] * 2,
        scratch_shapes=[pltpu.VMEM(w.shape, BF16) for w in weights]
        + [pltpu.VMEM(tokens.shape, BF16)] * 4
        + [pltpu.VMEM(rows, BF16)] * 2
        + [pltpu.VMEM(tokens.shape, BF16)]
        + [pltpu.VMEM((seqs + -seqs % 8, length), F32)] * 2
        + [pltpu.VMEM(wide, BF16)] * 2
        + [pltpu.VMEM((1, hidden), F32)]
        + [pltpu.SemaphoreType.DMA((7,)), pltpu.SemaphoreType.DMA((8,))]
        + [pltpu.SemaphoreType.DMA((seqs + 1,))] * 2,
        compiler_params=pltpu.CompilerParams(
            collective_id=2, has_side_effects=True, vmem_limit_bytes=63 * MIB
        ),
        cost_estimate=cost(
            2 * tokens.size * (9 * features + 4 * hidden + 8 * length), 2 * 20 * tokens.size, tokens.size * 24
        ),
        name="front",
    )(tokens, group_ids, valid, cotangent, *vectors, up_bias, *weights)


def feed_weights_kernel(blocks, first_ref, din_ref, feed_ref, act_ref, att_any, bg_any,
                        dwu_ref, dwd_ref, dwo_ref, up_s, up_in, down_s, down_in, out_s, out_in,
                        att_s, bg_s, near_sem, send_sem, recv_sem):
    step = pl.program_id(0)
    features = first_ref.shape[0]
    me = lax.axis_index("dp")
    core = me % 2
    other = {"dp": me + 1 - 2 * core}

    def loads():
        return [
            pltpu.make_async_copy(att_any, att_s, near_sem.at[0]),
            pltpu.make_async_copy(bg_any, bg_s, near_sem.at[1]),
        ]

    def swaps(block):
        if block == blocks:
            pairs = [(out_s.at[:, 1 - core], out_in)]
        else:
            pairs = [
                (up_s.at[block % 2, :, 1 - core], up_in.at[block]),
                (down_s.at[block % 2, :, 1 - core], down_in.at[block]),
            ]
        return [
            pltpu.make_async_remote_copy(
                src_ref=source,
                dst_ref=target,
                send_sem=send_sem.at[2 * block + i],
                recv_sem=recv_sem.at[2 * block + i],
                device_id=other,
                device_id_type=pl.DeviceIdType.MESH,
            )
            for i, (source, target) in enumerate(pairs)
        ]

    @pl.when(step == 0)
    def _():
        for load in loads():
            load.start()
        barrier = pltpu.get_barrier_semaphore()
        pl.semaphore_signal(barrier, inc=1, device_id=other, device_id_type=pl.DeviceIdType.MESH)
        pl.semaphore_wait(barrier, 1)

    @pl.when(step < blocks)
    def _():
        slot = step % 2
        up_s[slot] = dot(first_ref[...], din_ref[...]).astype(BF16).reshape(up_s.shape[1:])
        down_s[slot] = dot(feed_ref[...], act_ref[...]).astype(BF16).T.reshape(down_s.shape[1:])

    for block in range(blocks):

        @pl.when(step == block)
        def _(block=block):
            for swap in swaps(block):
                swap.start()

    @pl.when(step == blocks)
    def _():
        for load in loads():
            load.wait()
        out_s[...] = dot(att_s[...].T, bg_s[...]).astype(BF16).reshape(out_s.shape)
        for swap in swaps(blocks):
            swap.start()

    for block in range(blocks):

        @pl.when(step == block + 1)
        def _(block=block):
            for swap in swaps(block):
                swap.wait()
            dwu_ref[:, 0] = (up_s[block % 2, :, core].astype(F32) + up_in[block].astype(F32)).astype(BF16)
            dwd_ref[...] = (down_s[block % 2, :, core].astype(F32) + down_in[block].astype(F32)).astype(BF16)

    @pl.when(step == blocks + 1)
    def _():
        for swap in swaps(blocks):
            swap.wait()
        dwo_ref[...] = (out_s[:, core].astype(F32) + out_in[...].astype(F32)).astype(BF16)


def feed_weights(first_t, din, feed_t, act, att, bg):
    dp = lax.axis_size("dp")
    features, rows = first_t.shape
    hidden = act.shape[1]
    blocks, half, low, deep = hidden // features, dp // 2, features // dp, hidden // dp
    each = half // blocks
    wide_spec = pl.BlockSpec((rows, features), lambda i: (0, jnp.minimum(i, blocks - 1)))
    anywhere = pl.BlockSpec(memory_space=pl.ANY)

    def behind(i):
        return jnp.clip(i - 1, 0, blocks - 1)

    return pl.pallas_call(
        functools.partial(feed_weights_kernel, blocks),
        grid=(blocks + 2,),
        in_specs=[
            whole_spec(first_t.shape),
            wide_spec,
            whole_spec(feed_t.shape),
            wide_spec,
            anywhere,
            anywhere,
        ],
        out_specs=[
            pl.BlockSpec((half, 1, low, features), lambda i: (0, behind(i), 0, 0)),
            pl.BlockSpec((each, deep, features), lambda i: (behind(i), 0, 0)),
            pl.BlockSpec((half, low, features), lambda i: (0, 0, 0)),
        ],
        out_shape=[
            jax.ShapeDtypeStruct((half, blocks, low, features), BF16),
            jax.ShapeDtypeStruct((half, deep, features), BF16),
            jax.ShapeDtypeStruct((half, low, features), BF16),
        ],
        scratch_shapes=[
            pltpu.VMEM((2, half, 2, low, features), BF16),
            pltpu.VMEM((blocks, half, low, features), BF16),
            pltpu.VMEM((2, each, 2, deep, features), BF16),
            pltpu.VMEM((blocks, each, deep, features), BF16),
            pltpu.VMEM((half, 2, low, features), BF16),
            pltpu.VMEM((half, low, features), BF16),
            pltpu.VMEM(att.shape, BF16),
            pltpu.VMEM(bg.shape, BF16),
            pltpu.SemaphoreType.DMA((2,)),
            pltpu.SemaphoreType.DMA((2 * blocks + 2,)),
            pltpu.SemaphoreType.DMA((2 * blocks + 2,)),
        ],
        compiler_params=pltpu.CompilerParams(
            collective_id=3, has_side_effects=True, vmem_limit_bytes=63 * MIB
        ),
        cost_estimate=cost(
            2 * rows * features * (2 * hidden + features), 4 * rows * (hidden + 2 * features)
        ),
        name="feed_weights",
    )(first_t, din, feed_t, act, att, bg)


def own_back_kernel(bg_ref, dq_ref, dk_ref, dv_ref, wq_ref, wk_ref, wv_ref, out_ref):
    total = bg_ref[0].astype(F32) + dot(dq_ref[0], wq_ref[...], NT)
    total += dot(dk_ref[0], wk_ref[...], NT)
    total += dot(dv_ref[0], wv_ref[...], NT)
    out_ref[0] = total.astype(BF16)


def rem_back_kernel(dk_ref, dv_ref, wk_ref, wv_ref, out_ref):
    total = dot(dk_ref[0], wk_ref[...], NT) + dot(dv_ref[0], wv_ref[...], NT)
    out_ref[0] = total.astype(BF16)


def tokens_back(kernel, rows, weights):
    seqs, length, features = rows[0].shape
    tile = math.gcd(length, 512)
    row_spec = pl.BlockSpec((1, tile, features), lambda s, i: (s, i, 0))
    size = rows[0].size
    return pl.pallas_call(
        kernel,
        grid=(seqs, length // tile),
        in_specs=[row_spec] * len(rows) + [whole_spec(w.shape) for w in weights],
        out_specs=row_spec,
        out_shape=jax.ShapeDtypeStruct(rows[0].shape, BF16),
        compiler_params=params(60),
        cost_estimate=cost(2 * size * features * len(weights), 2 * size * (1 + len(rows))),
        name="tokens_back",
    )(*rows, *weights)


def weights_back_kernel(tok_ref, rem_ref, dq_ref, dko_ref, dvo_ref, dkr_ref, dvr_ref,
                        wq_ref, wk_ref, wv_ref, bq_ref, bv_ref, tok_t, rem_t):
    @pl.when(pl.program_id(0) == 0)
    def _():
        tok_t[...] = tok_ref[...].T
        rem_t[...] = rem_ref[...].T

    wq_ref[...] = dot(tok_t[...], dq_ref[...]).astype(BF16)
    wk_ref[...] = (dot(tok_t[...], dko_ref[...]) + dot(rem_t[...], dkr_ref[...])).astype(BF16)
    wv_ref[...] = (dot(tok_t[...], dvo_ref[...]) + dot(rem_t[...], dvr_ref[...])).astype(BF16)
    bq_ref[...] = column_sum(dq_ref[...].astype(F32))
    bv_ref[...] = column_sum(dvo_ref[...].astype(F32)) + column_sum(dvr_ref[...].astype(F32))


def weights_back(tok, rem, dq, dko, dvo, dkr, dvr):
    rows, features = tok.shape
    others = rem.shape[0]
    wide = math.gcd(features, 256)
    own_spec = pl.BlockSpec((rows, wide), lambda j: (0, j))
    rem_spec = pl.BlockSpec((others, wide), lambda j: (0, j))
    bias_spec = pl.BlockSpec((1, wide), lambda j: (0, j))
    return pl.pallas_call(
        weights_back_kernel,
        grid=(features // wide,),
        in_specs=[
            whole_spec(tok.shape),
            whole_spec(rem.shape),
            own_spec,
            own_spec,
            own_spec,
            rem_spec,
            rem_spec,
        ],
        out_specs=[pl.BlockSpec((features, wide), lambda j: (0, j))] * 3 + [bias_spec] * 2,
        out_shape=[jax.ShapeDtypeStruct((features, features), BF16)] * 3
        + [jax.ShapeDtypeStruct((1, features), F32)] * 2,
        scratch_shapes=[
            pltpu.VMEM((features, rows), BF16),
            pltpu.VMEM((features, others), BF16),
        ],
        compiler_params=params(60),
        cost_estimate=cost(
            2 * features * features * (3 * rows + 2 * others),
            2 * (4 * tok.size + 3 * rem.size + 3 * features * features),
        ),
        name="weights_back",
    )(tok, rem, dq, dko, dvo, dkr, dvr)


def halve(value, axis, bit):
    size = lax.axis_size(axis)
    mine = (lax.axis_index(axis) >> bit) & 1
    pairs = value.reshape((value.shape[0] // 2, 2) + value.shape[1:])
    keep = lax.dynamic_index_in_dim(pairs, mine, 1, keepdims=False)
    send = lax.dynamic_index_in_dim(pairs, 1 - mine, 1, keepdims=False)
    came = lax.ppermute(send, axis, [(i, i ^ (1 << bit)) for i in range(size)])
    return keep.astype(F32) + came.astype(F32)


def scatter_sum(value, low=True):
    dp, blk = lax.axis_size("dp"), lax.axis_size("blk")
    if dp & (dp - 1) or blk & (blk - 1):
        return lax.psum_scatter(
            value.astype(F32), ("dp", "blk"), scatter_dimension=0, tiled=True
        )
    kept = value.dtype
    each = value.shape[0] // (dp * blk)
    value = value.reshape((dp, blk * each) + value.shape[1:])
    for bit in range(dp.bit_length() - 1):
        value = halve(value, "dp", bit).astype(kept)
    value = value.reshape((blk, each) + value.shape[2:])
    for bit in range(blk.bit_length() - 1):
        value = halve(value, "blk", bit)
        value = value if (2 << bit) == blk else value.astype(kept)
    return value.reshape(value.shape[1:]).astype(F32)


class Unit:
    def __init__(self, parts, rows, columns, halves, outs):
        self.parts, self.rows, self.columns = parts, rows, columns
        self.halves, self.outs = halves, outs
        self.first = 1 if parts else 0
        self.half = rows // (2 * halves)
        self.last_type = BF16 if (rows // 2) % 16 == 0 else F32


def timetable(units, bits, seqs, groups, slot_us, token_us):
    free, pending, table = {}, [], []
    slots = seqs * groups * 2

    def launch(key, now):
        kind, which, step = key
        if kind == "tokens":
            link, us = "blk", token_us
        elif kind == "vectors":
            link, us = None, 1.0
        else:
            us = units[which].rows * units[which].columns * 2e-5
            us *= 1 << max(bits - 1 - step, 0)
            us *= {0: 0.3, bits - 1: 3.0}.get(step, 1.1)
            link = {0: "core", bits - 1: "far", bits: "blk"}.get(step, "near")
        start = max(now, free.get(link, 0.0))
        if link:
            free[link] = start + us
        if kind != "tokens":
            pending.append((start + us + 2.0, key))

    for u, unit in enumerate(units):
        if unit.parts:
            launch(("unit", u, 1), 3.0)
    first_group = sum(1 for unit in units if unit.parts)
    now = 0.0
    while len(table) < slots or pending:
        slot = len(table)
        if slot < slots:
            now = (slot + 1) * slot_us
            part, major, minor = slot // (seqs * groups), slot // groups % seqs, slot % groups
            if part == 0 and minor == groups - 1:
                launch(("tokens", major, 0), now)
            major, minor = divmod(slot - seqs * groups, seqs)
            if part == 1 and minor == seqs - 1:
                launch(("unit", first_group + major, 0), now)
            if slot == slots - 1:
                launch(("vectors", 0, 0), now)
            due = sorted(p for p in pending if p[0] <= now)
        else:
            due = [min(pending)]
            now = max(now + 0.3, due[0][0])
        table.append([key for _, key in due])
        for found in due:
            pending.remove(found)
            kind, which, step = found[1]
            if step < bits:
                launch((kind, which, step + 1), now)
    tail = [key for keys in table[slots:] for key in keys]
    return table[:slots], tail + [("tokens", s, 0) for s in range(seqs)]


def order_of(step, seqs, groups):
    part = step // (seqs * groups)
    left = step - part * (seqs * groups)
    s = left // groups * (1 - part) + left % seqs * part
    h = left % groups * (1 - part) + left // seqs * part
    return part, s, h


def back_kernel(units, bits, groups, table, tail, n_out, *refs):
    (q_ref, qm_ref, g_ref, lse_ref, k_ref, km_ref, v_ref,
     tok_ref, rem_ref, wq_ref, wk_ref, wv_ref, vg_ref, vu_ref) = refs[:14]
    sources, refs = refs[14:17], list(refs[17:])
    tokens_any, rem_in, *outs = refs[:n_out]
    refs = refs[n_out:]
    kept = [refs.pop(0) for _ in units]
    landed = [
        [refs.pop(0) if k >= unit.first else None for k in range(bits)] for unit in units
    ]
    wide = [refs.pop(0) for _ in units]
    parting = [refs.pop(0) for _ in units]
    last = [refs.pop(0) for _ in units]
    (weight_sum, group_src, total_s, turned, dq_part, dq_s, dk_s, dv_s,
     rem_out, vec, vec_in, bias_sum, send_sem, recv_sem, local_sem, out_sem) = refs
    step = pl.program_id(0)
    steps = pl.num_programs(0)
    seqs = rem_out.shape[0]
    part, s, h = order_of(step, seqs, groups)
    features = tok_ref.shape[2]
    me, side = lax.axis_index("dp"), lax.axis_index("blk")
    core = me % 2

    def swapped(k):
        return {1: 2, 2: 1}.get(k, k) if bits > 2 else k

    def pick(values, k):
        return values[k] + (values[swapped(k)] - values[k]) * core

    bit_own = [(me // (1 << bit)) % 2 for bit in range(bits)]
    across = [me + (1 << bit) * (1 - 2 * bit_own[bit]) for bit in range(bits)]
    own = [pick(bit_own, k) for k in range(bits)]
    partner = [{"dp": pick(across, k)} for k in range(bits)] + [{"blk": 1 - side}]
    first_group = sum(1 for unit in units if unit.parts)
    lead = (slice(None),) * (bits - 1)

    def natural(digits):
        by_step = [None] + list(digits[::-1])
        return tuple(pick(by_step, bit) for bit in range(bits - 1, 0, -1))

    def digits_of(n, count):
        return [(n // (1 << (count - 1 - i))) % 2 for i in range(count)]

    sems = {}
    for u, unit in enumerate(units):
        for k in range(unit.first, bits + 1):
            sems["unit", u, k, 0] = len(sems)
    for k in range(bits + 1):
        sems["vectors", 0, k, 0] = len(sems)
    for k in range(seqs):
        sems["tokens", k, 0, 0] = len(sems)

    def remote(source, target, device, key):
        return pltpu.make_async_remote_copy(
            src_ref=source,
            dst_ref=target,
            send_sem=send_sem.at[sems[key]],
            recv_sem=recv_sem.at[sems[key]],
            device_id=device,
            device_id_type=pl.DeviceIdType.MESH,
        )

    near_sems = {}
    for u, unit in enumerate(units):
        for p in range(len(unit.parts or ())):
            for n in range(1 << (bits - 1)):
                near_sems[u, p, n] = len(near_sems)

    def spot(k, value):
        return tuple(
            own[at] if at < k else value if at == k else slice(None) for at in range(bits - 1, 0, -1)
        )

    def copies(kind, which, k):
        if kind == "tokens":
            return [remote(rem_out.at[which], rem_in.at[which], partner[bits], (kind, which, 0, 0))]
        if kind == "vectors":
            return [remote(vec.at[k], vec_in.at[k], partner[k], (kind, 0, k, 0))]
        u, unit = which, units[which]
        if k == bits:
            return [remote(parting[u], last[u], partner[bits], (kind, u, k, 0))]
        if k:
            source = kept[u].at[spot(k, 1 - own[k])]
            return [remote(source, landed[u][k], partner[k], (kind, u, k, 0))]
        source = group_src.at[(u - first_group,) + lead + (1 - core,)]
        return [remote(source, landed[u][0], partner[0], (kind, u, 0, 0))]

    def near_copies(u):
        found, row = [], 0
        for p, (source, first, rows) in enumerate(units[u].parts):
            for n in range(1 << (bits - 1)):
                digits = digits_of(n, bits - 1)
                found.append(
                    pltpu.make_async_copy(
                        sources[source].at[natural(digits) + (pl.ds(first, rows),)],
                        kept[u].at[tuple(digits) + (pl.ds(row, rows),)],
                        local_sem.at[near_sems[u, p, n]],
                    )
                )
            row += rows
        return found

    def launch(*key):
        for copy in copies(*key):
            copy.start()

    def halves_of(u, which):
        unit = units[u]
        return [
            wide[u][pl.ds(pl.multiple_of(i * 2 * unit.half + which * unit.half, 8), unit.half)]
            for i in range(unit.halves)
        ]

    def receive(kind, which, k):
        for copy in copies(kind, which, k):
            copy.wait_recv()
        if kind == "tokens":
            return
        if kind == "vectors":
            vec[k + 1] = vec[k] + vec_in[k]
            if k < bits:
                launch(kind, 0, k + 1)
            return
        u, unit = which, units[which]
        if k == bits:
            for i, (mine, (out, rows, columns)) in enumerate(zip(halves_of(u, side), unit.outs)):
                came = last[u][...].astype(F32)[i * unit.half : (i + 1) * unit.half]
                outs[out][rows, columns] = mine + came
            return
        place = spot(k, own[k]) if k else lead
        open_at = [i for i, at in enumerate(place) if isinstance(at, slice)]

        def add(n, carry):
            at, where = list(place), digits_of(n, len(open_at))
            for i, digit in zip(open_at, where):
                at[i] = digit
            at = tuple(at)
            if k:
                mine, came = kept[u][at], landed[u][k][tuple(where)]
            else:
                mine = group_src[(u - first_group,) + natural(at) + (core,)]
                came = landed[u][0][natural(at)]
            total = mine.astype(F32) + came.astype(F32)
            if k == bits - 1:
                wide[u][...] = total
            else:
                kept[u][at] = total.astype(BF16)
            return carry

        if open_at:
            lax.fori_loop(0, 1 << len(open_at), add, 0)
        else:
            add(0, 0)
        if k == bits - 1:
            pieces = halves_of(u, 1 - side)
            pieces = pieces[0] if len(pieces) == 1 else jnp.concatenate(pieces, axis=0)
            parting[u][...] = pieces.astype(unit.last_type)
        launch(kind, u, k + 1)

    @pl.when(step == 0)
    def _():
        barrier = pltpu.get_barrier_semaphore()
        for other in partner:
            pl.semaphore_signal(barrier, inc=1, device_id=other, device_id_type=pl.DeviceIdType.MESH)
        pl.semaphore_wait(barrier, bits + 1)
        for u, unit in enumerate(units):
            if unit.parts:
                for copy in near_copies(u):
                    copy.start()
        for u, unit in enumerate(units):
            if unit.parts:
                for copy in near_copies(u):
                    copy.wait()
                launch("unit", u, 1)
        weight_sum[...] = jnp.zeros_like(weight_sum)
        bias_sum[...] = jnp.zeros_like(bias_sum)

    @pl.when((part == 0) & (h == 0))
    def _():
        turned[0] = rem_ref[0].T
        total_s[...] = jnp.zeros_like(total_s)

    @pl.when((part == 1) & (h == 0))
    def _():
        turned[s] = tok_ref[0].T

    width = q_ref.shape[2]
    columns = pl.ds(pl.multiple_of(h * width, width), width)

    found = attend_back_part(
        q_ref[0], qm_ref[0], g_ref[0], lse_ref.at[0], k_ref[0, 0], km_ref[0, 0], v_ref[0, 0],
        dk_s.at[s, :, columns], dv_s.at[s, :, columns],
    )
    dk, dv = dk_s[s, :, columns], dv_s[s, :, columns]
    x_t = turned[s * part]
    weight_sum[h, 1] += dot(x_t, dk)
    weight_sum[h, 2] += dot(x_t, dv)
    bias_sum[h, 1:2] += column_sum(dv.astype(F32))

    @pl.when(part == 0)
    def _():
        total_s[...] += dot(dk, wk_ref[:, columns], NT) + dot(dv, wv_ref[:, columns], NT)
        for pair, value in enumerate(found):
            dq_part[s, h, pair] = value.astype(dq_part.dtype)

    @pl.when(part == 1)
    def _():
        queries = []
        for pair, value in enumerate(found):
            value = (value + dq_part[s, h, pair].astype(F32)) * SCALE
            queries.append(value.T.astype(BF16))
        dq = jnp.concatenate(queries, axis=1)
        dq_s[s, :, columns] = dq
        weight_sum[h, 0] += dot(x_t, dq)
        bias_sum[h, 0:1] += column_sum(dq.astype(F32))

    for at in range(seqs):

        @pl.when(step == (at + 1) * groups - 1)
        def _(at=at):
            rem_out[at] = total_s[...].astype(BF16)
            launch("tokens", at, 0)

    for at in range(groups):

        @pl.when(step == steps - (groups - 1 - at) * seqs - 1)
        def _(at=at):
            rows = features // (1 << bits)
            for i in range(3):
                piece = weight_sum[at, i].astype(BF16)
                piece = piece.reshape((2,) * bits + (rows, piece.shape[1]))
                group_src[(at,) + (slice(None),) * bits + (slice(i * rows, (i + 1) * rows),)] = piece
            launch("unit", first_group + at, 0)

    @pl.when(step == steps - 1)
    def _():
        vec[0] = jnp.zeros_like(vec[0])
        vec[0, 0:6] = vg_ref[0:6]
        for at in range(groups):
            vec[0, 6:8, at * width : (at + 1) * width] = bias_sum[at, 0:2]
        blocks = vu_ref.shape[1] // features
        for at in range(blocks):
            vec[0, 8 + at : 9 + at] = vu_ref[:, at * features : (at + 1) * features]
        launch("vectors", 0, 0)

    for at, keys in enumerate(table):
        if keys:

            @pl.when(step == at)
            def _(keys=keys):
                for key in keys:
                    receive(*key)

    @pl.when(step == steps - 1)
    def _():
        def own_out(at):
            return pltpu.make_async_copy(dq_s.at[at], tokens_any.at[at], out_sem.at[at])

        left = list(tail)
        for at in range(seqs):
            total = dot(dq_s[at], wq_ref[...], NT)
            total += dot(dk_s[at], wk_ref[...], NT) + dot(dv_s[at], wv_ref[...], NT)
            dq_s[at] = total.astype(BF16)
            own_out(at).start()
            for _ in range(3):
                if left:
                    receive(*left.pop(0))
        for key in left:
            receive(*key)
        for at in range(seqs):
            own_out(at).wait()
        shards = (1 << bits) * 2
        place = me * 2 + side
        share = features // shards
        rows = pltpu.roll(vec[bits + 1, 0:8], (shards - place) * share % features, 1)
        outs[-1][0:8] = rows[:, :PAIR]
        share = vu_ref.shape[1] // shards
        each = features // share
        row = vec[bits + 1, pl.ds(8 + place // each, 1)]
        rows = pltpu.roll(jnp.broadcast_to(row, (8, features)), (each - place % each) * share % features, 1)
        outs[-1][8:16] = rows[:, :PAIR]
        for u, unit in enumerate(units):
            for k in range(unit.first, bits + 1):
                for copy in copies("unit", u, k):
                    copy.wait_send()
        for k in range(bits + 1):
            copies("vectors", 0, k)[0].wait_send()
        for k in range(seqs):
            copies("tokens", k, 0)[0].wait_send()


def back_and_sum(q, qm, g, lse, k, km, v, tokens, rem_tokens, weights, dwd, dwu, dwo, vg, vu):
    bits = lax.axis_size("dp").bit_length() - 1
    seqs, length, features = q.shape
    width = math.gcd(features, 2 * PAIR)
    groups, pairs = features // width, width // PAIR
    low, deep, blocks = dwo.shape[1], dwd.shape[1], dwu.shape[1]
    lead = (2,) * bits
    sources = [x.reshape(lead[1:] + (-1, features)) for x in (dwd, dwu, dwo)]
    every = slice(None)
    units = []
    quarter = deep // 4
    for i in range(2):
        at = slice(i * quarter, (i + 1) * quarter)
        parts = [(0, i * quarter, quarter), (0, (2 + i) * quarter, quarter)]
        units.append(Unit(parts, 2 * quarter, features, 1, [(0, at, every)]))
    for i in range(2):
        found = range(i * blocks // 2, (i + 1) * blocks // 2)
        units.append(
            Unit(
                [(1, found[0] * low, len(found) * low)],
                len(found) * low,
                features,
                len(found),
                [(1, every, slice(b * features, (b + 1) * features)) for b in found],
            )
        )
    units.append(Unit([(2, 0, low)], low, features, 1, [(2, every, every)]))
    for h in range(groups):
        columns = slice(h * width, (h + 1) * width)
        units.append(Unit(None, 3 * low, width, 3, [(3 + i, every, columns) for i in range(3)]))
    table, tail = timetable(units, bits, seqs, groups, 4.6, length * features * 4e-5)

    half = low // 2
    out_shape = [
        jax.ShapeDtypeStruct(q.shape, BF16),
        jax.ShapeDtypeStruct(q.shape, BF16),
        jax.ShapeDtypeStruct((deep // 2, features), F32),
        jax.ShapeDtypeStruct((half, blocks * features), F32),
        *(jax.ShapeDtypeStruct((half, features), F32) for _ in range(4)),
        jax.ShapeDtypeStruct((16, PAIR), F32),
    ]
    tops = lead[1:]
    scratch = [pltpu.VMEM(tops + (u.rows, u.columns), BF16) for u in units]
    for u in units:
        scratch += [pltpu.VMEM(tops[k:] + (u.rows, u.columns), BF16) for k in range(u.first, bits)]
    scratch += [pltpu.VMEM((u.rows, u.columns), F32) for u in units]
    scratch += [pltpu.VMEM((u.rows // 2, u.columns), u.last_type) for u in units] * 2
    count = len(units) * (bits + 1) + bits + 1 + seqs
    near = sum(len(u.parts) << (bits - 1) for u in units if u.parts)
    scratch += [
        pltpu.VMEM((groups, 3, features, width), F32),
        pltpu.VMEM((groups,) + lead + (3 * low, width), BF16),
        pltpu.VMEM((length, features), F32),
        pltpu.VMEM((seqs, features, length), BF16),
        pltpu.VMEM((seqs, groups, pairs, PAIR, length), F32),
        *(pltpu.VMEM((seqs, length, features), BF16) for _ in range(4)),
        pltpu.VMEM((bits + 2, 16, features), F32),
        pltpu.VMEM((bits + 1, 16, features), F32),
        pltpu.VMEM((groups, 8, width), F32),
        pltpu.SemaphoreType.DMA((count,)),
        pltpu.SemaphoreType.DMA((count,)),
        pltpu.SemaphoreType.DMA((near,)),
        pltpu.SemaphoreType.DMA((seqs,)),
    ]

    def at_step(shape, index):
        return pl.BlockSpec(shape, lambda i: index(*order_of(i, seqs, groups)))

    heads_at = at_step((1, length, width), lambda p, s, h: (s, 0, h))
    keys_at = at_step((1, 1, length, width), lambda p, s, h: (1 - p, s, 0, h))

    def rows_at(which):
        last = seqs - 1
        return pl.BlockSpec(
            (1, length, features),
            lambda i: (jnp.clip(i // groups if which == 0 else i - seqs * groups, 0, last), 0, 0),
            pipeline_mode=pl.Buffered(1),
        )

    def fixed(shape):
        return pl.BlockSpec(shape, lambda i: (0,) * len(shape), pipeline_mode=pl.Buffered(1))

    return pl.pallas_call(
        functools.partial(back_kernel, units, bits, groups, table, tail, len(out_shape)),
        grid=(2 * seqs * groups,),
        in_specs=[
            heads_at,
            at_step((1, length, PAIR), lambda p, s, h: (s, 0, 0)),
            heads_at,
            at_step((1, pairs, 8, length), lambda p, s, h: (s, h, 0, 0)),
            keys_at,
            at_step((1, 1, length, PAIR), lambda p, s, h: (1 - p, s, 0, 0)),
            keys_at,
            rows_at(1),
            rows_at(0),
        ]
        + [whole_spec(w.shape) for w in weights + (vg, vu)]
        + [pl.BlockSpec(memory_space=pl.ANY)] * 3,
        out_specs=[pl.BlockSpec(memory_space=pl.ANY)] * 2
        + [fixed(s.shape) for s in out_shape[2:]],
        out_shape=out_shape,
        scratch_shapes=scratch,
        compiler_params=pltpu.CompilerParams(
            collective_id=1, has_side_effects=True, vmem_limit_bytes=63 * MIB
        ),
        cost_estimate=cost(80 * q.size * length, 2 * q.size * 14, 2 * q.size * length // HEAD),
        name="back_and_sum",
    )(q, qm, g, lse, k, km, v, tokens, rem_tokens, *weights, vg, vu, *sources)


def finish_kernel(residual_ref, own_ref, rem_ref, *refs):
    ins, outs = refs[:7], refs[7:]
    total = residual_ref[...].astype(F32) + own_ref[...].astype(F32) + rem_ref[...].astype(F32)
    outs[0][...] = total.astype(BF16)

    @pl.when(pl.program_id(0) == 0)
    def _():
        for source, target in zip(ins[:6], outs[1:7]):
            target[...] = source[...]
        for i, target in enumerate(outs[7:]):
            target[...] = ins[6][i, : target.shape[0]]


def finish(residual, own, rem, matrices, vectors, shares):
    seqs, length, features = own.shape
    row_spec = pl.BlockSpec((1, length, features), lambda s: (s, 0, 0))

    def fixed(shape):
        return pl.BlockSpec(shape, lambda s: (0,) * len(shape))

    shapes = [m.shape for m in matrices] + [(n,) for n in shares]
    return pl.pallas_call(
        finish_kernel,
        grid=(seqs,),
        in_specs=[row_spec] * 3 + [fixed(m.shape) for m in matrices] + [fixed(vectors.shape)],
        out_specs=[row_spec] + [fixed(s) for s in shapes],
        out_shape=[jax.ShapeDtypeStruct(own.shape, BF16)] + [jax.ShapeDtypeStruct(s, F32) for s in shapes],
        compiler_params=params(60),
        cost_estimate=cost(2 * own.size, 8 * own.size),
        name="finish",
    )(residual, own, rem, *matrices, vectors)


def back_plainly(q, qm, o, g, lse, own, rem, bg, tokens, rem_tokens, weights, dwd, dwu, dwo, vg, vu):
    seqs, length, features = q.shape
    dp, blk = lax.axis_size("dp"), lax.axis_size("blk")
    dq, dko, dvo, dkr, dvr = attend_back(q, qm, o, g, lse, own, rem)
    rem_gradient = tokens_back(rem_back_kernel, (dkr, dvr), weights[1:])
    came = [
        lax.ppermute(part, "blk", [((i + r) % blk, i) for i in range(blk)])
        for r, part in enumerate(jnp.split(rem_gradient, blk - 1, axis=1), 1)
    ]
    flat = [v.reshape(-1, features) for v in (tokens, rem_tokens, dq, dko, dvo, dkr, dvr)]
    dwq, dwk, dwv, dbq, dbv = weights_back(*flat)
    total = tokens_back(own_back_kernel, (bg, dq, dko, dvo), weights).astype(F32)
    for part in came:
        total += part.astype(F32)
    dwu = jnp.moveaxis(dwu[0], 0, 1).reshape(features, -1)
    summed = [scatter_sum(w) for w in (dwd, dwu, dwo, dwq, dwk, dwv)]
    rows = [vg[i] for i in range(6)] + [dbq, dbv, vu]
    rows = [scatter_sum(v.reshape(dp * blk, -1)) for v in rows]
    return [total.astype(BF16)] + summed + [[v[0] for v in rows]]


def body(
    tokens,
    query_weight,
    query_bias,
    key_weight,
    value_weight,
    value_bias,
    out_weight,
    out_bias,
    gain_one,
    shift_one,
    up_weight,
    up_bias,
    down_weight,
    down_bias,
    gain_two,
    shift_two,
    group_ids,
    valid_mask,
    cotangent,
):
    seqs, length, features = tokens.shape
    rows = seqs * length
    blk = lax.axis_size("blk")

    def from_others(value):
        found = [
            lax.ppermute(value, "blk", [(i, (i + r) % blk) for i in range(blk)])
            for r in range(1, blk)
        ]
        return found[0] if len(found) == 1 else jnp.concatenate(found, axis=1)

    codes = jnp.where(valid_mask == 1, group_ids, -1)
    dp = lax.axis_size("dp")
    by_kernel = blk == 2 and dp & (dp - 1) == 0 and dp > 1 and (features // dp) % 16 == 0
    projections = (query_weight, key_weight, value_weight)
    vectors = (
        query_bias,
        value_bias,
        out_bias,
        gain_one,
        shift_one,
        down_bias,
        gain_two,
        shift_two,
    )

    if by_kernel:
        (block_out, branch_gradient, attended_gradient, attended, lse, query_mask, key_masks,
         first_t, feed_t, vector_gradients, up_bias_gradient, queries, keys, values,
         rem_tokens, active, inner_gradient) = front(
            tokens,
            group_ids,
            valid_mask,
            cotangent,
            vectors,
            up_bias,
            projections + (out_weight, up_weight, down_weight),
        )
        dwu, dwd, dwo = feed_weights(
            first_t,
            inner_gradient.reshape(rows, -1),
            feed_t,
            active.reshape(rows, -1),
            attended.reshape(rows, features),
            branch_gradient.reshape(rows, features),
        )
        own_gradient, rem_gradient, *matrices, vectors = back_and_sum(
            queries,
            query_mask,
            attended_gradient,
            lse,
            keys,
            key_masks,
            values,
            tokens,
            rem_tokens,
            projections,
            dwd,
            dwu,
            dwo,
            vector_gradients,
            up_bias_gradient,
        )
        shares = [features // (dp * blk)] * 8 + [up_bias.size // (dp * blk)]
        found = finish(branch_gradient, own_gradient, rem_gradient, matrices, vectors, shares)
        tokens_gradient, dwd, dwu, dwo, dwq, dwk, dwv, *rows_left = found
    else:
        rem_tokens = from_others(tokens)
        rem_codes = from_others(codes.astype(BF16)).astype(jnp.int32)
        slot = jnp.arange(PAIR, dtype=jnp.int32) % HEAD

        def key_mask(code):
            return jnp.where(code[:, :, None] == slot, 0.0, MASKED).astype(BF16)

        query_mask = (group_ids[:, :, None] == slot).astype(BF16)
        vectors = jnp.stack(vectors).astype(F32)
        queries, own_keys, own_values = project(tokens, vectors, projections)
        rem_keys, rem_values = project(rem_tokens, vectors, projections[1:])
        own = (own_keys, key_mask(codes), own_values)
        rem = (rem_keys, key_mask(rem_codes), rem_values)
        attended, lse = attend(queries, query_mask, own, rem)
        (block_out, branch_gradient, attended_gradient, vector_gradients, up_bias_gradient,
         dwu, dwd, dwo) = feed_both_ways(
            tokens.reshape(rows, features),
            attended.reshape(rows, features),
            cotangent.reshape(rows, features),
            vectors[2:],
            up_bias.astype(F32)[None],
            out_weight,
            up_weight,
            down_weight,
            1,
        )
        tokens_gradient, dwd, dwu, dwo, dwq, dwk, dwv, rows_left = back_plainly(
            queries,
            query_mask,
            attended,
            attended_gradient.reshape(tokens.shape),
            lse,
            own,
            rem,
            branch_gradient.reshape(tokens.shape),
            tokens,
            rem_tokens,
            projections,
            dwd,
            dwu,
            dwo,
            vector_gradients,
            up_bias_gradient,
        )
    dbo, dg1, ds1, dbd, dg2, ds2, dbq, dbv, dbu = rows_left
    return (
        block_out.reshape(tokens.shape),
        tokens_gradient,
        dwq,
        dbq,
        dwk,
        dwv,
        dbv,
        dwo,
        dbo,
        dg1,
        ds1,
        dwu,
        dbu,
        dwd,
        dbd,
        dg2,
        ds2,
    )


def solution(mesh):
    rows, shared, pair = P("dp", "blk", None), P(), P("dp", "blk")
    matrix, vector = P(("dp", "blk"), None), P(("dp", "blk"))
    return jax.shard_map(
        body,
        mesh=mesh,
        in_specs=(rows,) + (shared,) * 15 + (pair, pair, rows),
        out_specs=(
            rows,
            rows,
            matrix,
            vector,
            matrix,
            matrix,
            vector,
            matrix,
            vector,
            vector,
            vector,
            matrix,
            vector,
            matrix,
            vector,
            vector,
            vector,
        ),
        check_vma=False,
    )
```

```python
import functools
import math

import jax
import jax.numpy as jnp
from jax import lax
from jax.experimental import pallas as pl
from jax.experimental.pallas import tpu as pltpu
from jax.sharding import PartitionSpec as P

HEAD = 64
PAIR = 2 * HEAD
EPSILON = 1e-12
MASKED = -1e30
FLOOR = -3e38
SCALE = HEAD**-0.5
EXPO = SCALE * math.log2(math.e)
NN = (((1,), (0,)), ((), ()))
NT = (((1,), (1,)), ((), ()))
F32 = jnp.float32
BF16 = jnp.bfloat16
MIB = 1 << 20
FEED_ROWS = 512


def dot(left, right, dims=NN):
    return lax.dot_general(left, right, dims, preferred_element_type=F32)


def whole_spec(shape):
    return pl.BlockSpec(shape, lambda *_: (0,) * len(shape), pipeline_mode=pl.Buffered(1))


def params(limit):
    return pltpu.CompilerParams(vmem_limit_bytes=limit * MIB)


def cost(flops, touched, exps=0):
    return pl.CostEstimate(flops=int(flops), bytes_accessed=int(touched), transcendentals=int(exps))


def project_kernel(has_query, *refs):
    if has_query:
        x_ref, bias_ref, wq_ref, wk_ref, wv_ref, q_ref, k_ref, v_ref = refs
    else:
        x_ref, bias_ref, wk_ref, wv_ref, k_ref, v_ref = refs
    x = x_ref[0]
    if has_query:
        q_ref[0] = (dot(x, wq_ref[...]) + bias_ref[0:1]).astype(BF16)
    k_ref[0] = dot(x, wk_ref[...]).astype(BF16)
    v_ref[0] = (dot(x, wv_ref[...]) + bias_ref[1:2]).astype(BF16)


def project(x, bias, weights):
    seqs, length, features = x.shape
    tile = math.gcd(length, 512)
    grid = (seqs, length // tile)
    row_spec = pl.BlockSpec((1, tile, features), lambda s, i: (s, i, 0))
    return pl.pallas_call(
        functools.partial(project_kernel, len(weights) == 3),
        grid=grid,
        in_specs=[row_spec, whole_spec(bias.shape)] + [whole_spec(w.shape) for w in weights],
        out_specs=[row_spec] * len(weights),
        out_shape=[jax.ShapeDtypeStruct(x.shape, BF16)] * len(weights),
        compiler_params=params(60),
        cost_estimate=cost(
            2 * x.size * features * len(weights), 2 * x.size * (1 + len(weights))
        ),
        name="project",
    )(x, bias, *weights)


def low_lanes():
    return lax.broadcasted_iota(jnp.int32, (1, PAIR), 1) < HEAD


def attend_group(q, qm, sources, o_ref, lse_ref):
    length = q.shape[0]
    tile = math.gcd(length, 256)
    low = low_lanes()
    one = jnp.ones((1, PAIR), BF16)
    todo = [
        (pair, row, head)
        for pair in range(q.shape[1] // PAIR)
        for row in range(0, length, tile)
        for head in range(2)
    ]

    def lanes_of(pair):
        return slice(pair * PAIR, (pair + 1) * PAIR)

    def mine_of(head):
        return ~low if head else low

    def scores_of(pair, row, head):
        mine, lanes = mine_of(head), lanes_of(pair)
        q_side = jnp.where(mine, q[row : row + tile, lanes], qm[row : row + tile])
        return [dot(q_side, jnp.where(mine, k[:, lanes], km), NT) for k, km, _ in sources]

    ahead = scores_of(*todo[0])
    for i, (pair, row, head) in enumerate(todo):
        scores = ahead
        if i + 1 < len(todo):
            ahead = scores_of(*todo[i + 1])
        top = functools.reduce(
            jnp.maximum, [jnp.max(part, axis=-1, keepdims=True) for part in scores]
        )
        weights = [jnp.exp2((part - top) * EXPO).astype(BF16) for part in scores]
        total = sum(
            dot(w, jnp.where(mine_of(head), v[:, lanes_of(pair)], one))
            for w, (_, _, v) in zip(weights, sources)
        )
        if head == 0:
            earlier, earlier_top = total, top
            continue
        totals = pltpu.roll(jnp.where(low, total, earlier), HEAD, 1)
        rows = slice(row, row + tile)
        o_ref[rows, lanes_of(pair)] = (jnp.where(low, earlier, total) / totals).astype(BF16)
        lse = (jnp.where(low, earlier_top, top) * EXPO + jnp.log2(totals)).T
        lse_ref[pair, 0:1, rows] = lse[0:1]
        lse_ref[pair, 1:2, rows] = lse[HEAD : HEAD + 1]


def attend_kernel(q_ref, qm_ref, ko_ref, kmo_ref, vo_ref, kr_ref, kmr_ref, vr_ref, o_ref, lse_ref):
    sources = [(ko_ref[0], kmo_ref[0], vo_ref[0]), (kr_ref[0], kmr_ref[0], vr_ref[0])]
    attend_group(q_ref[0], qm_ref[0], sources, o_ref.at[0], lse_ref.at[0])


def pair_spec(length, lanes):
    return pl.BlockSpec((1, length, lanes), lambda s, h: (s, 0, h))


def mask_spec(length):
    return pl.BlockSpec((1, length, PAIR), lambda s, h: (s, 0, 0))


def lse_spec(length, lanes):
    return pl.BlockSpec((1, lanes // PAIR, 8, length), lambda s, h: (s, h, 0, 0))


def attend(q, qm, own, rem):
    seqs, length, features = q.shape
    lanes = math.gcd(features, 2 * PAIR)
    other = rem[0].shape[1]
    own_spec, rem_spec = pair_spec(length, lanes), pair_spec(other, lanes)
    return pl.pallas_call(
        attend_kernel,
        grid=(seqs, features // lanes),
        in_specs=[own_spec, mask_spec(length)]
        + [own_spec, mask_spec(length), own_spec]
        + [rem_spec, mask_spec(other), rem_spec],
        out_specs=[own_spec, lse_spec(length, lanes)],
        out_shape=[
            jax.ShapeDtypeStruct(q.shape, BF16),
            jax.ShapeDtypeStruct((seqs, features // PAIR, 8, length), F32),
        ],
        compiler_params=params(60),
        cost_estimate=cost(
            16 * q.size * (length + other), 2 * q.size * 6, q.size * (length + other) // HEAD
        ),
        name="attend",
    )(q, qm, *own, *rem)


def attend_back_part(q, qm, g, lse_ref, k, km, v, dk_ref, dv_ref):
    low = low_lanes()
    none = jnp.zeros((1, PAIR), BF16)
    pairs = q.shape[1] // PAIR
    todo = [(pair, head) for pair in range(pairs) for head in range(2)]

    def lanes_of(pair):
        return slice(pair * PAIR, (pair + 1) * PAIR)

    def mine_of(head):
        return ~low if head else low

    def products(pair, head):
        mine, lanes = mine_of(head), lanes_of(pair)
        return (
            dot(jnp.where(mine, k[:, lanes], km), jnp.where(mine, q[:, lanes], qm), NT),
            dot(jnp.where(mine, v[:, lanes], none), g[:, lanes], NT),
        )

    found = []
    ahead = products(*todo[0])
    for i, (pair, head) in enumerate(todo):
        scores, grads = ahead
        if i + 1 < len(todo):
            ahead = products(*todo[i + 1])
        lanes, mine = lanes_of(pair), mine_of(head)
        if head == 0:
            k_t = k[:, lanes].T
            dk = dv = 0.0
            dq = []
        probs = jnp.exp2(scores * EXPO - lse_ref[pair, head : head + 1, :])
        grads = (probs * (grads - lse_ref[pair, 2 + head : 3 + head, :])).astype(BF16)
        dv += dot(probs.astype(BF16), jnp.where(mine, g[:, lanes], none))
        dk += dot(grads, jnp.where(mine, q[:, lanes], none))
        dq.append(dot(k_t[head * HEAD : (head + 1) * HEAD], grads))
        if head == 1:
            dk_ref[:, lanes] = (dk * SCALE).astype(BF16)
            dv_ref[:, lanes] = dv.astype(BF16)
            found.append(jnp.concatenate(dq, axis=0))
    return found


def attend_back_kernel(q_ref, qm_ref, g_ref, lse_ref, ko_ref, kmo_ref, vo_ref, kr_ref, kmr_ref,
                       vr_ref, dq_ref, dko_ref, dvo_ref, dkr_ref, dvr_ref):
    parts = ((ko_ref, kmo_ref, vo_ref, dko_ref, dvo_ref), (kr_ref, kmr_ref, vr_ref, dkr_ref, dvr_ref))
    found = [
        attend_back_part(
            q_ref[0], qm_ref[0], g_ref[0], lse_ref.at[0], k[0], km[0], v[0], dk.at[0], dv.at[0]
        )
        for k, km, v, dk, dv in parts
    ]
    for pair, both in enumerate(zip(*found)):
        dq_ref[0, :, pair * PAIR : (pair + 1) * PAIR] = (sum(both) * SCALE).T.astype(BF16)


def attend_back(q, qm, o, g, lse, own, rem):
    seqs, length, features = q.shape
    delta = (g.astype(F32) * o.astype(F32)).reshape(seqs, length, features // PAIR, 2, HEAD).sum(-1)
    lse = lax.dynamic_update_slice(lse, jnp.transpose(delta, (0, 2, 3, 1)), (0, 0, 2, 0))
    lanes = math.gcd(features, 2 * PAIR)
    other = rem[0].shape[1]
    own_spec, rem_spec = pair_spec(length, lanes), pair_spec(other, lanes)
    return pl.pallas_call(
        attend_back_kernel,
        grid=(seqs, features // lanes),
        in_specs=[own_spec, mask_spec(length), own_spec, lse_spec(length, lanes)]
        + [own_spec, mask_spec(length), own_spec]
        + [rem_spec, mask_spec(other), rem_spec],
        out_specs=[own_spec] * 3 + [rem_spec] * 2,
        out_shape=[jax.ShapeDtypeStruct(q.shape, BF16)] * 3
        + [jax.ShapeDtypeStruct(rem[0].shape, BF16)] * 2,
        compiler_params=params(60),
        cost_estimate=cost(
            40 * q.size * (length + other), 2 * q.size * 14, q.size * (length + other) // HEAD
        ),
        name="attend_back",
    )(q, qm, g, lse, *own, *rem)


def gelu_and_slope(x):
    bell = jnp.exp2(x * x * (-0.5 * math.log2(math.e)))
    below = 1.0 + (0.3275911 / math.sqrt(2.0)) * jnp.abs(x)
    t = pl.reciprocal(below, approx=True)
    t = t * (2.0 - below * t)
    poly = 1.061405429 * t - 1.453152027
    poly = poly * t + 1.421413741
    poly = poly * t - 0.284496736
    poly = poly * t + 0.254829592
    tail = (0.5 * poly) * t * bell
    share = jnp.where(x >= 0.0, 1.0 - tail, tail)
    return x * share, share + x * bell * (1.0 / math.sqrt(2.0 * math.pi))


def mean(values):
    return jnp.sum(values, axis=-1, keepdims=True) * (1.0 / values.shape[-1])


def norm_parts(values):
    centred = values - mean(values)
    scale = lax.rsqrt(mean(centred * centred) + EPSILON)
    return centred * scale, scale


def norm_back(upper, normed, scale):
    return scale * (upper - mean(upper) - normed * mean(upper * normed))


def column_sum(values):
    return jnp.sum(values, axis=0, keepdims=True)


def feed_kernel(layout, tok_ref, att_ref, cot_ref, vec_ref, bu_ref, wo_ref, wu_ref, wd_ref,
                out_ref, bg_ref, ag_ref, vg_ref, dbu_ref, dwu_ref, dwd_ref, dwo_ref,
                act_s, din_s, first_t, feed_t, att_t, bg_s):
    tiles, ff_steps, chunk, wide, narrow = layout
    step = pl.program_id(0)
    tile = tok_ref.shape[0]
    hidden = act_s.shape[1]
    vec = [vec_ref[i : i + 1] for i in range(6)]
    out_bias, gain_one, shift_one, down_bias, gain_two, shift_two = vec

    @pl.when(step == 0)
    def _():
        vg_ref[...] = jnp.zeros_like(vg_ref)
        dbu_ref[...] = jnp.zeros_like(dbu_ref)

    @pl.when(step < tiles)
    def _():
        start = pl.multiple_of(step * tile, tile)
        rows = pl.ds(start, tile)
        att = att_ref[...]
        normed_one, scale_one = norm_parts(
            tok_ref[...].astype(F32) + (dot(att, wo_ref[...]) + out_bias)
        )
        first = normed_one * gain_one + shift_one
        first_low = first.astype(BF16)
        first_t[:, rows] = first_low.T
        att_t[:, rows] = att.T
        feed = jnp.zeros_like(first) + down_bias
        spans = [slice(c, c + chunk) for c in range(0, hidden, chunk)]
        ahead = dot(first_low, wu_ref[:, spans[0]])
        for i, cols in enumerate(spans):
            inner = ahead + bu_ref[:, cols]
            if i + 1 < len(spans):
                ahead = dot(first_low, wu_ref[:, spans[i + 1]])
            active, slope = gelu_and_slope(inner)
            active = active.astype(BF16)
            act_s[rows, cols] = active
            din_s[rows, cols] = slope.astype(BF16)
            feed += dot(active, wd_ref[cols])
        normed_two, scale_two = norm_parts(first + feed)
        out_ref[...] = (normed_two * gain_two + shift_two).astype(BF16)
        cot = cot_ref[...].astype(F32)
        second = norm_back(cot * gain_two, normed_two, scale_two)
        feed_low = second.astype(BF16)
        feed_t[:, rows] = feed_low.T
        back = second
        ahead = dot(feed_low, wd_ref[spans[0]], NT)
        for i, cols in enumerate(spans):
            inner = ahead
            if i + 1 < len(spans):
                ahead = dot(feed_low, wd_ref[spans[i + 1]], NT)
            inner = (inner * din_s[rows, cols].astype(F32)).astype(BF16)
            din_s[rows, cols] = inner
            dbu_ref[:, cols] += column_sum(inner.astype(F32))
            back += dot(inner, wu_ref[:, cols], NT)
        residual = norm_back(back * gain_one, normed_one, scale_one)
        branch_low = residual.astype(BF16)
        bg_ref[...] = branch_low
        bg_s[rows] = branch_low
        ag_ref[...] = dot(branch_low, wo_ref[...], NT).astype(BF16)
        for i, values in enumerate(
            (
                branch_low.astype(F32),
                back * normed_one,
                back,
                feed_low.astype(F32),
                cot * normed_two,
                cot,
            )
        ):
            vg_ref[i : i + 1] += column_sum(values)

    @pl.when((step >= tiles) & (step < tiles + ff_steps))
    def _():
        cols = pl.ds(pl.multiple_of((step - tiles) * wide, wide), wide)
        dwu = dot(first_t[...], din_s[:, cols]).astype(BF16)
        dwu_ref[...] = dwu.reshape(dwu_ref.shape)
        dwd_ref[...] = dot(feed_t[...], act_s[:, cols]).astype(BF16).T

    @pl.when(step >= tiles + ff_steps)
    def _():
        cols = pl.ds(pl.multiple_of((step - tiles - ff_steps) * narrow, narrow), narrow)
        dwo_ref[...] = dot(att_t[...], bg_s[:, cols]).astype(BF16)


def feed_both_ways(tokens, attended, cotangent, vectors, up_bias, wo, wu, wd, groups):
    rows, features = tokens.shape
    hidden = wu.shape[1]
    tile = math.gcd(rows, 256)
    tiles = rows // tile
    wide, narrow = features, math.gcd(features, 384)
    ff_steps, out_steps = hidden // wide, features // narrow
    layout = (tiles, ff_steps, math.gcd(hidden, 512), wide, narrow)
    blocked = (groups, ff_steps, features // groups, wide)
    row_spec = pl.BlockSpec((tile, features), lambda i: (jnp.minimum(i, tiles - 1), 0))

    def ff_at(i):
        return jnp.clip(i - tiles, 0, ff_steps - 1)

    return pl.pallas_call(
        functools.partial(feed_kernel, layout),
        grid=(tiles + ff_steps + out_steps,),
        in_specs=[row_spec] * 3
        + [whole_spec(a.shape) for a in (vectors, up_bias, wo, wu, wd)],
        out_specs=[row_spec] * 3
        + [
            pl.BlockSpec((8, features), lambda i: (0, 0)),
            pl.BlockSpec((1, hidden), lambda i: (0, 0)),
            pl.BlockSpec((groups, 1) + blocked[2:], lambda i: (0, ff_at(i), 0, 0)),
            pl.BlockSpec((wide, features), lambda i: (ff_at(i), 0)),
            pl.BlockSpec(
                (features, narrow),
                lambda i: (0, jnp.clip(i - tiles - ff_steps, 0, out_steps - 1)),
            ),
        ],
        out_shape=[jax.ShapeDtypeStruct(tokens.shape, BF16)] * 3
        + [
            jax.ShapeDtypeStruct((8, features), F32),
            jax.ShapeDtypeStruct((1, hidden), F32),
            jax.ShapeDtypeStruct(blocked, BF16),
            jax.ShapeDtypeStruct(wd.shape, BF16),
            jax.ShapeDtypeStruct(wo.shape, BF16),
        ],
        scratch_shapes=[
            pltpu.VMEM((rows, hidden), BF16),
            pltpu.VMEM((rows, hidden), BF16),
            pltpu.VMEM((features, rows), BF16),
            pltpu.VMEM((features, rows), BF16),
            pltpu.VMEM((features, rows), BF16),
            pltpu.VMEM((rows, features), BF16),
        ],
        compiler_params=params(60),
        cost_estimate=cost(
            6 * rows * features * (features + 2 * hidden),
            2 * (6 * rows * features + 4 * features * hidden + 2 * features * features),
            2 * rows * hidden,
        ),
        name="feed_both_ways",
    )(tokens, attended, cotangent, vectors, up_bias, wo, wu, wd)


def spread(row):
    return jnp.broadcast_to(row, (PAIR, row.shape[1])).T


def as_row(ref):
    return ref[...].astype(F32).reshape(1, ref.shape[0])


def front_kernel(tokens_ref, group_ref, valid_ref, cot_ref, bq_ref, bv_ref, bo_ref, g1_ref, s1_ref, bd_ref,
                 g2_ref, s2_ref, bu_in, wq_any, wk_any, wv_any, wo_any, wu_any, wd_any,
                 out_ref, bg_ref, ag_ref, att_ref, lse_ref, qm_ref, km_ref,
                 first_t, feed_t, vg_ref, dbu_ref, q_any, k_any, v_any, rem_any, act_any, din_any,
                 wq, wk, wv, wo, wu, wd, tok_s, q_s, k_s, v_s, kr_s, vr_s, rem_s, own_codes, code_s, act_s, din_s,
                 bu_ref, weight_sem, out_sem, send_sem, recv_sem):
    s = pl.program_id(0)
    seqs = tok_s.shape[0]
    length, features = tok_s.shape[1:]
    hidden = act_s.shape[1]
    side = lax.axis_index("blk")
    other = {"blk": 1 - side}
    query_bias, value_bias, out_bias, gain_one, shift_one, down_bias, gain_two, shift_two = [
        as_row(ref) for ref in (bq_ref, bv_ref, bo_ref, g1_ref, s1_ref, bd_ref, g2_ref, s2_ref)
    ]
    pairs_of = [(wq_any, wq), (wk_any, wk), (wv_any, wv), (wo_any, wo), (wu_any, wu), (wd_any, wd)]

    def weight(i):
        return pltpu.make_async_copy(*pairs_of[i], weight_sem.at[i])

    def remote(source, target, at):
        return pltpu.make_async_remote_copy(
            src_ref=source,
            dst_ref=target,
            send_sem=send_sem.at[at],
            recv_sem=recv_sem.at[at],
            device_id=other,
            device_id_type=pl.DeviceIdType.MESH,
        )

    def exchange(at):
        return remote(tokens_ref.at[at], rem_s.at[at], at)

    def code_exchange():
        return remote(own_codes, code_s, seqs)

    def whole_out(i):
        source, target = ((q_s, q_any), (k_s, k_any.at[0]), (v_s, v_any.at[0]))[i]
        return pltpu.make_async_copy(source, target, out_sem.at[i])

    def part_out(i, at):
        source, target = (
            (kr_s, k_any.at[1, at]),
            (vr_s, v_any.at[1, at]),
            (rem_s.at[at], rem_any.at[at]),
            (act_s, act_any.at[at]),
            (din_s, din_any.at[at]),
        )[i]
        return pltpu.make_async_copy(source, target, out_sem.at[3 + i])

    @pl.when(s == 0)
    def _():
        barrier = pltpu.get_barrier_semaphore()
        pl.semaphore_signal(barrier, inc=1, device_id=other, device_id_type=pl.DeviceIdType.MESH)
        load = pltpu.make_async_copy(tokens_ref, tok_s, weight_sem.at[len(pairs_of)])
        load.start()
        for i in range(3):
            weight(i).start()
        codes = jnp.where(valid_ref[...] == 1, group_ref[...], -1).astype(F32)
        own_codes[...] = jnp.zeros_like(own_codes)
        own_codes[0:seqs] = codes
        pl.semaphore_wait(barrier, 1)
        exchange(0).start()
        code_exchange().start()
        for i in range(3, len(pairs_of)):
            weight(i).start()
        vg_ref[...] = jnp.zeros_like(vg_ref)
        dbu_ref[...] = jnp.zeros_like(dbu_ref)
        bu_ref[...] = as_row(bu_in)
        load.wait()
        for i in range(3):
            weight(i).wait()

        def project_own(at, carry):
            x = tok_s[at]
            q_s[at] = (dot(x, wq[...]) + query_bias).astype(BF16)
            k_s[at] = dot(x, wk[...]).astype(BF16)
            v_s[at] = (dot(x, wv[...]) + value_bias).astype(BF16)
            return carry

        lax.fori_loop(0, seqs, project_own, 0)
        for i in range(3):
            whole_out(i).start()
        for i in range(3, len(pairs_of)):
            weight(i).wait()
        code_exchange().wait_recv()
        exchange(0).wait_send()
        if seqs > 1:
            exchange(1).start()

    for at in range(seqs):

        @pl.when(s == at)
        def _(at=at):
            exchange(at).wait_recv()
            if at:
                for i in range(3):
                    part_out(i, at - 1).wait()

    x = rem_s[s]
    kr_s[...] = dot(x, wk[...]).astype(BF16)
    vr_s[...] = (dot(x, wv[...]) + value_bias).astype(BF16)
    slot = lax.broadcasted_iota(jnp.int32, (1, PAIR), 1) % HEAD
    slot = slot.astype(F32)
    groups_row = group_ref[pl.ds(s, 1)].astype(F32)
    qm_ref[0] = jnp.where(spread(groups_row) == slot, 1.0, 0.0).astype(BF16)
    km_ref[0, 0] = jnp.where(spread(own_codes[pl.ds(s, 1)]) == slot, 0.0, MASKED).astype(BF16)
    km_ref[1, 0] = jnp.where(spread(code_s[pl.ds(s, 1)]) == slot, 0.0, MASKED).astype(BF16)
    for at in range(seqs):

        @pl.when(s == at)
        def _(at=at):
            for i in range(3):
                part_out(i, at).start()

    groups = features // (2 * PAIR)

    def heads(group, carry):
        lanes = pl.ds(pl.multiple_of(group * 2 * PAIR, 2 * PAIR), 2 * PAIR)
        attend_group(
            q_s[s, :, lanes],
            qm_ref[0],
            [(k_s[s, :, lanes], km_ref[0, 0], v_s[s, :, lanes]), (kr_s[:, lanes], km_ref[1, 0], vr_s[:, lanes])],
            att_ref.at[0, :, lanes],
            lse_ref.at[0, pl.ds(group * 2, 2)],
        )
        return carry

    lax.fori_loop(0, groups, heads, 0)

    for at in range(1, seqs):

        @pl.when(s == at)
        def _(at=at):
            for i in range(3, 5):
                part_out(i, at - 1).wait()

    tile = math.gcd(length, FEED_ROWS)
    chunk = math.gcd(hidden, 256)
    spans = [slice(c, c + chunk) for c in range(0, hidden, chunk)]

    def feed_rows(t, carry):
        rows = pl.ds(pl.multiple_of(t * tile, tile), tile)
        att = att_ref[0, rows]
        normed_one, scale_one = norm_parts(
            tok_s[s, rows].astype(F32) + (dot(att, wo[...]) + out_bias)
        )
        first = normed_one * gain_one + shift_one
        first_low = first.astype(BF16)
        first_t[:, rows] = first_low.T
        feed = jnp.zeros_like(first) + down_bias
        ahead = dot(first_low, wu[:, spans[0]])
        for i, cols in enumerate(spans):
            inner = ahead + bu_ref[:, cols]
            if i + 1 < len(spans):
                ahead = dot(first_low, wu[:, spans[i + 1]])
            active, slope = gelu_and_slope(inner)
            active = active.astype(BF16)
            act_s[rows, cols] = active
            din_s[rows, cols] = slope.astype(BF16)
            feed += dot(active, wd[cols])
        normed_two, scale_two = norm_parts(first + feed)
        out_ref[0, rows] = (normed_two * gain_two + shift_two).astype(BF16)
        cot = cot_ref[0, rows].astype(F32)
        second = norm_back(cot * gain_two, normed_two, scale_two)
        feed_low = second.astype(BF16)
        feed_t[:, rows] = feed_low.T
        back = second
        ahead = dot(feed_low, wd[spans[0]], NT)
        for i, cols in enumerate(spans):
            inner = ahead
            if i + 1 < len(spans):
                ahead = dot(feed_low, wd[spans[i + 1]], NT)
            inner = (inner * din_s[rows, cols].astype(F32)).astype(BF16)
            din_s[rows, cols] = inner
            dbu_ref[:, cols] += column_sum(inner.astype(F32))
            back += dot(inner, wu[:, cols], NT)
        residual = norm_back(back * gain_one, normed_one, scale_one)
        branch_low = residual.astype(BF16)
        bg_ref[0, rows] = branch_low
        att_grad = dot(branch_low, wo[...], NT).astype(BF16)
        ag_ref[0, rows] = att_grad
        product = att_grad.astype(F32) * att.astype(F32)
        coarse = product.astype(BF16)
        fine = (product - coarse.astype(F32)).astype(BF16)
        heads_count = features // HEAD
        of_head = lax.broadcasted_iota(jnp.int32, (heads_count, features), 1) // HEAD
        selector = (of_head == lax.broadcasted_iota(jnp.int32, of_head.shape, 0)).astype(F32)
        selector = selector.astype(BF16)
        delta = dot(selector, coarse, NT) + dot(selector, fine, NT)
        for pair in range(features // PAIR):
            lse_ref[0, pair, 2:4, rows] = delta[2 * pair : 2 * pair + 2]
        for i, values in enumerate(
            (
                branch_low.astype(F32),
                back * normed_one,
                back,
                feed_low.astype(F32),
                cot * normed_two,
                cot,
            )
        ):
            vg_ref[i : i + 1] += column_sum(values)
        return carry

    lax.fori_loop(0, length // tile, feed_rows, 0)

    for at in range(seqs):

        @pl.when(s == at)
        def _(at=at):
            for i in range(3, 5):
                part_out(i, at).start()
            if at < seqs - 1:
                exchange(at + 1).wait_send()
            if at + 2 < seqs:
                exchange(at + 2).start()
            if at == seqs - 1:
                for i in range(3):
                    whole_out(i).wait()
                for i in range(5):
                    part_out(i, at).wait()
                code_exchange().wait_send()


def front(tokens, group_ids, valid, cotangent, vectors, up_bias, weights):
    seqs, length, features = tokens.shape
    hidden = up_bias.shape[0]
    pairs = features // PAIR
    anywhere = pl.BlockSpec(memory_space=pl.ANY)

    def at_seq(*shape):
        return pl.BlockSpec((1,) + shape, lambda s: (s,) + (0,) * len(shape))

    def of_seqs(*shape, dtype=BF16):
        return jax.ShapeDtypeStruct((seqs,) + shape, dtype)

    def fixed(*shape):
        return pl.BlockSpec(shape, lambda s: (0,) * len(shape))

    rows, mask, lses, wide = (length, features), (length, PAIR), (pairs, 8, length), (length, hidden)
    turned = pl.BlockSpec((features, length), lambda s: (0, s))
    return pl.pallas_call(
        front_kernel,
        grid=(seqs,),
        in_specs=[anywhere, whole_spec(group_ids.shape), whole_spec(valid.shape), at_seq(*rows)]
        + [whole_spec(v.shape) for v in vectors + (up_bias,)]
        + [anywhere] * 6,
        out_specs=[at_seq(*rows)] * 4
        + [at_seq(*lses), at_seq(*mask)]
        + [pl.BlockSpec((2, 1) + mask, lambda s: (0, s, 0, 0))]
        + [turned] * 2
        + [fixed(8, features), fixed(1, hidden)]
        + [anywhere] * 6,
        out_shape=[of_seqs(*rows)] * 4
        + [of_seqs(*lses, dtype=F32), of_seqs(*mask)]
        + [jax.ShapeDtypeStruct((2, seqs) + mask, BF16)]
        + [jax.ShapeDtypeStruct((features, seqs * length), BF16)] * 2
        + [jax.ShapeDtypeStruct((8, features), F32), jax.ShapeDtypeStruct((1, hidden), F32)]
        + [of_seqs(*rows)]
        + [jax.ShapeDtypeStruct((2, seqs) + rows, BF16)] * 2
        + [of_seqs(*rows)]
        + [of_seqs(*wide)] * 2,
        scratch_shapes=[pltpu.VMEM(w.shape, BF16) for w in weights]
        + [pltpu.VMEM(tokens.shape, BF16)] * 4
        + [pltpu.VMEM(rows, BF16)] * 2
        + [pltpu.VMEM(tokens.shape, BF16)]
        + [pltpu.VMEM((seqs + -seqs % 8, length), F32)] * 2
        + [pltpu.VMEM(wide, BF16)] * 2
        + [pltpu.VMEM((1, hidden), F32)]
        + [pltpu.SemaphoreType.DMA((7,)), pltpu.SemaphoreType.DMA((8,))]
        + [pltpu.SemaphoreType.DMA((seqs + 1,))] * 2,
        compiler_params=pltpu.CompilerParams(
            collective_id=2, has_side_effects=True, vmem_limit_bytes=63 * MIB
        ),
        cost_estimate=cost(
            2 * tokens.size * (9 * features + 4 * hidden + 8 * length), 2 * 20 * tokens.size, tokens.size * 24
        ),
        name="front",
    )(tokens, group_ids, valid, cotangent, *vectors, up_bias, *weights)


def feed_weights_kernel(blocks, first_ref, din_ref, feed_ref, act_ref, att_any, bg_any,
                        dwu_ref, dwd_ref, dwo_ref, up_s, up_in, down_s, down_in, out_s, out_in,
                        att_s, bg_s, near_sem, send_sem, recv_sem):
    step = pl.program_id(0)
    features = first_ref.shape[0]
    me = lax.axis_index("dp")
    core = me % 2
    other = {"dp": me + 1 - 2 * core}

    def loads():
        return [
            pltpu.make_async_copy(att_any, att_s, near_sem.at[0]),
            pltpu.make_async_copy(bg_any, bg_s, near_sem.at[1]),
        ]

    def swaps(block):
        if block == blocks:
            pairs = [(out_s.at[:, 1 - core], out_in)]
        else:
            pairs = [
                (up_s.at[block % 2, :, 1 - core], up_in.at[block]),
                (down_s.at[block % 2, :, 1 - core], down_in.at[block]),
            ]
        return [
            pltpu.make_async_remote_copy(
                src_ref=source,
                dst_ref=target,
                send_sem=send_sem.at[2 * block + i],
                recv_sem=recv_sem.at[2 * block + i],
                device_id=other,
                device_id_type=pl.DeviceIdType.MESH,
            )
            for i, (source, target) in enumerate(pairs)
        ]

    @pl.when(step == 0)
    def _():
        for load in loads():
            load.start()
        barrier = pltpu.get_barrier_semaphore()
        pl.semaphore_signal(barrier, inc=1, device_id=other, device_id_type=pl.DeviceIdType.MESH)
        pl.semaphore_wait(barrier, 1)

    @pl.when(step < blocks)
    def _():
        slot = step % 2
        up_s[slot] = dot(first_ref[...], din_ref[...]).astype(BF16).reshape(up_s.shape[1:])
        down_s[slot] = dot(feed_ref[...], act_ref[...]).astype(BF16).T.reshape(down_s.shape[1:])

    for block in range(blocks):

        @pl.when(step == block)
        def _(block=block):
            for swap in swaps(block):
                swap.start()

    @pl.when(step == blocks)
    def _():
        for load in loads():
            load.wait()
        out_s[...] = dot(att_s[...].T, bg_s[...]).astype(BF16).reshape(out_s.shape)
        for swap in swaps(blocks):
            swap.start()

    for block in range(blocks):

        @pl.when(step == block + 1)
        def _(block=block):
            for swap in swaps(block):
                swap.wait()
            dwu_ref[:, 0] = (up_s[block % 2, :, core].astype(F32) + up_in[block].astype(F32)).astype(BF16)
            dwd_ref[...] = (down_s[block % 2, :, core].astype(F32) + down_in[block].astype(F32)).astype(BF16)

    @pl.when(step == blocks + 1)
    def _():
        for swap in swaps(blocks):
            swap.wait()
        dwo_ref[...] = (out_s[:, core].astype(F32) + out_in[...].astype(F32)).astype(BF16)


def feed_weights(first_t, din, feed_t, act, att, bg):
    dp = lax.axis_size("dp")
    features, rows = first_t.shape
    hidden = act.shape[1]
    blocks, half, low, deep = hidden // features, dp // 2, features // dp, hidden // dp
    each = half // blocks
    wide_spec = pl.BlockSpec((rows, features), lambda i: (0, jnp.minimum(i, blocks - 1)))
    anywhere = pl.BlockSpec(memory_space=pl.ANY)

    def behind(i):
        return jnp.clip(i - 1, 0, blocks - 1)

    return pl.pallas_call(
        functools.partial(feed_weights_kernel, blocks),
        grid=(blocks + 2,),
        in_specs=[
            whole_spec(first_t.shape),
            wide_spec,
            whole_spec(feed_t.shape),
            wide_spec,
            anywhere,
            anywhere,
        ],
        out_specs=[
            pl.BlockSpec((half, 1, low, features), lambda i: (0, behind(i), 0, 0)),
            pl.BlockSpec((each, deep, features), lambda i: (behind(i), 0, 0)),
            pl.BlockSpec((half, low, features), lambda i: (0, 0, 0)),
        ],
        out_shape=[
            jax.ShapeDtypeStruct((half, blocks, low, features), BF16),
            jax.ShapeDtypeStruct((half, deep, features), BF16),
            jax.ShapeDtypeStruct((half, low, features), BF16),
        ],
        scratch_shapes=[
            pltpu.VMEM((2, half, 2, low, features), BF16),
            pltpu.VMEM((blocks, half, low, features), BF16),
            pltpu.VMEM((2, each, 2, deep, features), BF16),
            pltpu.VMEM((blocks, each, deep, features), BF16),
            pltpu.VMEM((half, 2, low, features), BF16),
            pltpu.VMEM((half, low, features), BF16),
            pltpu.VMEM(att.shape, BF16),
            pltpu.VMEM(bg.shape, BF16),
            pltpu.SemaphoreType.DMA((2,)),
            pltpu.SemaphoreType.DMA((2 * blocks + 2,)),
            pltpu.SemaphoreType.DMA((2 * blocks + 2,)),
        ],
        compiler_params=pltpu.CompilerParams(
            collective_id=3, has_side_effects=True, vmem_limit_bytes=63 * MIB
        ),
        cost_estimate=cost(
            2 * rows * features * (2 * hidden + features), 4 * rows * (hidden + 2 * features)
        ),
        name="feed_weights",
    )(first_t, din, feed_t, act, att, bg)


def own_back_kernel(bg_ref, dq_ref, dk_ref, dv_ref, wq_ref, wk_ref, wv_ref, out_ref):
    total = bg_ref[0].astype(F32) + dot(dq_ref[0], wq_ref[...], NT)
    total += dot(dk_ref[0], wk_ref[...], NT)
    total += dot(dv_ref[0], wv_ref[...], NT)
    out_ref[0] = total.astype(BF16)


def rem_back_kernel(dk_ref, dv_ref, wk_ref, wv_ref, out_ref):
    total = dot(dk_ref[0], wk_ref[...], NT) + dot(dv_ref[0], wv_ref[...], NT)
    out_ref[0] = total.astype(BF16)


def tokens_back(kernel, rows, weights):
    seqs, length, features = rows[0].shape
    tile = math.gcd(length, 512)
    row_spec = pl.BlockSpec((1, tile, features), lambda s, i: (s, i, 0))
    size = rows[0].size
    return pl.pallas_call(
        kernel,
        grid=(seqs, length // tile),
        in_specs=[row_spec] * len(rows) + [whole_spec(w.shape) for w in weights],
        out_specs=row_spec,
        out_shape=jax.ShapeDtypeStruct(rows[0].shape, BF16),
        compiler_params=params(60),
        cost_estimate=cost(2 * size * features * len(weights), 2 * size * (1 + len(rows))),
        name="tokens_back",
    )(*rows, *weights)


def weights_back_kernel(tok_ref, rem_ref, dq_ref, dko_ref, dvo_ref, dkr_ref, dvr_ref,
                        wq_ref, wk_ref, wv_ref, bq_ref, bv_ref, tok_t, rem_t):
    @pl.when(pl.program_id(0) == 0)
    def _():
        tok_t[...] = tok_ref[...].T
        rem_t[...] = rem_ref[...].T

    wq_ref[...] = dot(tok_t[...], dq_ref[...]).astype(BF16)
    wk_ref[...] = (dot(tok_t[...], dko_ref[...]) + dot(rem_t[...], dkr_ref[...])).astype(BF16)
    wv_ref[...] = (dot(tok_t[...], dvo_ref[...]) + dot(rem_t[...], dvr_ref[...])).astype(BF16)
    bq_ref[...] = column_sum(dq_ref[...].astype(F32))
    bv_ref[...] = column_sum(dvo_ref[...].astype(F32)) + column_sum(dvr_ref[...].astype(F32))


def weights_back(tok, rem, dq, dko, dvo, dkr, dvr):
    rows, features = tok.shape
    others = rem.shape[0]
    wide = math.gcd(features, 256)
    own_spec = pl.BlockSpec((rows, wide), lambda j: (0, j))
    rem_spec = pl.BlockSpec((others, wide), lambda j: (0, j))
    bias_spec = pl.BlockSpec((1, wide), lambda j: (0, j))
    return pl.pallas_call(
        weights_back_kernel,
        grid=(features // wide,),
        in_specs=[
            whole_spec(tok.shape),
            whole_spec(rem.shape),
            own_spec,
            own_spec,
            own_spec,
            rem_spec,
            rem_spec,
        ],
        out_specs=[pl.BlockSpec((features, wide), lambda j: (0, j))] * 3 + [bias_spec] * 2,
        out_shape=[jax.ShapeDtypeStruct((features, features), BF16)] * 3
        + [jax.ShapeDtypeStruct((1, features), F32)] * 2,
        scratch_shapes=[
            pltpu.VMEM((features, rows), BF16),
            pltpu.VMEM((features, others), BF16),
        ],
        compiler_params=params(60),
        cost_estimate=cost(
            2 * features * features * (3 * rows + 2 * others),
            2 * (4 * tok.size + 3 * rem.size + 3 * features * features),
        ),
        name="weights_back",
    )(tok, rem, dq, dko, dvo, dkr, dvr)


def halve(value, axis, bit):
    size = lax.axis_size(axis)
    mine = (lax.axis_index(axis) >> bit) & 1
    pairs = value.reshape((value.shape[0] // 2, 2) + value.shape[1:])
    keep = lax.dynamic_index_in_dim(pairs, mine, 1, keepdims=False)
    send = lax.dynamic_index_in_dim(pairs, 1 - mine, 1, keepdims=False)
    came = lax.ppermute(send, axis, [(i, i ^ (1 << bit)) for i in range(size)])
    return keep.astype(F32) + came.astype(F32)


def scatter_sum(value, low=True):
    dp, blk = lax.axis_size("dp"), lax.axis_size("blk")
    if dp & (dp - 1) or blk & (blk - 1):
        return lax.psum_scatter(
            value.astype(F32), ("dp", "blk"), scatter_dimension=0, tiled=True
        )
    kept = value.dtype
    each = value.shape[0] // (dp * blk)
    value = value.reshape((dp, blk * each) + value.shape[1:])
    for bit in range(dp.bit_length() - 1):
        value = halve(value, "dp", bit).astype(kept)
    value = value.reshape((blk, each) + value.shape[2:])
    for bit in range(blk.bit_length() - 1):
        value = halve(value, "blk", bit)
        value = value if (2 << bit) == blk else value.astype(kept)
    return value.reshape(value.shape[1:]).astype(F32)


class Unit:
    def __init__(self, parts, rows, columns, halves, outs):
        self.parts, self.rows, self.columns = parts, rows, columns
        self.halves, self.outs = halves, outs
        self.first = 1 if parts else 0
        self.half = rows // (2 * halves)
        self.last_type = BF16 if (rows // 2) % 16 == 0 else F32


def timetable(units, bits, seqs, groups, slot_us, token_us):
    free, pending, table = {}, [], []
    slots = seqs * groups * 2

    def launch(key, now):
        kind, which, step = key
        if kind == "tokens":
            link, us = "blk", token_us
        elif kind == "vectors":
            link, us = None, 1.0
        else:
            us = units[which].rows * units[which].columns * 2e-5
            us *= 1 << max(bits - 1 - step, 0)
            us *= {0: 0.3, bits - 1: 3.0}.get(step, 1.1)
            link = {0: "core", bits - 1: "far", bits: "blk"}.get(step, "near")
        start = max(now, free.get(link, 0.0))
        if link:
            free[link] = start + us
        if kind != "tokens":
            pending.append((start + us + 2.0, key))

    for u, unit in enumerate(units):
        if unit.parts:
            launch(("unit", u, 1), slot_us)
    first_group = sum(1 for unit in units if unit.parts)
    now = 0.0
    while len(table) < slots or pending:
        slot = len(table)
        if slot < slots:
            now = (slot + 1) * slot_us
            part, major, minor = slot // (seqs * groups), slot // groups % seqs, slot % groups
            if part == 0 and minor == groups - 1:
                launch(("tokens", major, 0), now)
            major, minor = divmod(slot - seqs * groups, seqs)
            if part == 1 and minor == seqs - 1:
                launch(("unit", first_group + major, 0), now)
            if slot == slots - 1:
                launch(("vectors", 0, 0), now)
            due = sorted(p for p in pending if p[0] <= now)
        else:
            due = [min(pending)]
            now = max(now + 0.3, due[0][0])
        table.append([key for _, key in due])
        for found in due:
            pending.remove(found)
            kind, which, step = found[1]
            if step < bits:
                launch((kind, which, step + 1), now)
    tail = [key for keys in table[slots:] for key in keys]
    return table[:slots], tail + [("tokens", s, 0) for s in range(seqs)]


def order_of(step, seqs, groups):
    part = step // (seqs * groups)
    left = step - part * (seqs * groups)
    s = left // groups * (1 - part) + left % seqs * part
    h = left % groups * (1 - part) + left // seqs * part
    return part, s, h


def back_kernel(units, bits, groups, table, tail, n_out, *refs):
    (q_ref, qm_ref, g_ref, lse_ref, k_ref, km_ref, v_ref,
     tok_ref, rem_ref, wq_ref, wk_ref, wv_ref, vg_ref, vu_ref) = refs[:14]
    sources, refs = refs[14:17], list(refs[17:])
    tokens_any, rem_in, *outs = refs[:n_out]
    refs = refs[n_out:]
    kept = [refs.pop(0) for _ in units]
    landed = [
        [refs.pop(0) if k >= unit.first else None for k in range(bits)] for unit in units
    ]
    wide = [refs.pop(0) for _ in units]
    parting = [refs.pop(0) for _ in units]
    last = [refs.pop(0) for _ in units]
    (group_src, turned, dq_part, dq_s, dk_s, dv_s,
     rem_out, vec, vec_in, bias_sum, send_sem, recv_sem, local_sem, out_sem) = refs
    step = pl.program_id(0)
    steps = pl.num_programs(0)
    seqs = rem_out.shape[0]
    part, s, h = order_of(step, seqs, groups)
    features = tok_ref.shape[2]
    me, side = lax.axis_index("dp"), lax.axis_index("blk")
    core = me % 2

    def swapped(k):
        return {1: 2, 2: 1}.get(k, k) if bits > 2 else k

    def pick(values, k):
        return values[k] + (values[swapped(k)] - values[k]) * core

    bit_own = [(me // (1 << bit)) % 2 for bit in range(bits)]
    across = [me + (1 << bit) * (1 - 2 * bit_own[bit]) for bit in range(bits)]
    own = [pick(bit_own, k) for k in range(bits)]
    partner = [{"dp": pick(across, k)} for k in range(bits)] + [{"blk": 1 - side}]
    first_group = sum(1 for unit in units if unit.parts)
    lead = (slice(None),) * (bits - 1)

    def natural(digits):
        by_step = [None] + list(digits[::-1])
        return tuple(pick(by_step, bit) for bit in range(bits - 1, 0, -1))

    def digits_of(n, count):
        return [(n // (1 << (count - 1 - i))) % 2 for i in range(count)]

    sems = {}
    for u, unit in enumerate(units):
        for k in range(unit.first, bits + 1):
            sems["unit", u, k, 0] = len(sems)
    for k in range(bits + 1):
        sems["vectors", 0, k, 0] = len(sems)
    for k in range(seqs):
        sems["tokens", k, 0, 0] = len(sems)

    def remote(source, target, device, key):
        return pltpu.make_async_remote_copy(
            src_ref=source,
            dst_ref=target,
            send_sem=send_sem.at[sems[key]],
            recv_sem=recv_sem.at[sems[key]],
            device_id=device,
            device_id_type=pl.DeviceIdType.MESH,
        )

    near_sems = {}
    for u, unit in enumerate(units):
        for p in range(len(unit.parts or ())):
            for n in range(1 << (bits - 1)):
                near_sems[u, p, n] = len(near_sems)

    def spot(k, value):
        return tuple(
            own[at] if at < k else value if at == k else slice(None) for at in range(bits - 1, 0, -1)
        )

    def copies(kind, which, k):
        if kind == "tokens":
            return [remote(rem_out.at[which], rem_in.at[which], partner[bits], (kind, which, 0, 0))]
        if kind == "vectors":
            return [remote(vec.at[k], vec_in.at[k], partner[k], (kind, 0, k, 0))]
        u, unit = which, units[which]
        if k == bits:
            return [remote(parting[u], last[u], partner[bits], (kind, u, k, 0))]
        if k:
            source = kept[u].at[spot(k, 1 - own[k])]
            return [remote(source, landed[u][k], partner[k], (kind, u, k, 0))]
        source = group_src.at[(u - first_group,) + lead + (1 - core,)]
        return [remote(source, landed[u][0], partner[0], (kind, u, 0, 0))]

    def near_copies(u):
        found, row = [], 0
        for p, (source, first, rows) in enumerate(units[u].parts):
            for n in range(1 << (bits - 1)):
                digits = digits_of(n, bits - 1)
                found.append(
                    pltpu.make_async_copy(
                        sources[source].at[natural(digits) + (pl.ds(first, rows),)],
                        kept[u].at[tuple(digits) + (pl.ds(row, rows),)],
                        local_sem.at[near_sems[u, p, n]],
                    )
                )
            row += rows
        return found

    def launch(*key):
        for copy in copies(*key):
            copy.start()

    def halves_of(u, which):
        unit = units[u]
        return [
            wide[u][pl.ds(pl.multiple_of(i * 2 * unit.half + which * unit.half, 8), unit.half)]
            for i in range(unit.halves)
        ]

    def receive(kind, which, k):
        for copy in copies(kind, which, k):
            copy.wait_recv()
        if kind == "tokens":
            return
        if kind == "vectors":
            vec[k + 1] = vec[k] + vec_in[k]
            if k < bits:
                launch(kind, 0, k + 1)
            return
        u, unit = which, units[which]
        if k == bits:
            for i, (mine, (out, rows, columns)) in enumerate(zip(halves_of(u, side), unit.outs)):
                came = last[u][...].astype(F32)[i * unit.half : (i + 1) * unit.half]
                outs[out][rows, columns] = mine + came
            return
        place = spot(k, own[k]) if k else lead
        open_at = [i for i, at in enumerate(place) if isinstance(at, slice)]

        def add(n, carry):
            at, where = list(place), digits_of(n, len(open_at))
            for i, digit in zip(open_at, where):
                at[i] = digit
            at = tuple(at)
            if k:
                mine, came = kept[u][at], landed[u][k][tuple(where)]
            else:
                mine = group_src[(u - first_group,) + natural(at) + (core,)]
                came = landed[u][0][natural(at)]
            total = mine.astype(F32) + came.astype(F32)
            if k == bits - 1:
                wide[u][...] = total
            else:
                kept[u][at] = total.astype(BF16)
            return carry

        if open_at:
            lax.fori_loop(0, 1 << len(open_at), add, 0)
        else:
            add(0, 0)
        if k == bits - 1:
            pieces = halves_of(u, 1 - side)
            pieces = pieces[0] if len(pieces) == 1 else jnp.concatenate(pieces, axis=0)
            parting[u][...] = pieces.astype(unit.last_type)
        launch(kind, u, k + 1)

    @pl.when(step == 0)
    def _():
        barrier = pltpu.get_barrier_semaphore()
        for other in partner:
            pl.semaphore_signal(barrier, inc=1, device_id=other, device_id_type=pl.DeviceIdType.MESH)
        pl.semaphore_wait(barrier, bits + 1)
        for u, unit in enumerate(units):
            if unit.parts:
                for copy in near_copies(u):
                    copy.start()

    length = q_ref.shape[1]
    rows = pl.ds(pl.multiple_of(s * length, length), length)

    @pl.when((part == 0) & (h == 0))
    def _():
        turned[0, :, rows] = rem_ref[0].T

    @pl.when((part == 1) & (h == 0))
    def _():
        turned[1, :, rows] = tok_ref[0].T

    width = q_ref.shape[2]
    columns = pl.ds(pl.multiple_of(h * width, width), width)

    found = attend_back_part(
        q_ref[0], qm_ref[0], g_ref[0], lse_ref.at[0], k_ref[0, 0], km_ref[0, 0], v_ref[0, 0],
        dk_s.at[part, rows, columns], dv_s.at[part, rows, columns],
    )

    @pl.when(part == 0)
    def _():
        for pair, value in enumerate(found):
            dq_part[s, h, pair] = value.astype(dq_part.dtype)

    @pl.when(part == 1)
    def _():
        queries = []
        for pair, value in enumerate(found):
            value = (value + dq_part[s, h, pair].astype(F32)) * SCALE
            queries.append(value.T.astype(BF16))
        dq_s[rows, columns] = jnp.concatenate(queries, axis=1)

    @pl.when((part == 0) & (h == groups - 1))
    def _():
        total = dot(dk_s[0, rows], wk_ref[...], NT) + dot(dv_s[0, rows], wv_ref[...], NT)
        rem_out[s] = total.astype(BF16)

    @pl.when(step == 0)
    def _():
        for u, unit in enumerate(units):
            if unit.parts:
                for copy in near_copies(u):
                    copy.wait()
                launch("unit", u, 1)

    for at in range(seqs):

        @pl.when(step == (at + 1) * groups - 1)
        def _(at=at):
            launch("tokens", at, 0)

    @pl.when((part == 1) & (s == seqs - 1))
    def _():
        low = features // (1 << bits)
        dq = dq_s[:, columns]
        dko, dkr, dvo, dvr = dk_s[1, :, columns], dk_s[0, :, columns], dv_s[1, :, columns], dv_s[0, :, columns]
        sums = (
            lambda: dot(turned[1], dq),
            lambda: dot(turned[1], dko) + dot(turned[0], dkr),
            lambda: dot(turned[1], dvo) + dot(turned[0], dvr),
        )
        for i, of in enumerate(sums):
            piece = of().astype(BF16).reshape((2,) * bits + (low, width))
            group_src[(h,) + (slice(None),) * bits + (slice(i * low, (i + 1) * low),)] = piece
        bias_sum[h, 0:1] = column_sum(dq.astype(F32))
        bias_sum[h, 1:2] = column_sum(dvo.astype(F32)) + column_sum(dvr.astype(F32))

    for at in range(groups):

        @pl.when(step == steps - (groups - 1 - at) * seqs - 1)
        def _(at=at):
            launch("unit", first_group + at, 0)

    @pl.when(step == steps - 1)
    def _():
        vec[0] = jnp.zeros_like(vec[0])
        vec[0, 0:6] = vg_ref[0:6]
        for at in range(groups):
            vec[0, 6:8, at * width : (at + 1) * width] = bias_sum[at, 0:2]
        blocks = vu_ref.shape[1] // features
        for at in range(blocks):
            vec[0, 8 + at : 9 + at] = vu_ref[:, at * features : (at + 1) * features]
        launch("vectors", 0, 0)

    for at, keys in enumerate(table):
        if keys:

            @pl.when(step == at)
            def _(keys=keys):
                for key in keys:
                    receive(*key)

    @pl.when(step == steps - 1)
    def _():
        each = math.gcd(length, 256)
        todo = list(range(0, seqs * length, each))

        def own_out(row):
            return pltpu.make_async_copy(
                dq_s.at[pl.ds(row, each)], tokens_any.at[pl.ds(row, each)], out_sem.at[row // each]
            )

        def own_rows(row):
            at = slice(row, row + each)
            total = dot(dq_s[at], wq_ref[...], NT)
            total += dot(dk_s[1, at], wk_ref[...], NT) + dot(dv_s[1, at], wv_ref[...], NT)
            dq_s[at] = total.astype(BF16)
            own_out(row).start()

        left = list(todo)
        for key in tail:
            if left:
                own_rows(left.pop(0))
            receive(*key)
        for row in left:
            own_rows(row)
        for row in todo:
            own_out(row).wait()
        shards = (1 << bits) * 2
        place = me * 2 + side
        share = features // shards
        rows = pltpu.roll(vec[bits + 1, 0:8], (shards - place) * share % features, 1)
        outs[-1][0:8] = rows[:, :PAIR]
        share = vu_ref.shape[1] // shards
        each = features // share
        row = vec[bits + 1, pl.ds(8 + place // each, 1)]
        rows = pltpu.roll(jnp.broadcast_to(row, (8, features)), (each - place % each) * share % features, 1)
        outs[-1][8:16] = rows[:, :PAIR]
        for u, unit in enumerate(units):
            for k in range(unit.first, bits + 1):
                for copy in copies("unit", u, k):
                    copy.wait_send()
        for k in range(bits + 1):
            copies("vectors", 0, k)[0].wait_send()
        for k in range(seqs):
            copies("tokens", k, 0)[0].wait_send()


def back_and_sum(q, qm, g, lse, k, km, v, tokens, rem_tokens, weights, dwd, dwu, dwo, vg, vu):
    bits = lax.axis_size("dp").bit_length() - 1
    seqs, length, features = q.shape
    width = math.gcd(features, 2 * PAIR)
    groups, pairs = features // width, width // PAIR
    low, deep, blocks = dwo.shape[1], dwd.shape[1], dwu.shape[1]
    lead = (2,) * bits
    sources = [x.reshape(lead[1:] + (-1, features)) for x in (dwd, dwu, dwo)]
    every = slice(None)
    units = []
    quarter = deep // 4
    for i in range(2):
        at = slice(i * quarter, (i + 1) * quarter)
        parts = [(0, i * quarter, quarter), (0, (2 + i) * quarter, quarter)]
        units.append(Unit(parts, 2 * quarter, features, 1, [(0, at, every)]))
    for i in range(2):
        found = range(i * blocks // 2, (i + 1) * blocks // 2)
        units.append(
            Unit(
                [(1, found[0] * low, len(found) * low)],
                len(found) * low,
                features,
                len(found),
                [(1, every, slice(b * features, (b + 1) * features)) for b in found],
            )
        )
    units.append(Unit([(2, 0, low)], low, features, 1, [(2, every, every)]))
    for h in range(groups):
        columns = slice(h * width, (h + 1) * width)
        units.append(Unit(None, 3 * low, width, 3, [(3 + i, every, columns) for i in range(3)]))
    table, tail = timetable(units, bits, seqs, groups, 4.8, length * features * 4e-5)

    half = low // 2
    out_shape = [
        jax.ShapeDtypeStruct((seqs * length, features), BF16),
        jax.ShapeDtypeStruct(q.shape, BF16),
        jax.ShapeDtypeStruct((deep // 2, features), F32),
        jax.ShapeDtypeStruct((half, blocks * features), F32),
        *(jax.ShapeDtypeStruct((half, features), F32) for _ in range(4)),
        jax.ShapeDtypeStruct((16, PAIR), F32),
    ]
    tops = lead[1:]
    scratch = [pltpu.VMEM(tops + (u.rows, u.columns), BF16) for u in units]
    for u in units:
        scratch += [pltpu.VMEM(tops[k:] + (u.rows, u.columns), BF16) for k in range(u.first, bits)]
    scratch += [pltpu.VMEM((u.rows, u.columns), F32) for u in units]
    scratch += [pltpu.VMEM((u.rows // 2, u.columns), u.last_type) for u in units] * 2
    count = len(units) * (bits + 1) + bits + 1 + seqs
    near = sum(len(u.parts) << (bits - 1) for u in units if u.parts)
    scratch += [
        pltpu.VMEM((groups,) + lead + (3 * low, width), BF16),
        pltpu.VMEM((2, features, seqs * length), BF16),
        pltpu.VMEM((seqs, groups, pairs, PAIR, length), BF16),
        pltpu.VMEM((seqs * length, features), BF16),
        pltpu.VMEM((2, seqs * length, features), BF16),
        pltpu.VMEM((2, seqs * length, features), BF16),
        pltpu.VMEM((seqs, length, features), BF16),
        pltpu.VMEM((bits + 2, 16, features), F32),
        pltpu.VMEM((bits + 1, 16, features), F32),
        pltpu.VMEM((groups, 8, width), F32),
        pltpu.SemaphoreType.DMA((count,)),
        pltpu.SemaphoreType.DMA((count,)),
        pltpu.SemaphoreType.DMA((near,)),
        pltpu.SemaphoreType.DMA((seqs * length // math.gcd(length, 256),)),
    ]

    def at_step(shape, index):
        return pl.BlockSpec(shape, lambda i: index(*order_of(i, seqs, groups)))

    heads_at = at_step((1, length, width), lambda p, s, h: (s, 0, h))
    keys_at = at_step((1, 1, length, width), lambda p, s, h: (1 - p, s, 0, h))

    def rows_at(which):
        last = seqs - 1
        return pl.BlockSpec(
            (1, length, features),
            lambda i: (jnp.clip(i // groups if which == 0 else i - seqs * groups, 0, last), 0, 0),
            pipeline_mode=pl.Buffered(1),
        )

    def fixed(shape):
        return pl.BlockSpec(shape, lambda i: (0,) * len(shape), pipeline_mode=pl.Buffered(1))

    return pl.pallas_call(
        functools.partial(back_kernel, units, bits, groups, table, tail, len(out_shape)),
        grid=(2 * seqs * groups,),
        in_specs=[
            heads_at,
            at_step((1, length, PAIR), lambda p, s, h: (s, 0, 0)),
            heads_at,
            at_step((1, pairs, 8, length), lambda p, s, h: (s, h, 0, 0)),
            keys_at,
            at_step((1, 1, length, PAIR), lambda p, s, h: (1 - p, s, 0, 0)),
            keys_at,
            rows_at(1),
            rows_at(0),
        ]
        + [whole_spec(w.shape) for w in weights + (vg, vu)]
        + [pl.BlockSpec(memory_space=pl.ANY)] * 3,
        out_specs=[pl.BlockSpec(memory_space=pl.ANY)] * 2
        + [fixed(s.shape) for s in out_shape[2:]],
        out_shape=out_shape,
        scratch_shapes=scratch,
        compiler_params=pltpu.CompilerParams(
            collective_id=1, has_side_effects=True, vmem_limit_bytes=63 * MIB
        ),
        cost_estimate=cost(80 * q.size * length, 2 * q.size * 14, 2 * q.size * length // HEAD),
        name="back_and_sum",
    )(q, qm, g, lse, k, km, v, tokens, rem_tokens, *weights, vg, vu, *sources)


def finish_kernel(residual_ref, own_ref, rem_ref, *refs):
    ins, outs = refs[:7], refs[7:]
    total = residual_ref[...].astype(F32) + own_ref[...].astype(F32) + rem_ref[...].astype(F32)
    outs[0][...] = total.astype(BF16)

    @pl.when(pl.program_id(0) == 0)
    def _():
        for source, target in zip(ins[:6], outs[1:7]):
            target[...] = source[...]
        for i, target in enumerate(outs[7:]):
            target[...] = ins[6][i, : target.shape[0]]


def finish(residual, own, rem, matrices, vectors, shares):
    seqs, length, features = own.shape
    tile = math.gcd(length, 256)
    tiles = length // tile
    row_spec = pl.BlockSpec((1, tile, features), lambda i: (i // tiles, i % tiles, 0))

    def fixed(shape):
        return pl.BlockSpec(shape, lambda i: (0,) * len(shape))

    shapes = [m.shape for m in matrices] + [(n,) for n in shares]
    return pl.pallas_call(
        finish_kernel,
        grid=(seqs * tiles,),
        in_specs=[row_spec] * 3 + [fixed(m.shape) for m in matrices] + [fixed(vectors.shape)],
        out_specs=[row_spec] + [fixed(s) for s in shapes],
        out_shape=[jax.ShapeDtypeStruct(own.shape, BF16)] + [jax.ShapeDtypeStruct(s, F32) for s in shapes],
        compiler_params=params(60),
        cost_estimate=cost(2 * own.size, 8 * own.size),
        name="finish",
    )(residual, own, rem, *matrices, vectors)


def back_plainly(q, qm, o, g, lse, own, rem, bg, tokens, rem_tokens, weights, dwd, dwu, dwo, vg, vu):
    seqs, length, features = q.shape
    dp, blk = lax.axis_size("dp"), lax.axis_size("blk")
    dq, dko, dvo, dkr, dvr = attend_back(q, qm, o, g, lse, own, rem)
    rem_gradient = tokens_back(rem_back_kernel, (dkr, dvr), weights[1:])
    came = [
        lax.ppermute(part, "blk", [((i + r) % blk, i) for i in range(blk)])
        for r, part in enumerate(jnp.split(rem_gradient, blk - 1, axis=1), 1)
    ]
    flat = [v.reshape(-1, features) for v in (tokens, rem_tokens, dq, dko, dvo, dkr, dvr)]
    dwq, dwk, dwv, dbq, dbv = weights_back(*flat)
    total = tokens_back(own_back_kernel, (bg, dq, dko, dvo), weights).astype(F32)
    for part in came:
        total += part.astype(F32)
    dwu = jnp.moveaxis(dwu[0], 0, 1).reshape(features, -1)
    summed = [scatter_sum(w) for w in (dwd, dwu, dwo, dwq, dwk, dwv)]
    rows = [vg[i] for i in range(6)] + [dbq, dbv, vu]
    rows = [scatter_sum(v.reshape(dp * blk, -1)) for v in rows]
    return [total.astype(BF16)] + summed + [[v[0] for v in rows]]


def body(
    tokens,
    query_weight,
    query_bias,
    key_weight,
    value_weight,
    value_bias,
    out_weight,
    out_bias,
    gain_one,
    shift_one,
    up_weight,
    up_bias,
    down_weight,
    down_bias,
    gain_two,
    shift_two,
    group_ids,
    valid_mask,
    cotangent,
):
    seqs, length, features = tokens.shape
    rows = seqs * length
    blk = lax.axis_size("blk")

    def from_others(value):
        found = [
            lax.ppermute(value, "blk", [(i, (i + r) % blk) for i in range(blk)])
            for r in range(1, blk)
        ]
        return found[0] if len(found) == 1 else jnp.concatenate(found, axis=1)

    codes = jnp.where(valid_mask == 1, group_ids, -1)
    dp = lax.axis_size("dp")
    by_kernel = blk == 2 and dp & (dp - 1) == 0 and dp > 1 and (features // dp) % 16 == 0
    projections = (query_weight, key_weight, value_weight)
    vectors = (
        query_bias,
        value_bias,
        out_bias,
        gain_one,
        shift_one,
        down_bias,
        gain_two,
        shift_two,
    )

    if by_kernel:
        (block_out, branch_gradient, attended_gradient, attended, lse, query_mask, key_masks,
         first_t, feed_t, vector_gradients, up_bias_gradient, queries, keys, values,
         rem_tokens, active, inner_gradient) = front(
            tokens,
            group_ids,
            valid_mask,
            cotangent,
            vectors,
            up_bias,
            projections + (out_weight, up_weight, down_weight),
        )
        dwu, dwd, dwo = feed_weights(
            first_t,
            inner_gradient.reshape(rows, -1),
            feed_t,
            active.reshape(rows, -1),
            attended.reshape(rows, features),
            branch_gradient.reshape(rows, features),
        )
        own_gradient, rem_gradient, *matrices, vectors = back_and_sum(
            queries,
            query_mask,
            attended_gradient,
            lse,
            keys,
            key_masks,
            values,
            tokens,
            rem_tokens,
            projections,
            dwd,
            dwu,
            dwo,
            vector_gradients,
            up_bias_gradient,
        )
        shares = [features // (dp * blk)] * 8 + [up_bias.size // (dp * blk)]
        found = finish(
            branch_gradient, own_gradient.reshape(tokens.shape), rem_gradient, matrices, vectors, shares
        )
        tokens_gradient, dwd, dwu, dwo, dwq, dwk, dwv, *rows_left = found
    else:
        rem_tokens = from_others(tokens)
        rem_codes = from_others(codes.astype(BF16)).astype(jnp.int32)
        slot = jnp.arange(PAIR, dtype=jnp.int32) % HEAD

        def key_mask(code):
            return jnp.where(code[:, :, None] == slot, 0.0, MASKED).astype(BF16)

        query_mask = (group_ids[:, :, None] == slot).astype(BF16)
        vectors = jnp.stack(vectors).astype(F32)
        queries, own_keys, own_values = project(tokens, vectors, projections)
        rem_keys, rem_values = project(rem_tokens, vectors, projections[1:])
        own = (own_keys, key_mask(codes), own_values)
        rem = (rem_keys, key_mask(rem_codes), rem_values)
        attended, lse = attend(queries, query_mask, own, rem)
        (block_out, branch_gradient, attended_gradient, vector_gradients, up_bias_gradient,
         dwu, dwd, dwo) = feed_both_ways(
            tokens.reshape(rows, features),
            attended.reshape(rows, features),
            cotangent.reshape(rows, features),
            vectors[2:],
            up_bias.astype(F32)[None],
            out_weight,
            up_weight,
            down_weight,
            1,
        )
        tokens_gradient, dwd, dwu, dwo, dwq, dwk, dwv, rows_left = back_plainly(
            queries,
            query_mask,
            attended,
            attended_gradient.reshape(tokens.shape),
            lse,
            own,
            rem,
            branch_gradient.reshape(tokens.shape),
            tokens,
            rem_tokens,
            projections,
            dwd,
            dwu,
            dwo,
            vector_gradients,
            up_bias_gradient,
        )
    dbo, dg1, ds1, dbd, dg2, ds2, dbq, dbv, dbu = rows_left
    return (
        block_out.reshape(tokens.shape),
        tokens_gradient,
        dwq,
        dbq,
        dwk,
        dwv,
        dbv,
        dwo,
        dbo,
        dg1,
        ds1,
        dwu,
        dbu,
        dwd,
        dbd,
        dg2,
        ds2,
    )


def solution(mesh):
    rows, shared, pair = P("dp", "blk", None), P(), P("dp", "blk")
    matrix, vector = P(("dp", "blk"), None), P(("dp", "blk"))
    return jax.shard_map(
        body,
        mesh=mesh,
        in_specs=(rows,) + (shared,) * 15 + (pair, pair, rows),
        out_specs=(
            rows,
            rows,
            matrix,
            vector,
            matrix,
            matrix,
            vector,
            matrix,
            vector,
            vector,
            vector,
            matrix,
            vector,
            matrix,
            vector,
            vector,
            vector,
        ),
        check_vma=False,
    )
```

```python
import functools
import math

import jax
import jax.numpy as jnp
from jax import lax
from jax.experimental import pallas as pl
from jax.experimental.pallas import tpu as pltpu
from jax.sharding import PartitionSpec as P

HEAD = 64
PAIR = 2 * HEAD
EPSILON = 1e-12
MASKED = -1e30
FLOOR = -3e38
SCALE = HEAD**-0.5
EXPO = SCALE * math.log2(math.e)
NN = (((1,), (0,)), ((), ()))
NT = (((1,), (1,)), ((), ()))
F32 = jnp.float32
BF16 = jnp.bfloat16
MIB = 1 << 20
FEED_ROWS = 256


def dot(left, right, dims=NN):
    return lax.dot_general(left, right, dims, preferred_element_type=F32)


def whole_spec(shape):
    return pl.BlockSpec(shape, lambda *_: (0,) * len(shape), pipeline_mode=pl.Buffered(1))


def params(limit):
    return pltpu.CompilerParams(vmem_limit_bytes=limit * MIB)


def cost(flops, touched, exps=0):
    return pl.CostEstimate(flops=int(flops), bytes_accessed=int(touched), transcendentals=int(exps))


def project_kernel(has_query, *refs):
    if has_query:
        x_ref, bias_ref, wq_ref, wk_ref, wv_ref, q_ref, k_ref, v_ref = refs
    else:
        x_ref, bias_ref, wk_ref, wv_ref, k_ref, v_ref = refs
    x = x_ref[0]
    if has_query:
        q_ref[0] = (dot(x, wq_ref[...]) + bias_ref[0:1]).astype(BF16)
    k_ref[0] = dot(x, wk_ref[...]).astype(BF16)
    v_ref[0] = (dot(x, wv_ref[...]) + bias_ref[1:2]).astype(BF16)


def project(x, bias, weights):
    seqs, length, features = x.shape
    tile = math.gcd(length, 512)
    grid = (seqs, length // tile)
    row_spec = pl.BlockSpec((1, tile, features), lambda s, i: (s, i, 0))
    return pl.pallas_call(
        functools.partial(project_kernel, len(weights) == 3),
        grid=grid,
        in_specs=[row_spec, whole_spec(bias.shape)] + [whole_spec(w.shape) for w in weights],
        out_specs=[row_spec] * len(weights),
        out_shape=[jax.ShapeDtypeStruct(x.shape, BF16)] * len(weights),
        compiler_params=params(60),
        cost_estimate=cost(
            2 * x.size * features * len(weights), 2 * x.size * (1 + len(weights))
        ),
        name="project",
    )(x, bias, *weights)


def low_lanes():
    return lax.broadcasted_iota(jnp.int32, (1, PAIR), 1) < HEAD


def attend_group(q, qm, sources, o_ref, lse_ref):
    length = q.shape[0]
    tile = math.gcd(length, 256)
    low = low_lanes()
    one = jnp.ones((1, PAIR), BF16)
    todo = [
        (pair, row, head)
        for pair in range(q.shape[1] // PAIR)
        for row in range(0, length, tile)
        for head in range(2)
    ]

    def lanes_of(pair):
        return slice(pair * PAIR, (pair + 1) * PAIR)

    def mine_of(head):
        return ~low if head else low

    def scores_of(pair, row, head):
        mine, lanes = mine_of(head), lanes_of(pair)
        q_side = jnp.where(mine, q[row : row + tile, lanes], qm[row : row + tile])
        return [dot(q_side, jnp.where(mine, k[:, lanes], km), NT) for k, km, _ in sources]

    ahead = scores_of(*todo[0])
    for i, (pair, row, head) in enumerate(todo):
        scores = ahead
        if i + 1 < len(todo):
            ahead = scores_of(*todo[i + 1])
        top = functools.reduce(
            jnp.maximum, [jnp.max(part, axis=-1, keepdims=True) for part in scores]
        )
        weights = [jnp.exp2((part - top) * EXPO).astype(BF16) for part in scores]
        total = sum(
            dot(w, jnp.where(mine_of(head), v[:, lanes_of(pair)], one))
            for w, (_, _, v) in zip(weights, sources)
        )
        if head == 0:
            earlier, earlier_top = total, top
            continue
        totals = pltpu.roll(jnp.where(low, total, earlier), HEAD, 1)
        rows = slice(row, row + tile)
        o_ref[rows, lanes_of(pair)] = (jnp.where(low, earlier, total) / totals).astype(BF16)
        lse = (jnp.where(low, earlier_top, top) * EXPO + jnp.log2(totals)).T
        lse_ref[pair, 0:1, rows] = lse[0:1]
        lse_ref[pair, 1:2, rows] = lse[HEAD : HEAD + 1]


def attend_kernel(q_ref, qm_ref, ko_ref, kmo_ref, vo_ref, kr_ref, kmr_ref, vr_ref, o_ref, lse_ref):
    sources = [(ko_ref[0], kmo_ref[0], vo_ref[0]), (kr_ref[0], kmr_ref[0], vr_ref[0])]
    attend_group(q_ref[0], qm_ref[0], sources, o_ref.at[0], lse_ref.at[0])


def pair_spec(length, lanes):
    return pl.BlockSpec((1, length, lanes), lambda s, h: (s, 0, h))


def mask_spec(length):
    return pl.BlockSpec((1, length, PAIR), lambda s, h: (s, 0, 0))


def lse_spec(length, lanes):
    return pl.BlockSpec((1, lanes // PAIR, 8, length), lambda s, h: (s, h, 0, 0))


def attend(q, qm, own, rem):
    seqs, length, features = q.shape
    lanes = math.gcd(features, 2 * PAIR)
    other = rem[0].shape[1]
    own_spec, rem_spec = pair_spec(length, lanes), pair_spec(other, lanes)
    return pl.pallas_call(
        attend_kernel,
        grid=(seqs, features // lanes),
        in_specs=[own_spec, mask_spec(length)]
        + [own_spec, mask_spec(length), own_spec]
        + [rem_spec, mask_spec(other), rem_spec],
        out_specs=[own_spec, lse_spec(length, lanes)],
        out_shape=[
            jax.ShapeDtypeStruct(q.shape, BF16),
            jax.ShapeDtypeStruct((seqs, features // PAIR, 8, length), F32),
        ],
        compiler_params=params(60),
        cost_estimate=cost(
            16 * q.size * (length + other), 2 * q.size * 6, q.size * (length + other) // HEAD
        ),
        name="attend",
    )(q, qm, *own, *rem)


def attend_back_part(q, qm, g, lse_ref, k, km, v, dk_ref, dv_ref):
    low = low_lanes()
    none = jnp.zeros((1, PAIR), BF16)
    pairs = q.shape[1] // PAIR
    todo = [(pair, head) for pair in range(pairs) for head in range(2)]

    def lanes_of(pair):
        return slice(pair * PAIR, (pair + 1) * PAIR)

    def mine_of(head):
        return ~low if head else low

    def products(pair, head):
        mine, lanes = mine_of(head), lanes_of(pair)
        return (
            dot(jnp.where(mine, k[:, lanes], km), jnp.where(mine, q[:, lanes], qm), NT),
            dot(jnp.where(mine, v[:, lanes], none), g[:, lanes], NT),
        )

    found = []
    ahead = products(*todo[0])
    for i, (pair, head) in enumerate(todo):
        scores, grads = ahead
        if i + 1 < len(todo):
            ahead = products(*todo[i + 1])
        lanes, mine = lanes_of(pair), mine_of(head)
        if head == 0:
            k_t = k[:, lanes].T
            dk = dv = 0.0
            dq = []
        probs = jnp.exp2(scores * EXPO - lse_ref[pair, head : head + 1, :])
        grads = (probs * (grads - lse_ref[pair, 2 + head : 3 + head, :])).astype(BF16)
        dv += dot(probs.astype(BF16), jnp.where(mine, g[:, lanes], none))
        dk += dot(grads, jnp.where(mine, q[:, lanes], none))
        dq.append(dot(k_t[head * HEAD : (head + 1) * HEAD], grads))
        if head == 1:
            dk_ref[:, lanes] = (dk * SCALE).astype(BF16)
            dv_ref[:, lanes] = dv.astype(BF16)
            found.append(jnp.concatenate(dq, axis=0))
    return found


def attend_back_kernel(q_ref, qm_ref, g_ref, lse_ref, ko_ref, kmo_ref, vo_ref, kr_ref, kmr_ref,
                       vr_ref, dq_ref, dko_ref, dvo_ref, dkr_ref, dvr_ref):
    parts = ((ko_ref, kmo_ref, vo_ref, dko_ref, dvo_ref), (kr_ref, kmr_ref, vr_ref, dkr_ref, dvr_ref))
    found = [
        attend_back_part(
            q_ref[0], qm_ref[0], g_ref[0], lse_ref.at[0], k[0], km[0], v[0], dk.at[0], dv.at[0]
        )
        for k, km, v, dk, dv in parts
    ]
    for pair, both in enumerate(zip(*found)):
        dq_ref[0, :, pair * PAIR : (pair + 1) * PAIR] = (sum(both) * SCALE).T.astype(BF16)


def attend_back(q, qm, o, g, lse, own, rem):
    seqs, length, features = q.shape
    delta = (g.astype(F32) * o.astype(F32)).reshape(seqs, length, features // PAIR, 2, HEAD).sum(-1)
    lse = lax.dynamic_update_slice(lse, jnp.transpose(delta, (0, 2, 3, 1)), (0, 0, 2, 0))
    lanes = math.gcd(features, 2 * PAIR)
    other = rem[0].shape[1]
    own_spec, rem_spec = pair_spec(length, lanes), pair_spec(other, lanes)
    return pl.pallas_call(
        attend_back_kernel,
        grid=(seqs, features // lanes),
        in_specs=[own_spec, mask_spec(length), own_spec, lse_spec(length, lanes)]
        + [own_spec, mask_spec(length), own_spec]
        + [rem_spec, mask_spec(other), rem_spec],
        out_specs=[own_spec] * 3 + [rem_spec] * 2,
        out_shape=[jax.ShapeDtypeStruct(q.shape, BF16)] * 3
        + [jax.ShapeDtypeStruct(rem[0].shape, BF16)] * 2,
        compiler_params=params(60),
        cost_estimate=cost(
            40 * q.size * (length + other), 2 * q.size * 14, q.size * (length + other) // HEAD
        ),
        name="attend_back",
    )(q, qm, g, lse, *own, *rem)


def gelu_and_slope(x):
    bell = jnp.exp2(x * x * (-0.5 * math.log2(math.e)))
    below = 1.0 + (0.3275911 / math.sqrt(2.0)) * jnp.abs(x)
    t = pl.reciprocal(below, approx=True)
    t = t * (2.0 - below * t)
    poly = 1.061405429 * t - 1.453152027
    poly = poly * t + 1.421413741
    poly = poly * t - 0.284496736
    poly = poly * t + 0.254829592
    tail = (0.5 * poly) * t * bell
    share = jnp.where(x >= 0.0, 1.0 - tail, tail)
    return x * share, share + x * bell * (1.0 / math.sqrt(2.0 * math.pi))


def mean(values):
    return jnp.sum(values, axis=-1, keepdims=True) * (1.0 / values.shape[-1])


def norm_parts(values):
    centred = values - mean(values)
    scale = lax.rsqrt(mean(centred * centred) + EPSILON)
    return centred * scale, scale


def norm_back(upper, normed, scale):
    return scale * (upper - mean(upper) - normed * mean(upper * normed))


def column_sum(values):
    return jnp.sum(values, axis=0, keepdims=True)


def feed_kernel(layout, tok_ref, att_ref, cot_ref, vec_ref, bu_ref, wo_ref, wu_ref, wd_ref,
                out_ref, bg_ref, ag_ref, vg_ref, dbu_ref, dwu_ref, dwd_ref, dwo_ref,
                act_s, din_s, first_t, feed_t, att_t, bg_s):
    tiles, ff_steps, chunk, wide, narrow = layout
    step = pl.program_id(0)
    tile = tok_ref.shape[0]
    hidden = act_s.shape[1]
    vec = [vec_ref[i : i + 1] for i in range(6)]
    out_bias, gain_one, shift_one, down_bias, gain_two, shift_two = vec

    @pl.when(step == 0)
    def _():
        vg_ref[...] = jnp.zeros_like(vg_ref)
        dbu_ref[...] = jnp.zeros_like(dbu_ref)

    @pl.when(step < tiles)
    def _():
        start = pl.multiple_of(step * tile, tile)
        rows = pl.ds(start, tile)
        att = att_ref[...]
        normed_one, scale_one = norm_parts(
            tok_ref[...].astype(F32) + (dot(att, wo_ref[...]) + out_bias)
        )
        first = normed_one * gain_one + shift_one
        first_low = first.astype(BF16)
        first_t[:, rows] = first_low.T
        att_t[:, rows] = att.T
        feed = jnp.zeros_like(first) + down_bias
        spans = [slice(c, c + chunk) for c in range(0, hidden, chunk)]
        ahead = dot(first_low, wu_ref[:, spans[0]])
        for i, cols in enumerate(spans):
            inner = ahead + bu_ref[:, cols]
            if i + 1 < len(spans):
                ahead = dot(first_low, wu_ref[:, spans[i + 1]])
            active, slope = gelu_and_slope(inner)
            active = active.astype(BF16)
            act_s[rows, cols] = active
            din_s[rows, cols] = slope.astype(BF16)
            feed += dot(active, wd_ref[cols])
        normed_two, scale_two = norm_parts(first + feed)
        out_ref[...] = (normed_two * gain_two + shift_two).astype(BF16)
        cot = cot_ref[...].astype(F32)
        second = norm_back(cot * gain_two, normed_two, scale_two)
        feed_low = second.astype(BF16)
        feed_t[:, rows] = feed_low.T
        back = second
        ahead = dot(feed_low, wd_ref[spans[0]], NT)
        for i, cols in enumerate(spans):
            inner = ahead
            if i + 1 < len(spans):
                ahead = dot(feed_low, wd_ref[spans[i + 1]], NT)
            inner = (inner * din_s[rows, cols].astype(F32)).astype(BF16)
            din_s[rows, cols] = inner
            dbu_ref[:, cols] += column_sum(inner.astype(F32))
            back += dot(inner, wu_ref[:, cols], NT)
        residual = norm_back(back * gain_one, normed_one, scale_one)
        branch_low = residual.astype(BF16)
        bg_ref[...] = branch_low
        bg_s[rows] = branch_low
        ag_ref[...] = dot(branch_low, wo_ref[...], NT).astype(BF16)
        for i, values in enumerate(
            (
                branch_low.astype(F32),
                back * normed_one,
                back,
                feed_low.astype(F32),
                cot * normed_two,
                cot,
            )
        ):
            vg_ref[i : i + 1] += column_sum(values)

    @pl.when((step >= tiles) & (step < tiles + ff_steps))
    def _():
        cols = pl.ds(pl.multiple_of((step - tiles) * wide, wide), wide)
        dwu = dot(first_t[...], din_s[:, cols]).astype(BF16)
        dwu_ref[...] = dwu.reshape(dwu_ref.shape)
        dwd_ref[...] = dot(feed_t[...], act_s[:, cols]).astype(BF16).T

    @pl.when(step >= tiles + ff_steps)
    def _():
        cols = pl.ds(pl.multiple_of((step - tiles - ff_steps) * narrow, narrow), narrow)
        dwo_ref[...] = dot(att_t[...], bg_s[:, cols]).astype(BF16)


def feed_both_ways(tokens, attended, cotangent, vectors, up_bias, wo, wu, wd, groups):
    rows, features = tokens.shape
    hidden = wu.shape[1]
    tile = math.gcd(rows, 256)
    tiles = rows // tile
    wide, narrow = features, math.gcd(features, 384)
    ff_steps, out_steps = hidden // wide, features // narrow
    layout = (tiles, ff_steps, math.gcd(hidden, 512), wide, narrow)
    blocked = (groups, ff_steps, features // groups, wide)
    row_spec = pl.BlockSpec((tile, features), lambda i: (jnp.minimum(i, tiles - 1), 0))

    def ff_at(i):
        return jnp.clip(i - tiles, 0, ff_steps - 1)

    return pl.pallas_call(
        functools.partial(feed_kernel, layout),
        grid=(tiles + ff_steps + out_steps,),
        in_specs=[row_spec] * 3
        + [whole_spec(a.shape) for a in (vectors, up_bias, wo, wu, wd)],
        out_specs=[row_spec] * 3
        + [
            pl.BlockSpec((8, features), lambda i: (0, 0)),
            pl.BlockSpec((1, hidden), lambda i: (0, 0)),
            pl.BlockSpec((groups, 1) + blocked[2:], lambda i: (0, ff_at(i), 0, 0)),
            pl.BlockSpec((wide, features), lambda i: (ff_at(i), 0)),
            pl.BlockSpec(
                (features, narrow),
                lambda i: (0, jnp.clip(i - tiles - ff_steps, 0, out_steps - 1)),
            ),
        ],
        out_shape=[jax.ShapeDtypeStruct(tokens.shape, BF16)] * 3
        + [
            jax.ShapeDtypeStruct((8, features), F32),
            jax.ShapeDtypeStruct((1, hidden), F32),
            jax.ShapeDtypeStruct(blocked, BF16),
            jax.ShapeDtypeStruct(wd.shape, BF16),
            jax.ShapeDtypeStruct(wo.shape, BF16),
        ],
        scratch_shapes=[
            pltpu.VMEM((rows, hidden), BF16),
            pltpu.VMEM((rows, hidden), BF16),
            pltpu.VMEM((features, rows), BF16),
            pltpu.VMEM((features, rows), BF16),
            pltpu.VMEM((features, rows), BF16),
            pltpu.VMEM((rows, features), BF16),
        ],
        compiler_params=params(60),
        cost_estimate=cost(
            6 * rows * features * (features + 2 * hidden),
            2 * (6 * rows * features + 4 * features * hidden + 2 * features * features),
            2 * rows * hidden,
        ),
        name="feed_both_ways",
    )(tokens, attended, cotangent, vectors, up_bias, wo, wu, wd)


def spread(row):
    return jnp.broadcast_to(row, (PAIR, row.shape[1])).T


def as_row(ref):
    return ref[...].astype(F32).reshape(1, ref.shape[0])


def front_kernel(tokens_ref, group_ref, valid_ref, cot_ref, bq_ref, bv_ref, bo_ref, g1_ref, s1_ref, bd_ref,
                 g2_ref, s2_ref, bu_in, wq_any, wk_any, wv_any, wo_any, wu_any, wd_any,
                 out_ref, bg_ref, ag_ref, att_ref, lse_ref, qm_ref, km_ref,
                 first_t, feed_t, vg_ref, dbu_ref, q_any, k_any, v_any, rem_any, act_any, din_any,
                 wq, wk, wv, wo, wu, wd, tok_s, q_s, k_s, v_s, kr_s, vr_s, rem_s, own_codes, code_s, act_s, din_s,
                 bu_ref, weight_sem, out_sem, send_sem, recv_sem):
    s = pl.program_id(0)
    seqs = tok_s.shape[0]
    length, features = tok_s.shape[1:]
    hidden = act_s.shape[1]
    side = lax.axis_index("blk")
    other = {"blk": 1 - side}
    query_bias, value_bias, out_bias, gain_one, shift_one, down_bias, gain_two, shift_two = [
        as_row(ref) for ref in (bq_ref, bv_ref, bo_ref, g1_ref, s1_ref, bd_ref, g2_ref, s2_ref)
    ]
    pairs_of = [(wq_any, wq), (wk_any, wk), (wv_any, wv), (wo_any, wo), (wu_any, wu), (wd_any, wd)]

    def weight(i):
        return pltpu.make_async_copy(*pairs_of[i], weight_sem.at[i])

    def remote(source, target, at):
        return pltpu.make_async_remote_copy(
            src_ref=source,
            dst_ref=target,
            send_sem=send_sem.at[at],
            recv_sem=recv_sem.at[at],
            device_id=other,
            device_id_type=pl.DeviceIdType.MESH,
        )

    def exchange(at):
        return remote(tokens_ref.at[at], rem_s.at[at], at)

    def code_exchange():
        return remote(own_codes, code_s, seqs)

    def whole_out(i):
        source, target = ((q_s, q_any), (k_s, k_any.at[0]), (v_s, v_any.at[0]))[i]
        return pltpu.make_async_copy(source, target, out_sem.at[i])

    def part_out(i, at):
        source, target = (
            (kr_s, k_any.at[1, at]),
            (vr_s, v_any.at[1, at]),
            (rem_s.at[at], rem_any.at[at]),
            (act_s, act_any.at[at]),
            (din_s, din_any.at[at]),
        )[i]
        return pltpu.make_async_copy(source, target, out_sem.at[3 + i])

    @pl.when(s == 0)
    def _():
        barrier = pltpu.get_barrier_semaphore()
        pl.semaphore_signal(barrier, inc=1, device_id=other, device_id_type=pl.DeviceIdType.MESH)
        load = pltpu.make_async_copy(tokens_ref, tok_s, weight_sem.at[len(pairs_of)])
        load.start()
        for i in range(3):
            weight(i).start()
        codes = jnp.where(valid_ref[...] == 1, group_ref[...], -1).astype(F32)
        own_codes[...] = jnp.zeros_like(own_codes)
        own_codes[0:seqs] = codes
        pl.semaphore_wait(barrier, 1)
        exchange(0).start()
        code_exchange().start()
        for i in range(3, len(pairs_of)):
            weight(i).start()
        vg_ref[...] = jnp.zeros_like(vg_ref)
        dbu_ref[...] = jnp.zeros_like(dbu_ref)
        bu_ref[...] = as_row(bu_in)
        load.wait()
        for i in range(3):
            weight(i).wait()

        def project_own(at, carry):
            x = tok_s[at]
            q_s[at] = (dot(x, wq[...]) + query_bias).astype(BF16)
            k_s[at] = dot(x, wk[...]).astype(BF16)
            v_s[at] = (dot(x, wv[...]) + value_bias).astype(BF16)
            return carry

        lax.fori_loop(0, seqs, project_own, 0)
        for i in range(3):
            whole_out(i).start()
        for i in range(3, len(pairs_of)):
            weight(i).wait()
        code_exchange().wait_recv()
        exchange(0).wait_send()
        if seqs > 1:
            exchange(1).start()

    for at in range(seqs):

        @pl.when(s == at)
        def _(at=at):
            exchange(at).wait_recv()
            if at:
                for i in range(3):
                    part_out(i, at - 1).wait()

    x = rem_s[s]
    kr_s[...] = dot(x, wk[...]).astype(BF16)
    vr_s[...] = (dot(x, wv[...]) + value_bias).astype(BF16)
    slot = lax.broadcasted_iota(jnp.int32, (1, PAIR), 1) % HEAD
    slot = slot.astype(F32)
    groups_row = group_ref[pl.ds(s, 1)].astype(F32)
    qm_ref[0] = jnp.where(spread(groups_row) == slot, 1.0, 0.0).astype(BF16)
    km_ref[0, 0] = jnp.where(spread(own_codes[pl.ds(s, 1)]) == slot, 0.0, MASKED).astype(BF16)
    km_ref[1, 0] = jnp.where(spread(code_s[pl.ds(s, 1)]) == slot, 0.0, MASKED).astype(BF16)
    for at in range(seqs):

        @pl.when(s == at)
        def _(at=at):
            for i in range(3):
                part_out(i, at).start()

    groups = features // (2 * PAIR)

    def heads(group, carry):
        lanes = pl.ds(pl.multiple_of(group * 2 * PAIR, 2 * PAIR), 2 * PAIR)
        attend_group(
            q_s[s, :, lanes],
            qm_ref[0],
            [(k_s[s, :, lanes], km_ref[0, 0], v_s[s, :, lanes]), (kr_s[:, lanes], km_ref[1, 0], vr_s[:, lanes])],
            att_ref.at[0, :, lanes],
            lse_ref.at[0, pl.ds(group * 2, 2)],
        )
        return carry

    lax.fori_loop(0, groups, heads, 0)

    for at in range(1, seqs):

        @pl.when(s == at)
        def _(at=at):
            for i in range(3, 5):
                part_out(i, at - 1).wait()

    tile = math.gcd(length, FEED_ROWS)
    chunk = math.gcd(hidden, 512)
    spans = [slice(c, c + chunk) for c in range(0, hidden, chunk)]

    def feed_rows(t, carry):
        rows = pl.ds(pl.multiple_of(t * tile, tile), tile)
        att = att_ref[0, rows]
        normed_one, scale_one = norm_parts(
            tok_s[s, rows].astype(F32) + (dot(att, wo[...]) + out_bias)
        )
        first = normed_one * gain_one + shift_one
        first_low = first.astype(BF16)
        first_t[:, rows] = first_low.T
        ahead = dot(first_low, wu[:, spans[0]])
        for i, cols in enumerate(spans):
            inner = ahead + bu_ref[:, cols]
            if i + 1 < len(spans):
                ahead = dot(first_low, wu[:, spans[i + 1]])
            active, slope = gelu_and_slope(inner)
            act_s[rows, cols] = active.astype(BF16)
            din_s[rows, cols] = slope.astype(BF16)
        feed = dot(act_s[rows], wd[...]) + down_bias
        normed_two, scale_two = norm_parts(first + feed)
        out_ref[0, rows] = (normed_two * gain_two + shift_two).astype(BF16)
        cot = cot_ref[0, rows].astype(F32)
        second = norm_back(cot * gain_two, normed_two, scale_two)
        feed_low = second.astype(BF16)
        feed_t[:, rows] = feed_low.T
        ahead = dot(feed_low, wd[spans[0]], NT)
        for i, cols in enumerate(spans):
            inner = ahead
            if i + 1 < len(spans):
                ahead = dot(feed_low, wd[spans[i + 1]], NT)
            inner = (inner * din_s[rows, cols].astype(F32)).astype(BF16)
            din_s[rows, cols] = inner
            dbu_ref[:, cols] += column_sum(inner.astype(F32))
        back = second + dot(din_s[rows], wu[...], NT)
        residual = norm_back(back * gain_one, normed_one, scale_one)
        branch_low = residual.astype(BF16)
        bg_ref[0, rows] = branch_low
        att_grad = dot(branch_low, wo[...], NT).astype(BF16)
        ag_ref[0, rows] = att_grad
        product = att_grad.astype(F32) * att.astype(F32)
        coarse = product.astype(BF16)
        fine = (product - coarse.astype(F32)).astype(BF16)
        heads_count = features // HEAD
        of_head = lax.broadcasted_iota(jnp.int32, (heads_count, features), 1) // HEAD
        selector = (of_head == lax.broadcasted_iota(jnp.int32, of_head.shape, 0)).astype(F32)
        selector = selector.astype(BF16)
        delta = dot(selector, coarse, NT) + dot(selector, fine, NT)
        for pair in range(features // PAIR):
            lse_ref[0, pair, 2:4, rows] = delta[2 * pair : 2 * pair + 2]
        for i, values in enumerate(
            (
                branch_low.astype(F32),
                back * normed_one,
                back,
                feed_low.astype(F32),
                cot * normed_two,
                cot,
            )
        ):
            vg_ref[i : i + 1] += column_sum(values)
        return carry

    lax.fori_loop(0, length // tile, feed_rows, 0)

    for at in range(seqs):

        @pl.when(s == at)
        def _(at=at):
            for i in range(3, 5):
                part_out(i, at).start()
            if at < seqs - 1:
                exchange(at + 1).wait_send()
            if at + 2 < seqs:
                exchange(at + 2).start()
            if at == seqs - 1:
                for i in range(3):
                    whole_out(i).wait()
                for i in range(5):
                    part_out(i, at).wait()
                code_exchange().wait_send()


def front(tokens, group_ids, valid, cotangent, vectors, up_bias, weights):
    seqs, length, features = tokens.shape
    hidden = up_bias.shape[0]
    pairs = features // PAIR
    anywhere = pl.BlockSpec(memory_space=pl.ANY)

    def at_seq(*shape):
        return pl.BlockSpec((1,) + shape, lambda s: (s,) + (0,) * len(shape))

    def of_seqs(*shape, dtype=BF16):
        return jax.ShapeDtypeStruct((seqs,) + shape, dtype)

    def fixed(*shape):
        return pl.BlockSpec(shape, lambda s: (0,) * len(shape))

    rows, mask, lses, wide = (length, features), (length, PAIR), (pairs, 8, length), (length, hidden)
    turned = pl.BlockSpec((features, length), lambda s: (0, s))
    return pl.pallas_call(
        front_kernel,
        grid=(seqs,),
        in_specs=[anywhere, whole_spec(group_ids.shape), whole_spec(valid.shape), at_seq(*rows)]
        + [whole_spec(v.shape) for v in vectors + (up_bias,)]
        + [anywhere] * 6,
        out_specs=[at_seq(*rows)] * 4
        + [at_seq(*lses), at_seq(*mask)]
        + [pl.BlockSpec((2, 1) + mask, lambda s: (0, s, 0, 0))]
        + [turned] * 2
        + [fixed(8, features), fixed(1, hidden)]
        + [anywhere] * 6,
        out_shape=[of_seqs(*rows)] * 4
        + [of_seqs(*lses, dtype=F32), of_seqs(*mask)]
        + [jax.ShapeDtypeStruct((2, seqs) + mask, BF16)]
        + [jax.ShapeDtypeStruct((features, seqs * length), BF16)] * 2
        + [jax.ShapeDtypeStruct((8, features), F32), jax.ShapeDtypeStruct((1, hidden), F32)]
        + [of_seqs(*rows)]
        + [jax.ShapeDtypeStruct((2, seqs) + rows, BF16)] * 2
        + [of_seqs(*rows)]
        + [of_seqs(*wide)] * 2,
        scratch_shapes=[pltpu.VMEM(w.shape, BF16) for w in weights]
        + [pltpu.VMEM(tokens.shape, BF16)] * 4
        + [pltpu.VMEM(rows, BF16)] * 2
        + [pltpu.VMEM(tokens.shape, BF16)]
        + [pltpu.VMEM((seqs + -seqs % 8, length), F32)] * 2
        + [pltpu.VMEM(wide, BF16)] * 2
        + [pltpu.VMEM((1, hidden), F32)]
        + [pltpu.SemaphoreType.DMA((7,)), pltpu.SemaphoreType.DMA((8,))]
        + [pltpu.SemaphoreType.DMA((seqs + 1,))] * 2,
        compiler_params=pltpu.CompilerParams(
            collective_id=2, has_side_effects=True, vmem_limit_bytes=63 * MIB
        ),
        cost_estimate=cost(
            2 * tokens.size * (9 * features + 4 * hidden + 8 * length), 2 * 20 * tokens.size, tokens.size * 24
        ),
        name="front",
    )(tokens, group_ids, valid, cotangent, *vectors, up_bias, *weights)


def feed_weights_kernel(blocks, first_ref, din_ref, feed_ref, act_ref, att_any, bg_any,
                        dwu_ref, dwd_ref, dwo_ref, up_s, up_in, down_s, down_in, out_s, out_in,
                        att_s, bg_s, near_sem, send_sem, recv_sem):
    step = pl.program_id(0)
    features = first_ref.shape[0]
    me = lax.axis_index("dp")
    core = me % 2
    other = {"dp": me + 1 - 2 * core}

    def loads():
        return [
            pltpu.make_async_copy(att_any, att_s, near_sem.at[0]),
            pltpu.make_async_copy(bg_any, bg_s, near_sem.at[1]),
        ]

    def swaps(block):
        if block == blocks:
            pairs = [(out_s.at[:, 1 - core], out_in)]
        else:
            pairs = [
                (up_s.at[block % 2, :, 1 - core], up_in.at[block]),
                (down_s.at[block % 2, :, 1 - core], down_in.at[block]),
            ]
        return [
            pltpu.make_async_remote_copy(
                src_ref=source,
                dst_ref=target,
                send_sem=send_sem.at[2 * block + i],
                recv_sem=recv_sem.at[2 * block + i],
                device_id=other,
                device_id_type=pl.DeviceIdType.MESH,
            )
            for i, (source, target) in enumerate(pairs)
        ]

    @pl.when(step == 0)
    def _():
        for load in loads():
            load.start()
        barrier = pltpu.get_barrier_semaphore()
        pl.semaphore_signal(barrier, inc=1, device_id=other, device_id_type=pl.DeviceIdType.MESH)
        pl.semaphore_wait(barrier, 1)

    @pl.when(step < blocks)
    def _():
        slot = step % 2
        up_s[slot] = dot(first_ref[...], din_ref[...]).astype(BF16).reshape(up_s.shape[1:])
        down_s[slot] = dot(feed_ref[...], act_ref[...]).astype(BF16).T.reshape(down_s.shape[1:])

    for block in range(blocks):

        @pl.when(step == block)
        def _(block=block):
            for swap in swaps(block):
                swap.start()

    @pl.when(step == blocks)
    def _():
        for load in loads():
            load.wait()
        out_s[...] = dot(att_s[...].T, bg_s[...]).astype(BF16).reshape(out_s.shape)
        for swap in swaps(blocks):
            swap.start()

    for block in range(blocks):

        @pl.when(step == block + 1)
        def _(block=block):
            for swap in swaps(block):
                swap.wait()
            dwu_ref[:, 0] = (up_s[block % 2, :, core].astype(F32) + up_in[block].astype(F32)).astype(BF16)
            dwd_ref[...] = (down_s[block % 2, :, core].astype(F32) + down_in[block].astype(F32)).astype(BF16)

    @pl.when(step == blocks + 1)
    def _():
        for swap in swaps(blocks):
            swap.wait()
        dwo_ref[...] = (out_s[:, core].astype(F32) + out_in[...].astype(F32)).astype(BF16)


def feed_weights(first_t, din, feed_t, act, att, bg):
    dp = lax.axis_size("dp")
    features, rows = first_t.shape
    hidden = act.shape[1]
    blocks, half, low, deep = hidden // features, dp // 2, features // dp, hidden // dp
    each = half // blocks
    wide_spec = pl.BlockSpec((rows, features), lambda i: (0, jnp.minimum(i, blocks - 1)))
    anywhere = pl.BlockSpec(memory_space=pl.ANY)

    def behind(i):
        return jnp.clip(i - 1, 0, blocks - 1)

    return pl.pallas_call(
        functools.partial(feed_weights_kernel, blocks),
        grid=(blocks + 2,),
        in_specs=[
            whole_spec(first_t.shape),
            wide_spec,
            whole_spec(feed_t.shape),
            wide_spec,
            anywhere,
            anywhere,
        ],
        out_specs=[
            pl.BlockSpec((half, 1, low, features), lambda i: (0, behind(i), 0, 0)),
            pl.BlockSpec((each, deep, features), lambda i: (behind(i), 0, 0)),
            pl.BlockSpec((half, low, features), lambda i: (0, 0, 0)),
        ],
        out_shape=[
            jax.ShapeDtypeStruct((half, blocks, low, features), BF16),
            jax.ShapeDtypeStruct((half, deep, features), BF16),
            jax.ShapeDtypeStruct((half, low, features), BF16),
        ],
        scratch_shapes=[
            pltpu.VMEM((2, half, 2, low, features), BF16),
            pltpu.VMEM((blocks, half, low, features), BF16),
            pltpu.VMEM((2, each, 2, deep, features), BF16),
            pltpu.VMEM((blocks, each, deep, features), BF16),
            pltpu.VMEM((half, 2, low, features), BF16),
            pltpu.VMEM((half, low, features), BF16),
            pltpu.VMEM(att.shape, BF16),
            pltpu.VMEM(bg.shape, BF16),
            pltpu.SemaphoreType.DMA((2,)),
            pltpu.SemaphoreType.DMA((2 * blocks + 2,)),
            pltpu.SemaphoreType.DMA((2 * blocks + 2,)),
        ],
        compiler_params=pltpu.CompilerParams(
            collective_id=3, has_side_effects=True, vmem_limit_bytes=63 * MIB
        ),
        cost_estimate=cost(
            2 * rows * features * (2 * hidden + features), 4 * rows * (hidden + 2 * features)
        ),
        name="feed_weights",
    )(first_t, din, feed_t, act, att, bg)


def own_back_kernel(bg_ref, dq_ref, dk_ref, dv_ref, wq_ref, wk_ref, wv_ref, out_ref):
    total = bg_ref[0].astype(F32) + dot(dq_ref[0], wq_ref[...], NT)
    total += dot(dk_ref[0], wk_ref[...], NT)
    total += dot(dv_ref[0], wv_ref[...], NT)
    out_ref[0] = total.astype(BF16)


def rem_back_kernel(dk_ref, dv_ref, wk_ref, wv_ref, out_ref):
    total = dot(dk_ref[0], wk_ref[...], NT) + dot(dv_ref[0], wv_ref[...], NT)
    out_ref[0] = total.astype(BF16)


def tokens_back(kernel, rows, weights):
    seqs, length, features = rows[0].shape
    tile = math.gcd(length, 512)
    row_spec = pl.BlockSpec((1, tile, features), lambda s, i: (s, i, 0))
    size = rows[0].size
    return pl.pallas_call(
        kernel,
        grid=(seqs, length // tile),
        in_specs=[row_spec] * len(rows) + [whole_spec(w.shape) for w in weights],
        out_specs=row_spec,
        out_shape=jax.ShapeDtypeStruct(rows[0].shape, BF16),
        compiler_params=params(60),
        cost_estimate=cost(2 * size * features * len(weights), 2 * size * (1 + len(rows))),
        name="tokens_back",
    )(*rows, *weights)


def weights_back_kernel(tok_ref, rem_ref, dq_ref, dko_ref, dvo_ref, dkr_ref, dvr_ref,
                        wq_ref, wk_ref, wv_ref, bq_ref, bv_ref, tok_t, rem_t):
    @pl.when(pl.program_id(0) == 0)
    def _():
        tok_t[...] = tok_ref[...].T
        rem_t[...] = rem_ref[...].T

    wq_ref[...] = dot(tok_t[...], dq_ref[...]).astype(BF16)
    wk_ref[...] = (dot(tok_t[...], dko_ref[...]) + dot(rem_t[...], dkr_ref[...])).astype(BF16)
    wv_ref[...] = (dot(tok_t[...], dvo_ref[...]) + dot(rem_t[...], dvr_ref[...])).astype(BF16)
    bq_ref[...] = column_sum(dq_ref[...].astype(F32))
    bv_ref[...] = column_sum(dvo_ref[...].astype(F32)) + column_sum(dvr_ref[...].astype(F32))


def weights_back(tok, rem, dq, dko, dvo, dkr, dvr):
    rows, features = tok.shape
    others = rem.shape[0]
    wide = math.gcd(features, 256)
    own_spec = pl.BlockSpec((rows, wide), lambda j: (0, j))
    rem_spec = pl.BlockSpec((others, wide), lambda j: (0, j))
    bias_spec = pl.BlockSpec((1, wide), lambda j: (0, j))
    return pl.pallas_call(
        weights_back_kernel,
        grid=(features // wide,),
        in_specs=[
            whole_spec(tok.shape),
            whole_spec(rem.shape),
            own_spec,
            own_spec,
            own_spec,
            rem_spec,
            rem_spec,
        ],
        out_specs=[pl.BlockSpec((features, wide), lambda j: (0, j))] * 3 + [bias_spec] * 2,
        out_shape=[jax.ShapeDtypeStruct((features, features), BF16)] * 3
        + [jax.ShapeDtypeStruct((1, features), F32)] * 2,
        scratch_shapes=[
            pltpu.VMEM((features, rows), BF16),
            pltpu.VMEM((features, others), BF16),
        ],
        compiler_params=params(60),
        cost_estimate=cost(
            2 * features * features * (3 * rows + 2 * others),
            2 * (4 * tok.size + 3 * rem.size + 3 * features * features),
        ),
        name="weights_back",
    )(tok, rem, dq, dko, dvo, dkr, dvr)


def halve(value, axis, bit):
    size = lax.axis_size(axis)
    mine = (lax.axis_index(axis) >> bit) & 1
    pairs = value.reshape((value.shape[0] // 2, 2) + value.shape[1:])
    keep = lax.dynamic_index_in_dim(pairs, mine, 1, keepdims=False)
    send = lax.dynamic_index_in_dim(pairs, 1 - mine, 1, keepdims=False)
    came = lax.ppermute(send, axis, [(i, i ^ (1 << bit)) for i in range(size)])
    return keep.astype(F32) + came.astype(F32)


def scatter_sum(value, low=True):
    dp, blk = lax.axis_size("dp"), lax.axis_size("blk")
    if dp & (dp - 1) or blk & (blk - 1):
        return lax.psum_scatter(
            value.astype(F32), ("dp", "blk"), scatter_dimension=0, tiled=True
        )
    kept = value.dtype
    each = value.shape[0] // (dp * blk)
    value = value.reshape((dp, blk * each) + value.shape[1:])
    for bit in range(dp.bit_length() - 1):
        value = halve(value, "dp", bit).astype(kept)
    value = value.reshape((blk, each) + value.shape[2:])
    for bit in range(blk.bit_length() - 1):
        value = halve(value, "blk", bit)
        value = value if (2 << bit) == blk else value.astype(kept)
    return value.reshape(value.shape[1:]).astype(F32)


class Unit:
    def __init__(self, parts, rows, columns, halves, outs):
        self.parts, self.rows, self.columns = parts, rows, columns
        self.halves, self.outs = halves, outs
        self.first = 1 if parts else 0
        self.half = rows // (2 * halves)
        self.last_type = BF16 if (rows // 2) % 16 == 0 else F32


def timetable(units, bits, seqs, groups, slot_us, token_us):
    free, pending, table = {}, [], []
    slots = seqs * groups * 2

    def launch(key, now):
        kind, which, step = key
        if kind == "tokens":
            link, us = "blk", token_us
        elif kind == "vectors":
            link, us = None, 1.0
        else:
            us = units[which].rows * units[which].columns * 2e-5
            us *= 1 << max(bits - 1 - step, 0)
            us *= {0: 0.3, bits - 1: 3.0}.get(step, 1.1)
            link = {0: "core", bits - 1: "far", bits: "blk"}.get(step, "near")
        start = max(now, free.get(link, 0.0))
        if link:
            free[link] = start + us
        if kind != "tokens":
            pending.append((start + us + 2.0, key))

    for u, unit in enumerate(units):
        if unit.parts:
            launch(("unit", u, 1), 4.0)
    first_group = sum(1 for unit in units if unit.parts)
    now = 0.0
    while len(table) < slots or pending:
        slot = len(table)
        if slot < slots:
            now = (slot + 1) * slot_us
            part, major, minor = slot // (seqs * groups), slot // groups % seqs, slot % groups
            if part == 0 and minor == groups - 1:
                launch(("tokens", major, 0), now)
            major, minor = divmod(slot - seqs * groups, seqs)
            if part == 1 and minor == seqs - 1:
                launch(("unit", first_group + major, 0), now)
            if slot == slots - 1:
                launch(("vectors", 0, 0), now)
            due = sorted(p for p in pending if p[0] <= now)
        else:
            due = [min(pending)]
            now = max(now + 0.3, due[0][0])
        table.append([key for _, key in due])
        for found in due:
            pending.remove(found)
            kind, which, step = found[1]
            if step < bits:
                launch((kind, which, step + 1), now)
    tail = [key for keys in table[slots:] for key in keys]
    return table[:slots], tail + [("tokens", s, 0) for s in range(seqs)]


def order_of(step, seqs, groups):
    part = step // (seqs * groups)
    left = step - part * (seqs * groups)
    s = left // groups * (1 - part) + left % seqs * part
    h = left % groups * (1 - part) + left // seqs * part
    return part, s, h


def back_kernel(units, bits, groups, table, tail, n_out, *refs):
    (q_ref, qm_ref, g_ref, lse_ref, k_ref, km_ref, v_ref,
     tok_ref, rem_ref, wq_ref, wk_ref, wv_ref, vg_ref, vu_ref) = refs[:14]
    sources, refs = refs[14:17], list(refs[17:])
    tokens_any, rem_in, *outs = refs[:n_out]
    refs = refs[n_out:]
    kept = [refs.pop(0) for _ in units]
    landed = [
        [refs.pop(0) if k >= unit.first else None for k in range(bits)] for unit in units
    ]
    wide = [refs.pop(0) for _ in units]
    parting = [refs.pop(0) for _ in units]
    last = [refs.pop(0) for _ in units]
    (group_src, turned, dq_part, dq_s, dk_s, dv_s,
     rem_out, vec, vec_in, bias_sum, send_sem, recv_sem, local_sem, out_sem) = refs
    step = pl.program_id(0)
    steps = pl.num_programs(0)
    seqs = rem_out.shape[0]
    part, s, h = order_of(step, seqs, groups)
    features = tok_ref.shape[2]
    me, side = lax.axis_index("dp"), lax.axis_index("blk")
    core = me % 2

    def swapped(k):
        return {1: 2, 2: 1}.get(k, k) if bits > 2 else k

    def pick(values, k):
        return values[k] + (values[swapped(k)] - values[k]) * core

    bit_own = [(me // (1 << bit)) % 2 for bit in range(bits)]
    across = [me + (1 << bit) * (1 - 2 * bit_own[bit]) for bit in range(bits)]
    own = [pick(bit_own, k) for k in range(bits)]
    partner = [{"dp": pick(across, k)} for k in range(bits)] + [{"blk": 1 - side}]
    first_group = sum(1 for unit in units if unit.parts)
    lead = (slice(None),) * (bits - 1)

    def natural(digits):
        by_step = [None] + list(digits[::-1])
        return tuple(
            by_step[bit] if swapped(bit) == bit else pick(by_step, bit) for bit in range(bits - 1, 0, -1)
        )

    def digits_of(n, count):
        return [(n // (1 << (count - 1 - i))) % 2 for i in range(count)]

    sems = {}
    for u, unit in enumerate(units):
        for k in range(unit.first, bits + 1):
            sems["unit", u, k, 0] = len(sems)
    for k in range(bits + 1):
        sems["vectors", 0, k, 0] = len(sems)
    for k in range(seqs):
        sems["tokens", k, 0, 0] = len(sems)

    def remote(source, target, device, key):
        return pltpu.make_async_remote_copy(
            src_ref=source,
            dst_ref=target,
            send_sem=send_sem.at[sems[key]],
            recv_sem=recv_sem.at[sems[key]],
            device_id=device,
            device_id_type=pl.DeviceIdType.MESH,
        )

    near_sems = {}
    for u, unit in enumerate(units):
        for p in range(len(unit.parts or ())):
            for n in range(1 << min(bits - 1, 2)):
                near_sems[u, p, n] = len(near_sems)

    def spot(k, value):
        return tuple(
            own[at] if at < k else value if at == k else slice(None) for at in range(bits - 1, 0, -1)
        )

    def copies(kind, which, k):
        if kind == "tokens":
            return [remote(rem_out.at[which], rem_in.at[which], partner[bits], (kind, which, 0, 0))]
        if kind == "vectors":
            return [remote(vec.at[k], vec_in.at[k], partner[k], (kind, 0, k, 0))]
        u, unit = which, units[which]
        if k == bits:
            return [remote(parting[u], last[u], partner[bits], (kind, u, k, 0))]
        if k:
            source = kept[u].at[spot(k, 1 - own[k])]
            return [remote(source, landed[u][k], partner[k], (kind, u, k, 0))]
        source = group_src.at[(u - first_group,) + lead + (1 - core,)]
        return [remote(source, landed[u][0], partner[0], (kind, u, 0, 0))]

    def near_copies(u):
        found, row = [], 0
        for p, (source, first, rows) in enumerate(units[u].parts):
            for n in range(1 << min(bits - 1, 2)):
                digits = digits_of(n, min(bits - 1, 2))
                digits = [slice(None)] * (bits - 1 - len(digits)) + digits
                found.append(
                    pltpu.make_async_copy(
                        sources[source].at[natural(digits) + (pl.ds(first, rows),)],
                        kept[u].at[tuple(digits) + (pl.ds(row, rows),)],
                        local_sem.at[near_sems[u, p, n]],
                    )
                )
            row += rows
        return found

    def launch(*key):
        for copy in copies(*key):
            copy.start()

    def halves_of(u, which):
        unit = units[u]
        return [
            wide[u][pl.ds(pl.multiple_of(i * 2 * unit.half + which * unit.half, 8), unit.half)]
            for i in range(unit.halves)
        ]

    def receive(kind, which, k):
        for copy in copies(kind, which, k):
            copy.wait_recv()
        if kind == "tokens":
            return
        if kind == "vectors":
            vec[k + 1] = vec[k] + vec_in[k]
            if k < bits:
                launch(kind, 0, k + 1)
            return
        u, unit = which, units[which]
        if k == bits:
            for i, (mine, (out, rows, columns)) in enumerate(zip(halves_of(u, side), unit.outs)):
                came = last[u][...].astype(F32)[i * unit.half : (i + 1) * unit.half]
                outs[out][rows, columns] = mine + came
            return
        place = spot(k, own[k]) if k else lead
        open_at = [i for i, at in enumerate(place) if isinstance(at, slice)]

        def add(n, carry):
            at, where = list(place), digits_of(n, len(open_at))
            for i, digit in zip(open_at, where):
                at[i] = digit
            at = tuple(at)
            if k:
                mine, came = kept[u][at], landed[u][k][tuple(where)]
            else:
                mine = group_src[(u - first_group,) + natural(at) + (core,)]
                came = landed[u][0][natural(at)]
            total = mine.astype(F32) + came.astype(F32)
            if k == bits - 1:
                wide[u][...] = total
            else:
                kept[u][at] = total.astype(BF16)
            return carry

        if open_at:
            lax.fori_loop(0, 1 << len(open_at), add, 0)
        else:
            add(0, 0)
        if k == bits - 1:
            pieces = halves_of(u, 1 - side)
            pieces = pieces[0] if len(pieces) == 1 else jnp.concatenate(pieces, axis=0)
            parting[u][...] = pieces.astype(unit.last_type)
        launch(kind, u, k + 1)

    @pl.when(step == 0)
    def _():
        barrier = pltpu.get_barrier_semaphore()
        for other in partner:
            pl.semaphore_signal(barrier, inc=1, device_id=other, device_id_type=pl.DeviceIdType.MESH)
        pl.semaphore_wait(barrier, bits + 1)
        for u, unit in enumerate(units):
            if unit.parts:
                for copy in near_copies(u):
                    copy.start()
        for u, unit in enumerate(units):
            if unit.parts:
                for copy in near_copies(u):
                    copy.wait()
                launch("unit", u, 1)

    length = q_ref.shape[1]
    rows = pl.ds(pl.multiple_of(s * length, length), length)

    @pl.when((part == 0) & (h == 0))
    def _():
        turned[0, :, rows] = rem_ref[0].T

    @pl.when((part == 1) & (h == 0))
    def _():
        turned[1, :, rows] = tok_ref[0].T

    width = q_ref.shape[2]
    columns = pl.ds(pl.multiple_of(h * width, width), width)

    found = attend_back_part(
        q_ref[0], qm_ref[0], g_ref[0], lse_ref.at[0], k_ref[0, 0], km_ref[0, 0], v_ref[0, 0],
        dk_s.at[part, rows, columns], dv_s.at[part, rows, columns],
    )

    @pl.when(part == 0)
    def _():
        for pair, value in enumerate(found):
            dq_part[s, h, pair] = value.astype(dq_part.dtype)

    @pl.when(part == 1)
    def _():
        queries = []
        for pair, value in enumerate(found):
            value = (value + dq_part[s, h, pair].astype(F32)) * SCALE
            queries.append(value.T.astype(BF16))
        dq_s[rows, columns] = jnp.concatenate(queries, axis=1)

    @pl.when((part == 0) & (h == groups - 1))
    def _():
        total = dot(dk_s[0, rows], wk_ref[...], NT) + dot(dv_s[0, rows], wv_ref[...], NT)
        rem_out[s] = total.astype(BF16)

    for at in range(seqs):

        @pl.when(step == (at + 1) * groups - 1)
        def _(at=at):
            launch("tokens", at, 0)

    @pl.when((part == 1) & (s == seqs - 1))
    def _():
        low = features // (1 << bits)
        ones = jnp.ones((8, seqs * length), BF16)
        sums = (
            lambda: dot(turned[1], dq_s[:, columns]),
            lambda: dot(turned[1], dk_s[1, :, columns]) + dot(turned[0], dk_s[0, :, columns]),
            lambda: dot(turned[1], dv_s[1, :, columns]) + dot(turned[0], dv_s[0, :, columns]),
        )
        for i, of in enumerate(sums):
            piece = of().astype(BF16).reshape((2,) * bits + (low, width))
            group_src[(h,) + (slice(None),) * bits + (slice(i * low, (i + 1) * low),)] = piece
        bias_sum[h, 0:1] = dot(ones, dq_s[:, columns])[0:1]
        both = dot(ones, dv_s[1, :, columns]) + dot(ones, dv_s[0, :, columns])
        bias_sum[h, 1:2] = both[0:1]

    for at in range(groups):

        @pl.when(step == steps - (groups - 1 - at) * seqs - 1)
        def _(at=at):
            launch("unit", first_group + at, 0)

    @pl.when(step == steps - 1)
    def _():
        vec[0] = jnp.zeros_like(vec[0])
        vec[0, 0:6] = vg_ref[0:6]
        for at in range(groups):
            vec[0, 6:8, at * width : (at + 1) * width] = bias_sum[at, 0:2]
        blocks = vu_ref.shape[1] // features
        for at in range(blocks):
            vec[0, 8 + at : 9 + at] = vu_ref[:, at * features : (at + 1) * features]
        launch("vectors", 0, 0)

    for at, keys in enumerate(table):
        if keys:

            @pl.when(step == at)
            def _(keys=keys):
                for key in keys:
                    receive(*key)

    @pl.when(step == steps - 1)
    def _():
        each = length
        todo = list(range(0, seqs * length, each))

        def own_out(row):
            return pltpu.make_async_copy(
                dq_s.at[pl.ds(row, each)], tokens_any.at[pl.ds(row, each)], out_sem.at[row // each]
            )

        def own_rows(row):
            at = slice(row, row + each)
            total = dot(dq_s[at], wq_ref[...], NT)
            total += dot(dk_s[1, at], wk_ref[...], NT) + dot(dv_s[1, at], wv_ref[...], NT)
            dq_s[at] = total.astype(BF16)
            own_out(row).start()

        left = list(todo)
        for i, key in enumerate(tail):
            if left and i % 3 == 0:
                own_rows(left.pop(0))
            receive(*key)
        for row in left:
            own_rows(row)
        for row in todo:
            own_out(row).wait()
        shards = (1 << bits) * 2
        place = me * 2 + side
        share = features // shards
        rows = pltpu.roll(vec[bits + 1, 0:8], (shards - place) * share % features, 1)
        outs[-1][0:8] = rows[:, :PAIR]
        share = vu_ref.shape[1] // shards
        each = features // share
        row = vec[bits + 1, pl.ds(8 + place // each, 1)]
        rows = pltpu.roll(jnp.broadcast_to(row, (8, features)), (each - place % each) * share % features, 1)
        outs[-1][8:16] = rows[:, :PAIR]
        for u, unit in enumerate(units):
            for k in range(unit.first, bits + 1):
                for copy in copies("unit", u, k):
                    copy.wait_send()
        for k in range(bits + 1):
            copies("vectors", 0, k)[0].wait_send()
        for k in range(seqs):
            copies("tokens", k, 0)[0].wait_send()


def back_and_sum(q, qm, g, lse, k, km, v, tokens, rem_tokens, weights, dwd, dwu, dwo, vg, vu):
    bits = lax.axis_size("dp").bit_length() - 1
    seqs, length, features = q.shape
    width = math.gcd(features, 2 * PAIR)
    groups, pairs = features // width, width // PAIR
    low, deep, blocks = dwo.shape[1], dwd.shape[1], dwu.shape[1]
    lead = (2,) * bits
    sources = [x.reshape(lead[1:] + (-1, features)) for x in (dwd, dwu, dwo)]
    every = slice(None)
    units = []
    quarter = deep // 4
    for i in range(2):
        at = slice(i * quarter, (i + 1) * quarter)
        parts = [(0, i * quarter, quarter), (0, (2 + i) * quarter, quarter)]
        units.append(Unit(parts, 2 * quarter, features, 1, [(0, at, every)]))
    for i in range(2):
        found = range(i * blocks // 2, (i + 1) * blocks // 2)
        units.append(
            Unit(
                [(1, found[0] * low, len(found) * low)],
                len(found) * low,
                features,
                len(found),
                [(1, every, slice(b * features, (b + 1) * features)) for b in found],
            )
        )
    units.append(Unit([(2, 0, low)], low, features, 1, [(2, every, every)]))
    for h in range(groups):
        columns = slice(h * width, (h + 1) * width)
        units.append(Unit(None, 3 * low, width, 3, [(3 + i, every, columns) for i in range(3)]))
    table, tail = timetable(units, bits, seqs, groups, 4.8, length * features * 4e-5)

    half = low // 2
    out_shape = [
        jax.ShapeDtypeStruct((seqs * length, features), BF16),
        jax.ShapeDtypeStruct(q.shape, BF16),
        jax.ShapeDtypeStruct((deep // 2, features), F32),
        jax.ShapeDtypeStruct((half, blocks * features), F32),
        *(jax.ShapeDtypeStruct((half, features), F32) for _ in range(4)),
        jax.ShapeDtypeStruct((16, PAIR), F32),
    ]
    tops = lead[1:]
    scratch = [pltpu.VMEM(tops + (u.rows, u.columns), BF16) for u in units]
    for u in units:
        scratch += [pltpu.VMEM(tops[k:] + (u.rows, u.columns), BF16) for k in range(u.first, bits)]
    scratch += [pltpu.VMEM((u.rows, u.columns), F32) for u in units]
    scratch += [pltpu.VMEM((u.rows // 2, u.columns), u.last_type) for u in units] * 2
    count = len(units) * (bits + 1) + bits + 1 + seqs
    near = sum(len(u.parts) << min(bits - 1, 2) for u in units if u.parts)
    scratch += [
        pltpu.VMEM((groups,) + lead + (3 * low, width), BF16),
        pltpu.VMEM((2, features, seqs * length), BF16),
        pltpu.VMEM((seqs, groups, pairs, PAIR, length), BF16),
        pltpu.VMEM((seqs * length, features), BF16),
        pltpu.VMEM((2, seqs * length, features), BF16),
        pltpu.VMEM((2, seqs * length, features), BF16),
        pltpu.VMEM((seqs, length, features), BF16),
        pltpu.VMEM((bits + 2, 16, features), F32),
        pltpu.VMEM((bits + 1, 16, features), F32),
        pltpu.VMEM((groups, 8, width), F32),
        pltpu.SemaphoreType.DMA((count,)),
        pltpu.SemaphoreType.DMA((count,)),
        pltpu.SemaphoreType.DMA((near,)),
        pltpu.SemaphoreType.DMA((seqs,)),
    ]

    def at_step(shape, index):
        return pl.BlockSpec(shape, lambda i: index(*order_of(i, seqs, groups)))

    heads_at = at_step((1, length, width), lambda p, s, h: (s, 0, h))
    keys_at = at_step((1, 1, length, width), lambda p, s, h: (1 - p, s, 0, h))

    def rows_at(which):
        last = seqs - 1
        return pl.BlockSpec(
            (1, length, features),
            lambda i: (jnp.clip(i // groups if which == 0 else i - seqs * groups, 0, last), 0, 0),
            pipeline_mode=pl.Buffered(1),
        )

    def fixed(shape):
        return pl.BlockSpec(shape, lambda i: (0,) * len(shape), pipeline_mode=pl.Buffered(1))

    return pl.pallas_call(
        functools.partial(back_kernel, units, bits, groups, table, tail, len(out_shape)),
        grid=(2 * seqs * groups,),
        in_specs=[
            heads_at,
            at_step((1, length, PAIR), lambda p, s, h: (s, 0, 0)),
            heads_at,
            at_step((1, pairs, 8, length), lambda p, s, h: (s, h, 0, 0)),
            keys_at,
            at_step((1, 1, length, PAIR), lambda p, s, h: (1 - p, s, 0, 0)),
            keys_at,
            rows_at(1),
            rows_at(0),
        ]
        + [whole_spec(w.shape) for w in weights + (vg, vu)]
        + [pl.BlockSpec(memory_space=pl.ANY)] * 3,
        out_specs=[pl.BlockSpec(memory_space=pl.ANY)] * 2
        + [fixed(s.shape) for s in out_shape[2:]],
        out_shape=out_shape,
        scratch_shapes=scratch,
        compiler_params=pltpu.CompilerParams(
            collective_id=1, has_side_effects=True, vmem_limit_bytes=63 * MIB
        ),
        cost_estimate=cost(80 * q.size * length, 2 * q.size * 14, 2 * q.size * length // HEAD),
        name="back_and_sum",
    )(q, qm, g, lse, k, km, v, tokens, rem_tokens, *weights, vg, vu, *sources)


def finish_kernel(residual_ref, own_ref, rem_ref, *refs):
    ins, outs = refs[:7], refs[7:]
    total = residual_ref[...].astype(F32) + own_ref[...].astype(F32) + rem_ref[...].astype(F32)
    outs[0][...] = total.astype(BF16)

    @pl.when(pl.program_id(0) == 0)
    def _():
        for source, target in zip(ins[:6], outs[1:7]):
            target[...] = source[...]
        for i, target in enumerate(outs[7:]):
            target[...] = ins[6][i, : target.shape[0]]


def finish(residual, own, rem, matrices, vectors, shares):
    seqs, length, features = own.shape
    tile = math.gcd(length, 512)
    tiles = length // tile
    row_spec = pl.BlockSpec((1, tile, features), lambda i: (i // tiles, i % tiles, 0))

    def fixed(shape):
        return pl.BlockSpec(shape, lambda i: (0,) * len(shape))

    shapes = [m.shape for m in matrices] + [(n,) for n in shares]
    return pl.pallas_call(
        finish_kernel,
        grid=(seqs * tiles,),
        in_specs=[row_spec] * 3 + [fixed(m.shape) for m in matrices] + [fixed(vectors.shape)],
        out_specs=[row_spec] + [fixed(s) for s in shapes],
        out_shape=[jax.ShapeDtypeStruct(own.shape, BF16)] + [jax.ShapeDtypeStruct(s, F32) for s in shapes],
        compiler_params=params(60),
        cost_estimate=cost(2 * own.size, 8 * own.size),
        name="finish",
    )(residual, own, rem, *matrices, vectors)


def back_plainly(q, qm, o, g, lse, own, rem, bg, tokens, rem_tokens, weights, dwd, dwu, dwo, vg, vu):
    seqs, length, features = q.shape
    dp, blk = lax.axis_size("dp"), lax.axis_size("blk")
    dq, dko, dvo, dkr, dvr = attend_back(q, qm, o, g, lse, own, rem)
    rem_gradient = tokens_back(rem_back_kernel, (dkr, dvr), weights[1:])
    came = [
        lax.ppermute(part, "blk", [((i + r) % blk, i) for i in range(blk)])
        for r, part in enumerate(jnp.split(rem_gradient, blk - 1, axis=1), 1)
    ]
    flat = [v.reshape(-1, features) for v in (tokens, rem_tokens, dq, dko, dvo, dkr, dvr)]
    dwq, dwk, dwv, dbq, dbv = weights_back(*flat)
    total = tokens_back(own_back_kernel, (bg, dq, dko, dvo), weights).astype(F32)
    for part in came:
        total += part.astype(F32)
    dwu = jnp.moveaxis(dwu[0], 0, 1).reshape(features, -1)
    summed = [scatter_sum(w) for w in (dwd, dwu, dwo, dwq, dwk, dwv)]
    rows = [vg[i] for i in range(6)] + [dbq, dbv, vu]
    rows = [scatter_sum(v.reshape(dp * blk, -1)) for v in rows]
    return [total.astype(BF16)] + summed + [[v[0] for v in rows]]


def body(
    tokens,
    query_weight,
    query_bias,
    key_weight,
    value_weight,
    value_bias,
    out_weight,
    out_bias,
    gain_one,
    shift_one,
    up_weight,
    up_bias,
    down_weight,
    down_bias,
    gain_two,
    shift_two,
    group_ids,
    valid_mask,
    cotangent,
):
    seqs, length, features = tokens.shape
    rows = seqs * length
    blk = lax.axis_size("blk")

    def from_others(value):
        found = [
            lax.ppermute(value, "blk", [(i, (i + r) % blk) for i in range(blk)])
            for r in range(1, blk)
        ]
        return found[0] if len(found) == 1 else jnp.concatenate(found, axis=1)

    codes = jnp.where(valid_mask == 1, group_ids, -1)
    dp = lax.axis_size("dp")
    by_kernel = blk == 2 and dp & (dp - 1) == 0 and dp > 1 and (features // dp) % 16 == 0
    projections = (query_weight, key_weight, value_weight)
    vectors = (
        query_bias,
        value_bias,
        out_bias,
        gain_one,
        shift_one,
        down_bias,
        gain_two,
        shift_two,
    )

    if by_kernel:
        (block_out, branch_gradient, attended_gradient, attended, lse, query_mask, key_masks,
         first_t, feed_t, vector_gradients, up_bias_gradient, queries, keys, values,
         rem_tokens, active, inner_gradient) = front(
            tokens,
            group_ids,
            valid_mask,
            cotangent,
            vectors,
            up_bias,
            projections + (out_weight, up_weight, down_weight),
        )
        dwu, dwd, dwo = feed_weights(
            first_t,
            inner_gradient.reshape(rows, -1),
            feed_t,
            active.reshape(rows, -1),
            attended.reshape(rows, features),
            branch_gradient.reshape(rows, features),
        )
        own_gradient, rem_gradient, *matrices, vectors = back_and_sum(
            queries,
            query_mask,
            attended_gradient,
            lse,
            keys,
            key_masks,
            values,
            tokens,
            rem_tokens,
            projections,
            dwd,
            dwu,
            dwo,
            vector_gradients,
            up_bias_gradient,
        )
        shares = [features // (dp * blk)] * 8 + [up_bias.size // (dp * blk)]
        found = finish(
            branch_gradient, own_gradient.reshape(tokens.shape), rem_gradient, matrices, vectors, shares
        )
        tokens_gradient, dwd, dwu, dwo, dwq, dwk, dwv, *rows_left = found
    else:
        rem_tokens = from_others(tokens)
        rem_codes = from_others(codes.astype(BF16)).astype(jnp.int32)
        slot = jnp.arange(PAIR, dtype=jnp.int32) % HEAD

        def key_mask(code):
            return jnp.where(code[:, :, None] == slot, 0.0, MASKED).astype(BF16)

        query_mask = (group_ids[:, :, None] == slot).astype(BF16)
        vectors = jnp.stack(vectors).astype(F32)
        queries, own_keys, own_values = project(tokens, vectors, projections)
        rem_keys, rem_values = project(rem_tokens, vectors, projections[1:])
        own = (own_keys, key_mask(codes), own_values)
        rem = (rem_keys, key_mask(rem_codes), rem_values)
        attended, lse = attend(queries, query_mask, own, rem)
        (block_out, branch_gradient, attended_gradient, vector_gradients, up_bias_gradient,
         dwu, dwd, dwo) = feed_both_ways(
            tokens.reshape(rows, features),
            attended.reshape(rows, features),
            cotangent.reshape(rows, features),
            vectors[2:],
            up_bias.astype(F32)[None],
            out_weight,
            up_weight,
            down_weight,
            1,
        )
        tokens_gradient, dwd, dwu, dwo, dwq, dwk, dwv, rows_left = back_plainly(
            queries,
            query_mask,
            attended,
            attended_gradient.reshape(tokens.shape),
            lse,
            own,
            rem,
            branch_gradient.reshape(tokens.shape),
            tokens,
            rem_tokens,
            projections,
            dwd,
            dwu,
            dwo,
            vector_gradients,
            up_bias_gradient,
        )
    dbo, dg1, ds1, dbd, dg2, ds2, dbq, dbv, dbu = rows_left
    return (
        block_out.reshape(tokens.shape),
        tokens_gradient,
        dwq,
        dbq,
        dwk,
        dwv,
        dbv,
        dwo,
        dbo,
        dg1,
        ds1,
        dwu,
        dbu,
        dwd,
        dbd,
        dg2,
        ds2,
    )


def solution(mesh):
    rows, shared, pair = P("dp", "blk", None), P(), P("dp", "blk")
    matrix, vector = P(("dp", "blk"), None), P(("dp", "blk"))
    return jax.shard_map(
        body,
        mesh=mesh,
        in_specs=(rows,) + (shared,) * 15 + (pair, pair, rows),
        out_specs=(
            rows,
            rows,
            matrix,
            vector,
            matrix,
            matrix,
            vector,
            matrix,
            vector,
            vector,
            vector,
            matrix,
            vector,
            matrix,
            vector,
            vector,
            vector,
        ),
        check_vma=False,
    )
```

```python
import functools
import math

import jax
import jax.numpy as jnp
from jax import lax
from jax.experimental import pallas as pl
from jax.experimental.pallas import tpu as pltpu
from jax.sharding import PartitionSpec as P

HEAD = 64
PAIR = 2 * HEAD
EPSILON = 1e-12
MASKED = -1e30
FLOOR = -3e38
SCALE = HEAD**-0.5
EXPO = SCALE * math.log2(math.e)
NN = (((1,), (0,)), ((), ()))
NT = (((1,), (1,)), ((), ()))
F32 = jnp.float32
BF16 = jnp.bfloat16
MIB = 1 << 20
FEED_ROWS = 256


def dot(left, right, dims=NN):
    return lax.dot_general(left, right, dims, preferred_element_type=F32)


def whole_spec(shape):
    return pl.BlockSpec(shape, lambda *_: (0,) * len(shape), pipeline_mode=pl.Buffered(1))


def params(limit):
    return pltpu.CompilerParams(vmem_limit_bytes=limit * MIB)


def cost(flops, touched, exps=0):
    return pl.CostEstimate(flops=int(flops), bytes_accessed=int(touched), transcendentals=int(exps))


def project_kernel(has_query, *refs):
    if has_query:
        x_ref, bias_ref, wq_ref, wk_ref, wv_ref, q_ref, k_ref, v_ref = refs
    else:
        x_ref, bias_ref, wk_ref, wv_ref, k_ref, v_ref = refs
    x = x_ref[0]
    if has_query:
        q_ref[0] = (dot(x, wq_ref[...]) + bias_ref[0:1]).astype(BF16)
    k_ref[0] = dot(x, wk_ref[...]).astype(BF16)
    v_ref[0] = (dot(x, wv_ref[...]) + bias_ref[1:2]).astype(BF16)


def project(x, bias, weights):
    seqs, length, features = x.shape
    tile = math.gcd(length, 512)
    grid = (seqs, length // tile)
    row_spec = pl.BlockSpec((1, tile, features), lambda s, i: (s, i, 0))
    return pl.pallas_call(
        functools.partial(project_kernel, len(weights) == 3),
        grid=grid,
        in_specs=[row_spec, whole_spec(bias.shape)] + [whole_spec(w.shape) for w in weights],
        out_specs=[row_spec] * len(weights),
        out_shape=[jax.ShapeDtypeStruct(x.shape, BF16)] * len(weights),
        compiler_params=params(60),
        cost_estimate=cost(
            2 * x.size * features * len(weights), 2 * x.size * (1 + len(weights))
        ),
        name="project",
    )(x, bias, *weights)


def low_lanes():
    return lax.broadcasted_iota(jnp.int32, (1, PAIR), 1) < HEAD


def attend_group(q, qm, sources, o_ref, lse_ref):
    length = q.shape[0]
    tile = math.gcd(length, 512)
    low = low_lanes()
    one = jnp.ones((1, PAIR), BF16)
    todo = [
        (pair, row, head)
        for pair in range(q.shape[1] // PAIR)
        for row in range(0, length, tile)
        for head in range(2)
    ]

    def lanes_of(pair):
        return slice(pair * PAIR, (pair + 1) * PAIR)

    def mine_of(head):
        return ~low if head else low

    def scores_of(pair, row, head):
        mine, lanes = mine_of(head), lanes_of(pair)
        q_side = jnp.where(mine, q[row : row + tile, lanes], qm[row : row + tile])
        return [dot(q_side, jnp.where(mine, k[:, lanes], km), NT) for k, km, _ in sources]

    ahead = scores_of(*todo[0])
    for i, (pair, row, head) in enumerate(todo):
        scores = ahead
        if i + 1 < len(todo):
            ahead = scores_of(*todo[i + 1])
        top = functools.reduce(
            jnp.maximum, [jnp.max(part, axis=-1, keepdims=True) for part in scores]
        )
        weights = [jnp.exp2((part - top) * EXPO).astype(BF16) for part in scores]
        total = sum(
            dot(w, jnp.where(mine_of(head), v[:, lanes_of(pair)], one))
            for w, (_, _, v) in zip(weights, sources)
        )
        if head == 0:
            earlier, earlier_top = total, top
            continue
        totals = pltpu.roll(jnp.where(low, total, earlier), HEAD, 1)
        rows = slice(row, row + tile)
        o_ref[rows, lanes_of(pair)] = (jnp.where(low, earlier, total) / totals).astype(BF16)
        lse = (jnp.where(low, earlier_top, top) * EXPO + jnp.log2(totals)).T
        lse_ref[pair, 0:1, rows] = lse[0:1]
        lse_ref[pair, 1:2, rows] = lse[HEAD : HEAD + 1]


def attend_kernel(q_ref, qm_ref, ko_ref, kmo_ref, vo_ref, kr_ref, kmr_ref, vr_ref, o_ref, lse_ref):
    sources = [(ko_ref[0], kmo_ref[0], vo_ref[0]), (kr_ref[0], kmr_ref[0], vr_ref[0])]
    attend_group(q_ref[0], qm_ref[0], sources, o_ref.at[0], lse_ref.at[0])


def pair_spec(length, lanes):
    return pl.BlockSpec((1, length, lanes), lambda s, h: (s, 0, h))


def mask_spec(length):
    return pl.BlockSpec((1, length, PAIR), lambda s, h: (s, 0, 0))


def lse_spec(length, lanes):
    return pl.BlockSpec((1, lanes // PAIR, 8, length), lambda s, h: (s, h, 0, 0))


def attend(q, qm, own, rem):
    seqs, length, features = q.shape
    lanes = math.gcd(features, 2 * PAIR)
    other = rem[0].shape[1]
    own_spec, rem_spec = pair_spec(length, lanes), pair_spec(other, lanes)
    return pl.pallas_call(
        attend_kernel,
        grid=(seqs, features // lanes),
        in_specs=[own_spec, mask_spec(length)]
        + [own_spec, mask_spec(length), own_spec]
        + [rem_spec, mask_spec(other), rem_spec],
        out_specs=[own_spec, lse_spec(length, lanes)],
        out_shape=[
            jax.ShapeDtypeStruct(q.shape, BF16),
            jax.ShapeDtypeStruct((seqs, features // PAIR, 8, length), F32),
        ],
        compiler_params=params(60),
        cost_estimate=cost(
            16 * q.size * (length + other), 2 * q.size * 6, q.size * (length + other) // HEAD
        ),
        name="attend",
    )(q, qm, *own, *rem)


def attend_back_part(q, qm, g, lse_ref, k, km, v, dk_ref, dv_ref):
    low = low_lanes()
    none = jnp.zeros((1, PAIR), BF16)
    pairs = q.shape[1] // PAIR
    todo = [(pair, head) for pair in range(pairs) for head in range(2)]

    def lanes_of(pair):
        return slice(pair * PAIR, (pair + 1) * PAIR)

    def mine_of(head):
        return ~low if head else low

    def products(pair, head):
        mine, lanes = mine_of(head), lanes_of(pair)
        return (
            dot(jnp.where(mine, k[:, lanes], km), jnp.where(mine, q[:, lanes], qm), NT),
            dot(jnp.where(mine, v[:, lanes], none), g[:, lanes], NT),
        )

    found = []
    ahead = products(*todo[0])
    for i, (pair, head) in enumerate(todo):
        scores, grads = ahead
        if i + 1 < len(todo):
            ahead = products(*todo[i + 1])
        lanes, mine = lanes_of(pair), mine_of(head)
        if head == 0:
            k_t = k[:, lanes].T
            dk = dv = 0.0
            dq = []
        probs = jnp.exp2(scores * EXPO - lse_ref[pair, head : head + 1, :])
        grads = (probs * (grads - lse_ref[pair, 2 + head : 3 + head, :])).astype(BF16)
        dv += dot(probs.astype(BF16), jnp.where(mine, g[:, lanes], none))
        dk += dot(grads, jnp.where(mine, q[:, lanes], none))
        dq.append(dot(k_t[head * HEAD : (head + 1) * HEAD], grads))
        if head == 1:
            dk_ref[:, lanes] = (dk * SCALE).astype(BF16)
            dv_ref[:, lanes] = dv.astype(BF16)
            found.append(jnp.concatenate(dq, axis=0))
    return found


def attend_back_kernel(q_ref, qm_ref, g_ref, lse_ref, ko_ref, kmo_ref, vo_ref, kr_ref, kmr_ref,
                       vr_ref, dq_ref, dko_ref, dvo_ref, dkr_ref, dvr_ref):
    parts = ((ko_ref, kmo_ref, vo_ref, dko_ref, dvo_ref), (kr_ref, kmr_ref, vr_ref, dkr_ref, dvr_ref))
    found = [
        attend_back_part(
            q_ref[0], qm_ref[0], g_ref[0], lse_ref.at[0], k[0], km[0], v[0], dk.at[0], dv.at[0]
        )
        for k, km, v, dk, dv in parts
    ]
    for pair, both in enumerate(zip(*found)):
        dq_ref[0, :, pair * PAIR : (pair + 1) * PAIR] = (sum(both) * SCALE).T.astype(BF16)


def attend_back(q, qm, o, g, lse, own, rem):
    seqs, length, features = q.shape
    delta = (g.astype(F32) * o.astype(F32)).reshape(seqs, length, features // PAIR, 2, HEAD).sum(-1)
    lse = lax.dynamic_update_slice(lse, jnp.transpose(delta, (0, 2, 3, 1)), (0, 0, 2, 0))
    lanes = math.gcd(features, 2 * PAIR)
    other = rem[0].shape[1]
    own_spec, rem_spec = pair_spec(length, lanes), pair_spec(other, lanes)
    return pl.pallas_call(
        attend_back_kernel,
        grid=(seqs, features // lanes),
        in_specs=[own_spec, mask_spec(length), own_spec, lse_spec(length, lanes)]
        + [own_spec, mask_spec(length), own_spec]
        + [rem_spec, mask_spec(other), rem_spec],
        out_specs=[own_spec] * 3 + [rem_spec] * 2,
        out_shape=[jax.ShapeDtypeStruct(q.shape, BF16)] * 3
        + [jax.ShapeDtypeStruct(rem[0].shape, BF16)] * 2,
        compiler_params=params(60),
        cost_estimate=cost(
            40 * q.size * (length + other), 2 * q.size * 14, q.size * (length + other) // HEAD
        ),
        name="attend_back",
    )(q, qm, g, lse, *own, *rem)


def gelu_and_slope(x):
    bell = jnp.exp2(x * x * (-0.5 * math.log2(math.e)))
    below = 1.0 + (0.3275911 / math.sqrt(2.0)) * jnp.abs(x)
    t = pl.reciprocal(below, approx=True)
    t = t * (2.0 - below * t)
    poly = 1.061405429 * t - 1.453152027
    poly = poly * t + 1.421413741
    poly = poly * t - 0.284496736
    poly = poly * t + 0.254829592
    tail = (0.5 * poly) * t * bell
    share = jnp.where(x >= 0.0, 1.0 - tail, tail)
    return x * share, share + x * bell * (1.0 / math.sqrt(2.0 * math.pi))


def mean(values):
    return jnp.sum(values, axis=-1, keepdims=True) * (1.0 / values.shape[-1])


def norm_parts(values):
    centred = values - mean(values)
    scale = lax.rsqrt(mean(centred * centred) + EPSILON)
    return centred * scale, scale


def norm_back(upper, normed, scale):
    return scale * (upper - mean(upper) - normed * mean(upper * normed))


def column_sum(values):
    return jnp.sum(values, axis=0, keepdims=True)


def feed_kernel(layout, tok_ref, att_ref, cot_ref, vec_ref, bu_ref, wo_ref, wu_ref, wd_ref,
                out_ref, bg_ref, ag_ref, vg_ref, dbu_ref, dwu_ref, dwd_ref, dwo_ref,
                act_s, din_s, first_t, feed_t, att_t, bg_s):
    tiles, ff_steps, chunk, wide, narrow = layout
    step = pl.program_id(0)
    tile = tok_ref.shape[0]
    hidden = act_s.shape[1]
    vec = [vec_ref[i : i + 1] for i in range(6)]
    out_bias, gain_one, shift_one, down_bias, gain_two, shift_two = vec

    @pl.when(step == 0)
    def _():
        vg_ref[...] = jnp.zeros_like(vg_ref)
        dbu_ref[...] = jnp.zeros_like(dbu_ref)

    @pl.when(step < tiles)
    def _():
        start = pl.multiple_of(step * tile, tile)
        rows = pl.ds(start, tile)
        att = att_ref[...]
        normed_one, scale_one = norm_parts(
            tok_ref[...].astype(F32) + (dot(att, wo_ref[...]) + out_bias)
        )
        first = normed_one * gain_one + shift_one
        first_low = first.astype(BF16)
        first_t[:, rows] = first_low.T
        att_t[:, rows] = att.T
        feed = jnp.zeros_like(first) + down_bias
        spans = [slice(c, c + chunk) for c in range(0, hidden, chunk)]
        ahead = dot(first_low, wu_ref[:, spans[0]])
        for i, cols in enumerate(spans):
            inner = ahead + bu_ref[:, cols]
            if i + 1 < len(spans):
                ahead = dot(first_low, wu_ref[:, spans[i + 1]])
            active, slope = gelu_and_slope(inner)
            active = active.astype(BF16)
            act_s[rows, cols] = active
            din_s[rows, cols] = slope.astype(BF16)
            feed += dot(active, wd_ref[cols])
        normed_two, scale_two = norm_parts(first + feed)
        out_ref[...] = (normed_two * gain_two + shift_two).astype(BF16)
        cot = cot_ref[...].astype(F32)
        second = norm_back(cot * gain_two, normed_two, scale_two)
        feed_low = second.astype(BF16)
        feed_t[:, rows] = feed_low.T
        back = second
        ahead = dot(feed_low, wd_ref[spans[0]], NT)
        for i, cols in enumerate(spans):
            inner = ahead
            if i + 1 < len(spans):
                ahead = dot(feed_low, wd_ref[spans[i + 1]], NT)
            inner = (inner * din_s[rows, cols].astype(F32)).astype(BF16)
            din_s[rows, cols] = inner
            dbu_ref[:, cols] += column_sum(inner.astype(F32))
            back += dot(inner, wu_ref[:, cols], NT)
        residual = norm_back(back * gain_one, normed_one, scale_one)
        branch_low = residual.astype(BF16)
        bg_ref[...] = branch_low
        bg_s[rows] = branch_low
        ag_ref[...] = dot(branch_low, wo_ref[...], NT).astype(BF16)
        for i, values in enumerate(
            (
                branch_low.astype(F32),
                back * normed_one,
                back,
                feed_low.astype(F32),
                cot * normed_two,
                cot,
            )
        ):
            vg_ref[i : i + 1] += column_sum(values)

    @pl.when((step >= tiles) & (step < tiles + ff_steps))
    def _():
        cols = pl.ds(pl.multiple_of((step - tiles) * wide, wide), wide)
        dwu = dot(first_t[...], din_s[:, cols]).astype(BF16)
        dwu_ref[...] = dwu.reshape(dwu_ref.shape)
        dwd_ref[...] = dot(feed_t[...], act_s[:, cols]).astype(BF16).T

    @pl.when(step >= tiles + ff_steps)
    def _():
        cols = pl.ds(pl.multiple_of((step - tiles - ff_steps) * narrow, narrow), narrow)
        dwo_ref[...] = dot(att_t[...], bg_s[:, cols]).astype(BF16)


def feed_both_ways(tokens, attended, cotangent, vectors, up_bias, wo, wu, wd, groups):
    rows, features = tokens.shape
    hidden = wu.shape[1]
    tile = math.gcd(rows, 256)
    tiles = rows // tile
    wide, narrow = features, math.gcd(features, 384)
    ff_steps, out_steps = hidden // wide, features // narrow
    layout = (tiles, ff_steps, math.gcd(hidden, 512), wide, narrow)
    blocked = (groups, ff_steps, features // groups, wide)
    row_spec = pl.BlockSpec((tile, features), lambda i: (jnp.minimum(i, tiles - 1), 0))

    def ff_at(i):
        return jnp.clip(i - tiles, 0, ff_steps - 1)

    return pl.pallas_call(
        functools.partial(feed_kernel, layout),
        grid=(tiles + ff_steps + out_steps,),
        in_specs=[row_spec] * 3
        + [whole_spec(a.shape) for a in (vectors, up_bias, wo, wu, wd)],
        out_specs=[row_spec] * 3
        + [
            pl.BlockSpec((8, features), lambda i: (0, 0)),
            pl.BlockSpec((1, hidden), lambda i: (0, 0)),
            pl.BlockSpec((groups, 1) + blocked[2:], lambda i: (0, ff_at(i), 0, 0)),
            pl.BlockSpec((wide, features), lambda i: (ff_at(i), 0)),
            pl.BlockSpec(
                (features, narrow),
                lambda i: (0, jnp.clip(i - tiles - ff_steps, 0, out_steps - 1)),
            ),
        ],
        out_shape=[jax.ShapeDtypeStruct(tokens.shape, BF16)] * 3
        + [
            jax.ShapeDtypeStruct((8, features), F32),
            jax.ShapeDtypeStruct((1, hidden), F32),
            jax.ShapeDtypeStruct(blocked, BF16),
            jax.ShapeDtypeStruct(wd.shape, BF16),
            jax.ShapeDtypeStruct(wo.shape, BF16),
        ],
        scratch_shapes=[
            pltpu.VMEM((rows, hidden), BF16),
            pltpu.VMEM((rows, hidden), BF16),
            pltpu.VMEM((features, rows), BF16),
            pltpu.VMEM((features, rows), BF16),
            pltpu.VMEM((features, rows), BF16),
            pltpu.VMEM((rows, features), BF16),
        ],
        compiler_params=params(60),
        cost_estimate=cost(
            6 * rows * features * (features + 2 * hidden),
            2 * (6 * rows * features + 4 * features * hidden + 2 * features * features),
            2 * rows * hidden,
        ),
        name="feed_both_ways",
    )(tokens, attended, cotangent, vectors, up_bias, wo, wu, wd)


def spread(row):
    return jnp.broadcast_to(row, (PAIR, row.shape[1])).T


def as_row(ref):
    return ref[...].astype(F32).reshape(1, ref.shape[0])


def front_kernel(tokens_ref, group_ref, valid_ref, cot_ref, bq_ref, bv_ref, bo_ref, g1_ref, s1_ref, bd_ref,
                 g2_ref, s2_ref, bu_in, wq_any, wk_any, wv_any, wo_any, wu_any, wd_any,
                 out_ref, bg_ref, ag_ref, att_ref, lse_ref, qm_ref, km_ref,
                 first_t, feed_t, vg_ref, dbu_ref, q_any, k_any, v_any, rem_any, act_any, din_any,
                 wq, wk, wv, wo, wu, wd, tok_s, q_s, k_s, v_s, kr_s, vr_s, rem_s, own_codes, code_s, act_s, din_s,
                 bu_ref, weight_sem, out_sem, send_sem, recv_sem):
    s = pl.program_id(0)
    seqs = tok_s.shape[0]
    length, features = tok_s.shape[1:]
    hidden = act_s.shape[1]
    side = lax.axis_index("blk")
    other = {"blk": 1 - side}
    query_bias, value_bias, out_bias, gain_one, shift_one, down_bias, gain_two, shift_two = [
        as_row(ref) for ref in (bq_ref, bv_ref, bo_ref, g1_ref, s1_ref, bd_ref, g2_ref, s2_ref)
    ]
    pairs_of = [(wq_any, wq), (wk_any, wk), (wv_any, wv), (wo_any, wo), (wu_any, wu), (wd_any, wd)]

    def weight(i):
        return pltpu.make_async_copy(*pairs_of[i], weight_sem.at[i])

    def remote(source, target, at):
        return pltpu.make_async_remote_copy(
            src_ref=source,
            dst_ref=target,
            send_sem=send_sem.at[at],
            recv_sem=recv_sem.at[at],
            device_id=other,
            device_id_type=pl.DeviceIdType.MESH,
        )

    def exchange(at):
        return remote(tokens_ref.at[at], rem_s.at[at], at)

    def code_exchange():
        return remote(own_codes, code_s, seqs)

    def whole_out(i):
        source, target = ((q_s, q_any), (k_s, k_any.at[0]), (v_s, v_any.at[0]))[i]
        return pltpu.make_async_copy(source, target, out_sem.at[i])

    def part_out(i, at):
        source, target = (
            (kr_s, k_any.at[1, at]),
            (vr_s, v_any.at[1, at]),
            (rem_s.at[at], rem_any.at[at]),
            (act_s, act_any.at[at]),
            (din_s, din_any.at[at]),
        )[i]
        return pltpu.make_async_copy(source, target, out_sem.at[3 + i])

    @pl.when(s == 0)
    def _():
        barrier = pltpu.get_barrier_semaphore()
        pl.semaphore_signal(barrier, inc=1, device_id=other, device_id_type=pl.DeviceIdType.MESH)
        load = pltpu.make_async_copy(tokens_ref, tok_s, weight_sem.at[len(pairs_of)])
        load.start()
        for i in range(3):
            weight(i).start()
        codes = jnp.where(valid_ref[...] == 1, group_ref[...], -1).astype(F32)
        own_codes[...] = jnp.zeros_like(own_codes)
        own_codes[0:seqs] = codes
        pl.semaphore_wait(barrier, 1)
        exchange(0).start()
        code_exchange().start()
        for i in range(3, len(pairs_of)):
            weight(i).start()
        vg_ref[...] = jnp.zeros_like(vg_ref)
        dbu_ref[...] = jnp.zeros_like(dbu_ref)
        bu_ref[...] = as_row(bu_in)
        load.wait()
        for i in range(3):
            weight(i).wait()

        def project_own(at, carry):
            x = tok_s[at]
            q_s[at] = (dot(x, wq[...]) + query_bias).astype(BF16)
            k_s[at] = dot(x, wk[...]).astype(BF16)
            v_s[at] = (dot(x, wv[...]) + value_bias).astype(BF16)
            return carry

        lax.fori_loop(0, seqs, project_own, 0)
        for i in range(3):
            whole_out(i).start()
        for i in range(3, len(pairs_of)):
            weight(i).wait()
        code_exchange().wait_recv()
        exchange(0).wait_send()
        if seqs > 1:
            exchange(1).start()

    for at in range(seqs):

        @pl.when(s == at)
        def _(at=at):
            exchange(at).wait_recv()
            if at:
                for i in range(3):
                    part_out(i, at - 1).wait()

    x = rem_s[s]
    kr_s[...] = dot(x, wk[...]).astype(BF16)
    vr_s[...] = (dot(x, wv[...]) + value_bias).astype(BF16)
    slot = lax.broadcasted_iota(jnp.int32, (1, PAIR), 1) % HEAD
    slot = slot.astype(F32)
    groups_row = group_ref[pl.ds(s, 1)].astype(F32)
    qm_ref[0] = jnp.where(spread(groups_row) == slot, 1.0, 0.0).astype(BF16)
    km_ref[0, 0] = jnp.where(spread(own_codes[pl.ds(s, 1)]) == slot, 0.0, MASKED).astype(BF16)
    km_ref[1, 0] = jnp.where(spread(code_s[pl.ds(s, 1)]) == slot, 0.0, MASKED).astype(BF16)
    for at in range(seqs):

        @pl.when(s == at)
        def _(at=at):
            for i in range(3):
                part_out(i, at).start()

    groups = features // (2 * PAIR)

    def heads(group, carry):
        lanes = pl.ds(pl.multiple_of(group * 2 * PAIR, 2 * PAIR), 2 * PAIR)
        attend_group(
            q_s[s, :, lanes],
            qm_ref[0],
            [(k_s[s, :, lanes], km_ref[0, 0], v_s[s, :, lanes]), (kr_s[:, lanes], km_ref[1, 0], vr_s[:, lanes])],
            att_ref.at[0, :, lanes],
            lse_ref.at[0, pl.ds(group * 2, 2)],
        )
        return carry

    lax.fori_loop(0, groups, heads, 0)

    for at in range(1, seqs):

        @pl.when(s == at)
        def _(at=at):
            for i in range(3, 5):
                part_out(i, at - 1).wait()

    tile = math.gcd(length, FEED_ROWS)
    chunk = math.gcd(hidden, 1024)
    spans = [slice(c, c + chunk) for c in range(0, hidden, chunk)]

    def feed_rows(t, carry):
        rows = pl.ds(pl.multiple_of(t * tile, tile), tile)
        att = att_ref[0, rows]
        normed_one, scale_one = norm_parts(
            tok_s[s, rows].astype(F32) + (dot(att, wo[...]) + out_bias)
        )
        first = normed_one * gain_one + shift_one
        first_low = first.astype(BF16)
        first_t[:, rows] = first_low.T
        feed = jnp.zeros_like(first) + down_bias
        ahead = dot(first_low, wu[:, spans[0]])
        for i, cols in enumerate(spans):
            inner = ahead + bu_ref[:, cols]
            if i + 1 < len(spans):
                ahead = dot(first_low, wu[:, spans[i + 1]])
            active, slope = gelu_and_slope(inner)
            active = active.astype(BF16)
            act_s[rows, cols] = active
            din_s[rows, cols] = slope.astype(BF16)
            feed += dot(active, wd[cols])
        normed_two, scale_two = norm_parts(first + feed)
        out_ref[0, rows] = (normed_two * gain_two + shift_two).astype(BF16)
        cot = cot_ref[0, rows].astype(F32)
        second = norm_back(cot * gain_two, normed_two, scale_two)
        feed_low = second.astype(BF16)
        feed_t[:, rows] = feed_low.T
        back = second
        ahead = dot(feed_low, wd[spans[0]], NT)
        for i, cols in enumerate(spans):
            inner = ahead
            if i + 1 < len(spans):
                ahead = dot(feed_low, wd[spans[i + 1]], NT)
            inner = (inner * din_s[rows, cols].astype(F32)).astype(BF16)
            din_s[rows, cols] = inner
            dbu_ref[:, cols] += column_sum(inner.astype(F32))
            back += dot(inner, wu[:, cols], NT)
        residual = norm_back(back * gain_one, normed_one, scale_one)
        branch_low = residual.astype(BF16)
        bg_ref[0, rows] = branch_low
        att_grad = dot(branch_low, wo[...], NT).astype(BF16)
        ag_ref[0, rows] = att_grad
        product = att_grad.astype(F32) * att.astype(F32)
        coarse = product.astype(BF16)
        fine = (product - coarse.astype(F32)).astype(BF16)
        heads_count = features // HEAD
        of_head = lax.broadcasted_iota(jnp.int32, (heads_count, features), 1) // HEAD
        selector = (of_head == lax.broadcasted_iota(jnp.int32, of_head.shape, 0)).astype(F32)
        selector = selector.astype(BF16)
        delta = dot(selector, coarse, NT) + dot(selector, fine, NT)
        for pair in range(features // PAIR):
            lse_ref[0, pair, 2:4, rows] = delta[2 * pair : 2 * pair + 2]
        for i, values in enumerate(
            (
                branch_low.astype(F32),
                back * normed_one,
                back,
                feed_low.astype(F32),
                cot * normed_two,
                cot,
            )
        ):
            vg_ref[i : i + 1] += column_sum(values)
        return carry

    lax.fori_loop(0, length // tile, feed_rows, 0)

    for at in range(seqs):

        @pl.when(s == at)
        def _(at=at):
            for i in range(3, 5):
                part_out(i, at).start()
            if at < seqs - 1:
                exchange(at + 1).wait_send()
            if at + 2 < seqs:
                exchange(at + 2).start()
            if at == seqs - 1:
                for i in range(3):
                    whole_out(i).wait()
                for i in range(5):
                    part_out(i, at).wait()
                code_exchange().wait_send()


def front(tokens, group_ids, valid, cotangent, vectors, up_bias, weights):
    seqs, length, features = tokens.shape
    hidden = up_bias.shape[0]
    pairs = features // PAIR
    anywhere = pl.BlockSpec(memory_space=pl.ANY)

    def at_seq(*shape):
        return pl.BlockSpec((1,) + shape, lambda s: (s,) + (0,) * len(shape))

    def of_seqs(*shape, dtype=BF16):
        return jax.ShapeDtypeStruct((seqs,) + shape, dtype)

    def fixed(*shape):
        return pl.BlockSpec(shape, lambda s: (0,) * len(shape))

    rows, mask, lses, wide = (length, features), (length, PAIR), (pairs, 8, length), (length, hidden)
    turned = pl.BlockSpec((features, length), lambda s: (0, s))
    return pl.pallas_call(
        front_kernel,
        grid=(seqs,),
        in_specs=[anywhere, whole_spec(group_ids.shape), whole_spec(valid.shape), at_seq(*rows)]
        + [whole_spec(v.shape) for v in vectors + (up_bias,)]
        + [anywhere] * 6,
        out_specs=[at_seq(*rows)] * 4
        + [at_seq(*lses), at_seq(*mask)]
        + [pl.BlockSpec((2, 1) + mask, lambda s: (0, s, 0, 0))]
        + [turned] * 2
        + [fixed(8, features), fixed(1, hidden)]
        + [anywhere] * 6,
        out_shape=[of_seqs(*rows)] * 4
        + [of_seqs(*lses, dtype=F32), of_seqs(*mask)]
        + [jax.ShapeDtypeStruct((2, seqs) + mask, BF16)]
        + [jax.ShapeDtypeStruct((features, seqs * length), BF16)] * 2
        + [jax.ShapeDtypeStruct((8, features), F32), jax.ShapeDtypeStruct((1, hidden), F32)]
        + [of_seqs(*rows)]
        + [jax.ShapeDtypeStruct((2, seqs) + rows, BF16)] * 2
        + [of_seqs(*rows)]
        + [of_seqs(*wide)] * 2,
        scratch_shapes=[pltpu.VMEM(w.shape, BF16) for w in weights]
        + [pltpu.VMEM(tokens.shape, BF16)] * 4
        + [pltpu.VMEM(rows, BF16)] * 2
        + [pltpu.VMEM(tokens.shape, BF16)]
        + [pltpu.VMEM((seqs + -seqs % 8, length), F32)] * 2
        + [pltpu.VMEM(wide, BF16)] * 2
        + [pltpu.VMEM((1, hidden), F32)]
        + [pltpu.SemaphoreType.DMA((7,)), pltpu.SemaphoreType.DMA((8,))]
        + [pltpu.SemaphoreType.DMA((seqs + 1,))] * 2,
        compiler_params=pltpu.CompilerParams(
            collective_id=2, has_side_effects=True, vmem_limit_bytes=63 * MIB
        ),
        cost_estimate=cost(
            2 * tokens.size * (9 * features + 4 * hidden + 8 * length), 2 * 20 * tokens.size, tokens.size * 24
        ),
        name="front",
    )(tokens, group_ids, valid, cotangent, *vectors, up_bias, *weights)


def feed_weights_kernel(blocks, first_ref, din_ref, feed_ref, act_ref, att_any, bg_any,
                        dwu_ref, dwd_ref, dwo_ref, up_s, up_in, down_s, down_in, out_s, out_in,
                        att_s, bg_s, near_sem, send_sem, recv_sem):
    step = pl.program_id(0)
    features = first_ref.shape[0]
    me = lax.axis_index("dp")
    core = me % 2
    other = {"dp": me + 1 - 2 * core}

    def loads():
        return [
            pltpu.make_async_copy(att_any, att_s, near_sem.at[0]),
            pltpu.make_async_copy(bg_any, bg_s, near_sem.at[1]),
        ]

    each, deep = down_in.shape[1:3]

    def piece(i, side):
        return pl.ds(pl.multiple_of((2 * i + side) * deep, 16), deep)

    def swaps(block):
        if block == blocks:
            pairs = [(out_s.at[:, 1 - core], out_in)]
        else:
            pairs = [(up_s.at[block % 2, :, 1 - core], up_in.at[block])]
            for i in range(each):
                pairs.append((down_s.at[block % 2, piece(i, 1 - core)], down_in.at[block, i]))
        return [
            pltpu.make_async_remote_copy(
                src_ref=source,
                dst_ref=target,
                send_sem=send_sem.at[(each + 1) * block + i],
                recv_sem=recv_sem.at[(each + 1) * block + i],
                device_id=other,
                device_id_type=pl.DeviceIdType.MESH,
            )
            for i, (source, target) in enumerate(pairs)
        ]

    @pl.when(step == 0)
    def _():
        for load in loads():
            load.start()
        barrier = pltpu.get_barrier_semaphore()
        pl.semaphore_signal(barrier, inc=1, device_id=other, device_id_type=pl.DeviceIdType.MESH)
        pl.semaphore_wait(barrier, 1)

    @pl.when(step < blocks)
    def _():
        slot = step % 2
        tile = math.gcd(features, 256)
        for start in range(0, features, tile):
            cols = slice(start, start + tile)
            up = dot(first_ref[...], din_ref[:, cols]).astype(BF16)
            up_s[slot, :, :, :, cols] = up.reshape(up_s.shape[1:4] + (tile,))
            down_s[slot, cols] = dot(feed_ref[...], act_ref[:, cols]).astype(BF16).T

    for block in range(blocks):

        @pl.when(step == block)
        def _(block=block):
            for swap in swaps(block):
                swap.start()

    @pl.when(step == blocks)
    def _():
        for load in loads():
            load.wait()
        out_s[...] = dot(att_s[...].T, bg_s[...]).astype(BF16).reshape(out_s.shape)
        for swap in swaps(blocks):
            swap.start()

    for block in range(blocks):

        @pl.when(step == block + 1)
        def _(block=block):
            for swap in swaps(block):
                swap.wait()
            dwu_ref[:, 0] = (up_s[block % 2, :, core].astype(F32) + up_in[block].astype(F32)).astype(BF16)
            for i in range(each):
                mine = down_s[block % 2, piece(i, core)].astype(F32)
                dwd_ref[i] = (mine + down_in[block, i].astype(F32)).astype(BF16)

    @pl.when(step == blocks + 1)
    def _():
        for swap in swaps(blocks):
            swap.wait()
        dwo_ref[...] = (out_s[:, core].astype(F32) + out_in[...].astype(F32)).astype(BF16)


def feed_weights(first_t, din, feed_t, act, att, bg):
    dp = lax.axis_size("dp")
    features, rows = first_t.shape
    hidden = act.shape[1]
    blocks, half, low, deep = hidden // features, dp // 2, features // dp, hidden // dp
    each = half // blocks
    wide_spec = pl.BlockSpec((rows, features), lambda i: (0, jnp.minimum(i, blocks - 1)))
    anywhere = pl.BlockSpec(memory_space=pl.ANY)

    def behind(i):
        return jnp.clip(i - 1, 0, blocks - 1)

    return pl.pallas_call(
        functools.partial(feed_weights_kernel, blocks),
        grid=(blocks + 2,),
        in_specs=[
            whole_spec(first_t.shape),
            wide_spec,
            whole_spec(feed_t.shape),
            wide_spec,
            anywhere,
            anywhere,
        ],
        out_specs=[
            pl.BlockSpec((half, 1, low, features), lambda i: (0, behind(i), 0, 0)),
            pl.BlockSpec((each, deep, features), lambda i: (behind(i), 0, 0)),
            pl.BlockSpec((half, low, features), lambda i: (0, 0, 0)),
        ],
        out_shape=[
            jax.ShapeDtypeStruct((half, blocks, low, features), BF16),
            jax.ShapeDtypeStruct((half, deep, features), BF16),
            jax.ShapeDtypeStruct((half, low, features), BF16),
        ],
        scratch_shapes=[
            pltpu.VMEM((2, half, 2, low, features), BF16),
            pltpu.VMEM((blocks, half, low, features), BF16),
            pltpu.VMEM((2, features, features), BF16),
            pltpu.VMEM((blocks, each, deep, features), BF16),
            pltpu.VMEM((half, 2, low, features), BF16),
            pltpu.VMEM((half, low, features), BF16),
            pltpu.VMEM(att.shape, BF16),
            pltpu.VMEM(bg.shape, BF16),
            pltpu.SemaphoreType.DMA((2,)),
            pltpu.SemaphoreType.DMA(((each + 1) * blocks + 1,)),
            pltpu.SemaphoreType.DMA(((each + 1) * blocks + 1,)),
        ],
        compiler_params=pltpu.CompilerParams(
            collective_id=3, has_side_effects=True, vmem_limit_bytes=63 * MIB
        ),
        cost_estimate=cost(
            2 * rows * features * (2 * hidden + features), 4 * rows * (hidden + 2 * features)
        ),
        name="feed_weights",
    )(first_t, din, feed_t, act, att, bg)


def own_back_kernel(bg_ref, dq_ref, dk_ref, dv_ref, wq_ref, wk_ref, wv_ref, out_ref):
    total = bg_ref[0].astype(F32) + dot(dq_ref[0], wq_ref[...], NT)
    total += dot(dk_ref[0], wk_ref[...], NT)
    total += dot(dv_ref[0], wv_ref[...], NT)
    out_ref[0] = total.astype(BF16)


def rem_back_kernel(dk_ref, dv_ref, wk_ref, wv_ref, out_ref):
    total = dot(dk_ref[0], wk_ref[...], NT) + dot(dv_ref[0], wv_ref[...], NT)
    out_ref[0] = total.astype(BF16)


def tokens_back(kernel, rows, weights):
    seqs, length, features = rows[0].shape
    tile = math.gcd(length, 512)
    row_spec = pl.BlockSpec((1, tile, features), lambda s, i: (s, i, 0))
    size = rows[0].size
    return pl.pallas_call(
        kernel,
        grid=(seqs, length // tile),
        in_specs=[row_spec] * len(rows) + [whole_spec(w.shape) for w in weights],
        out_specs=row_spec,
        out_shape=jax.ShapeDtypeStruct(rows[0].shape, BF16),
        compiler_params=params(60),
        cost_estimate=cost(2 * size * features * len(weights), 2 * size * (1 + len(rows))),
        name="tokens_back",
    )(*rows, *weights)


def weights_back_kernel(tok_ref, rem_ref, dq_ref, dko_ref, dvo_ref, dkr_ref, dvr_ref,
                        wq_ref, wk_ref, wv_ref, bq_ref, bv_ref, tok_t, rem_t):
    @pl.when(pl.program_id(0) == 0)
    def _():
        tok_t[...] = tok_ref[...].T
        rem_t[...] = rem_ref[...].T

    wq_ref[...] = dot(tok_t[...], dq_ref[...]).astype(BF16)
    wk_ref[...] = (dot(tok_t[...], dko_ref[...]) + dot(rem_t[...], dkr_ref[...])).astype(BF16)
    wv_ref[...] = (dot(tok_t[...], dvo_ref[...]) + dot(rem_t[...], dvr_ref[...])).astype(BF16)
    bq_ref[...] = column_sum(dq_ref[...].astype(F32))
    bv_ref[...] = column_sum(dvo_ref[...].astype(F32)) + column_sum(dvr_ref[...].astype(F32))


def weights_back(tok, rem, dq, dko, dvo, dkr, dvr):
    rows, features = tok.shape
    others = rem.shape[0]
    wide = math.gcd(features, 256)
    own_spec = pl.BlockSpec((rows, wide), lambda j: (0, j))
    rem_spec = pl.BlockSpec((others, wide), lambda j: (0, j))
    bias_spec = pl.BlockSpec((1, wide), lambda j: (0, j))
    return pl.pallas_call(
        weights_back_kernel,
        grid=(features // wide,),
        in_specs=[
            whole_spec(tok.shape),
            whole_spec(rem.shape),
            own_spec,
            own_spec,
            own_spec,
            rem_spec,
            rem_spec,
        ],
        out_specs=[pl.BlockSpec((features, wide), lambda j: (0, j))] * 3 + [bias_spec] * 2,
        out_shape=[jax.ShapeDtypeStruct((features, features), BF16)] * 3
        + [jax.ShapeDtypeStruct((1, features), F32)] * 2,
        scratch_shapes=[
            pltpu.VMEM((features, rows), BF16),
            pltpu.VMEM((features, others), BF16),
        ],
        compiler_params=params(60),
        cost_estimate=cost(
            2 * features * features * (3 * rows + 2 * others),
            2 * (4 * tok.size + 3 * rem.size + 3 * features * features),
        ),
        name="weights_back",
    )(tok, rem, dq, dko, dvo, dkr, dvr)


def halve(value, axis, bit):
    size = lax.axis_size(axis)
    mine = (lax.axis_index(axis) >> bit) & 1
    pairs = value.reshape((value.shape[0] // 2, 2) + value.shape[1:])
    keep = lax.dynamic_index_in_dim(pairs, mine, 1, keepdims=False)
    send = lax.dynamic_index_in_dim(pairs, 1 - mine, 1, keepdims=False)
    came = lax.ppermute(send, axis, [(i, i ^ (1 << bit)) for i in range(size)])
    return keep.astype(F32) + came.astype(F32)


def scatter_sum(value, low=True):
    dp, blk = lax.axis_size("dp"), lax.axis_size("blk")
    if dp & (dp - 1) or blk & (blk - 1):
        return lax.psum_scatter(
            value.astype(F32), ("dp", "blk"), scatter_dimension=0, tiled=True
        )
    kept = value.dtype
    each = value.shape[0] // (dp * blk)
    value = value.reshape((dp, blk * each) + value.shape[1:])
    for bit in range(dp.bit_length() - 1):
        value = halve(value, "dp", bit).astype(kept)
    value = value.reshape((blk, each) + value.shape[2:])
    for bit in range(blk.bit_length() - 1):
        value = halve(value, "blk", bit)
        value = value if (2 << bit) == blk else value.astype(kept)
    return value.reshape(value.shape[1:]).astype(F32)


class Unit:
    def __init__(self, parts, rows, columns, halves, outs):
        self.parts, self.rows, self.columns = parts, rows, columns
        self.halves, self.outs = halves, outs
        self.first = 1 if parts else 0
        self.half = rows // (2 * halves)
        self.last_type = BF16 if (rows // 2) % 16 == 0 else F32


def timetable(units, bits, seqs, groups, slot_us, token_us):
    free, pending, table = {}, [], []
    slots = seqs * groups * 2

    def launch(key, now):
        kind, which, step = key
        if kind == "tokens":
            link, us = "blk", token_us
        elif kind == "vectors":
            link, us = None, 1.0
        else:
            us = units[which].rows * units[which].columns * 2e-5
            us *= 1 << max(bits - 1 - step, 0)
            us *= {0: 0.3, bits - 1: 3.0}.get(step, 1.1)
            link = {0: "core", bits - 1: "far", bits: "blk"}.get(step, "near")
        start = max(now, free.get(link, 0.0))
        if link:
            free[link] = start + us
        if kind != "tokens":
            pending.append((start + us + 2.0, key))

    for u, unit in enumerate(units):
        if unit.parts:
            launch(("unit", u, 1), 3.0)
    first_group = sum(1 for unit in units if unit.parts)
    now = 0.0
    while len(table) < slots or pending:
        slot = len(table)
        if slot < slots:
            now = (slot + 1) * slot_us
            part, major, minor = slot // (seqs * groups), slot // groups % seqs, slot % groups
            if part == 0 and minor == groups - 1:
                launch(("tokens", major, 0), now)
            major, minor = divmod(slot - seqs * groups, seqs)
            if part == 1 and minor == seqs - 1:
                launch(("unit", first_group + major, 0), now)
            if slot == slots - 1:
                launch(("vectors", 0, 0), now)
            due = sorted(p for p in pending if p[0] <= now)
        else:
            due = [min(pending)]
            now = max(now + 0.3, due[0][0])
        table.append([key for _, key in due])
        for found in due:
            pending.remove(found)
            kind, which, step = found[1]
            if step < bits:
                launch((kind, which, step + 1), now)
    tail = [key for keys in table[slots:] for key in keys]
    return table[:slots], tail + [("tokens", s, 0) for s in range(seqs)]


def order_of(step, seqs, groups):
    part = step // (seqs * groups)
    left = step - part * (seqs * groups)
    s = left // groups * (1 - part) + left % seqs * part
    h = left % groups * (1 - part) + left // seqs * part
    return part, s, h


def back_kernel(units, bits, groups, table, tail, n_out, *refs):
    (q_ref, qm_ref, g_ref, lse_ref, k_ref, km_ref, v_ref,
     tok_ref, rem_ref, wq_ref, wk_ref, wv_ref, vg_ref, vu_ref) = refs[:14]
    sources, refs = refs[14:17], list(refs[17:])
    tokens_any, rem_in, *outs = refs[:n_out]
    refs = refs[n_out:]
    kept = [refs.pop(0) for _ in units]
    landed = [
        [refs.pop(0) if k >= unit.first else None for k in range(bits)] for unit in units
    ]
    wide = [refs.pop(0) for _ in units]
    parting = [refs.pop(0) for _ in units]
    last = [refs.pop(0) for _ in units]
    (weight_sum, group_src, total_s, turned, dq_part, dq_s, dk_s, dv_s,
     rem_out, vec, vec_in, bias_sum, send_sem, recv_sem, local_sem, out_sem) = refs
    step = pl.program_id(0)
    steps = pl.num_programs(0)
    seqs = rem_out.shape[0]
    part, s, h = order_of(step, seqs, groups)
    features = tok_ref.shape[2]
    me, side = lax.axis_index("dp"), lax.axis_index("blk")
    core = me % 2

    def swapped(k):
        return {1: 2, 2: 1}.get(k, k) if bits > 2 else k

    def pick(values, k):
        return values[k] + (values[swapped(k)] - values[k]) * core

    bit_own = [(me // (1 << bit)) % 2 for bit in range(bits)]
    across = [me + (1 << bit) * (1 - 2 * bit_own[bit]) for bit in range(bits)]
    own = [pick(bit_own, k) for k in range(bits)]
    partner = [{"dp": pick(across, k)} for k in range(bits)] + [{"blk": 1 - side}]
    first_group = sum(1 for unit in units if unit.parts)
    lead = (slice(None),) * (bits - 1)

    def natural(digits):
        by_step = [None] + list(digits[::-1])
        return tuple(
            by_step[bit] if swapped(bit) == bit else pick(by_step, bit) for bit in range(bits - 1, 0, -1)
        )

    def digits_of(n, count):
        return [(n // (1 << (count - 1 - i))) % 2 for i in range(count)]

    sems = {}
    for u, unit in enumerate(units):
        for k in range(unit.first, bits + 1):
            sems["unit", u, k, 0] = len(sems)
    for k in range(bits + 1):
        sems["vectors", 0, k, 0] = len(sems)
    for k in range(seqs):
        sems["tokens", k, 0, 0] = len(sems)

    def remote(source, target, device, key):
        return pltpu.make_async_remote_copy(
            src_ref=source,
            dst_ref=target,
            send_sem=send_sem.at[sems[key]],
            recv_sem=recv_sem.at[sems[key]],
            device_id=device,
            device_id_type=pl.DeviceIdType.MESH,
        )

    near_sems = {}
    for u, unit in enumerate(units):
        for p in range(len(unit.parts or ())):
            for n in range(1 << min(bits - 1, 2)):
                near_sems[u, p, n] = len(near_sems)

    def spot(k, value):
        return tuple(
            own[at] if at < k else value if at == k else slice(None) for at in range(bits - 1, 0, -1)
        )

    def copies(kind, which, k):
        if kind == "tokens":
            return [remote(rem_out.at[which], rem_in.at[which], partner[bits], (kind, which, 0, 0))]
        if kind == "vectors":
            return [remote(vec.at[k], vec_in.at[k], partner[k], (kind, 0, k, 0))]
        u, unit = which, units[which]
        if k == bits:
            return [remote(parting[u], last[u], partner[bits], (kind, u, k, 0))]
        if k:
            source = kept[u].at[spot(k, 1 - own[k])]
            return [remote(source, landed[u][k], partner[k], (kind, u, k, 0))]
        source = group_src.at[(u - first_group,) + lead + (1 - core,)]
        return [remote(source, landed[u][0], partner[0], (kind, u, 0, 0))]

    def near_copies(u):
        found, row = [], 0
        for p, (source, first, rows) in enumerate(units[u].parts):
            for n in range(1 << min(bits - 1, 2)):
                digits = digits_of(n, min(bits - 1, 2))
                digits = [slice(None)] * (bits - 1 - len(digits)) + digits
                found.append(
                    pltpu.make_async_copy(
                        sources[source].at[natural(digits) + (pl.ds(first, rows),)],
                        kept[u].at[tuple(digits) + (pl.ds(row, rows),)],
                        local_sem.at[near_sems[u, p, n]],
                    )
                )
            row += rows
        return found

    def launch(*key):
        for copy in copies(*key):
            copy.start()

    def halves_of(u, which):
        unit = units[u]
        return [
            wide[u][pl.ds(pl.multiple_of(i * 2 * unit.half + which * unit.half, 8), unit.half)]
            for i in range(unit.halves)
        ]

    def receive(kind, which, k):
        for copy in copies(kind, which, k):
            copy.wait_recv()
        if kind == "tokens":
            return
        if kind == "vectors":
            vec[k + 1] = vec[k] + vec_in[k]
            if k < bits:
                launch(kind, 0, k + 1)
            return
        u, unit = which, units[which]
        if k == bits:
            for i, (mine, (out, rows, columns)) in enumerate(zip(halves_of(u, side), unit.outs)):
                came = last[u][...].astype(F32)[i * unit.half : (i + 1) * unit.half]
                outs[out][rows, columns] = mine + came
            return
        place = spot(k, own[k]) if k else lead
        open_at = [i for i, at in enumerate(place) if isinstance(at, slice)]

        def add(n, carry):
            at, where = list(place), digits_of(n, len(open_at))
            for i, digit in zip(open_at, where):
                at[i] = digit
            at = tuple(at)
            if k:
                mine, came = kept[u][at], landed[u][k][tuple(where)]
            else:
                mine = group_src[(u - first_group,) + natural(at) + (core,)]
                came = landed[u][0][natural(at)]
            total = mine.astype(F32) + came.astype(F32)
            if k == bits - 1:
                wide[u][...] = total
            else:
                kept[u][at] = total.astype(BF16)
            return carry

        if open_at:
            lax.fori_loop(0, 1 << len(open_at), add, 0)
        else:
            add(0, 0)
        if k == bits - 1:
            pieces = halves_of(u, 1 - side)
            pieces = pieces[0] if len(pieces) == 1 else jnp.concatenate(pieces, axis=0)
            parting[u][...] = pieces.astype(unit.last_type)
        launch(kind, u, k + 1)

    @pl.when(step == 0)
    def _():
        barrier = pltpu.get_barrier_semaphore()
        for other in partner:
            pl.semaphore_signal(barrier, inc=1, device_id=other, device_id_type=pl.DeviceIdType.MESH)
        pl.semaphore_wait(barrier, bits + 1)
        for u, unit in enumerate(units):
            if unit.parts:
                for copy in near_copies(u):
                    copy.start()
        for u, unit in enumerate(units):
            if unit.parts:
                for copy in near_copies(u):
                    copy.wait()
                launch("unit", u, 1)
        weight_sum[...] = jnp.zeros_like(weight_sum)
        bias_sum[...] = jnp.zeros_like(bias_sum)

    @pl.when((part == 0) & (h == 0))
    def _():
        turned[0] = rem_ref[0].T
        total_s[...] = jnp.zeros_like(total_s)

    @pl.when((part == 1) & (h == 0))
    def _():
        turned[s] = tok_ref[0].T

    width = q_ref.shape[2]
    columns = pl.ds(pl.multiple_of(h * width, width), width)

    found = attend_back_part(
        q_ref[0], qm_ref[0], g_ref[0], lse_ref.at[0], k_ref[0, 0], km_ref[0, 0], v_ref[0, 0],
        dk_s.at[s, :, columns], dv_s.at[s, :, columns],
    )
    dk, dv = dk_s[s, :, columns], dv_s[s, :, columns]
    x_t = turned[s * part]
    weight_sum[h, 1] += dot(x_t, dk)
    weight_sum[h, 2] += dot(x_t, dv)
    bias_sum[h, 1:2] += column_sum(dv.astype(F32))

    @pl.when(part == 0)
    def _():
        total_s[...] += dot(dk, wk_ref[:, columns], NT) + dot(dv, wv_ref[:, columns], NT)
        for pair, value in enumerate(found):
            dq_part[s, h, pair] = value.astype(dq_part.dtype)

    @pl.when(part == 1)
    def _():
        queries = []
        for pair, value in enumerate(found):
            value = (value + dq_part[s, h, pair].astype(F32)) * SCALE
            queries.append(value.T.astype(BF16))
        dq = jnp.concatenate(queries, axis=1)
        dq_s[s, :, columns] = dq
        weight_sum[h, 0] += dot(x_t, dq)
        bias_sum[h, 0:1] += column_sum(dq.astype(F32))

    for at in range(seqs):

        @pl.when(step == (at + 1) * groups - 1)
        def _(at=at):
            rem_out[at] = total_s[...].astype(BF16)
            launch("tokens", at, 0)

    for at in range(groups):

        @pl.when(step == steps - (groups - 1 - at) * seqs - 1)
        def _(at=at):
            rows = features // (1 << bits)
            for i in range(3):
                piece = weight_sum[at, i].astype(BF16)
                piece = piece.reshape((2,) * bits + (rows, piece.shape[1]))
                group_src[(at,) + (slice(None),) * bits + (slice(i * rows, (i + 1) * rows),)] = piece
            launch("unit", first_group + at, 0)

    @pl.when(step == steps - 1)
    def _():
        vec[0] = jnp.zeros_like(vec[0])
        vec[0, 0:6] = vg_ref[0:6]
        for at in range(groups):
            vec[0, 6:8, at * width : (at + 1) * width] = bias_sum[at, 0:2]
        blocks = vu_ref.shape[1] // features
        for at in range(blocks):
            vec[0, 8 + at : 9 + at] = vu_ref[:, at * features : (at + 1) * features]
        launch("vectors", 0, 0)

    for at, keys in enumerate(table):
        if keys:

            @pl.when(step == at)
            def _(keys=keys):
                for key in keys:
                    receive(*key)

    @pl.when(step == steps - 1)
    def _():
        def own_out(at):
            return pltpu.make_async_copy(dq_s.at[at], tokens_any.at[at], out_sem.at[at])

        left = list(tail)
        for at in range(seqs):
            total = dot(dq_s[at], wq_ref[...], NT)
            total += dot(dk_s[at], wk_ref[...], NT) + dot(dv_s[at], wv_ref[...], NT)
            dq_s[at] = total.astype(BF16)
            own_out(at).start()
            for _ in range(3):
                if left:
                    receive(*left.pop(0))
        for key in left:
            receive(*key)
        for at in range(seqs):
            own_out(at).wait()
        shards = (1 << bits) * 2
        place = me * 2 + side
        share = features // shards
        rows = pltpu.roll(vec[bits + 1, 0:8], (shards - place) * share % features, 1)
        outs[-1][0:8] = rows[:, :PAIR]
        share = vu_ref.shape[1] // shards
        each = features // share
        row = vec[bits + 1, pl.ds(8 + place // each, 1)]
        rows = pltpu.roll(jnp.broadcast_to(row, (8, features)), (each - place % each) * share % features, 1)
        outs[-1][8:16] = rows[:, :PAIR]
        for u, unit in enumerate(units):
            for k in range(unit.first, bits + 1):
                for copy in copies("unit", u, k):
                    copy.wait_send()
        for k in range(bits + 1):
            copies("vectors", 0, k)[0].wait_send()
        for k in range(seqs):
            copies("tokens", k, 0)[0].wait_send()


def back_and_sum(q, qm, g, lse, k, km, v, tokens, rem_tokens, weights, dwd, dwu, dwo, vg, vu):
    bits = lax.axis_size("dp").bit_length() - 1
    seqs, length, features = q.shape
    width = math.gcd(features, 2 * PAIR)
    groups, pairs = features // width, width // PAIR
    low, deep, blocks = dwo.shape[1], dwd.shape[1], dwu.shape[1]
    lead = (2,) * bits
    sources = [x.reshape(lead[1:] + (-1, features)) for x in (dwd, dwu, dwo)]
    every = slice(None)
    units = []
    quarter = deep // 4
    for i in range(2):
        at = slice(i * quarter, (i + 1) * quarter)
        parts = [(0, i * quarter, quarter), (0, (2 + i) * quarter, quarter)]
        units.append(Unit(parts, 2 * quarter, features, 1, [(0, at, every)]))
    for i in range(2):
        found = range(i * blocks // 2, (i + 1) * blocks // 2)
        units.append(
            Unit(
                [(1, found[0] * low, len(found) * low)],
                len(found) * low,
                features,
                len(found),
                [(1, every, slice(b * features, (b + 1) * features)) for b in found],
            )
        )
    units.append(Unit([(2, 0, low)], low, features, 1, [(2, every, every)]))
    for h in range(groups):
        columns = slice(h * width, (h + 1) * width)
        units.append(Unit(None, 3 * low, width, 3, [(3 + i, every, columns) for i in range(3)]))
    table, tail = timetable(units, bits, seqs, groups, 4.6, length * features * 4e-5)

    half = low // 2
    out_shape = [
        jax.ShapeDtypeStruct(q.shape, BF16),
        jax.ShapeDtypeStruct(q.shape, BF16),
        jax.ShapeDtypeStruct((deep // 2, features), F32),
        jax.ShapeDtypeStruct((half, blocks * features), F32),
        *(jax.ShapeDtypeStruct((half, features), F32) for _ in range(4)),
        jax.ShapeDtypeStruct((16, PAIR), F32),
    ]
    tops = lead[1:]
    scratch = [pltpu.VMEM(tops + (u.rows, u.columns), BF16) for u in units]
    for u in units:
        scratch += [pltpu.VMEM(tops[k:] + (u.rows, u.columns), BF16) for k in range(u.first, bits)]
    scratch += [pltpu.VMEM((u.rows, u.columns), F32) for u in units]
    scratch += [pltpu.VMEM((u.rows // 2, u.columns), u.last_type) for u in units] * 2
    count = len(units) * (bits + 1) + bits + 1 + seqs
    near = sum(len(u.parts) << min(bits - 1, 2) for u in units if u.parts)
    scratch += [
        pltpu.VMEM((groups, 3, features, width), F32),
        pltpu.VMEM((groups,) + lead + (3 * low, width), BF16),
        pltpu.VMEM((length, features), F32),
        pltpu.VMEM((seqs, features, length), BF16),
        pltpu.VMEM((seqs, groups, pairs, PAIR, length), F32),
        *(pltpu.VMEM((seqs, length, features), BF16) for _ in range(4)),
        pltpu.VMEM((bits + 2, 16, features), F32),
        pltpu.VMEM((bits + 1, 16, features), F32),
        pltpu.VMEM((groups, 8, width), F32),
        pltpu.SemaphoreType.DMA((count,)),
        pltpu.SemaphoreType.DMA((count,)),
        pltpu.SemaphoreType.DMA((near,)),
        pltpu.SemaphoreType.DMA((seqs,)),
    ]

    def at_step(shape, index):
        return pl.BlockSpec(shape, lambda i: index(*order_of(i, seqs, groups)))

    heads_at = at_step((1, length, width), lambda p, s, h: (s, 0, h))
    keys_at = at_step((1, 1, length, width), lambda p, s, h: (1 - p, s, 0, h))

    def rows_at(which):
        last = seqs - 1
        return pl.BlockSpec(
            (1, length, features),
            lambda i: (jnp.clip(i // groups if which == 0 else i - seqs * groups, 0, last), 0, 0),
            pipeline_mode=pl.Buffered(1),
        )

    def fixed(shape):
        return pl.BlockSpec(shape, lambda i: (0,) * len(shape), pipeline_mode=pl.Buffered(1))

    return pl.pallas_call(
        functools.partial(back_kernel, units, bits, groups, table, tail, len(out_shape)),
        grid=(2 * seqs * groups,),
        in_specs=[
            heads_at,
            at_step((1, length, PAIR), lambda p, s, h: (s, 0, 0)),
            heads_at,
            at_step((1, pairs, 8, length), lambda p, s, h: (s, h, 0, 0)),
            keys_at,
            at_step((1, 1, length, PAIR), lambda p, s, h: (1 - p, s, 0, 0)),
            keys_at,
            rows_at(1),
            rows_at(0),
        ]
        + [whole_spec(w.shape) for w in weights + (vg, vu)]
        + [pl.BlockSpec(memory_space=pl.ANY)] * 3,
        out_specs=[pl.BlockSpec(memory_space=pl.ANY)] * 2
        + [fixed(s.shape) for s in out_shape[2:]],
        out_shape=out_shape,
        scratch_shapes=scratch,
        compiler_params=pltpu.CompilerParams(
            collective_id=1, has_side_effects=True, vmem_limit_bytes=63 * MIB
        ),
        cost_estimate=cost(80 * q.size * length, 2 * q.size * 14, 2 * q.size * length // HEAD),
        name="back_and_sum",
    )(q, qm, g, lse, k, km, v, tokens, rem_tokens, *weights, vg, vu, *sources)


def finish_kernel(residual_ref, own_ref, rem_ref, *refs):
    ins, outs = refs[:7], refs[7:]
    total = residual_ref[...].astype(F32) + own_ref[...].astype(F32) + rem_ref[...].astype(F32)
    outs[0][...] = total.astype(BF16)

    @pl.when(pl.program_id(0) == 0)
    def _():
        for source, target in zip(ins[:6], outs[1:7]):
            target[...] = source[...]
        for i, target in enumerate(outs[7:]):
            target[...] = ins[6][i, : target.shape[0]]


def finish(residual, own, rem, matrices, vectors, shares):
    seqs, length, features = own.shape
    row_spec = pl.BlockSpec((1, length, features), lambda s: (s, 0, 0))

    def fixed(shape):
        return pl.BlockSpec(shape, lambda s: (0,) * len(shape))

    shapes = [m.shape for m in matrices] + [(n,) for n in shares]
    return pl.pallas_call(
        finish_kernel,
        grid=(seqs,),
        in_specs=[row_spec] * 3 + [fixed(m.shape) for m in matrices] + [fixed(vectors.shape)],
        out_specs=[row_spec] + [fixed(s) for s in shapes],
        out_shape=[jax.ShapeDtypeStruct(own.shape, BF16)] + [jax.ShapeDtypeStruct(s, F32) for s in shapes],
        compiler_params=params(60),
        cost_estimate=cost(2 * own.size, 8 * own.size),
        name="finish",
    )(residual, own, rem, *matrices, vectors)


def back_plainly(q, qm, o, g, lse, own, rem, bg, tokens, rem_tokens, weights, dwd, dwu, dwo, vg, vu):
    seqs, length, features = q.shape
    dp, blk = lax.axis_size("dp"), lax.axis_size("blk")
    dq, dko, dvo, dkr, dvr = attend_back(q, qm, o, g, lse, own, rem)
    rem_gradient = tokens_back(rem_back_kernel, (dkr, dvr), weights[1:])
    came = [
        lax.ppermute(part, "blk", [((i + r) % blk, i) for i in range(blk)])
        for r, part in enumerate(jnp.split(rem_gradient, blk - 1, axis=1), 1)
    ]
    flat = [v.reshape(-1, features) for v in (tokens, rem_tokens, dq, dko, dvo, dkr, dvr)]
    dwq, dwk, dwv, dbq, dbv = weights_back(*flat)
    total = tokens_back(own_back_kernel, (bg, dq, dko, dvo), weights).astype(F32)
    for part in came:
        total += part.astype(F32)
    dwu = jnp.moveaxis(dwu[0], 0, 1).reshape(features, -1)
    summed = [scatter_sum(w) for w in (dwd, dwu, dwo, dwq, dwk, dwv)]
    rows = [vg[i] for i in range(6)] + [dbq, dbv, vu]
    rows = [scatter_sum(v.reshape(dp * blk, -1)) for v in rows]
    return [total.astype(BF16)] + summed + [[v[0] for v in rows]]


def body(
    tokens,
    query_weight,
    query_bias,
    key_weight,
    value_weight,
    value_bias,
    out_weight,
    out_bias,
    gain_one,
    shift_one,
    up_weight,
    up_bias,
    down_weight,
    down_bias,
    gain_two,
    shift_two,
    group_ids,
    valid_mask,
    cotangent,
):
    seqs, length, features = tokens.shape
    rows = seqs * length
    blk = lax.axis_size("blk")

    def from_others(value):
        found = [
            lax.ppermute(value, "blk", [(i, (i + r) % blk) for i in range(blk)])
            for r in range(1, blk)
        ]
        return found[0] if len(found) == 1 else jnp.concatenate(found, axis=1)

    codes = jnp.where(valid_mask == 1, group_ids, -1)
    dp = lax.axis_size("dp")
    by_kernel = blk == 2 and dp & (dp - 1) == 0 and dp > 1 and (features // dp) % 16 == 0
    projections = (query_weight, key_weight, value_weight)
    vectors = (
        query_bias,
        value_bias,
        out_bias,
        gain_one,
        shift_one,
        down_bias,
        gain_two,
        shift_two,
    )

    if by_kernel:
        (block_out, branch_gradient, attended_gradient, attended, lse, query_mask, key_masks,
         first_t, feed_t, vector_gradients, up_bias_gradient, queries, keys, values,
         rem_tokens, active, inner_gradient) = front(
            tokens,
            group_ids,
            valid_mask,
            cotangent,
            vectors,
            up_bias,
            projections + (out_weight, up_weight, down_weight),
        )
        dwu, dwd, dwo = feed_weights(
            first_t,
            inner_gradient.reshape(rows, -1),
            feed_t,
            active.reshape(rows, -1),
            attended.reshape(rows, features),
            branch_gradient.reshape(rows, features),
        )
        own_gradient, rem_gradient, *matrices, vectors = back_and_sum(
            queries,
            query_mask,
            attended_gradient,
            lse,
            keys,
            key_masks,
            values,
            tokens,
            rem_tokens,
            projections,
            dwd,
            dwu,
            dwo,
            vector_gradients,
            up_bias_gradient,
        )
        shares = [features // (dp * blk)] * 8 + [up_bias.size // (dp * blk)]
        found = finish(branch_gradient, own_gradient, rem_gradient, matrices, vectors, shares)
        tokens_gradient, dwd, dwu, dwo, dwq, dwk, dwv, *rows_left = found
    else:
        rem_tokens = from_others(tokens)
        rem_codes = from_others(codes.astype(BF16)).astype(jnp.int32)
        slot = jnp.arange(PAIR, dtype=jnp.int32) % HEAD

        def key_mask(code):
            return jnp.where(code[:, :, None] == slot, 0.0, MASKED).astype(BF16)

        query_mask = (group_ids[:, :, None] == slot).astype(BF16)
        vectors = jnp.stack(vectors).astype(F32)
        queries, own_keys, own_values = project(tokens, vectors, projections)
        rem_keys, rem_values = project(rem_tokens, vectors, projections[1:])
        own = (own_keys, key_mask(codes), own_values)
        rem = (rem_keys, key_mask(rem_codes), rem_values)
        attended, lse = attend(queries, query_mask, own, rem)
        (block_out, branch_gradient, attended_gradient, vector_gradients, up_bias_gradient,
         dwu, dwd, dwo) = feed_both_ways(
            tokens.reshape(rows, features),
            attended.reshape(rows, features),
            cotangent.reshape(rows, features),
            vectors[2:],
            up_bias.astype(F32)[None],
            out_weight,
            up_weight,
            down_weight,
            1,
        )
        tokens_gradient, dwd, dwu, dwo, dwq, dwk, dwv, rows_left = back_plainly(
            queries,
            query_mask,
            attended,
            attended_gradient.reshape(tokens.shape),
            lse,
            own,
            rem,
            branch_gradient.reshape(tokens.shape),
            tokens,
            rem_tokens,
            projections,
            dwd,
            dwu,
            dwo,
            vector_gradients,
            up_bias_gradient,
        )
    dbo, dg1, ds1, dbd, dg2, ds2, dbq, dbv, dbu = rows_left
    return (
        block_out.reshape(tokens.shape),
        tokens_gradient,
        dwq,
        dbq,
        dwk,
        dwv,
        dbv,
        dwo,
        dbo,
        dg1,
        ds1,
        dwu,
        dbu,
        dwd,
        dbd,
        dg2,
        ds2,
    )


def solution(mesh):
    rows, shared, pair = P("dp", "blk", None), P(), P("dp", "blk")
    matrix, vector = P(("dp", "blk"), None), P(("dp", "blk"))
    return jax.shard_map(
        body,
        mesh=mesh,
        in_specs=(rows,) + (shared,) * 15 + (pair, pair, rows),
        out_specs=(
            rows,
            rows,
            matrix,
            vector,
            matrix,
            matrix,
            vector,
            matrix,
            vector,
            vector,
            vector,
            matrix,
            vector,
            matrix,
            vector,
            vector,
            vector,
        ),
        check_vma=False,
    )
```

```python
import functools
import math

import jax
import jax.numpy as jnp
from jax import lax
from jax.experimental import pallas as pl
from jax.experimental.pallas import tpu as pltpu
from jax.sharding import PartitionSpec as P

HEAD = 64
PAIR = 2 * HEAD
EPSILON = 1e-12
MASKED = -1e30
FLOOR = -3e38
SCALE = HEAD**-0.5
EXPO = SCALE * math.log2(math.e)
NN = (((1,), (0,)), ((), ()))
NT = (((1,), (1,)), ((), ()))
F32 = jnp.float32
BF16 = jnp.bfloat16
MIB = 1 << 20
FEED_ROWS = 256


def dot(left, right, dims=NN):
    return lax.dot_general(left, right, dims, preferred_element_type=F32)


def whole_spec(shape):
    return pl.BlockSpec(shape, lambda *_: (0,) * len(shape), pipeline_mode=pl.Buffered(1))


def params(limit):
    return pltpu.CompilerParams(vmem_limit_bytes=limit * MIB)


def cost(flops, touched, exps=0):
    return pl.CostEstimate(flops=int(flops), bytes_accessed=int(touched), transcendentals=int(exps))


def project_kernel(has_query, *refs):
    if has_query:
        x_ref, bias_ref, wq_ref, wk_ref, wv_ref, q_ref, k_ref, v_ref = refs
    else:
        x_ref, bias_ref, wk_ref, wv_ref, k_ref, v_ref = refs
    x = x_ref[0]
    if has_query:
        q_ref[0] = ((dot(x, wq_ref[...]) + bias_ref[0:1]) * EXPO).astype(BF16)
    k_ref[0] = dot(x, wk_ref[...]).astype(BF16)
    v_ref[0] = (dot(x, wv_ref[...]) + bias_ref[1:2]).astype(BF16)


def project(x, bias, weights):
    seqs, length, features = x.shape
    tile = math.gcd(length, 512)
    grid = (seqs, length // tile)
    row_spec = pl.BlockSpec((1, tile, features), lambda s, i: (s, i, 0))
    return pl.pallas_call(
        functools.partial(project_kernel, len(weights) == 3),
        grid=grid,
        in_specs=[row_spec, whole_spec(bias.shape)] + [whole_spec(w.shape) for w in weights],
        out_specs=[row_spec] * len(weights),
        out_shape=[jax.ShapeDtypeStruct(x.shape, BF16)] * len(weights),
        compiler_params=params(60),
        cost_estimate=cost(
            2 * x.size * features * len(weights), 2 * x.size * (1 + len(weights))
        ),
        name="project",
    )(x, bias, *weights)


def low_lanes():
    return lax.broadcasted_iota(jnp.int32, (1, PAIR), 1) < HEAD


def attend_group(q, qm, sources, o_ref, lse_ref):
    length = q.shape[0]
    tile = math.gcd(length, 512)
    low = low_lanes()
    one = jnp.ones((1, PAIR), BF16)
    todo = [
        (pair, row, head)
        for pair in range(q.shape[1] // PAIR)
        for row in range(0, length, tile)
        for head in range(2)
    ]

    def lanes_of(pair):
        return slice(pair * PAIR, (pair + 1) * PAIR)

    def mine_of(head):
        return ~low if head else low

    def scores_of(pair, row, head):
        mine, lanes = mine_of(head), lanes_of(pair)
        q_side = jnp.where(mine, q[row : row + tile, lanes], qm[row : row + tile])
        return [dot(q_side, jnp.where(mine, k[:, lanes], km), NT) for k, km, _ in sources]

    ahead = scores_of(*todo[0])
    for i, (pair, row, head) in enumerate(todo):
        scores = ahead
        if i + 1 < len(todo):
            ahead = scores_of(*todo[i + 1])
        top = functools.reduce(
            jnp.maximum, [jnp.max(part, axis=-1, keepdims=True) for part in scores]
        )
        weights = [jnp.exp2(part - top).astype(BF16) for part in scores]
        total = sum(
            dot(w, jnp.where(mine_of(head), v[:, lanes_of(pair)], one))
            for w, (_, _, v) in zip(weights, sources)
        )
        if head == 0:
            earlier, earlier_top = total, top
            continue
        totals = pltpu.roll(jnp.where(low, total, earlier), HEAD, 1)
        rows = slice(row, row + tile)
        o_ref[rows, lanes_of(pair)] = (jnp.where(low, earlier, total) / totals).astype(BF16)
        lse = (jnp.where(low, earlier_top, top) + jnp.log2(totals)).T
        lse_ref[pair, 0:1, rows] = lse[0:1]
        lse_ref[pair, 1:2, rows] = lse[HEAD : HEAD + 1]


def attend_kernel(q_ref, qm_ref, ko_ref, kmo_ref, vo_ref, kr_ref, kmr_ref, vr_ref, o_ref, lse_ref):
    sources = [(ko_ref[0], kmo_ref[0], vo_ref[0]), (kr_ref[0], kmr_ref[0], vr_ref[0])]
    attend_group(q_ref[0], qm_ref[0], sources, o_ref.at[0], lse_ref.at[0])


def pair_spec(length, lanes):
    return pl.BlockSpec((1, length, lanes), lambda s, h: (s, 0, h))


def mask_spec(length):
    return pl.BlockSpec((1, length, PAIR), lambda s, h: (s, 0, 0))


def lse_spec(length, lanes):
    return pl.BlockSpec((1, lanes // PAIR, 8, length), lambda s, h: (s, h, 0, 0))


def attend(q, qm, own, rem):
    seqs, length, features = q.shape
    lanes = math.gcd(features, 2 * PAIR)
    other = rem[0].shape[1]
    own_spec, rem_spec = pair_spec(length, lanes), pair_spec(other, lanes)
    return pl.pallas_call(
        attend_kernel,
        grid=(seqs, features // lanes),
        in_specs=[own_spec, mask_spec(length)]
        + [own_spec, mask_spec(length), own_spec]
        + [rem_spec, mask_spec(other), rem_spec],
        out_specs=[own_spec, lse_spec(length, lanes)],
        out_shape=[
            jax.ShapeDtypeStruct(q.shape, BF16),
            jax.ShapeDtypeStruct((seqs, features // PAIR, 8, length), F32),
        ],
        compiler_params=params(60),
        cost_estimate=cost(
            16 * q.size * (length + other), 2 * q.size * 6, q.size * (length + other) // HEAD
        ),
        name="attend",
    )(q, qm, *own, *rem)


def attend_back_part(q, qm, g, lse_ref, k, km, v, dk_ref, dv_ref):
    low = low_lanes()
    none = jnp.zeros((1, PAIR), BF16)
    pairs = q.shape[1] // PAIR
    todo = [(pair, head) for pair in range(pairs) for head in range(2)]

    def lanes_of(pair):
        return slice(pair * PAIR, (pair + 1) * PAIR)

    def mine_of(head):
        return ~low if head else low

    def products(pair, head):
        mine, lanes = mine_of(head), lanes_of(pair)
        return (
            dot(jnp.where(mine, k[:, lanes], km), jnp.where(mine, q[:, lanes], qm), NT),
            dot(jnp.where(mine, v[:, lanes], none), g[:, lanes], NT),
        )

    found = []
    ahead = products(*todo[0])
    for i, (pair, head) in enumerate(todo):
        scores, grads = ahead
        if i + 1 < len(todo):
            ahead = products(*todo[i + 1])
        lanes, mine = lanes_of(pair), mine_of(head)
        if head == 0:
            k_t = k[:, lanes].T
            dk = dv = 0.0
            dq = []
        probs = jnp.exp2(scores - lse_ref[pair, head : head + 1, :])
        grads = (probs * (grads - lse_ref[pair, 2 + head : 3 + head, :])).astype(BF16)
        dv += dot(probs.astype(BF16), jnp.where(mine, g[:, lanes], none))
        dk += dot(grads, jnp.where(mine, q[:, lanes], none))
        dq.append(dot(k_t[head * HEAD : (head + 1) * HEAD], grads))
        if head == 1:
            dk_ref[:, lanes] = (dk * (SCALE / EXPO)).astype(BF16)
            dv_ref[:, lanes] = dv.astype(BF16)
            found.append(jnp.concatenate(dq, axis=0))
    return found


def attend_back_kernel(q_ref, qm_ref, g_ref, lse_ref, ko_ref, kmo_ref, vo_ref, kr_ref, kmr_ref,
                       vr_ref, dq_ref, dko_ref, dvo_ref, dkr_ref, dvr_ref):
    parts = ((ko_ref, kmo_ref, vo_ref, dko_ref, dvo_ref), (kr_ref, kmr_ref, vr_ref, dkr_ref, dvr_ref))
    found = [
        attend_back_part(
            q_ref[0], qm_ref[0], g_ref[0], lse_ref.at[0], k[0], km[0], v[0], dk.at[0], dv.at[0]
        )
        for k, km, v, dk, dv in parts
    ]
    for pair, both in enumerate(zip(*found)):
        dq_ref[0, :, pair * PAIR : (pair + 1) * PAIR] = (sum(both) * SCALE).T.astype(BF16)


def attend_back(q, qm, o, g, lse, own, rem):
    seqs, length, features = q.shape
    delta = (g.astype(F32) * o.astype(F32)).reshape(seqs, length, features // PAIR, 2, HEAD).sum(-1)
    lse = lax.dynamic_update_slice(lse, jnp.transpose(delta, (0, 2, 3, 1)), (0, 0, 2, 0))
    lanes = math.gcd(features, 2 * PAIR)
    other = rem[0].shape[1]
    own_spec, rem_spec = pair_spec(length, lanes), pair_spec(other, lanes)
    return pl.pallas_call(
        attend_back_kernel,
        grid=(seqs, features // lanes),
        in_specs=[own_spec, mask_spec(length), own_spec, lse_spec(length, lanes)]
        + [own_spec, mask_spec(length), own_spec]
        + [rem_spec, mask_spec(other), rem_spec],
        out_specs=[own_spec] * 3 + [rem_spec] * 2,
        out_shape=[jax.ShapeDtypeStruct(q.shape, BF16)] * 3
        + [jax.ShapeDtypeStruct(rem[0].shape, BF16)] * 2,
        compiler_params=params(60),
        cost_estimate=cost(
            40 * q.size * (length + other), 2 * q.size * 14, q.size * (length + other) // HEAD
        ),
        name="attend_back",
    )(q, qm, g, lse, *own, *rem)


def gelu_and_slope(x):
    bell = jnp.exp2(x * x * (-0.5 * math.log2(math.e)))
    below = 1.0 + (0.3275911 / math.sqrt(2.0)) * jnp.abs(x)
    t = pl.reciprocal(below, approx=True)
    t = t * (2.0 - below * t)
    poly = 1.061405429 * t - 1.453152027
    poly = poly * t + 1.421413741
    poly = poly * t - 0.284496736
    poly = poly * t + 0.254829592
    tail = (0.5 * poly) * t * bell
    share = jnp.where(x >= 0.0, 1.0 - tail, tail)
    return x * share, share + x * bell * (1.0 / math.sqrt(2.0 * math.pi))


def mean(values):
    return jnp.sum(values, axis=-1, keepdims=True) * (1.0 / values.shape[-1])


def norm_parts(values):
    centred = values - mean(values)
    scale = lax.rsqrt(mean(centred * centred) + EPSILON)
    return centred * scale, scale


def norm_back(upper, normed, scale):
    return scale * (upper - mean(upper) - normed * mean(upper * normed))


def column_sum(values):
    return jnp.sum(values, axis=0, keepdims=True)


def feed_kernel(layout, tok_ref, att_ref, cot_ref, vec_ref, bu_ref, wo_ref, wu_ref, wd_ref,
                out_ref, bg_ref, ag_ref, vg_ref, dbu_ref, dwu_ref, dwd_ref, dwo_ref,
                act_s, din_s, first_t, feed_t, att_t, bg_s):
    tiles, ff_steps, chunk, wide, narrow = layout
    step = pl.program_id(0)
    tile = tok_ref.shape[0]
    hidden = act_s.shape[1]
    vec = [vec_ref[i : i + 1] for i in range(6)]
    out_bias, gain_one, shift_one, down_bias, gain_two, shift_two = vec

    @pl.when(step == 0)
    def _():
        vg_ref[...] = jnp.zeros_like(vg_ref)
        dbu_ref[...] = jnp.zeros_like(dbu_ref)

    @pl.when(step < tiles)
    def _():
        start = pl.multiple_of(step * tile, tile)
        rows = pl.ds(start, tile)
        att = att_ref[...]
        normed_one, scale_one = norm_parts(
            tok_ref[...].astype(F32) + (dot(att, wo_ref[...]) + out_bias)
        )
        first = normed_one * gain_one + shift_one
        first_low = first.astype(BF16)
        first_t[:, rows] = first_low.T
        att_t[:, rows] = att.T
        feed = jnp.zeros_like(first) + down_bias
        spans = [slice(c, c + chunk) for c in range(0, hidden, chunk)]
        ahead = dot(first_low, wu_ref[:, spans[0]])
        for i, cols in enumerate(spans):
            inner = ahead + bu_ref[:, cols]
            if i + 1 < len(spans):
                ahead = dot(first_low, wu_ref[:, spans[i + 1]])
            active, slope = gelu_and_slope(inner)
            active = active.astype(BF16)
            act_s[rows, cols] = active
            din_s[rows, cols] = slope.astype(BF16)
            feed += dot(active, wd_ref[cols])
        normed_two, scale_two = norm_parts(first + feed)
        out_ref[...] = (normed_two * gain_two + shift_two).astype(BF16)
        cot = cot_ref[...].astype(F32)
        second = norm_back(cot * gain_two, normed_two, scale_two)
        feed_low = second.astype(BF16)
        feed_t[:, rows] = feed_low.T
        back = second
        ahead = dot(feed_low, wd_ref[spans[0]], NT)
        for i, cols in enumerate(spans):
            inner = ahead
            if i + 1 < len(spans):
                ahead = dot(feed_low, wd_ref[spans[i + 1]], NT)
            inner = (inner * din_s[rows, cols].astype(F32)).astype(BF16)
            din_s[rows, cols] = inner
            dbu_ref[:, cols] += column_sum(inner.astype(F32))
            back += dot(inner, wu_ref[:, cols], NT)
        residual = norm_back(back * gain_one, normed_one, scale_one)
        branch_low = residual.astype(BF16)
        bg_ref[...] = branch_low
        bg_s[rows] = branch_low
        ag_ref[...] = dot(branch_low, wo_ref[...], NT).astype(BF16)
        for i, values in enumerate(
            (
                branch_low.astype(F32),
                back * normed_one,
                back,
                feed_low.astype(F32),
                cot * normed_two,
                cot,
            )
        ):
            vg_ref[i : i + 1] += column_sum(values)

    @pl.when((step >= tiles) & (step < tiles + ff_steps))
    def _():
        cols = pl.ds(pl.multiple_of((step - tiles) * wide, wide), wide)
        dwu = dot(first_t[...], din_s[:, cols]).astype(BF16)
        dwu_ref[...] = dwu.reshape(dwu_ref.shape)
        dwd_ref[...] = dot(feed_t[...], act_s[:, cols]).astype(BF16).T

    @pl.when(step >= tiles + ff_steps)
    def _():
        cols = pl.ds(pl.multiple_of((step - tiles - ff_steps) * narrow, narrow), narrow)
        dwo_ref[...] = dot(att_t[...], bg_s[:, cols]).astype(BF16)


def feed_both_ways(tokens, attended, cotangent, vectors, up_bias, wo, wu, wd, groups):
    rows, features = tokens.shape
    hidden = wu.shape[1]
    tile = math.gcd(rows, 256)
    tiles = rows // tile
    wide, narrow = features, math.gcd(features, 384)
    ff_steps, out_steps = hidden // wide, features // narrow
    layout = (tiles, ff_steps, math.gcd(hidden, 512), wide, narrow)
    blocked = (groups, ff_steps, features // groups, wide)
    row_spec = pl.BlockSpec((tile, features), lambda i: (jnp.minimum(i, tiles - 1), 0))

    def ff_at(i):
        return jnp.clip(i - tiles, 0, ff_steps - 1)

    return pl.pallas_call(
        functools.partial(feed_kernel, layout),
        grid=(tiles + ff_steps + out_steps,),
        in_specs=[row_spec] * 3
        + [whole_spec(a.shape) for a in (vectors, up_bias, wo, wu, wd)],
        out_specs=[row_spec] * 3
        + [
            pl.BlockSpec((8, features), lambda i: (0, 0)),
            pl.BlockSpec((1, hidden), lambda i: (0, 0)),
            pl.BlockSpec((groups, 1) + blocked[2:], lambda i: (0, ff_at(i), 0, 0)),
            pl.BlockSpec((wide, features), lambda i: (ff_at(i), 0)),
            pl.BlockSpec(
                (features, narrow),
                lambda i: (0, jnp.clip(i - tiles - ff_steps, 0, out_steps - 1)),
            ),
        ],
        out_shape=[jax.ShapeDtypeStruct(tokens.shape, BF16)] * 3
        + [
            jax.ShapeDtypeStruct((8, features), F32),
            jax.ShapeDtypeStruct((1, hidden), F32),
            jax.ShapeDtypeStruct(blocked, BF16),
            jax.ShapeDtypeStruct(wd.shape, BF16),
            jax.ShapeDtypeStruct(wo.shape, BF16),
        ],
        scratch_shapes=[
            pltpu.VMEM((rows, hidden), BF16),
            pltpu.VMEM((rows, hidden), BF16),
            pltpu.VMEM((features, rows), BF16),
            pltpu.VMEM((features, rows), BF16),
            pltpu.VMEM((features, rows), BF16),
            pltpu.VMEM((rows, features), BF16),
        ],
        compiler_params=params(60),
        cost_estimate=cost(
            6 * rows * features * (features + 2 * hidden),
            2 * (6 * rows * features + 4 * features * hidden + 2 * features * features),
            2 * rows * hidden,
        ),
        name="feed_both_ways",
    )(tokens, attended, cotangent, vectors, up_bias, wo, wu, wd)


def spread(row):
    return jnp.broadcast_to(row, (PAIR, row.shape[1])).T


def as_row(ref):
    return ref[...].astype(F32).reshape(1, ref.shape[0])


def front_kernel(tokens_ref, group_ref, valid_ref, cot_ref, bq_ref, bv_ref, bo_ref, g1_ref, s1_ref, bd_ref,
                 g2_ref, s2_ref, bu_in, wq_any, wk_any, wv_any, wo_any, wu_any, wd_any,
                 out_ref, bg_ref, ag_ref, att_ref, lse_ref, qm_ref, km_ref,
                 first_t, feed_t, vg_ref, dbu_ref, q_any, k_any, v_any, rem_any, act_any, din_any,
                 wq, wk, wv, wo, wu, wd, tok_s, q_s, k_s, v_s, kr_s, vr_s, rem_s, own_codes, code_s, act_s, din_s,
                 bu_ref, weight_sem, out_sem, send_sem, recv_sem):
    s = pl.program_id(0)
    seqs = tok_s.shape[0]
    length, features = tok_s.shape[1:]
    hidden = act_s.shape[1]
    side = lax.axis_index("blk")
    other = {"blk": 1 - side}
    query_bias, value_bias, out_bias, gain_one, shift_one, down_bias, gain_two, shift_two = [
        as_row(ref) for ref in (bq_ref, bv_ref, bo_ref, g1_ref, s1_ref, bd_ref, g2_ref, s2_ref)
    ]
    pairs_of = [(wq_any, wq), (wk_any, wk), (wv_any, wv), (wo_any, wo), (wu_any, wu), (wd_any, wd)]

    def weight(i):
        return pltpu.make_async_copy(*pairs_of[i], weight_sem.at[i])

    def remote(source, target, at):
        return pltpu.make_async_remote_copy(
            src_ref=source,
            dst_ref=target,
            send_sem=send_sem.at[at],
            recv_sem=recv_sem.at[at],
            device_id=other,
            device_id_type=pl.DeviceIdType.MESH,
        )

    def exchange(at):
        return remote(tokens_ref.at[at], rem_s.at[at], at)

    def code_exchange():
        return remote(own_codes, code_s, seqs)

    def whole_out(i):
        source, target = ((q_s, q_any), (k_s, k_any.at[0]), (v_s, v_any.at[0]))[i]
        return pltpu.make_async_copy(source, target, out_sem.at[i])

    def part_out(i, at):
        source, target = (
            (kr_s, k_any.at[1, at]),
            (vr_s, v_any.at[1, at]),
            (rem_s.at[at], rem_any.at[at]),
            (act_s, act_any.at[at]),
            (din_s, din_any.at[at]),
        )[i]
        return pltpu.make_async_copy(source, target, out_sem.at[3 + i])

    @pl.when(s == 0)
    def _():
        barrier = pltpu.get_barrier_semaphore()
        pl.semaphore_signal(barrier, inc=1, device_id=other, device_id_type=pl.DeviceIdType.MESH)
        load = pltpu.make_async_copy(tokens_ref, tok_s, weight_sem.at[len(pairs_of)])
        load.start()
        for i in range(3):
            weight(i).start()
        codes = jnp.where(valid_ref[...] == 1, group_ref[...], -1).astype(F32)
        own_codes[...] = jnp.zeros_like(own_codes)
        own_codes[0:seqs] = codes
        pl.semaphore_wait(barrier, 1)
        exchange(0).start()
        code_exchange().start()
        for i in range(3, len(pairs_of)):
            weight(i).start()
        vg_ref[...] = jnp.zeros_like(vg_ref)
        dbu_ref[...] = jnp.zeros_like(dbu_ref)
        bu_ref[...] = as_row(bu_in)
        load.wait()
        for i in range(3):
            weight(i).wait()

        def project_own(at, carry):
            x = tok_s[at]
            q_s[at] = ((dot(x, wq[...]) + query_bias) * EXPO).astype(BF16)
            k_s[at] = dot(x, wk[...]).astype(BF16)
            v_s[at] = (dot(x, wv[...]) + value_bias).astype(BF16)
            return carry

        lax.fori_loop(0, seqs, project_own, 0)
        for i in range(3):
            whole_out(i).start()
        for i in range(3, len(pairs_of)):
            weight(i).wait()
        code_exchange().wait_recv()
        exchange(0).wait_send()
        if seqs > 1:
            exchange(1).start()

    for at in range(seqs):

        @pl.when(s == at)
        def _(at=at):
            exchange(at).wait_recv()
            if at:
                for i in range(3):
                    part_out(i, at - 1).wait()

    x = rem_s[s]
    kr_s[...] = dot(x, wk[...]).astype(BF16)
    vr_s[...] = (dot(x, wv[...]) + value_bias).astype(BF16)
    slot = lax.broadcasted_iota(jnp.int32, (1, PAIR), 1) % HEAD
    slot = slot.astype(F32)
    groups_row = group_ref[pl.ds(s, 1)].astype(F32)
    qm_ref[0] = jnp.where(spread(groups_row) == slot, 1.0, 0.0).astype(BF16)
    km_ref[0, 0] = jnp.where(spread(own_codes[pl.ds(s, 1)]) == slot, 0.0, MASKED).astype(BF16)
    km_ref[1, 0] = jnp.where(spread(code_s[pl.ds(s, 1)]) == slot, 0.0, MASKED).astype(BF16)
    for at in range(seqs):

        @pl.when(s == at)
        def _(at=at):
            for i in range(3):
                part_out(i, at).start()

    groups = features // (2 * PAIR)

    def heads(group, carry):
        lanes = pl.ds(pl.multiple_of(group * 2 * PAIR, 2 * PAIR), 2 * PAIR)
        attend_group(
            q_s[s, :, lanes],
            qm_ref[0],
            [(k_s[s, :, lanes], km_ref[0, 0], v_s[s, :, lanes]), (kr_s[:, lanes], km_ref[1, 0], vr_s[:, lanes])],
            att_ref.at[0, :, lanes],
            lse_ref.at[0, pl.ds(group * 2, 2)],
        )
        return carry

    lax.fori_loop(0, groups, heads, 0)

    for at in range(1, seqs):

        @pl.when(s == at)
        def _(at=at):
            for i in range(3, 5):
                part_out(i, at - 1).wait()

    tile = math.gcd(length, FEED_ROWS)
    chunk = math.gcd(hidden, 1024)
    spans = [slice(c, c + chunk) for c in range(0, hidden, chunk)]

    def feed_rows(t, carry):
        rows = pl.ds(pl.multiple_of(t * tile, tile), tile)
        att = att_ref[0, rows]
        normed_one, scale_one = norm_parts(
            tok_s[s, rows].astype(F32) + (dot(att, wo[...]) + out_bias)
        )
        first = normed_one * gain_one + shift_one
        first_low = first.astype(BF16)
        first_t[:, rows] = first_low.T
        feed = jnp.zeros_like(first) + down_bias
        ahead = dot(first_low, wu[:, spans[0]])
        for i, cols in enumerate(spans):
            inner = ahead + bu_ref[:, cols]
            if i + 1 < len(spans):
                ahead = dot(first_low, wu[:, spans[i + 1]])
            active, slope = gelu_and_slope(inner)
            active = active.astype(BF16)
            act_s[rows, cols] = active
            din_s[rows, cols] = slope.astype(BF16)
            feed += dot(active, wd[cols])
        normed_two, scale_two = norm_parts(first + feed)
        out_ref[0, rows] = (normed_two * gain_two + shift_two).astype(BF16)
        cot = cot_ref[0, rows].astype(F32)
        second = norm_back(cot * gain_two, normed_two, scale_two)
        feed_low = second.astype(BF16)
        feed_t[:, rows] = feed_low.T
        back = second
        ahead = dot(feed_low, wd[spans[0]], NT)
        for i, cols in enumerate(spans):
            inner = ahead
            if i + 1 < len(spans):
                ahead = dot(feed_low, wd[spans[i + 1]], NT)
            inner = (inner * din_s[rows, cols].astype(F32)).astype(BF16)
            din_s[rows, cols] = inner
            dbu_ref[:, cols] += column_sum(inner.astype(F32))
            back += dot(inner, wu[:, cols], NT)
        residual = norm_back(back * gain_one, normed_one, scale_one)
        branch_low = residual.astype(BF16)
        bg_ref[0, rows] = branch_low
        att_grad = dot(branch_low, wo[...], NT).astype(BF16)
        ag_ref[0, rows] = att_grad
        product = att_grad.astype(F32) * att.astype(F32)
        coarse = product.astype(BF16)
        fine = (product - coarse.astype(F32)).astype(BF16)
        heads_count = features // HEAD
        of_head = lax.broadcasted_iota(jnp.int32, (heads_count, features), 1) // HEAD
        selector = (of_head == lax.broadcasted_iota(jnp.int32, of_head.shape, 0)).astype(F32)
        selector = selector.astype(BF16)
        delta = dot(selector, coarse, NT) + dot(selector, fine, NT)
        for pair in range(features // PAIR):
            lse_ref[0, pair, 2:4, rows] = delta[2 * pair : 2 * pair + 2]
        for i, values in enumerate(
            (
                branch_low.astype(F32),
                back * normed_one,
                back,
                feed_low.astype(F32),
                cot * normed_two,
                cot,
            )
        ):
            vg_ref[i : i + 1] += column_sum(values)
        return carry

    lax.fori_loop(0, length // tile, feed_rows, 0)

    for at in range(seqs):

        @pl.when(s == at)
        def _(at=at):
            for i in range(3, 5):
                part_out(i, at).start()
            if at < seqs - 1:
                exchange(at + 1).wait_send()
            if at + 2 < seqs:
                exchange(at + 2).start()
            if at == seqs - 1:
                for i in range(3):
                    whole_out(i).wait()
                for i in range(5):
                    part_out(i, at).wait()
                code_exchange().wait_send()


def front(tokens, group_ids, valid, cotangent, vectors, up_bias, weights):
    seqs, length, features = tokens.shape
    hidden = up_bias.shape[0]
    pairs = features // PAIR
    anywhere = pl.BlockSpec(memory_space=pl.ANY)

    def at_seq(*shape):
        return pl.BlockSpec((1,) + shape, lambda s: (s,) + (0,) * len(shape))

    def of_seqs(*shape, dtype=BF16):
        return jax.ShapeDtypeStruct((seqs,) + shape, dtype)

    def fixed(*shape):
        return pl.BlockSpec(shape, lambda s: (0,) * len(shape))

    rows, mask, lses, wide = (length, features), (length, PAIR), (pairs, 8, length), (length, hidden)
    turned = pl.BlockSpec((features, length), lambda s: (0, s))
    return pl.pallas_call(
        front_kernel,
        grid=(seqs,),
        in_specs=[anywhere, whole_spec(group_ids.shape), whole_spec(valid.shape), at_seq(*rows)]
        + [whole_spec(v.shape) for v in vectors + (up_bias,)]
        + [anywhere] * 6,
        out_specs=[at_seq(*rows)] * 4
        + [at_seq(*lses), at_seq(*mask)]
        + [pl.BlockSpec((2, 1) + mask, lambda s: (0, s, 0, 0))]
        + [turned] * 2
        + [fixed(8, features), fixed(1, hidden)]
        + [anywhere] * 6,
        out_shape=[of_seqs(*rows)] * 4
        + [of_seqs(*lses, dtype=F32), of_seqs(*mask)]
        + [jax.ShapeDtypeStruct((2, seqs) + mask, BF16)]
        + [jax.ShapeDtypeStruct((features, seqs * length), BF16)] * 2
        + [jax.ShapeDtypeStruct((8, features), F32), jax.ShapeDtypeStruct((1, hidden), F32)]
        + [of_seqs(*rows)]
        + [jax.ShapeDtypeStruct((2, seqs) + rows, BF16)] * 2
        + [of_seqs(*rows)]
        + [of_seqs(*wide)] * 2,
        scratch_shapes=[pltpu.VMEM(w.shape, BF16) for w in weights]
        + [pltpu.VMEM(tokens.shape, BF16)] * 4
        + [pltpu.VMEM(rows, BF16)] * 2
        + [pltpu.VMEM(tokens.shape, BF16)]
        + [pltpu.VMEM((seqs + -seqs % 8, length), F32)] * 2
        + [pltpu.VMEM(wide, BF16)] * 2
        + [pltpu.VMEM((1, hidden), F32)]
        + [pltpu.SemaphoreType.DMA((7,)), pltpu.SemaphoreType.DMA((8,))]
        + [pltpu.SemaphoreType.DMA((seqs + 1,))] * 2,
        compiler_params=pltpu.CompilerParams(
            collective_id=2, has_side_effects=True, vmem_limit_bytes=63 * MIB
        ),
        cost_estimate=cost(
            2 * tokens.size * (9 * features + 4 * hidden + 8 * length), 2 * 20 * tokens.size, tokens.size * 24
        ),
        name="front",
    )(tokens, group_ids, valid, cotangent, *vectors, up_bias, *weights)


def feed_weights_kernel(blocks, first_ref, din_ref, feed_ref, act_ref, att_any, bg_any,
                        dwu_ref, dwd_ref, dwo_ref, up_s, up_in, down_s, down_in, out_s, out_in,
                        att_s, bg_s, near_sem, send_sem, recv_sem):
    step = pl.program_id(0)
    features = first_ref.shape[0]
    me = lax.axis_index("dp")
    core = me % 2
    other = {"dp": me + 1 - 2 * core}

    def loads():
        return [
            pltpu.make_async_copy(att_any, att_s, near_sem.at[0]),
            pltpu.make_async_copy(bg_any, bg_s, near_sem.at[1]),
        ]

    each, deep = down_in.shape[1:3]

    def piece(i, side):
        return pl.ds(pl.multiple_of((2 * i + side) * deep, 16), deep)

    def swaps(block):
        if block == blocks:
            pairs = [(out_s.at[:, 1 - core], out_in)]
        else:
            pairs = [(up_s.at[block % 2, :, 1 - core], up_in.at[block])]
            for i in range(each):
                pairs.append((down_s.at[block % 2, piece(i, 1 - core)], down_in.at[block, i]))
        return [
            pltpu.make_async_remote_copy(
                src_ref=source,
                dst_ref=target,
                send_sem=send_sem.at[(each + 1) * block + i],
                recv_sem=recv_sem.at[(each + 1) * block + i],
                device_id=other,
                device_id_type=pl.DeviceIdType.MESH,
            )
            for i, (source, target) in enumerate(pairs)
        ]

    @pl.when(step == 0)
    def _():
        for load in loads():
            load.start()
        barrier = pltpu.get_barrier_semaphore()
        pl.semaphore_signal(barrier, inc=1, device_id=other, device_id_type=pl.DeviceIdType.MESH)
        pl.semaphore_wait(barrier, 1)

    @pl.when(step < blocks)
    def _():
        slot = step % 2
        tile = math.gcd(features, 256)
        for start in range(0, features, tile):
            cols = slice(start, start + tile)
            up = dot(first_ref[...], din_ref[:, cols]).astype(BF16)
            up_s[slot, :, :, :, cols] = up.reshape(up_s.shape[1:4] + (tile,))
            down_s[slot, cols] = dot(feed_ref[...], act_ref[:, cols]).astype(BF16).T

    for block in range(blocks):

        @pl.when(step == block)
        def _(block=block):
            for swap in swaps(block):
                swap.start()

    @pl.when(step == blocks)
    def _():
        for load in loads():
            load.wait()
        out_s[...] = dot(att_s[...].T, bg_s[...]).astype(BF16).reshape(out_s.shape)
        for swap in swaps(blocks):
            swap.start()

    for block in range(blocks):

        @pl.when(step == block + 1)
        def _(block=block):
            for swap in swaps(block):
                swap.wait()
            dwu_ref[:, 0] = (up_s[block % 2, :, core].astype(F32) + up_in[block].astype(F32)).astype(BF16)
            for i in range(each):
                mine = down_s[block % 2, piece(i, core)].astype(F32)
                dwd_ref[i] = (mine + down_in[block, i].astype(F32)).astype(BF16)

    @pl.when(step == blocks + 1)
    def _():
        for swap in swaps(blocks):
            swap.wait()
        dwo_ref[...] = (out_s[:, core].astype(F32) + out_in[...].astype(F32)).astype(BF16)


def feed_weights(first_t, din, feed_t, act, att, bg):
    dp = lax.axis_size("dp")
    features, rows = first_t.shape
    hidden = act.shape[1]
    blocks, half, low, deep = hidden // features, dp // 2, features // dp, hidden // dp
    each = half // blocks
    wide_spec = pl.BlockSpec((rows, features), lambda i: (0, jnp.minimum(i, blocks - 1)))
    anywhere = pl.BlockSpec(memory_space=pl.ANY)

    def behind(i):
        return jnp.clip(i - 1, 0, blocks - 1)

    return pl.pallas_call(
        functools.partial(feed_weights_kernel, blocks),
        grid=(blocks + 2,),
        in_specs=[
            whole_spec(first_t.shape),
            wide_spec,
            whole_spec(feed_t.shape),
            wide_spec,
            anywhere,
            anywhere,
        ],
        out_specs=[
            pl.BlockSpec((half, 1, low, features), lambda i: (0, behind(i), 0, 0)),
            pl.BlockSpec((each, deep, features), lambda i: (behind(i), 0, 0)),
            pl.BlockSpec((half, low, features), lambda i: (0, 0, 0)),
        ],
        out_shape=[
            jax.ShapeDtypeStruct((half, blocks, low, features), BF16),
            jax.ShapeDtypeStruct((half, deep, features), BF16),
            jax.ShapeDtypeStruct((half, low, features), BF16),
        ],
        scratch_shapes=[
            pltpu.VMEM((2, half, 2, low, features), BF16),
            pltpu.VMEM((blocks, half, low, features), BF16),
            pltpu.VMEM((2, features, features), BF16),
            pltpu.VMEM((blocks, each, deep, features), BF16),
            pltpu.VMEM((half, 2, low, features), BF16),
            pltpu.VMEM((half, low, features), BF16),
            pltpu.VMEM(att.shape, BF16),
            pltpu.VMEM(bg.shape, BF16),
            pltpu.SemaphoreType.DMA((2,)),
            pltpu.SemaphoreType.DMA(((each + 1) * blocks + 1,)),
            pltpu.SemaphoreType.DMA(((each + 1) * blocks + 1,)),
        ],
        compiler_params=pltpu.CompilerParams(
            collective_id=3, has_side_effects=True, vmem_limit_bytes=63 * MIB
        ),
        cost_estimate=cost(
            2 * rows * features * (2 * hidden + features), 4 * rows * (hidden + 2 * features)
        ),
        name="feed_weights",
    )(first_t, din, feed_t, act, att, bg)


def own_back_kernel(bg_ref, dq_ref, dk_ref, dv_ref, wq_ref, wk_ref, wv_ref, out_ref):
    total = bg_ref[0].astype(F32) + dot(dq_ref[0], wq_ref[...], NT)
    total += dot(dk_ref[0], wk_ref[...], NT)
    total += dot(dv_ref[0], wv_ref[...], NT)
    out_ref[0] = total.astype(BF16)


def rem_back_kernel(dk_ref, dv_ref, wk_ref, wv_ref, out_ref):
    total = dot(dk_ref[0], wk_ref[...], NT) + dot(dv_ref[0], wv_ref[...], NT)
    out_ref[0] = total.astype(BF16)


def tokens_back(kernel, rows, weights):
    seqs, length, features = rows[0].shape
    tile = math.gcd(length, 512)
    row_spec = pl.BlockSpec((1, tile, features), lambda s, i: (s, i, 0))
    size = rows[0].size
    return pl.pallas_call(
        kernel,
        grid=(seqs, length // tile),
        in_specs=[row_spec] * len(rows) + [whole_spec(w.shape) for w in weights],
        out_specs=row_spec,
        out_shape=jax.ShapeDtypeStruct(rows[0].shape, BF16),
        compiler_params=params(60),
        cost_estimate=cost(2 * size * features * len(weights), 2 * size * (1 + len(rows))),
        name="tokens_back",
    )(*rows, *weights)


def weights_back_kernel(tok_ref, rem_ref, dq_ref, dko_ref, dvo_ref, dkr_ref, dvr_ref,
                        wq_ref, wk_ref, wv_ref, bq_ref, bv_ref, tok_t, rem_t):
    @pl.when(pl.program_id(0) == 0)
    def _():
        tok_t[...] = tok_ref[...].T
        rem_t[...] = rem_ref[...].T

    wq_ref[...] = dot(tok_t[...], dq_ref[...]).astype(BF16)
    wk_ref[...] = (dot(tok_t[...], dko_ref[...]) + dot(rem_t[...], dkr_ref[...])).astype(BF16)
    wv_ref[...] = (dot(tok_t[...], dvo_ref[...]) + dot(rem_t[...], dvr_ref[...])).astype(BF16)
    bq_ref[...] = column_sum(dq_ref[...].astype(F32))
    bv_ref[...] = column_sum(dvo_ref[...].astype(F32)) + column_sum(dvr_ref[...].astype(F32))


def weights_back(tok, rem, dq, dko, dvo, dkr, dvr):
    rows, features = tok.shape
    others = rem.shape[0]
    wide = math.gcd(features, 256)
    own_spec = pl.BlockSpec((rows, wide), lambda j: (0, j))
    rem_spec = pl.BlockSpec((others, wide), lambda j: (0, j))
    bias_spec = pl.BlockSpec((1, wide), lambda j: (0, j))
    return pl.pallas_call(
        weights_back_kernel,
        grid=(features // wide,),
        in_specs=[
            whole_spec(tok.shape),
            whole_spec(rem.shape),
            own_spec,
            own_spec,
            own_spec,
            rem_spec,
            rem_spec,
        ],
        out_specs=[pl.BlockSpec((features, wide), lambda j: (0, j))] * 3 + [bias_spec] * 2,
        out_shape=[jax.ShapeDtypeStruct((features, features), BF16)] * 3
        + [jax.ShapeDtypeStruct((1, features), F32)] * 2,
        scratch_shapes=[
            pltpu.VMEM((features, rows), BF16),
            pltpu.VMEM((features, others), BF16),
        ],
        compiler_params=params(60),
        cost_estimate=cost(
            2 * features * features * (3 * rows + 2 * others),
            2 * (4 * tok.size + 3 * rem.size + 3 * features * features),
        ),
        name="weights_back",
    )(tok, rem, dq, dko, dvo, dkr, dvr)


def halve(value, axis, bit):
    size = lax.axis_size(axis)
    mine = (lax.axis_index(axis) >> bit) & 1
    pairs = value.reshape((value.shape[0] // 2, 2) + value.shape[1:])
    keep = lax.dynamic_index_in_dim(pairs, mine, 1, keepdims=False)
    send = lax.dynamic_index_in_dim(pairs, 1 - mine, 1, keepdims=False)
    came = lax.ppermute(send, axis, [(i, i ^ (1 << bit)) for i in range(size)])
    return keep.astype(F32) + came.astype(F32)


def scatter_sum(value, low=True):
    dp, blk = lax.axis_size("dp"), lax.axis_size("blk")
    if dp & (dp - 1) or blk & (blk - 1):
        return lax.psum_scatter(
            value.astype(F32), ("dp", "blk"), scatter_dimension=0, tiled=True
        )
    kept = value.dtype
    each = value.shape[0] // (dp * blk)
    value = value.reshape((dp, blk * each) + value.shape[1:])
    for bit in range(dp.bit_length() - 1):
        value = halve(value, "dp", bit).astype(kept)
    value = value.reshape((blk, each) + value.shape[2:])
    for bit in range(blk.bit_length() - 1):
        value = halve(value, "blk", bit)
        value = value if (2 << bit) == blk else value.astype(kept)
    return value.reshape(value.shape[1:]).astype(F32)


class Unit:
    def __init__(self, parts, rows, columns, halves, outs):
        self.parts, self.rows, self.columns = parts, rows, columns
        self.halves, self.outs = halves, outs
        self.first = 1 if parts else 0
        self.half = rows // (2 * halves)
        self.last_type = BF16 if (rows // 2) % 16 == 0 else F32


def timetable(units, bits, seqs, groups, slot_us, token_us):
    free, pending, table = {}, [], []
    slots = seqs * groups * 2

    def launch(key, now):
        kind, which, step = key
        if kind == "tokens":
            link, us = "blk", token_us
        elif kind == "vectors":
            link, us = None, 1.0
        else:
            us = units[which].rows * units[which].columns * 2e-5
            us *= 1 << max(bits - 1 - step, 0)
            us *= {0: 0.3, bits - 1: 3.0}.get(step, 1.1)
            link = {0: "core", bits - 1: "far", bits: "blk"}.get(step, "near")
        start = max(now, free.get(link, 0.0))
        if link:
            free[link] = start + us
        if kind != "tokens":
            pending.append((start + us + 2.0, key))

    for u, unit in enumerate(units):
        if unit.parts:
            launch(("unit", u, 1), 3.0)
    first_group = sum(1 for unit in units if unit.parts)
    now = 0.0
    while len(table) < slots or pending:
        slot = len(table)
        if slot < slots:
            now = (slot + 1) * slot_us
            part, major, minor = slot // (seqs * groups), slot // groups % seqs, slot % groups
            if part == 0 and minor == groups - 1:
                launch(("tokens", major, 0), now)
            major, minor = divmod(slot - seqs * groups, seqs)
            if part == 1 and minor == seqs - 1:
                launch(("unit", first_group + major, 0), now)
            if slot == slots - 1:
                launch(("vectors", 0, 0), now)
            due = sorted(p for p in pending if p[0] <= now)
        else:
            due = [min(pending)]
            now = max(now + 0.3, due[0][0])
        table.append([key for _, key in due])
        for found in due:
            pending.remove(found)
            kind, which, step = found[1]
            if step < bits:
                launch((kind, which, step + 1), now)
    tail = [key for keys in table[slots:] for key in keys]
    return table[:slots], tail + [("tokens", s, 0) for s in range(seqs)]


def order_of(step, seqs, groups):
    part = step // (seqs * groups)
    left = step - part * (seqs * groups)
    s = left // groups * (1 - part) + left % seqs * part
    h = left % groups * (1 - part) + left // seqs * part
    return part, s, h


def back_kernel(units, bits, groups, table, tail, n_out, *refs):
    (q_ref, qm_ref, g_ref, lse_ref, k_ref, km_ref, v_ref,
     tok_ref, rem_ref, wq_ref, wk_ref, wv_ref, vg_ref, vu_ref) = refs[:14]
    sources, refs = refs[14:17], list(refs[17:])
    tokens_any, rem_in, *outs = refs[:n_out]
    refs = refs[n_out:]
    kept = [refs.pop(0) for _ in units]
    landed = [
        [refs.pop(0) if k >= unit.first else None for k in range(bits)] for unit in units
    ]
    wide = [refs.pop(0) for _ in units]
    parting = [refs.pop(0) for _ in units]
    last = [refs.pop(0) for _ in units]
    (weight_sum, group_src, total_s, turned, dq_part, dq_s, dk_s, dv_s,
     rem_out, vec, vec_in, bias_sum, send_sem, recv_sem, local_sem, out_sem) = refs
    step = pl.program_id(0)
    steps = pl.num_programs(0)
    seqs = rem_out.shape[0]
    part, s, h = order_of(step, seqs, groups)
    features = tok_ref.shape[2]
    me, side = lax.axis_index("dp"), lax.axis_index("blk")
    core = me % 2

    def swapped(k):
        return {1: 2, 2: 1}.get(k, k) if bits > 2 else k

    def pick(values, k):
        return values[k] + (values[swapped(k)] - values[k]) * core

    bit_own = [(me // (1 << bit)) % 2 for bit in range(bits)]
    across = [me + (1 << bit) * (1 - 2 * bit_own[bit]) for bit in range(bits)]
    own = [pick(bit_own, k) for k in range(bits)]
    partner = [{"dp": pick(across, k)} for k in range(bits)] + [{"blk": 1 - side}]
    first_group = sum(1 for unit in units if unit.parts)
    lead = (slice(None),) * (bits - 1)

    def natural(digits):
        by_step = [None] + list(digits[::-1])
        return tuple(
            by_step[bit] if swapped(bit) == bit else pick(by_step, bit) for bit in range(bits - 1, 0, -1)
        )

    def digits_of(n, count):
        return [(n // (1 << (count - 1 - i))) % 2 for i in range(count)]

    sems = {}
    for u, unit in enumerate(units):
        for k in range(unit.first, bits + 1):
            sems["unit", u, k, 0] = len(sems)
    for k in range(bits + 1):
        sems["vectors", 0, k, 0] = len(sems)
    for k in range(seqs):
        sems["tokens", k, 0, 0] = len(sems)

    def remote(source, target, device, key):
        return pltpu.make_async_remote_copy(
            src_ref=source,
            dst_ref=target,
            send_sem=send_sem.at[sems[key]],
            recv_sem=recv_sem.at[sems[key]],
            device_id=device,
            device_id_type=pl.DeviceIdType.MESH,
        )

    near_sems = {}
    for u, unit in enumerate(units):
        for p in range(len(unit.parts or ())):
            for n in range(1 << min(bits - 1, 2)):
                near_sems[u, p, n] = len(near_sems)

    def spot(k, value):
        return tuple(
            own[at] if at < k else value if at == k else slice(None) for at in range(bits - 1, 0, -1)
        )

    def copies(kind, which, k):
        if kind == "tokens":
            return [remote(rem_out.at[which], rem_in.at[which], partner[bits], (kind, which, 0, 0))]
        if kind == "vectors":
            return [remote(vec.at[k], vec_in.at[k], partner[k], (kind, 0, k, 0))]
        u, unit = which, units[which]
        if k == bits:
            return [remote(parting[u], last[u], partner[bits], (kind, u, k, 0))]
        if k:
            source = kept[u].at[spot(k, 1 - own[k])]
            return [remote(source, landed[u][k], partner[k], (kind, u, k, 0))]
        source = group_src.at[(u - first_group,) + lead + (1 - core,)]
        return [remote(source, landed[u][0], partner[0], (kind, u, 0, 0))]

    def near_copies(u):
        found, row = [], 0
        for p, (source, first, rows) in enumerate(units[u].parts):
            for n in range(1 << min(bits - 1, 2)):
                digits = digits_of(n, min(bits - 1, 2))
                digits = [slice(None)] * (bits - 1 - len(digits)) + digits
                found.append(
                    pltpu.make_async_copy(
                        sources[source].at[natural(digits) + (pl.ds(first, rows),)],
                        kept[u].at[tuple(digits) + (pl.ds(row, rows),)],
                        local_sem.at[near_sems[u, p, n]],
                    )
                )
            row += rows
        return found

    def launch(*key):
        for copy in copies(*key):
            copy.start()

    def halves_of(u, which):
        unit = units[u]
        return [
            wide[u][pl.ds(pl.multiple_of(i * 2 * unit.half + which * unit.half, 8), unit.half)]
            for i in range(unit.halves)
        ]

    def receive(kind, which, k):
        for copy in copies(kind, which, k):
            copy.wait_recv()
        if kind == "tokens":
            return
        if kind == "vectors":
            vec[k + 1] = vec[k] + vec_in[k]
            if k < bits:
                launch(kind, 0, k + 1)
            return
        u, unit = which, units[which]
        if k == bits:
            for i, (mine, (out, rows, columns)) in enumerate(zip(halves_of(u, side), unit.outs)):
                came = last[u][...].astype(F32)[i * unit.half : (i + 1) * unit.half]
                outs[out][rows, columns] = mine + came
            return
        place = spot(k, own[k]) if k else lead
        open_at = [i for i, at in enumerate(place) if isinstance(at, slice)]

        def add(n, carry):
            at, where = list(place), digits_of(n, len(open_at))
            for i, digit in zip(open_at, where):
                at[i] = digit
            at = tuple(at)
            if k:
                mine, came = kept[u][at], landed[u][k][tuple(where)]
            else:
                mine = group_src[(u - first_group,) + natural(at) + (core,)]
                came = landed[u][0][natural(at)]
            total = mine.astype(F32) + came.astype(F32)
            if k == bits - 1:
                wide[u][...] = total
            else:
                kept[u][at] = total.astype(BF16)
            return carry

        if open_at:
            lax.fori_loop(0, 1 << len(open_at), add, 0)
        else:
            add(0, 0)
        if k == bits - 1:
            pieces = halves_of(u, 1 - side)
            pieces = pieces[0] if len(pieces) == 1 else jnp.concatenate(pieces, axis=0)
            parting[u][...] = pieces.astype(unit.last_type)
        launch(kind, u, k + 1)

    @pl.when(step == 0)
    def _():
        barrier = pltpu.get_barrier_semaphore()
        for other in partner:
            pl.semaphore_signal(barrier, inc=1, device_id=other, device_id_type=pl.DeviceIdType.MESH)
        pl.semaphore_wait(barrier, bits + 1)
        for u, unit in enumerate(units):
            if unit.parts:
                for copy in near_copies(u):
                    copy.start()
        for u, unit in enumerate(units):
            if unit.parts:
                for copy in near_copies(u):
                    copy.wait()
                launch("unit", u, 1)
        weight_sum[...] = jnp.zeros_like(weight_sum)
        bias_sum[...] = jnp.zeros_like(bias_sum)

    @pl.when((part == 0) & (h == 0))
    def _():
        turned[0] = rem_ref[0].T
        total_s[...] = jnp.zeros_like(total_s)

    @pl.when((part == 1) & (h == 0))
    def _():
        turned[s] = tok_ref[0].T

    width = q_ref.shape[2]
    columns = pl.ds(pl.multiple_of(h * width, width), width)

    found = attend_back_part(
        q_ref[0], qm_ref[0], g_ref[0], lse_ref.at[0], k_ref[0, 0], km_ref[0, 0], v_ref[0, 0],
        dk_s.at[s, :, columns], dv_s.at[s, :, columns],
    )
    dk, dv = dk_s[s, :, columns], dv_s[s, :, columns]
    x_t = turned[s * part]
    weight_sum[h, 1] += dot(x_t, dk)
    weight_sum[h, 2] += dot(x_t, dv)
    bias_sum[h, 1:2] += column_sum(dv.astype(F32))

    @pl.when(part == 0)
    def _():
        total_s[...] += dot(dk, wk_ref[:, columns], NT) + dot(dv, wv_ref[:, columns], NT)
        for pair, value in enumerate(found):
            dq_part[s, h, pair] = value.astype(dq_part.dtype)

    @pl.when(part == 1)
    def _():
        queries = []
        for pair, value in enumerate(found):
            value = (value + dq_part[s, h, pair].astype(F32)) * SCALE
            queries.append(value.T.astype(BF16))
        dq = jnp.concatenate(queries, axis=1)
        dq_s[s, :, columns] = dq
        weight_sum[h, 0] += dot(x_t, dq)
        bias_sum[h, 0:1] += column_sum(dq.astype(F32))

    for at in range(seqs):

        @pl.when(step == (at + 1) * groups - 1)
        def _(at=at):
            rem_out[at] = total_s[...].astype(BF16)
            launch("tokens", at, 0)

    for at in range(groups):

        @pl.when(step == steps - (groups - 1 - at) * seqs - 1)
        def _(at=at):
            rows = features // (1 << bits)
            for i in range(3):
                piece = weight_sum[at, i].astype(BF16)
                piece = piece.reshape((2,) * bits + (rows, piece.shape[1]))
                group_src[(at,) + (slice(None),) * bits + (slice(i * rows, (i + 1) * rows),)] = piece
            launch("unit", first_group + at, 0)

    @pl.when(step == steps - 1)
    def _():
        vec[0] = jnp.zeros_like(vec[0])
        vec[0, 0:6] = vg_ref[0:6]
        for at in range(groups):
            vec[0, 6:8, at * width : (at + 1) * width] = bias_sum[at, 0:2]
        blocks = vu_ref.shape[1] // features
        for at in range(blocks):
            vec[0, 8 + at : 9 + at] = vu_ref[:, at * features : (at + 1) * features]
        launch("vectors", 0, 0)

    for at, keys in enumerate(table):
        if keys:

            @pl.when(step == at)
            def _(keys=keys):
                for key in keys:
                    receive(*key)

    @pl.when(step == steps - 1)
    def _():
        def own_out(at):
            return pltpu.make_async_copy(dq_s.at[at], tokens_any.at[at], out_sem.at[at])

        left = list(tail)
        for at in range(seqs):
            total = dot(dq_s[at], wq_ref[...], NT)
            total += dot(dk_s[at], wk_ref[...], NT) + dot(dv_s[at], wv_ref[...], NT)
            dq_s[at] = total.astype(BF16)
            own_out(at).start()
            for _ in range(3):
                if left:
                    receive(*left.pop(0))
        for key in left:
            receive(*key)
        for at in range(seqs):
            own_out(at).wait()
        shards = (1 << bits) * 2
        place = me * 2 + side
        share = features // shards
        rows = pltpu.roll(vec[bits + 1, 0:8], (shards - place) * share % features, 1)
        outs[-1][0:8] = rows[:, :PAIR]
        share = vu_ref.shape[1] // shards
        each = features // share
        row = vec[bits + 1, pl.ds(8 + place // each, 1)]
        rows = pltpu.roll(jnp.broadcast_to(row, (8, features)), (each - place % each) * share % features, 1)
        outs[-1][8:16] = rows[:, :PAIR]
        for u, unit in enumerate(units):
            for k in range(unit.first, bits + 1):
                for copy in copies("unit", u, k):
                    copy.wait_send()
        for k in range(bits + 1):
            copies("vectors", 0, k)[0].wait_send()
        for k in range(seqs):
            copies("tokens", k, 0)[0].wait_send()


def back_and_sum(q, qm, g, lse, k, km, v, tokens, rem_tokens, weights, dwd, dwu, dwo, vg, vu):
    bits = lax.axis_size("dp").bit_length() - 1
    seqs, length, features = q.shape
    width = math.gcd(features, 2 * PAIR)
    groups, pairs = features // width, width // PAIR
    low, deep, blocks = dwo.shape[1], dwd.shape[1], dwu.shape[1]
    lead = (2,) * bits
    sources = [x.reshape(lead[1:] + (-1, features)) for x in (dwd, dwu, dwo)]
    every = slice(None)
    units = []
    quarter = deep // 4
    for i in range(2):
        at = slice(i * quarter, (i + 1) * quarter)
        parts = [(0, i * quarter, quarter), (0, (2 + i) * quarter, quarter)]
        units.append(Unit(parts, 2 * quarter, features, 1, [(0, at, every)]))
    for i in range(2):
        found = range(i * blocks // 2, (i + 1) * blocks // 2)
        units.append(
            Unit(
                [(1, found[0] * low, len(found) * low)],
                len(found) * low,
                features,
                len(found),
                [(1, every, slice(b * features, (b + 1) * features)) for b in found],
            )
        )
    units.append(Unit([(2, 0, low)], low, features, 1, [(2, every, every)]))
    for h in range(groups):
        columns = slice(h * width, (h + 1) * width)
        units.append(Unit(None, 3 * low, width, 3, [(3 + i, every, columns) for i in range(3)]))
    table, tail = timetable(units, bits, seqs, groups, 5.6, length * features * 4e-5)

    half = low // 2
    out_shape = [
        jax.ShapeDtypeStruct(q.shape, BF16),
        jax.ShapeDtypeStruct(q.shape, BF16),
        jax.ShapeDtypeStruct((deep // 2, features), F32),
        jax.ShapeDtypeStruct((half, blocks * features), F32),
        *(jax.ShapeDtypeStruct((half, features), F32) for _ in range(4)),
        jax.ShapeDtypeStruct((16, PAIR), F32),
    ]
    tops = lead[1:]
    scratch = [pltpu.VMEM(tops + (u.rows, u.columns), BF16) for u in units]
    for u in units:
        scratch += [pltpu.VMEM(tops[k:] + (u.rows, u.columns), BF16) for k in range(u.first, bits)]
    scratch += [pltpu.VMEM((u.rows, u.columns), F32) for u in units]
    scratch += [pltpu.VMEM((u.rows // 2, u.columns), u.last_type) for u in units] * 2
    count = len(units) * (bits + 1) + bits + 1 + seqs
    near = sum(len(u.parts) << min(bits - 1, 2) for u in units if u.parts)
    scratch += [
        pltpu.VMEM((groups, 3, features, width), F32),
        pltpu.VMEM((groups,) + lead + (3 * low, width), BF16),
        pltpu.VMEM((length, features), F32),
        pltpu.VMEM((seqs, features, length), BF16),
        pltpu.VMEM((seqs, groups, pairs, PAIR, length), F32),
        *(pltpu.VMEM((seqs, length, features), BF16) for _ in range(4)),
        pltpu.VMEM((bits + 2, 16, features), F32),
        pltpu.VMEM((bits + 1, 16, features), F32),
        pltpu.VMEM((groups, 8, width), F32),
        pltpu.SemaphoreType.DMA((count,)),
        pltpu.SemaphoreType.DMA((count,)),
        pltpu.SemaphoreType.DMA((near,)),
        pltpu.SemaphoreType.DMA((seqs,)),
    ]

    def at_step(shape, index):
        return pl.BlockSpec(shape, lambda i: index(*order_of(i, seqs, groups)))

    heads_at = at_step((1, length, width), lambda p, s, h: (s, 0, h))
    keys_at = at_step((1, 1, length, width), lambda p, s, h: (1 - p, s, 0, h))

    def rows_at(which):
        last = seqs - 1
        return pl.BlockSpec(
            (1, length, features),
            lambda i: (jnp.clip(i // groups if which == 0 else i - seqs * groups, 0, last), 0, 0),
            pipeline_mode=pl.Buffered(1),
        )

    def fixed(shape):
        return pl.BlockSpec(shape, lambda i: (0,) * len(shape), pipeline_mode=pl.Buffered(1))

    return pl.pallas_call(
        functools.partial(back_kernel, units, bits, groups, table, tail, len(out_shape)),
        grid=(2 * seqs * groups,),
        in_specs=[
            heads_at,
            at_step((1, length, PAIR), lambda p, s, h: (s, 0, 0)),
            heads_at,
            at_step((1, pairs, 8, length), lambda p, s, h: (s, h, 0, 0)),
            keys_at,
            at_step((1, 1, length, PAIR), lambda p, s, h: (1 - p, s, 0, 0)),
            keys_at,
            rows_at(1),
            rows_at(0),
        ]
        + [whole_spec(w.shape) for w in weights + (vg, vu)]
        + [pl.BlockSpec(memory_space=pl.ANY)] * 3,
        out_specs=[pl.BlockSpec(memory_space=pl.ANY)] * 2
        + [fixed(s.shape) for s in out_shape[2:]],
        out_shape=out_shape,
        scratch_shapes=scratch,
        compiler_params=pltpu.CompilerParams(
            collective_id=1, has_side_effects=True, vmem_limit_bytes=63 * MIB
        ),
        cost_estimate=cost(80 * q.size * length, 2 * q.size * 14, 2 * q.size * length // HEAD),
        name="back_and_sum",
    )(q, qm, g, lse, k, km, v, tokens, rem_tokens, *weights, vg, vu, *sources)


def finish_kernel(residual_ref, own_ref, rem_ref, *refs):
    ins, outs = refs[:7], refs[7:]
    total = residual_ref[...].astype(F32) + own_ref[...].astype(F32) + rem_ref[...].astype(F32)
    outs[0][...] = total.astype(BF16)

    @pl.when(pl.program_id(0) == 0)
    def _():
        for source, target in zip(ins[:6], outs[1:7]):
            target[...] = source[...]
        for i, target in enumerate(outs[7:]):
            target[...] = ins[6][i, : target.shape[0]]


def finish(residual, own, rem, matrices, vectors, shares):
    seqs, length, features = own.shape
    row_spec = pl.BlockSpec((1, length, features), lambda s: (s, 0, 0))

    def fixed(shape):
        return pl.BlockSpec(shape, lambda s: (0,) * len(shape))

    shapes = [m.shape for m in matrices] + [(n,) for n in shares]
    return pl.pallas_call(
        finish_kernel,
        grid=(seqs,),
        in_specs=[row_spec] * 3 + [fixed(m.shape) for m in matrices] + [fixed(vectors.shape)],
        out_specs=[row_spec] + [fixed(s) for s in shapes],
        out_shape=[jax.ShapeDtypeStruct(own.shape, BF16)] + [jax.ShapeDtypeStruct(s, F32) for s in shapes],
        compiler_params=params(60),
        cost_estimate=cost(2 * own.size, 8 * own.size),
        name="finish",
    )(residual, own, rem, *matrices, vectors)


def back_plainly(q, qm, o, g, lse, own, rem, bg, tokens, rem_tokens, weights, dwd, dwu, dwo, vg, vu):
    seqs, length, features = q.shape
    dp, blk = lax.axis_size("dp"), lax.axis_size("blk")
    dq, dko, dvo, dkr, dvr = attend_back(q, qm, o, g, lse, own, rem)
    rem_gradient = tokens_back(rem_back_kernel, (dkr, dvr), weights[1:])
    came = [
        lax.ppermute(part, "blk", [((i + r) % blk, i) for i in range(blk)])
        for r, part in enumerate(jnp.split(rem_gradient, blk - 1, axis=1), 1)
    ]
    flat = [v.reshape(-1, features) for v in (tokens, rem_tokens, dq, dko, dvo, dkr, dvr)]
    dwq, dwk, dwv, dbq, dbv = weights_back(*flat)
    total = tokens_back(own_back_kernel, (bg, dq, dko, dvo), weights).astype(F32)
    for part in came:
        total += part.astype(F32)
    dwu = jnp.moveaxis(dwu[0], 0, 1).reshape(features, -1)
    summed = [scatter_sum(w) for w in (dwd, dwu, dwo, dwq, dwk, dwv)]
    rows = [vg[i] for i in range(6)] + [dbq, dbv, vu]
    rows = [scatter_sum(v.reshape(dp * blk, -1)) for v in rows]
    return [total.astype(BF16)] + summed + [[v[0] for v in rows]]


def body(
    tokens,
    query_weight,
    query_bias,
    key_weight,
    value_weight,
    value_bias,
    out_weight,
    out_bias,
    gain_one,
    shift_one,
    up_weight,
    up_bias,
    down_weight,
    down_bias,
    gain_two,
    shift_two,
    group_ids,
    valid_mask,
    cotangent,
):
    seqs, length, features = tokens.shape
    rows = seqs * length
    blk = lax.axis_size("blk")

    def from_others(value):
        found = [
            lax.ppermute(value, "blk", [(i, (i + r) % blk) for i in range(blk)])
            for r in range(1, blk)
        ]
        return found[0] if len(found) == 1 else jnp.concatenate(found, axis=1)

    codes = jnp.where(valid_mask == 1, group_ids, -1)
    dp = lax.axis_size("dp")
    by_kernel = blk == 2 and dp & (dp - 1) == 0 and dp > 1 and (features // dp) % 16 == 0
    projections = (query_weight, key_weight, value_weight)
    vectors = (
        query_bias,
        value_bias,
        out_bias,
        gain_one,
        shift_one,
        down_bias,
        gain_two,
        shift_two,
    )

    if by_kernel:
        (block_out, branch_gradient, attended_gradient, attended, lse, query_mask, key_masks,
         first_t, feed_t, vector_gradients, up_bias_gradient, queries, keys, values,
         rem_tokens, active, inner_gradient) = front(
            tokens,
            group_ids,
            valid_mask,
            cotangent,
            vectors,
            up_bias,
            projections + (out_weight, up_weight, down_weight),
        )
        dwu, dwd, dwo = feed_weights(
            first_t,
            inner_gradient.reshape(rows, -1),
            feed_t,
            active.reshape(rows, -1),
            attended.reshape(rows, features),
            branch_gradient.reshape(rows, features),
        )
        own_gradient, rem_gradient, *matrices, vectors = back_and_sum(
            queries,
            query_mask,
            attended_gradient,
            lse,
            keys,
            key_masks,
            values,
            tokens,
            rem_tokens,
            projections,
            dwd,
            dwu,
            dwo,
            vector_gradients,
            up_bias_gradient,
        )
        shares = [features // (dp * blk)] * 8 + [up_bias.size // (dp * blk)]
        found = finish(branch_gradient, own_gradient, rem_gradient, matrices, vectors, shares)
        tokens_gradient, dwd, dwu, dwo, dwq, dwk, dwv, *rows_left = found
    else:
        rem_tokens = from_others(tokens)
        rem_codes = from_others(codes.astype(BF16)).astype(jnp.int32)
        slot = jnp.arange(PAIR, dtype=jnp.int32) % HEAD

        def key_mask(code):
            return jnp.where(code[:, :, None] == slot, 0.0, MASKED).astype(BF16)

        query_mask = (group_ids[:, :, None] == slot).astype(BF16)
        vectors = jnp.stack(vectors).astype(F32)
        queries, own_keys, own_values = project(tokens, vectors, projections)
        rem_keys, rem_values = project(rem_tokens, vectors, projections[1:])
        own = (own_keys, key_mask(codes), own_values)
        rem = (rem_keys, key_mask(rem_codes), rem_values)
        attended, lse = attend(queries, query_mask, own, rem)
        (block_out, branch_gradient, attended_gradient, vector_gradients, up_bias_gradient,
         dwu, dwd, dwo) = feed_both_ways(
            tokens.reshape(rows, features),
            attended.reshape(rows, features),
            cotangent.reshape(rows, features),
            vectors[2:],
            up_bias.astype(F32)[None],
            out_weight,
            up_weight,
            down_weight,
            1,
        )
        tokens_gradient, dwd, dwu, dwo, dwq, dwk, dwv, rows_left = back_plainly(
            queries,
            query_mask,
            attended,
            attended_gradient.reshape(tokens.shape),
            lse,
            own,
            rem,
            branch_gradient.reshape(tokens.shape),
            tokens,
            rem_tokens,
            projections,
            dwd,
            dwu,
            dwo,
            vector_gradients,
            up_bias_gradient,
        )
    dbo, dg1, ds1, dbd, dg2, ds2, dbq, dbv, dbu = rows_left
    return (
        block_out.reshape(tokens.shape),
        tokens_gradient,
        dwq,
        dbq,
        dwk,
        dwv,
        dbv,
        dwo,
        dbo,
        dg1,
        ds1,
        dwu,
        dbu,
        dwd,
        dbd,
        dg2,
        ds2,
    )


def solution(mesh):
    rows, shared, pair = P("dp", "blk", None), P(), P("dp", "blk")
    matrix, vector = P(("dp", "blk"), None), P(("dp", "blk"))
    return jax.shard_map(
        body,
        mesh=mesh,
        in_specs=(rows,) + (shared,) * 15 + (pair, pair, rows),
        out_specs=(
            rows,
            rows,
            matrix,
            vector,
            matrix,
            matrix,
            vector,
            matrix,
            vector,
            vector,
            vector,
            matrix,
            vector,
            matrix,
            vector,
            vector,
            vector,
        ),
        check_vma=False,
    )
```

```python
import functools
import math

import jax
import jax.numpy as jnp
from jax import lax
from jax.experimental import pallas as pl
from jax.experimental.pallas import tpu as pltpu
from jax.sharding import PartitionSpec as P

HEAD = 64
PAIR = 2 * HEAD
EPSILON = 1e-12
MASKED = -1e30
FLOOR = -3e38
SCALE = HEAD**-0.5
EXPO = SCALE * math.log2(math.e)
NN = (((1,), (0,)), ((), ()))
NT = (((1,), (1,)), ((), ()))
F32 = jnp.float32
BF16 = jnp.bfloat16
MIB = 1 << 20
FEED_ROWS = 256


def dot(left, right, dims=NN):
    return lax.dot_general(left, right, dims, preferred_element_type=F32)


def whole_spec(shape):
    return pl.BlockSpec(shape, lambda *_: (0,) * len(shape), pipeline_mode=pl.Buffered(1))


def params(limit):
    return pltpu.CompilerParams(vmem_limit_bytes=limit * MIB)


def cost(flops, touched, exps=0):
    return pl.CostEstimate(flops=int(flops), bytes_accessed=int(touched), transcendentals=int(exps))


def project_kernel(has_query, *refs):
    if has_query:
        x_ref, bias_ref, wq_ref, wk_ref, wv_ref, q_ref, k_ref, v_ref = refs
    else:
        x_ref, bias_ref, wk_ref, wv_ref, k_ref, v_ref = refs
    x = x_ref[0]
    if has_query:
        q_ref[0] = ((dot(x, wq_ref[...]) + bias_ref[0:1]) * EXPO).astype(BF16)
    k_ref[0] = dot(x, wk_ref[...]).astype(BF16)
    v_ref[0] = (dot(x, wv_ref[...]) + bias_ref[1:2]).astype(BF16)


def project(x, bias, weights):
    seqs, length, features = x.shape
    tile = math.gcd(length, 512)
    grid = (seqs, length // tile)
    row_spec = pl.BlockSpec((1, tile, features), lambda s, i: (s, i, 0))
    return pl.pallas_call(
        functools.partial(project_kernel, len(weights) == 3),
        grid=grid,
        in_specs=[row_spec, whole_spec(bias.shape)] + [whole_spec(w.shape) for w in weights],
        out_specs=[row_spec] * len(weights),
        out_shape=[jax.ShapeDtypeStruct(x.shape, BF16)] * len(weights),
        compiler_params=params(60),
        cost_estimate=cost(
            2 * x.size * features * len(weights), 2 * x.size * (1 + len(weights))
        ),
        name="project",
    )(x, bias, *weights)


def low_lanes():
    return lax.broadcasted_iota(jnp.int32, (1, PAIR), 1) < HEAD


def attend_group(q, qm, sources, o_ref, lse_ref):
    length = q.shape[0]
    tile = math.gcd(length, 512)
    low = low_lanes()
    one = jnp.ones((1, PAIR), BF16)
    todo = [
        (pair, row, head)
        for pair in range(q.shape[1] // PAIR)
        for row in range(0, length, tile)
        for head in range(2)
    ]

    def lanes_of(pair):
        return slice(pair * PAIR, (pair + 1) * PAIR)

    def mine_of(head):
        return ~low if head else low

    def scores_of(pair, row, head):
        mine, lanes = mine_of(head), lanes_of(pair)
        q_side = jnp.where(mine, q[row : row + tile, lanes], qm[row : row + tile])
        return [dot(q_side, jnp.where(mine, k[:, lanes], km), NT) for k, km, _ in sources]

    ahead = scores_of(*todo[0])
    for i, (pair, row, head) in enumerate(todo):
        scores = ahead
        if i + 1 < len(todo):
            ahead = scores_of(*todo[i + 1])
        top = functools.reduce(
            jnp.maximum, [jnp.max(part, axis=-1, keepdims=True) for part in scores]
        )
        weights = [jnp.exp2(part - top).astype(BF16) for part in scores]
        total = sum(
            dot(w, jnp.where(mine_of(head), v[:, lanes_of(pair)], one))
            for w, (_, _, v) in zip(weights, sources)
        )
        if head == 0:
            earlier, earlier_top = total, top
            continue
        totals = pltpu.roll(jnp.where(low, total, earlier), HEAD, 1)
        rows = slice(row, row + tile)
        o_ref[rows, lanes_of(pair)] = (jnp.where(low, earlier, total) / totals).astype(BF16)
        lse = (jnp.where(low, earlier_top, top) + jnp.log2(totals)).T
        lse_ref[pair, 0:1, rows] = lse[0:1]
        lse_ref[pair, 1:2, rows] = lse[HEAD : HEAD + 1]


def attend_kernel(q_ref, qm_ref, ko_ref, kmo_ref, vo_ref, kr_ref, kmr_ref, vr_ref, o_ref, lse_ref):
    sources = [(ko_ref[0], kmo_ref[0], vo_ref[0]), (kr_ref[0], kmr_ref[0], vr_ref[0])]
    attend_group(q_ref[0], qm_ref[0], sources, o_ref.at[0], lse_ref.at[0])


def pair_spec(length, lanes):
    return pl.BlockSpec((1, length, lanes), lambda s, h: (s, 0, h))


def mask_spec(length):
    return pl.BlockSpec((1, length, PAIR), lambda s, h: (s, 0, 0))


def lse_spec(length, lanes):
    return pl.BlockSpec((1, lanes // PAIR, 8, length), lambda s, h: (s, h, 0, 0))


def attend(q, qm, own, rem):
    seqs, length, features = q.shape
    lanes = math.gcd(features, 2 * PAIR)
    other = rem[0].shape[1]
    own_spec, rem_spec = pair_spec(length, lanes), pair_spec(other, lanes)
    return pl.pallas_call(
        attend_kernel,
        grid=(seqs, features // lanes),
        in_specs=[own_spec, mask_spec(length)]
        + [own_spec, mask_spec(length), own_spec]
        + [rem_spec, mask_spec(other), rem_spec],
        out_specs=[own_spec, lse_spec(length, lanes)],
        out_shape=[
            jax.ShapeDtypeStruct(q.shape, BF16),
            jax.ShapeDtypeStruct((seqs, features // PAIR, 8, length), F32),
        ],
        compiler_params=params(60),
        cost_estimate=cost(
            16 * q.size * (length + other), 2 * q.size * 6, q.size * (length + other) // HEAD
        ),
        name="attend",
    )(q, qm, *own, *rem)


def attend_back_part(q, qm, g, lse_ref, k, km, v, dk_ref, dv_ref):
    low = low_lanes()
    none = jnp.zeros((1, PAIR), BF16)
    pairs = q.shape[1] // PAIR
    todo = [(pair, head) for pair in range(pairs) for head in range(2)]

    def lanes_of(pair):
        return slice(pair * PAIR, (pair + 1) * PAIR)

    def mine_of(head):
        return ~low if head else low

    def products(pair, head):
        mine, lanes = mine_of(head), lanes_of(pair)
        return (
            dot(jnp.where(mine, k[:, lanes], km), jnp.where(mine, q[:, lanes], qm), NT),
            dot(jnp.where(mine, v[:, lanes], none), g[:, lanes], NT),
        )

    found = []
    ahead = products(*todo[0])
    for i, (pair, head) in enumerate(todo):
        scores, grads = ahead
        if i + 1 < len(todo):
            ahead = products(*todo[i + 1])
        lanes, mine = lanes_of(pair), mine_of(head)
        if head == 0:
            k_t = k[:, lanes].T
            dk = dv = 0.0
            dq = []
        probs = jnp.exp2(scores - lse_ref[pair, head : head + 1, :])
        grads = (probs * (grads - lse_ref[pair, 2 + head : 3 + head, :])).astype(BF16)
        dv += dot(probs.astype(BF16), jnp.where(mine, g[:, lanes], none))
        dk += dot(grads, jnp.where(mine, q[:, lanes], none))
        dq.append(dot(k_t[head * HEAD : (head + 1) * HEAD], grads))
        if head == 1:
            dk_ref[:, lanes] = (dk * (SCALE / EXPO)).astype(BF16)
            dv_ref[:, lanes] = dv.astype(BF16)
            found.append(jnp.concatenate(dq, axis=0))
    return found


def attend_back_kernel(q_ref, qm_ref, g_ref, lse_ref, ko_ref, kmo_ref, vo_ref, kr_ref, kmr_ref,
                       vr_ref, dq_ref, dko_ref, dvo_ref, dkr_ref, dvr_ref):
    parts = ((ko_ref, kmo_ref, vo_ref, dko_ref, dvo_ref), (kr_ref, kmr_ref, vr_ref, dkr_ref, dvr_ref))
    found = [
        attend_back_part(
            q_ref[0], qm_ref[0], g_ref[0], lse_ref.at[0], k[0], km[0], v[0], dk.at[0], dv.at[0]
        )
        for k, km, v, dk, dv in parts
    ]
    for pair, both in enumerate(zip(*found)):
        dq_ref[0, :, pair * PAIR : (pair + 1) * PAIR] = (sum(both) * SCALE).T.astype(BF16)


def attend_back(q, qm, o, g, lse, own, rem):
    seqs, length, features = q.shape
    delta = (g.astype(F32) * o.astype(F32)).reshape(seqs, length, features // PAIR, 2, HEAD).sum(-1)
    lse = lax.dynamic_update_slice(lse, jnp.transpose(delta, (0, 2, 3, 1)), (0, 0, 2, 0))
    lanes = math.gcd(features, 2 * PAIR)
    other = rem[0].shape[1]
    own_spec, rem_spec = pair_spec(length, lanes), pair_spec(other, lanes)
    return pl.pallas_call(
        attend_back_kernel,
        grid=(seqs, features // lanes),
        in_specs=[own_spec, mask_spec(length), own_spec, lse_spec(length, lanes)]
        + [own_spec, mask_spec(length), own_spec]
        + [rem_spec, mask_spec(other), rem_spec],
        out_specs=[own_spec] * 3 + [rem_spec] * 2,
        out_shape=[jax.ShapeDtypeStruct(q.shape, BF16)] * 3
        + [jax.ShapeDtypeStruct(rem[0].shape, BF16)] * 2,
        compiler_params=params(60),
        cost_estimate=cost(
            40 * q.size * (length + other), 2 * q.size * 14, q.size * (length + other) // HEAD
        ),
        name="attend_back",
    )(q, qm, g, lse, *own, *rem)


def gelu_and_slope(x):
    bell = jnp.exp2(x * x * (-0.5 * math.log2(math.e)))
    below = 1.0 + (0.3275911 / math.sqrt(2.0)) * jnp.abs(x)
    t = pl.reciprocal(below, approx=True)
    t = t * (2.0 - below * t)
    poly = 1.061405429 * t - 1.453152027
    poly = poly * t + 1.421413741
    poly = poly * t - 0.284496736
    poly = poly * t + 0.254829592
    tail = (0.5 * poly) * t * bell
    share = jnp.where(x >= 0.0, 1.0 - tail, tail)
    return x * share, share + x * bell * (1.0 / math.sqrt(2.0 * math.pi))


def mean(values):
    return jnp.sum(values, axis=-1, keepdims=True) * (1.0 / values.shape[-1])


def norm_parts(values):
    centred = values - mean(values)
    scale = lax.rsqrt(mean(centred * centred) + EPSILON)
    return centred * scale, scale


def norm_back(upper, normed, scale):
    return scale * (upper - mean(upper) - normed * mean(upper * normed))


def column_sum(values):
    return jnp.sum(values, axis=0, keepdims=True)


def feed_kernel(layout, tok_ref, att_ref, cot_ref, vec_ref, bu_ref, wo_ref, wu_ref, wd_ref,
                out_ref, bg_ref, ag_ref, vg_ref, dbu_ref, dwu_ref, dwd_ref, dwo_ref,
                act_s, din_s, first_t, feed_t, att_t, bg_s):
    tiles, ff_steps, chunk, wide, narrow = layout
    step = pl.program_id(0)
    tile = tok_ref.shape[0]
    hidden = act_s.shape[1]
    vec = [vec_ref[i : i + 1] for i in range(6)]
    out_bias, gain_one, shift_one, down_bias, gain_two, shift_two = vec

    @pl.when(step == 0)
    def _():
        vg_ref[...] = jnp.zeros_like(vg_ref)
        dbu_ref[...] = jnp.zeros_like(dbu_ref)

    @pl.when(step < tiles)
    def _():
        start = pl.multiple_of(step * tile, tile)
        rows = pl.ds(start, tile)
        att = att_ref[...]
        normed_one, scale_one = norm_parts(
            tok_ref[...].astype(F32) + (dot(att, wo_ref[...]) + out_bias)
        )
        first = normed_one * gain_one + shift_one
        first_low = first.astype(BF16)
        first_t[:, rows] = first_low.T
        att_t[:, rows] = att.T
        feed = jnp.zeros_like(first) + down_bias
        spans = [slice(c, c + chunk) for c in range(0, hidden, chunk)]
        ahead = dot(first_low, wu_ref[:, spans[0]])
        for i, cols in enumerate(spans):
            inner = ahead + bu_ref[:, cols]
            if i + 1 < len(spans):
                ahead = dot(first_low, wu_ref[:, spans[i + 1]])
            active, slope = gelu_and_slope(inner)
            active = active.astype(BF16)
            act_s[rows, cols] = active
            din_s[rows, cols] = slope.astype(BF16)
            feed += dot(active, wd_ref[cols])
        normed_two, scale_two = norm_parts(first + feed)
        out_ref[...] = (normed_two * gain_two + shift_two).astype(BF16)
        cot = cot_ref[...].astype(F32)
        second = norm_back(cot * gain_two, normed_two, scale_two)
        feed_low = second.astype(BF16)
        feed_t[:, rows] = feed_low.T
        back = second
        ahead = dot(feed_low, wd_ref[spans[0]], NT)
        for i, cols in enumerate(spans):
            inner = ahead
            if i + 1 < len(spans):
                ahead = dot(feed_low, wd_ref[spans[i + 1]], NT)
            inner = (inner * din_s[rows, cols].astype(F32)).astype(BF16)
            din_s[rows, cols] = inner
            dbu_ref[:, cols] += column_sum(inner.astype(F32))
            back += dot(inner, wu_ref[:, cols], NT)
        residual = norm_back(back * gain_one, normed_one, scale_one)
        branch_low = residual.astype(BF16)
        bg_ref[...] = branch_low
        bg_s[rows] = branch_low
        ag_ref[...] = dot(branch_low, wo_ref[...], NT).astype(BF16)
        for i, values in enumerate(
            (
                branch_low.astype(F32),
                back * normed_one,
                back,
                feed_low.astype(F32),
                cot * normed_two,
                cot,
            )
        ):
            vg_ref[i : i + 1] += column_sum(values)

    @pl.when((step >= tiles) & (step < tiles + ff_steps))
    def _():
        cols = pl.ds(pl.multiple_of((step - tiles) * wide, wide), wide)
        dwu = dot(first_t[...], din_s[:, cols]).astype(BF16)
        dwu_ref[...] = dwu.reshape(dwu_ref.shape)
        dwd_ref[...] = dot(feed_t[...], act_s[:, cols]).astype(BF16).T

    @pl.when(step >= tiles + ff_steps)
    def _():
        cols = pl.ds(pl.multiple_of((step - tiles - ff_steps) * narrow, narrow), narrow)
        dwo_ref[...] = dot(att_t[...], bg_s[:, cols]).astype(BF16)


def feed_both_ways(tokens, attended, cotangent, vectors, up_bias, wo, wu, wd, groups):
    rows, features = tokens.shape
    hidden = wu.shape[1]
    tile = math.gcd(rows, 256)
    tiles = rows // tile
    wide, narrow = features, math.gcd(features, 384)
    ff_steps, out_steps = hidden // wide, features // narrow
    layout = (tiles, ff_steps, math.gcd(hidden, 512), wide, narrow)
    blocked = (groups, ff_steps, features // groups, wide)
    row_spec = pl.BlockSpec((tile, features), lambda i: (jnp.minimum(i, tiles - 1), 0))

    def ff_at(i):
        return jnp.clip(i - tiles, 0, ff_steps - 1)

    return pl.pallas_call(
        functools.partial(feed_kernel, layout),
        grid=(tiles + ff_steps + out_steps,),
        in_specs=[row_spec] * 3
        + [whole_spec(a.shape) for a in (vectors, up_bias, wo, wu, wd)],
        out_specs=[row_spec] * 3
        + [
            pl.BlockSpec((8, features), lambda i: (0, 0)),
            pl.BlockSpec((1, hidden), lambda i: (0, 0)),
            pl.BlockSpec((groups, 1) + blocked[2:], lambda i: (0, ff_at(i), 0, 0)),
            pl.BlockSpec((wide, features), lambda i: (ff_at(i), 0)),
            pl.BlockSpec(
                (features, narrow),
                lambda i: (0, jnp.clip(i - tiles - ff_steps, 0, out_steps - 1)),
            ),
        ],
        out_shape=[jax.ShapeDtypeStruct(tokens.shape, BF16)] * 3
        + [
            jax.ShapeDtypeStruct((8, features), F32),
            jax.ShapeDtypeStruct((1, hidden), F32),
            jax.ShapeDtypeStruct(blocked, BF16),
            jax.ShapeDtypeStruct(wd.shape, BF16),
            jax.ShapeDtypeStruct(wo.shape, BF16),
        ],
        scratch_shapes=[
            pltpu.VMEM((rows, hidden), BF16),
            pltpu.VMEM((rows, hidden), BF16),
            pltpu.VMEM((features, rows), BF16),
            pltpu.VMEM((features, rows), BF16),
            pltpu.VMEM((features, rows), BF16),
            pltpu.VMEM((rows, features), BF16),
        ],
        compiler_params=params(60),
        cost_estimate=cost(
            6 * rows * features * (features + 2 * hidden),
            2 * (6 * rows * features + 4 * features * hidden + 2 * features * features),
            2 * rows * hidden,
        ),
        name="feed_both_ways",
    )(tokens, attended, cotangent, vectors, up_bias, wo, wu, wd)


def spread(row):
    return jnp.broadcast_to(row, (PAIR, row.shape[1])).T


def as_row(ref):
    return ref[...].astype(F32).reshape(1, ref.shape[0])


def front_kernel(tokens_ref, group_ref, valid_ref, cot_ref, bq_ref, bv_ref, bo_ref, g1_ref, s1_ref, bd_ref,
                 g2_ref, s2_ref, bu_in, wq_any, wk_any, wv_any, wo_any, wu_any, wd_any,
                 out_ref, bg_ref, ag_ref, att_ref, lse_ref, qm_ref, km_ref,
                 first_t, feed_t, vg_ref, dbu_ref, q_any, k_any, v_any, rem_any, act_any, din_any,
                 wq, wk, wv, wo, wu, wd, tok_s, q_s, k_s, v_s, kr_s, vr_s, rem_s, own_codes, code_s, act_s, din_s,
                 bu_ref, weight_sem, out_sem, send_sem, recv_sem):
    s = pl.program_id(0)
    seqs = tok_s.shape[0]
    length, features = tok_s.shape[1:]
    hidden = act_s.shape[1]
    side = lax.axis_index("blk")
    other = {"blk": 1 - side}
    query_bias, value_bias, out_bias, gain_one, shift_one, down_bias, gain_two, shift_two = [
        as_row(ref) for ref in (bq_ref, bv_ref, bo_ref, g1_ref, s1_ref, bd_ref, g2_ref, s2_ref)
    ]
    pairs_of = [(wq_any, wq), (wk_any, wk), (wv_any, wv), (wo_any, wo), (wu_any, wu), (wd_any, wd)]

    def weight(i):
        return pltpu.make_async_copy(*pairs_of[i], weight_sem.at[i])

    def remote(source, target, at):
        return pltpu.make_async_remote_copy(
            src_ref=source,
            dst_ref=target,
            send_sem=send_sem.at[at],
            recv_sem=recv_sem.at[at],
            device_id=other,
            device_id_type=pl.DeviceIdType.MESH,
        )

    def exchange(at):
        return remote(tokens_ref.at[at], rem_s.at[at], at)

    def code_exchange():
        return remote(own_codes, code_s, seqs)

    def whole_out(i):
        source, target = ((q_s, q_any), (k_s, k_any.at[0]), (v_s, v_any.at[0]))[i]
        return pltpu.make_async_copy(source, target, out_sem.at[i])

    def part_out(i, at):
        source, target = (
            (kr_s, k_any.at[1, at]),
            (vr_s, v_any.at[1, at]),
            (rem_s.at[at], rem_any.at[at]),
            (act_s, act_any.at[at]),
            (din_s, din_any.at[at]),
        )[i]
        return pltpu.make_async_copy(source, target, out_sem.at[3 + i])

    @pl.when(s == 0)
    def _():
        barrier = pltpu.get_barrier_semaphore()
        pl.semaphore_signal(barrier, inc=1, device_id=other, device_id_type=pl.DeviceIdType.MESH)
        load = pltpu.make_async_copy(tokens_ref, tok_s, weight_sem.at[len(pairs_of)])
        load.start()
        for i in range(3):
            weight(i).start()
        codes = jnp.where(valid_ref[...] == 1, group_ref[...], -1).astype(F32)
        own_codes[...] = jnp.zeros_like(own_codes)
        own_codes[0:seqs] = codes
        pl.semaphore_wait(barrier, 1)
        exchange(0).start()
        code_exchange().start()
        for i in range(3, len(pairs_of)):
            weight(i).start()
        vg_ref[...] = jnp.zeros_like(vg_ref)
        dbu_ref[...] = jnp.zeros_like(dbu_ref)
        bu_ref[...] = as_row(bu_in)
        load.wait()
        for i in range(3):
            weight(i).wait()

        def project_own(at, carry):
            x = tok_s[at]
            q_s[at] = ((dot(x, wq[...]) + query_bias) * EXPO).astype(BF16)
            k_s[at] = dot(x, wk[...]).astype(BF16)
            v_s[at] = (dot(x, wv[...]) + value_bias).astype(BF16)
            return carry

        lax.fori_loop(0, seqs, project_own, 0)
        for i in range(3):
            whole_out(i).start()
        for i in range(3, len(pairs_of)):
            weight(i).wait()
        code_exchange().wait_recv()
        exchange(0).wait_send()
        if seqs > 1:
            exchange(1).start()

    for at in range(seqs):

        @pl.when(s == at)
        def _(at=at):
            exchange(at).wait_recv()
            if at:
                for i in range(3):
                    part_out(i, at - 1).wait()

    x = rem_s[s]
    kr_s[...] = dot(x, wk[...]).astype(BF16)
    vr_s[...] = (dot(x, wv[...]) + value_bias).astype(BF16)
    slot = lax.broadcasted_iota(jnp.int32, (1, PAIR), 1) % HEAD
    slot = slot.astype(F32)
    groups_row = group_ref[pl.ds(s, 1)].astype(F32)
    qm_ref[0] = jnp.where(spread(groups_row) == slot, 1.0, 0.0).astype(BF16)
    km_ref[0, 0] = jnp.where(spread(own_codes[pl.ds(s, 1)]) == slot, 0.0, MASKED).astype(BF16)
    km_ref[1, 0] = jnp.where(spread(code_s[pl.ds(s, 1)]) == slot, 0.0, MASKED).astype(BF16)
    for at in range(seqs):

        @pl.when(s == at)
        def _(at=at):
            for i in range(3):
                part_out(i, at).start()

    groups = features // (2 * PAIR)

    def heads(group, carry):
        lanes = pl.ds(pl.multiple_of(group * 2 * PAIR, 2 * PAIR), 2 * PAIR)
        attend_group(
            q_s[s, :, lanes],
            qm_ref[0],
            [(k_s[s, :, lanes], km_ref[0, 0], v_s[s, :, lanes]), (kr_s[:, lanes], km_ref[1, 0], vr_s[:, lanes])],
            att_ref.at[0, :, lanes],
            lse_ref.at[0, pl.ds(group * 2, 2)],
        )
        return carry

    lax.fori_loop(0, groups, heads, 0)

    for at in range(1, seqs):

        @pl.when(s == at)
        def _(at=at):
            for i in range(3, 5):
                part_out(i, at - 1).wait()

    tile = math.gcd(length, FEED_ROWS)
    chunk = math.gcd(hidden, 1024)
    spans = [slice(c, c + chunk) for c in range(0, hidden, chunk)]

    def feed_rows(t, carry):
        rows = pl.ds(pl.multiple_of(t * tile, tile), tile)
        att = att_ref[0, rows]
        normed_one, scale_one = norm_parts(
            tok_s[s, rows].astype(F32) + (dot(att, wo[...]) + out_bias)
        )
        first = normed_one * gain_one + shift_one
        first_low = first.astype(BF16)
        first_t[:, rows] = first_low.T
        feed = jnp.zeros_like(first) + down_bias
        ahead = dot(first_low, wu[:, spans[0]])
        for i, cols in enumerate(spans):
            inner = ahead + bu_ref[:, cols]
            if i + 1 < len(spans):
                ahead = dot(first_low, wu[:, spans[i + 1]])
            active, slope = gelu_and_slope(inner)
            active = active.astype(BF16)
            act_s[rows, cols] = active
            din_s[rows, cols] = slope.astype(BF16)
            feed += dot(active, wd[cols])
        normed_two, scale_two = norm_parts(first + feed)
        out_ref[0, rows] = (normed_two * gain_two + shift_two).astype(BF16)
        cot = cot_ref[0, rows].astype(F32)
        second = norm_back(cot * gain_two, normed_two, scale_two)
        feed_low = second.astype(BF16)
        feed_t[:, rows] = feed_low.T
        back = second
        ahead = dot(feed_low, wd[spans[0]], NT)
        for i, cols in enumerate(spans):
            inner = ahead
            if i + 1 < len(spans):
                ahead = dot(feed_low, wd[spans[i + 1]], NT)
            inner = (inner * din_s[rows, cols].astype(F32)).astype(BF16)
            din_s[rows, cols] = inner
            dbu_ref[:, cols] += column_sum(inner.astype(F32))
            back += dot(inner, wu[:, cols], NT)
        residual = norm_back(back * gain_one, normed_one, scale_one)
        branch_low = residual.astype(BF16)
        bg_ref[0, rows] = branch_low
        att_grad = dot(branch_low, wo[...], NT).astype(BF16)
        ag_ref[0, rows] = att_grad
        product = att_grad.astype(F32) * att.astype(F32)
        coarse = product.astype(BF16)
        fine = (product - coarse.astype(F32)).astype(BF16)
        heads_count = features // HEAD
        of_head = lax.broadcasted_iota(jnp.int32, (heads_count, features), 1) // HEAD
        selector = (of_head == lax.broadcasted_iota(jnp.int32, of_head.shape, 0)).astype(F32)
        selector = selector.astype(BF16)
        delta = dot(selector, coarse, NT) + dot(selector, fine, NT)
        for pair in range(features // PAIR):
            lse_ref[0, pair, 2:4, rows] = delta[2 * pair : 2 * pair + 2]
        for i, values in enumerate(
            (
                branch_low.astype(F32),
                back * normed_one,
                back,
                feed_low.astype(F32),
                cot * normed_two,
                cot,
            )
        ):
            vg_ref[i : i + 1] += column_sum(values)
        return carry

    lax.fori_loop(0, length // tile, feed_rows, 0)

    for at in range(seqs):

        @pl.when(s == at)
        def _(at=at):
            for i in range(3, 5):
                part_out(i, at).start()
            if at < seqs - 1:
                exchange(at + 1).wait_send()
            if at + 2 < seqs:
                exchange(at + 2).start()
            if at == seqs - 1:
                for i in range(3):
                    whole_out(i).wait()
                for i in range(5):
                    part_out(i, at).wait()
                code_exchange().wait_send()


def front(tokens, group_ids, valid, cotangent, vectors, up_bias, weights):
    seqs, length, features = tokens.shape
    hidden = up_bias.shape[0]
    pairs = features // PAIR
    anywhere = pl.BlockSpec(memory_space=pl.ANY)

    def at_seq(*shape):
        return pl.BlockSpec((1,) + shape, lambda s: (s,) + (0,) * len(shape))

    def of_seqs(*shape, dtype=BF16):
        return jax.ShapeDtypeStruct((seqs,) + shape, dtype)

    def fixed(*shape):
        return pl.BlockSpec(shape, lambda s: (0,) * len(shape))

    rows, mask, lses, wide = (length, features), (length, PAIR), (pairs, 8, length), (length, hidden)
    turned = pl.BlockSpec((features, length), lambda s: (0, s))
    return pl.pallas_call(
        front_kernel,
        grid=(seqs,),
        in_specs=[anywhere, whole_spec(group_ids.shape), whole_spec(valid.shape), at_seq(*rows)]
        + [whole_spec(v.shape) for v in vectors + (up_bias,)]
        + [anywhere] * 6,
        out_specs=[at_seq(*rows)] * 4
        + [at_seq(*lses), at_seq(*mask)]
        + [pl.BlockSpec((2, 1) + mask, lambda s: (0, s, 0, 0))]
        + [turned] * 2
        + [fixed(8, features), fixed(1, hidden)]
        + [anywhere] * 6,
        out_shape=[of_seqs(*rows)] * 4
        + [of_seqs(*lses, dtype=F32), of_seqs(*mask)]
        + [jax.ShapeDtypeStruct((2, seqs) + mask, BF16)]
        + [jax.ShapeDtypeStruct((features, seqs * length), BF16)] * 2
        + [jax.ShapeDtypeStruct((8, features), F32), jax.ShapeDtypeStruct((1, hidden), F32)]
        + [of_seqs(*rows)]
        + [jax.ShapeDtypeStruct((2, seqs) + rows, BF16)] * 2
        + [of_seqs(*rows)]
        + [of_seqs(*wide)] * 2,
        scratch_shapes=[pltpu.VMEM(w.shape, BF16) for w in weights]
        + [pltpu.VMEM(tokens.shape, BF16)] * 4
        + [pltpu.VMEM(rows, BF16)] * 2
        + [pltpu.VMEM(tokens.shape, BF16)]
        + [pltpu.VMEM((seqs + -seqs % 8, length), F32)] * 2
        + [pltpu.VMEM(wide, BF16)] * 2
        + [pltpu.VMEM((1, hidden), F32)]
        + [pltpu.SemaphoreType.DMA((7,)), pltpu.SemaphoreType.DMA((8,))]
        + [pltpu.SemaphoreType.DMA((seqs + 1,))] * 2,
        compiler_params=pltpu.CompilerParams(
            collective_id=2, has_side_effects=True, vmem_limit_bytes=63 * MIB
        ),
        cost_estimate=cost(
            2 * tokens.size * (9 * features + 4 * hidden + 8 * length), 2 * 20 * tokens.size, tokens.size * 24
        ),
        name="front",
    )(tokens, group_ids, valid, cotangent, *vectors, up_bias, *weights)


def feed_weights_kernel(blocks, first_ref, din_ref, feed_ref, act_ref, att_any, bg_any,
                        dwu_ref, dwd_ref, dwo_ref, up_s, up_in, down_s, down_in, out_s, out_in,
                        att_s, bg_s, near_sem, send_sem, recv_sem):
    step = pl.program_id(0)
    features = first_ref.shape[0]
    me = lax.axis_index("dp")
    core = me % 2
    other = {"dp": me + 1 - 2 * core}

    def loads():
        return [
            pltpu.make_async_copy(att_any, att_s, near_sem.at[0]),
            pltpu.make_async_copy(bg_any, bg_s, near_sem.at[1]),
        ]

    each, deep = down_in.shape[1:3]

    def piece(i, side):
        return pl.ds(pl.multiple_of((2 * i + side) * deep, 16), deep)

    def swaps(block):
        if block == blocks:
            pairs = [(out_s.at[:, 1 - core], out_in)]
        else:
            pairs = [(up_s.at[block % 2, :, 1 - core], up_in.at[block])]
            for i in range(each):
                pairs.append((down_s.at[block % 2, piece(i, 1 - core)], down_in.at[block, i]))
        return [
            pltpu.make_async_remote_copy(
                src_ref=source,
                dst_ref=target,
                send_sem=send_sem.at[(each + 1) * block + i],
                recv_sem=recv_sem.at[(each + 1) * block + i],
                device_id=other,
                device_id_type=pl.DeviceIdType.MESH,
            )
            for i, (source, target) in enumerate(pairs)
        ]

    @pl.when(step == 0)
    def _():
        for load in loads():
            load.start()
        barrier = pltpu.get_barrier_semaphore()
        pl.semaphore_signal(barrier, inc=1, device_id=other, device_id_type=pl.DeviceIdType.MESH)
        pl.semaphore_wait(barrier, 1)

    @pl.when(step < blocks)
    def _():
        slot = step % 2
        tile = math.gcd(features, 256)
        for start in range(0, features, tile):
            cols = slice(start, start + tile)
            up = dot(first_ref[...], din_ref[:, cols]).astype(BF16)
            up_s[slot, :, :, :, cols] = up.reshape(up_s.shape[1:4] + (tile,))
            down_s[slot, cols] = dot(feed_ref[...], act_ref[:, cols]).astype(BF16).T

    for block in range(blocks):

        @pl.when(step == block)
        def _(block=block):
            for swap in swaps(block):
                swap.start()

    @pl.when(step == blocks)
    def _():
        for load in loads():
            load.wait()
        out_s[...] = dot(att_s[...].T, bg_s[...]).astype(BF16).reshape(out_s.shape)
        for swap in swaps(blocks):
            swap.start()

    for block in range(blocks):

        @pl.when(step == block + 1)
        def _(block=block):
            for swap in swaps(block):
                swap.wait()
            dwu_ref[:, 0] = (up_s[block % 2, :, core].astype(F32) + up_in[block].astype(F32)).astype(BF16)
            for i in range(each):
                mine = down_s[block % 2, piece(i, core)].astype(F32)
                dwd_ref[i] = (mine + down_in[block, i].astype(F32)).astype(BF16)

    @pl.when(step == blocks + 1)
    def _():
        for swap in swaps(blocks):
            swap.wait()
        dwo_ref[...] = (out_s[:, core].astype(F32) + out_in[...].astype(F32)).astype(BF16)


def feed_weights(first_t, din, feed_t, act, att, bg):
    dp = lax.axis_size("dp")
    features, rows = first_t.shape
    hidden = act.shape[1]
    blocks, half, low, deep = hidden // features, dp // 2, features // dp, hidden // dp
    each = half // blocks
    wide_spec = pl.BlockSpec((rows, features), lambda i: (0, jnp.minimum(i, blocks - 1)))
    anywhere = pl.BlockSpec(memory_space=pl.ANY)

    def behind(i):
        return jnp.clip(i - 1, 0, blocks - 1)

    return pl.pallas_call(
        functools.partial(feed_weights_kernel, blocks),
        grid=(blocks + 2,),
        in_specs=[
            whole_spec(first_t.shape),
            wide_spec,
            whole_spec(feed_t.shape),
            wide_spec,
            anywhere,
            anywhere,
        ],
        out_specs=[
            pl.BlockSpec((half, 1, low, features), lambda i: (0, behind(i), 0, 0)),
            pl.BlockSpec((each, deep, features), lambda i: (behind(i), 0, 0)),
            pl.BlockSpec((half, low, features), lambda i: (0, 0, 0)),
        ],
        out_shape=[
            jax.ShapeDtypeStruct((half, blocks, low, features), BF16),
            jax.ShapeDtypeStruct((half, deep, features), BF16),
            jax.ShapeDtypeStruct((half, low, features), BF16),
        ],
        scratch_shapes=[
            pltpu.VMEM((2, half, 2, low, features), BF16),
            pltpu.VMEM((blocks, half, low, features), BF16),
            pltpu.VMEM((2, features, features), BF16),
            pltpu.VMEM((blocks, each, deep, features), BF16),
            pltpu.VMEM((half, 2, low, features), BF16),
            pltpu.VMEM((half, low, features), BF16),
            pltpu.VMEM(att.shape, BF16),
            pltpu.VMEM(bg.shape, BF16),
            pltpu.SemaphoreType.DMA((2,)),
            pltpu.SemaphoreType.DMA(((each + 1) * blocks + 1,)),
            pltpu.SemaphoreType.DMA(((each + 1) * blocks + 1,)),
        ],
        compiler_params=pltpu.CompilerParams(
            collective_id=3, has_side_effects=True, vmem_limit_bytes=63 * MIB
        ),
        cost_estimate=cost(
            2 * rows * features * (2 * hidden + features), 4 * rows * (hidden + 2 * features)
        ),
        name="feed_weights",
    )(first_t, din, feed_t, act, att, bg)


def own_back_kernel(bg_ref, dq_ref, dk_ref, dv_ref, wq_ref, wk_ref, wv_ref, out_ref):
    total = bg_ref[0].astype(F32) + dot(dq_ref[0], wq_ref[...], NT)
    total += dot(dk_ref[0], wk_ref[...], NT)
    total += dot(dv_ref[0], wv_ref[...], NT)
    out_ref[0] = total.astype(BF16)


def rem_back_kernel(dk_ref, dv_ref, wk_ref, wv_ref, out_ref):
    total = dot(dk_ref[0], wk_ref[...], NT) + dot(dv_ref[0], wv_ref[...], NT)
    out_ref[0] = total.astype(BF16)


def tokens_back(kernel, rows, weights):
    seqs, length, features = rows[0].shape
    tile = math.gcd(length, 512)
    row_spec = pl.BlockSpec((1, tile, features), lambda s, i: (s, i, 0))
    size = rows[0].size
    return pl.pallas_call(
        kernel,
        grid=(seqs, length // tile),
        in_specs=[row_spec] * len(rows) + [whole_spec(w.shape) for w in weights],
        out_specs=row_spec,
        out_shape=jax.ShapeDtypeStruct(rows[0].shape, BF16),
        compiler_params=params(60),
        cost_estimate=cost(2 * size * features * len(weights), 2 * size * (1 + len(rows))),
        name="tokens_back",
    )(*rows, *weights)


def weights_back_kernel(tok_ref, rem_ref, dq_ref, dko_ref, dvo_ref, dkr_ref, dvr_ref,
                        wq_ref, wk_ref, wv_ref, bq_ref, bv_ref, tok_t, rem_t):
    @pl.when(pl.program_id(0) == 0)
    def _():
        tok_t[...] = tok_ref[...].T
        rem_t[...] = rem_ref[...].T

    wq_ref[...] = dot(tok_t[...], dq_ref[...]).astype(BF16)
    wk_ref[...] = (dot(tok_t[...], dko_ref[...]) + dot(rem_t[...], dkr_ref[...])).astype(BF16)
    wv_ref[...] = (dot(tok_t[...], dvo_ref[...]) + dot(rem_t[...], dvr_ref[...])).astype(BF16)
    bq_ref[...] = column_sum(dq_ref[...].astype(F32))
    bv_ref[...] = column_sum(dvo_ref[...].astype(F32)) + column_sum(dvr_ref[...].astype(F32))


def weights_back(tok, rem, dq, dko, dvo, dkr, dvr):
    rows, features = tok.shape
    others = rem.shape[0]
    wide = math.gcd(features, 256)
    own_spec = pl.BlockSpec((rows, wide), lambda j: (0, j))
    rem_spec = pl.BlockSpec((others, wide), lambda j: (0, j))
    bias_spec = pl.BlockSpec((1, wide), lambda j: (0, j))
    return pl.pallas_call(
        weights_back_kernel,
        grid=(features // wide,),
        in_specs=[
            whole_spec(tok.shape),
            whole_spec(rem.shape),
            own_spec,
            own_spec,
            own_spec,
            rem_spec,
            rem_spec,
        ],
        out_specs=[pl.BlockSpec((features, wide), lambda j: (0, j))] * 3 + [bias_spec] * 2,
        out_shape=[jax.ShapeDtypeStruct((features, features), BF16)] * 3
        + [jax.ShapeDtypeStruct((1, features), F32)] * 2,
        scratch_shapes=[
            pltpu.VMEM((features, rows), BF16),
            pltpu.VMEM((features, others), BF16),
        ],
        compiler_params=params(60),
        cost_estimate=cost(
            2 * features * features * (3 * rows + 2 * others),
            2 * (4 * tok.size + 3 * rem.size + 3 * features * features),
        ),
        name="weights_back",
    )(tok, rem, dq, dko, dvo, dkr, dvr)


def halve(value, axis, bit):
    size = lax.axis_size(axis)
    mine = (lax.axis_index(axis) >> bit) & 1
    pairs = value.reshape((value.shape[0] // 2, 2) + value.shape[1:])
    keep = lax.dynamic_index_in_dim(pairs, mine, 1, keepdims=False)
    send = lax.dynamic_index_in_dim(pairs, 1 - mine, 1, keepdims=False)
    came = lax.ppermute(send, axis, [(i, i ^ (1 << bit)) for i in range(size)])
    return keep.astype(F32) + came.astype(F32)


def scatter_sum(value, low=True):
    dp, blk = lax.axis_size("dp"), lax.axis_size("blk")
    if dp & (dp - 1) or blk & (blk - 1):
        return lax.psum_scatter(
            value.astype(F32), ("dp", "blk"), scatter_dimension=0, tiled=True
        )
    kept = value.dtype
    each = value.shape[0] // (dp * blk)
    value = value.reshape((dp, blk * each) + value.shape[1:])
    for bit in range(dp.bit_length() - 1):
        value = halve(value, "dp", bit).astype(kept)
    value = value.reshape((blk, each) + value.shape[2:])
    for bit in range(blk.bit_length() - 1):
        value = halve(value, "blk", bit)
        value = value if (2 << bit) == blk else value.astype(kept)
    return value.reshape(value.shape[1:]).astype(F32)


class Unit:
    def __init__(self, parts, rows, columns, halves, outs):
        self.parts, self.rows, self.columns = parts, rows, columns
        self.halves, self.outs = halves, outs
        self.first = 1 if parts else 0
        self.half = rows // (2 * halves)
        self.last_type = BF16 if (rows // 2) % 16 == 0 else F32


def timetable(units, bits, seqs, groups, slot_us, token_us):
    free, pending, table = {}, [], []
    slots = seqs * groups * 2

    def launch(key, now):
        kind, which, step = key
        if kind == "tokens":
            link, us = "blk", token_us
        elif kind == "vectors":
            link, us = None, 1.0
        else:
            us = units[which].rows * units[which].columns * 2e-5
            us *= 1 << max(bits - 1 - step, 0)
            us *= {0: 0.4, bits - 1: 3.0}.get(step, 1.2)
            link = {0: "core", bits - 1: "far", bits: "blk"}.get(step, "near")
        start = max(now, free.get(link, 0.0))
        if link:
            free[link] = start + us
        if kind != "tokens":
            pending.append((start + us + 2.5, key))

    for u, unit in enumerate(units):
        if unit.parts:
            launch(("unit", u, 1), 3.0)
    first_group = sum(1 for unit in units if unit.parts)
    now = 0.0
    while len(table) < slots or pending:
        slot = len(table)
        if slot < slots:
            now = (slot + 1) * slot_us
            part, major, minor = slot // (seqs * groups), slot // groups % seqs, slot % groups
            if part == 0 and minor == groups - 1:
                launch(("tokens", major, 0), now)
            major, minor = divmod(slot - seqs * groups, seqs)
            if part == 1 and minor == seqs - 1:
                launch(("unit", first_group + major, 0), now)
            if slot == slots - 1:
                launch(("vectors", 0, 0), now)
            due = sorted(p for p in pending if p[0] <= now)
        else:
            due = [min(pending)]
            now = max(now + 0.3, due[0][0])
        table.append([key for _, key in due])
        for found in due:
            pending.remove(found)
            kind, which, step = found[1]
            if step < bits:
                launch((kind, which, step + 1), now)
    tail = [key for keys in table[slots:] for key in keys]
    return table[:slots], tail + [("tokens", s, 0) for s in range(seqs)]


def order_of(step, seqs, groups):
    part = step // (seqs * groups)
    left = step - part * (seqs * groups)
    s = left // groups * (1 - part) + left % seqs * part
    h = left % groups * (1 - part) + left // seqs * part
    return part, s, h


def back_kernel(units, bits, groups, table, tail, n_out, *refs):
    (q_ref, qm_ref, g_ref, lse_ref, k_ref, km_ref, v_ref,
     tok_ref, rem_ref, wq_ref, wk_ref, wv_ref, vg_ref, vu_ref) = refs[:14]
    sources, refs = refs[14:17], list(refs[17:])
    tokens_any, rem_in, *outs = refs[:n_out]
    refs = refs[n_out:]
    kept = [refs.pop(0) for _ in units]
    landed = [
        [refs.pop(0) if k >= unit.first else None for k in range(bits)] for unit in units
    ]
    wide = [refs.pop(0) for _ in units]
    parting = [refs.pop(0) for _ in units]
    last = [refs.pop(0) for _ in units]
    (weight_sum, group_src, total_s, turned, dq_part, dq_s, dk_s, dv_s,
     rem_out, vec, vec_in, bias_sum, send_sem, recv_sem, local_sem, out_sem) = refs
    step = pl.program_id(0)
    steps = pl.num_programs(0)
    seqs = rem_out.shape[0]
    part, s, h = order_of(step, seqs, groups)
    features = tok_ref.shape[2]
    me, side = lax.axis_index("dp"), lax.axis_index("blk")
    core = me % 2

    def swapped(k):
        return {1: 2, 2: 1}.get(k, k) if bits > 2 else k

    def pick(values, k):
        return values[k] + (values[swapped(k)] - values[k]) * core

    bit_own = [(me // (1 << bit)) % 2 for bit in range(bits)]
    across = [me + (1 << bit) * (1 - 2 * bit_own[bit]) for bit in range(bits)]
    own = [pick(bit_own, k) for k in range(bits)]
    partner = [{"dp": pick(across, k)} for k in range(bits)] + [{"blk": 1 - side}]
    first_group = sum(1 for unit in units if unit.parts)
    lead = (slice(None),) * (bits - 1)

    def natural(digits):
        by_step = [None] + list(digits[::-1])
        return tuple(
            by_step[bit] if swapped(bit) == bit else pick(by_step, bit) for bit in range(bits - 1, 0, -1)
        )

    def digits_of(n, count):
        return [(n // (1 << (count - 1 - i))) % 2 for i in range(count)]

    sems = {}
    for u, unit in enumerate(units):
        for k in range(unit.first, bits + 1):
            sems["unit", u, k, 0] = len(sems)
    for k in range(bits + 1):
        sems["vectors", 0, k, 0] = len(sems)
    for k in range(seqs):
        sems["tokens", k, 0, 0] = len(sems)

    def remote(source, target, device, key):
        return pltpu.make_async_remote_copy(
            src_ref=source,
            dst_ref=target,
            send_sem=send_sem.at[sems[key]],
            recv_sem=recv_sem.at[sems[key]],
            device_id=device,
            device_id_type=pl.DeviceIdType.MESH,
        )

    near_sems = {}
    for u, unit in enumerate(units):
        for p in range(len(unit.parts or ())):
            for n in range(1 << min(bits - 1, 2)):
                near_sems[u, p, n] = len(near_sems)

    def spot(k, value):
        return tuple(
            own[at] if at < k else value if at == k else slice(None) for at in range(bits - 1, 0, -1)
        )

    def copies(kind, which, k):
        if kind == "tokens":
            return [remote(rem_out.at[which], rem_in.at[which], partner[bits], (kind, which, 0, 0))]
        if kind == "vectors":
            return [remote(vec.at[k], vec_in.at[k], partner[k], (kind, 0, k, 0))]
        u, unit = which, units[which]
        if k == bits:
            return [remote(parting[u], last[u], partner[bits], (kind, u, k, 0))]
        if k:
            source = kept[u].at[spot(k, 1 - own[k])]
            return [remote(source, landed[u][k], partner[k], (kind, u, k, 0))]
        source = group_src.at[(u - first_group,) + lead + (1 - core,)]
        return [remote(source, landed[u][0], partner[0], (kind, u, 0, 0))]

    def near_copies(u):
        found, row = [], 0
        for p, (source, first, rows) in enumerate(units[u].parts):
            for n in range(1 << min(bits - 1, 2)):
                digits = digits_of(n, min(bits - 1, 2))
                digits = [slice(None)] * (bits - 1 - len(digits)) + digits
                found.append(
                    pltpu.make_async_copy(
                        sources[source].at[natural(digits) + (pl.ds(first, rows),)],
                        kept[u].at[tuple(digits) + (pl.ds(row, rows),)],
                        local_sem.at[near_sems[u, p, n]],
                    )
                )
            row += rows
        return found

    def launch(*key):
        for copy in copies(*key):
            copy.start()

    def halves_of(u, which):
        unit = units[u]
        return [
            wide[u][pl.ds(pl.multiple_of(i * 2 * unit.half + which * unit.half, 8), unit.half)]
            for i in range(unit.halves)
        ]

    def receive(kind, which, k):
        for copy in copies(kind, which, k):
            copy.wait_recv()
        if kind == "tokens":
            return
        if kind == "vectors":
            vec[k + 1] = vec[k] + vec_in[k]
            if k < bits:
                launch(kind, 0, k + 1)
            return
        u, unit = which, units[which]
        if k == bits:
            for i, (mine, (out, rows, columns)) in enumerate(zip(halves_of(u, side), unit.outs)):
                came = last[u][...].astype(F32)[i * unit.half : (i + 1) * unit.half]
                outs[out][rows, columns] = mine + came
            return
        place = spot(k, own[k]) if k else lead
        open_at = [i for i, at in enumerate(place) if isinstance(at, slice)]

        def add(n, carry):
            at, where = list(place), digits_of(n, len(open_at))
            for i, digit in zip(open_at, where):
                at[i] = digit
            at = tuple(at)
            if k:
                mine, came = kept[u][at], landed[u][k][tuple(where)]
            else:
                mine = group_src[(u - first_group,) + natural(at) + (core,)]
                came = landed[u][0][natural(at)]
            total = mine.astype(F32) + came.astype(F32)
            if k == bits - 1:
                wide[u][...] = total
            else:
                kept[u][at] = total.astype(BF16)
            return carry

        if open_at:
            lax.fori_loop(0, 1 << len(open_at), add, 0)
        else:
            add(0, 0)
        if k == bits - 1:
            pieces = halves_of(u, 1 - side)
            pieces = pieces[0] if len(pieces) == 1 else jnp.concatenate(pieces, axis=0)
            parting[u][...] = pieces.astype(unit.last_type)
        launch(kind, u, k + 1)

    @pl.when(step == 0)
    def _():
        barrier = pltpu.get_barrier_semaphore()
        for other in partner:
            pl.semaphore_signal(barrier, inc=1, device_id=other, device_id_type=pl.DeviceIdType.MESH)
        pl.semaphore_wait(barrier, bits + 1)
        for u, unit in enumerate(units):
            if unit.parts:
                for copy in near_copies(u):
                    copy.start()
        for u, unit in enumerate(units):
            if unit.parts:
                for copy in near_copies(u):
                    copy.wait()
                launch("unit", u, 1)
        weight_sum[...] = jnp.zeros_like(weight_sum)
        bias_sum[...] = jnp.zeros_like(bias_sum)

    @pl.when((part == 0) & (h == 0))
    def _():
        turned[0] = rem_ref[0].T
        total_s[...] = jnp.zeros_like(total_s)

    @pl.when((part == 1) & (h == 0))
    def _():
        turned[s] = tok_ref[0].T

    width = q_ref.shape[2]
    columns = pl.ds(pl.multiple_of(h * width, width), width)

    found = attend_back_part(
        q_ref[0], qm_ref[0], g_ref[0], lse_ref.at[0], k_ref[0, 0], km_ref[0, 0], v_ref[0, 0],
        dk_s.at[s, :, columns], dv_s.at[s, :, columns],
    )
    dk, dv = dk_s[s, :, columns], dv_s[s, :, columns]
    x_t = turned[s * part]
    weight_sum[h, 1] += dot(x_t, dk)
    weight_sum[h, 2] += dot(x_t, dv)
    bias_sum[h, 1:2] += column_sum(dv.astype(F32))

    @pl.when(part == 0)
    def _():
        total_s[...] += dot(dk, wk_ref[:, columns], NT) + dot(dv, wv_ref[:, columns], NT)
        for pair, value in enumerate(found):
            dq_part[s, h, pair] = value.astype(dq_part.dtype)

    @pl.when(part == 1)
    def _():
        queries = []
        for pair, value in enumerate(found):
            value = (value + dq_part[s, h, pair].astype(F32)) * SCALE
            queries.append(value.T.astype(BF16))
        dq = jnp.concatenate(queries, axis=1)
        dq_s[s, :, columns] = dq
        weight_sum[h, 0] += dot(x_t, dq)
        bias_sum[h, 0:1] += column_sum(dq.astype(F32))

    for at in range(seqs):

        @pl.when(step == (at + 1) * groups - 1)
        def _(at=at):
            rem_out[at] = total_s[...].astype(BF16)
            launch("tokens", at, 0)

    for at in range(groups):

        @pl.when(step == steps - (groups - 1 - at) * seqs - 1)
        def _(at=at):
            rows = features // (1 << bits)
            for i in range(3):
                piece = weight_sum[at, i].astype(BF16)
                piece = piece.reshape((2,) * bits + (rows, piece.shape[1]))
                group_src[(at,) + (slice(None),) * bits + (slice(i * rows, (i + 1) * rows),)] = piece
            launch("unit", first_group + at, 0)

    @pl.when(step == steps - 1)
    def _():
        vec[0] = jnp.zeros_like(vec[0])
        vec[0, 0:6] = vg_ref[0:6]
        for at in range(groups):
            vec[0, 6:8, at * width : (at + 1) * width] = bias_sum[at, 0:2]
        blocks = vu_ref.shape[1] // features
        for at in range(blocks):
            vec[0, 8 + at : 9 + at] = vu_ref[:, at * features : (at + 1) * features]
        launch("vectors", 0, 0)

    for at, keys in enumerate(table):
        if keys:

            @pl.when(step == at)
            def _(keys=keys):
                for key in keys:
                    receive(*key)

    @pl.when(step == steps - 1)
    def _():
        def own_out(at):
            return pltpu.make_async_copy(dq_s.at[at], tokens_any.at[at], out_sem.at[at])

        left = list(tail)
        for at in range(seqs):
            total = dot(dq_s[at], wq_ref[...], NT)
            total += dot(dk_s[at], wk_ref[...], NT) + dot(dv_s[at], wv_ref[...], NT)
            dq_s[at] = total.astype(BF16)
            own_out(at).start()
            for _ in range(3):
                if left:
                    receive(*left.pop(0))
        for key in left:
            receive(*key)
        for at in range(seqs):
            own_out(at).wait()
        shards = (1 << bits) * 2
        place = me * 2 + side
        share = features // shards
        rows = pltpu.roll(vec[bits + 1, 0:8], (shards - place) * share % features, 1)
        outs[-1][0:8] = rows[:, :PAIR]
        share = vu_ref.shape[1] // shards
        each = features // share
        row = vec[bits + 1, pl.ds(8 + place // each, 1)]
        rows = pltpu.roll(jnp.broadcast_to(row, (8, features)), (each - place % each) * share % features, 1)
        outs[-1][8:16] = rows[:, :PAIR]
        for u, unit in enumerate(units):
            for k in range(unit.first, bits + 1):
                for copy in copies("unit", u, k):
                    copy.wait_send()
        for k in range(bits + 1):
            copies("vectors", 0, k)[0].wait_send()
        for k in range(seqs):
            copies("tokens", k, 0)[0].wait_send()


def back_and_sum(q, qm, g, lse, k, km, v, tokens, rem_tokens, weights, dwd, dwu, dwo, vg, vu):
    bits = lax.axis_size("dp").bit_length() - 1
    seqs, length, features = q.shape
    width = math.gcd(features, 2 * PAIR)
    groups, pairs = features // width, width // PAIR
    low, deep, blocks = dwo.shape[1], dwd.shape[1], dwu.shape[1]
    lead = (2,) * bits
    sources = [x.reshape(lead[1:] + (-1, features)) for x in (dwd, dwu, dwo)]
    every = slice(None)
    units = []
    quarter = deep // 4
    for i in range(2):
        at = slice(i * quarter, (i + 1) * quarter)
        parts = [(0, i * quarter, quarter), (0, (2 + i) * quarter, quarter)]
        units.append(Unit(parts, 2 * quarter, features, 1, [(0, at, every)]))
    for i in range(2):
        found = range(i * blocks // 2, (i + 1) * blocks // 2)
        units.append(
            Unit(
                [(1, found[0] * low, len(found) * low)],
                len(found) * low,
                features,
                len(found),
                [(1, every, slice(b * features, (b + 1) * features)) for b in found],
            )
        )
    units.append(Unit([(2, 0, low)], low, features, 1, [(2, every, every)]))
    for h in range(groups):
        columns = slice(h * width, (h + 1) * width)
        units.append(Unit(None, 3 * low, width, 3, [(3 + i, every, columns) for i in range(3)]))
    table, tail = timetable(units, bits, seqs, groups, 4.2, length * features * 4e-5)

    half = low // 2
    out_shape = [
        jax.ShapeDtypeStruct(q.shape, BF16),
        jax.ShapeDtypeStruct(q.shape, BF16),
        jax.ShapeDtypeStruct((deep // 2, features), F32),
        jax.ShapeDtypeStruct((half, blocks * features), F32),
        *(jax.ShapeDtypeStruct((half, features), F32) for _ in range(4)),
        jax.ShapeDtypeStruct((16, PAIR), F32),
    ]
    tops = lead[1:]
    scratch = [pltpu.VMEM(tops + (u.rows, u.columns), BF16) for u in units]
    for u in units:
        scratch += [pltpu.VMEM(tops[k:] + (u.rows, u.columns), BF16) for k in range(u.first, bits)]
    scratch += [pltpu.VMEM((u.rows, u.columns), F32) for u in units]
    scratch += [pltpu.VMEM((u.rows // 2, u.columns), u.last_type) for u in units] * 2
    count = len(units) * (bits + 1) + bits + 1 + seqs
    near = sum(len(u.parts) << min(bits - 1, 2) for u in units if u.parts)
    scratch += [
        pltpu.VMEM((groups, 3, features, width), F32),
        pltpu.VMEM((groups,) + lead + (3 * low, width), BF16),
        pltpu.VMEM((length, features), F32),
        pltpu.VMEM((seqs, features, length), BF16),
        pltpu.VMEM((seqs, groups, pairs, PAIR, length), F32),
        *(pltpu.VMEM((seqs, length, features), BF16) for _ in range(4)),
        pltpu.VMEM((bits + 2, 16, features), F32),
        pltpu.VMEM((bits + 1, 16, features), F32),
        pltpu.VMEM((groups, 8, width), F32),
        pltpu.SemaphoreType.DMA((count,)),
        pltpu.SemaphoreType.DMA((count,)),
        pltpu.SemaphoreType.DMA((near,)),
        pltpu.SemaphoreType.DMA((seqs,)),
    ]

    def at_step(shape, index):
        return pl.BlockSpec(shape, lambda i: index(*order_of(i, seqs, groups)))

    heads_at = at_step((1, length, width), lambda p, s, h: (s, 0, h))
    keys_at = at_step((1, 1, length, width), lambda p, s, h: (1 - p, s, 0, h))

    def rows_at(which):
        last = seqs - 1
        return pl.BlockSpec(
            (1, length, features),
            lambda i: (jnp.clip(i // groups if which == 0 else i - seqs * groups, 0, last), 0, 0),
            pipeline_mode=pl.Buffered(1),
        )

    def fixed(shape):
        return pl.BlockSpec(shape, lambda i: (0,) * len(shape), pipeline_mode=pl.Buffered(1))

    return pl.pallas_call(
        functools.partial(back_kernel, units, bits, groups, table, tail, len(out_shape)),
        grid=(2 * seqs * groups,),
        in_specs=[
            heads_at,
            at_step((1, length, PAIR), lambda p, s, h: (s, 0, 0)),
            heads_at,
            at_step((1, pairs, 8, length), lambda p, s, h: (s, h, 0, 0)),
            keys_at,
            at_step((1, 1, length, PAIR), lambda p, s, h: (1 - p, s, 0, 0)),
            keys_at,
            rows_at(1),
            rows_at(0),
        ]
        + [whole_spec(w.shape) for w in weights + (vg, vu)]
        + [pl.BlockSpec(memory_space=pl.ANY)] * 3,
        out_specs=[pl.BlockSpec(memory_space=pl.ANY)] * 2
        + [fixed(s.shape) for s in out_shape[2:]],
        out_shape=out_shape,
        scratch_shapes=scratch,
        compiler_params=pltpu.CompilerParams(
            collective_id=1, has_side_effects=True, vmem_limit_bytes=63 * MIB
        ),
        cost_estimate=cost(80 * q.size * length, 2 * q.size * 14, 2 * q.size * length // HEAD),
        name="back_and_sum",
    )(q, qm, g, lse, k, km, v, tokens, rem_tokens, *weights, vg, vu, *sources)


def finish_kernel(residual_ref, own_ref, rem_ref, *refs):
    ins, outs = refs[:7], refs[7:]
    total = residual_ref[...].astype(F32) + own_ref[...].astype(F32) + rem_ref[...].astype(F32)
    outs[0][...] = total.astype(BF16)

    @pl.when(pl.program_id(0) == 0)
    def _():
        for source, target in zip(ins[:6], outs[1:7]):
            target[...] = source[...]
        for i, target in enumerate(outs[7:]):
            target[...] = ins[6][i, : target.shape[0]]


def finish(residual, own, rem, matrices, vectors, shares):
    seqs, length, features = own.shape
    row_spec = pl.BlockSpec((1, length, features), lambda s: (s, 0, 0))

    def fixed(shape):
        return pl.BlockSpec(shape, lambda s: (0,) * len(shape))

    shapes = [m.shape for m in matrices] + [(n,) for n in shares]
    return pl.pallas_call(
        finish_kernel,
        grid=(seqs,),
        in_specs=[row_spec] * 3 + [fixed(m.shape) for m in matrices] + [fixed(vectors.shape)],
        out_specs=[row_spec] + [fixed(s) for s in shapes],
        out_shape=[jax.ShapeDtypeStruct(own.shape, BF16)] + [jax.ShapeDtypeStruct(s, F32) for s in shapes],
        compiler_params=params(60),
        cost_estimate=cost(2 * own.size, 8 * own.size),
        name="finish",
    )(residual, own, rem, *matrices, vectors)


def back_plainly(q, qm, o, g, lse, own, rem, bg, tokens, rem_tokens, weights, dwd, dwu, dwo, vg, vu):
    seqs, length, features = q.shape
    dp, blk = lax.axis_size("dp"), lax.axis_size("blk")
    dq, dko, dvo, dkr, dvr = attend_back(q, qm, o, g, lse, own, rem)
    rem_gradient = tokens_back(rem_back_kernel, (dkr, dvr), weights[1:])
    came = [
        lax.ppermute(part, "blk", [((i + r) % blk, i) for i in range(blk)])
        for r, part in enumerate(jnp.split(rem_gradient, blk - 1, axis=1), 1)
    ]
    flat = [v.reshape(-1, features) for v in (tokens, rem_tokens, dq, dko, dvo, dkr, dvr)]
    dwq, dwk, dwv, dbq, dbv = weights_back(*flat)
    total = tokens_back(own_back_kernel, (bg, dq, dko, dvo), weights).astype(F32)
    for part in came:
        total += part.astype(F32)
    dwu = jnp.moveaxis(dwu[0], 0, 1).reshape(features, -1)
    summed = [scatter_sum(w) for w in (dwd, dwu, dwo, dwq, dwk, dwv)]
    rows = [vg[i] for i in range(6)] + [dbq, dbv, vu]
    rows = [scatter_sum(v.reshape(dp * blk, -1)) for v in rows]
    return [total.astype(BF16)] + summed + [[v[0] for v in rows]]


def body(
    tokens,
    query_weight,
    query_bias,
    key_weight,
    value_weight,
    value_bias,
    out_weight,
    out_bias,
    gain_one,
    shift_one,
    up_weight,
    up_bias,
    down_weight,
    down_bias,
    gain_two,
    shift_two,
    group_ids,
    valid_mask,
    cotangent,
):
    seqs, length, features = tokens.shape
    rows = seqs * length
    blk = lax.axis_size("blk")

    def from_others(value):
        found = [
            lax.ppermute(value, "blk", [(i, (i + r) % blk) for i in range(blk)])
            for r in range(1, blk)
        ]
        return found[0] if len(found) == 1 else jnp.concatenate(found, axis=1)

    codes = jnp.where(valid_mask == 1, group_ids, -1)
    dp = lax.axis_size("dp")
    by_kernel = blk == 2 and dp & (dp - 1) == 0 and dp > 1 and (features // dp) % 16 == 0
    projections = (query_weight, key_weight, value_weight)
    vectors = (
        query_bias,
        value_bias,
        out_bias,
        gain_one,
        shift_one,
        down_bias,
        gain_two,
        shift_two,
    )

    if by_kernel:
        (block_out, branch_gradient, attended_gradient, attended, lse, query_mask, key_masks,
         first_t, feed_t, vector_gradients, up_bias_gradient, queries, keys, values,
         rem_tokens, active, inner_gradient) = front(
            tokens,
            group_ids,
            valid_mask,
            cotangent,
            vectors,
            up_bias,
            projections + (out_weight, up_weight, down_weight),
        )
        dwu, dwd, dwo = feed_weights(
            first_t,
            inner_gradient.reshape(rows, -1),
            feed_t,
            active.reshape(rows, -1),
            attended.reshape(rows, features),
            branch_gradient.reshape(rows, features),
        )
        own_gradient, rem_gradient, *matrices, vectors = back_and_sum(
            queries,
            query_mask,
            attended_gradient,
            lse,
            keys,
            key_masks,
            values,
            tokens,
            rem_tokens,
            projections,
            dwd,
            dwu,
            dwo,
            vector_gradients,
            up_bias_gradient,
        )
        shares = [features // (dp * blk)] * 8 + [up_bias.size // (dp * blk)]
        found = finish(branch_gradient, own_gradient, rem_gradient, matrices, vectors, shares)
        tokens_gradient, dwd, dwu, dwo, dwq, dwk, dwv, *rows_left = found
    else:
        rem_tokens = from_others(tokens)
        rem_codes = from_others(codes.astype(BF16)).astype(jnp.int32)
        slot = jnp.arange(PAIR, dtype=jnp.int32) % HEAD

        def key_mask(code):
            return jnp.where(code[:, :, None] == slot, 0.0, MASKED).astype(BF16)

        query_mask = (group_ids[:, :, None] == slot).astype(BF16)
        vectors = jnp.stack(vectors).astype(F32)
        queries, own_keys, own_values = project(tokens, vectors, projections)
        rem_keys, rem_values = project(rem_tokens, vectors, projections[1:])
        own = (own_keys, key_mask(codes), own_values)
        rem = (rem_keys, key_mask(rem_codes), rem_values)
        attended, lse = attend(queries, query_mask, own, rem)
        (block_out, branch_gradient, attended_gradient, vector_gradients, up_bias_gradient,
         dwu, dwd, dwo) = feed_both_ways(
            tokens.reshape(rows, features),
            attended.reshape(rows, features),
            cotangent.reshape(rows, features),
            vectors[2:],
            up_bias.astype(F32)[None],
            out_weight,
            up_weight,
            down_weight,
            1,
        )
        tokens_gradient, dwd, dwu, dwo, dwq, dwk, dwv, rows_left = back_plainly(
            queries,
            query_mask,
            attended,
            attended_gradient.reshape(tokens.shape),
            lse,
            own,
            rem,
            branch_gradient.reshape(tokens.shape),
            tokens,
            rem_tokens,
            projections,
            dwd,
            dwu,
            dwo,
            vector_gradients,
            up_bias_gradient,
        )
    dbo, dg1, ds1, dbd, dg2, ds2, dbq, dbv, dbu = rows_left
    return (
        block_out.reshape(tokens.shape),
        tokens_gradient,
        dwq,
        dbq,
        dwk,
        dwv,
        dbv,
        dwo,
        dbo,
        dg1,
        ds1,
        dwu,
        dbu,
        dwd,
        dbd,
        dg2,
        ds2,
    )


def solution(mesh):
    rows, shared, pair = P("dp", "blk", None), P(), P("dp", "blk")
    matrix, vector = P(("dp", "blk"), None), P(("dp", "blk"))
    return jax.shard_map(
        body,
        mesh=mesh,
        in_specs=(rows,) + (shared,) * 15 + (pair, pair, rows),
        out_specs=(
            rows,
            rows,
            matrix,
            vector,
            matrix,
            matrix,
            vector,
            matrix,
            vector,
            vector,
            vector,
            matrix,
            vector,
            matrix,
            vector,
            vector,
            vector,
        ),
        check_vma=False,
    )
```

```python
import functools
import math

import jax
import jax.numpy as jnp
from jax import lax
from jax.experimental import pallas as pl
from jax.experimental.pallas import tpu as pltpu
from jax.sharding import PartitionSpec as P

HEAD = 64
PAIR = 2 * HEAD
EPSILON = 1e-12
MASKED = -1e30
FLOOR = -3e38
SCALE = HEAD**-0.5
EXPO = SCALE * math.log2(math.e)
NN = (((1,), (0,)), ((), ()))
NT = (((1,), (1,)), ((), ()))
F32 = jnp.float32
BF16 = jnp.bfloat16
MIB = 1 << 20
FEED_ROWS = 256


def dot(left, right, dims=NN):
    return lax.dot_general(left, right, dims, preferred_element_type=F32)


def whole_spec(shape):
    return pl.BlockSpec(shape, lambda *_: (0,) * len(shape), pipeline_mode=pl.Buffered(1))


def params(limit):
    return pltpu.CompilerParams(vmem_limit_bytes=limit * MIB)


def cost(flops, touched, exps=0):
    return pl.CostEstimate(flops=int(flops), bytes_accessed=int(touched), transcendentals=int(exps))


def project_kernel(has_query, *refs):
    if has_query:
        x_ref, bias_ref, wq_ref, wk_ref, wv_ref, q_ref, k_ref, v_ref = refs
    else:
        x_ref, bias_ref, wk_ref, wv_ref, k_ref, v_ref = refs
    x = x_ref[0]
    if has_query:
        q_ref[0] = ((dot(x, wq_ref[...]) + bias_ref[0:1]) * EXPO).astype(BF16)
    k_ref[0] = dot(x, wk_ref[...]).astype(BF16)
    v_ref[0] = (dot(x, wv_ref[...]) + bias_ref[1:2]).astype(BF16)


def project(x, bias, weights):
    seqs, length, features = x.shape
    tile = math.gcd(length, 512)
    grid = (seqs, length // tile)
    row_spec = pl.BlockSpec((1, tile, features), lambda s, i: (s, i, 0))
    return pl.pallas_call(
        functools.partial(project_kernel, len(weights) == 3),
        grid=grid,
        in_specs=[row_spec, whole_spec(bias.shape)] + [whole_spec(w.shape) for w in weights],
        out_specs=[row_spec] * len(weights),
        out_shape=[jax.ShapeDtypeStruct(x.shape, BF16)] * len(weights),
        compiler_params=params(60),
        cost_estimate=cost(
            2 * x.size * features * len(weights), 2 * x.size * (1 + len(weights))
        ),
        name="project",
    )(x, bias, *weights)


def low_lanes():
    return lax.broadcasted_iota(jnp.int32, (1, PAIR), 1) < HEAD


def attend_group(q, qm, sources, o_ref, lse_ref):
    length = q.shape[0]
    tile = math.gcd(length, 512)
    low = low_lanes()
    one = jnp.ones((1, PAIR), BF16)
    todo = [
        (pair, row, head)
        for pair in range(q.shape[1] // PAIR)
        for row in range(0, length, tile)
        for head in range(2)
    ]

    def lanes_of(pair):
        return slice(pair * PAIR, (pair + 1) * PAIR)

    def mine_of(head):
        return ~low if head else low

    def scores_of(pair, row, head):
        mine, lanes = mine_of(head), lanes_of(pair)
        q_side = jnp.where(mine, q[row : row + tile, lanes], qm[row : row + tile])
        return [dot(q_side, jnp.where(mine, k[:, lanes], km), NT) for k, km, _ in sources]

    ahead = scores_of(*todo[0])
    for i, (pair, row, head) in enumerate(todo):
        scores = ahead
        if i + 1 < len(todo):
            ahead = scores_of(*todo[i + 1])
        top = functools.reduce(
            jnp.maximum, [jnp.max(part, axis=-1, keepdims=True) for part in scores]
        )
        weights = [jnp.exp2(part - top).astype(BF16) for part in scores]
        total = sum(
            dot(w, jnp.where(mine_of(head), v[:, lanes_of(pair)], one))
            for w, (_, _, v) in zip(weights, sources)
        )
        if head == 0:
            earlier, earlier_top = total, top
            continue
        totals = pltpu.roll(jnp.where(low, total, earlier), HEAD, 1)
        rows = slice(row, row + tile)
        o_ref[rows, lanes_of(pair)] = (jnp.where(low, earlier, total) / totals).astype(BF16)
        lse = (jnp.where(low, earlier_top, top) + jnp.log2(totals)).T
        lse_ref[pair, 0:1, rows] = lse[0:1]
        lse_ref[pair, 1:2, rows] = lse[HEAD : HEAD + 1]


def attend_kernel(q_ref, qm_ref, ko_ref, kmo_ref, vo_ref, kr_ref, kmr_ref, vr_ref, o_ref, lse_ref):
    sources = [(ko_ref[0], kmo_ref[0], vo_ref[0]), (kr_ref[0], kmr_ref[0], vr_ref[0])]
    attend_group(q_ref[0], qm_ref[0], sources, o_ref.at[0], lse_ref.at[0])


def pair_spec(length, lanes):
    return pl.BlockSpec((1, length, lanes), lambda s, h: (s, 0, h))


def mask_spec(length):
    return pl.BlockSpec((1, length, PAIR), lambda s, h: (s, 0, 0))


def lse_spec(length, lanes):
    return pl.BlockSpec((1, lanes // PAIR, 8, length), lambda s, h: (s, h, 0, 0))


def attend(q, qm, own, rem):
    seqs, length, features = q.shape
    lanes = math.gcd(features, 2 * PAIR)
    other = rem[0].shape[1]
    own_spec, rem_spec = pair_spec(length, lanes), pair_spec(other, lanes)
    return pl.pallas_call(
        attend_kernel,
        grid=(seqs, features // lanes),
        in_specs=[own_spec, mask_spec(length)]
        + [own_spec, mask_spec(length), own_spec]
        + [rem_spec, mask_spec(other), rem_spec],
        out_specs=[own_spec, lse_spec(length, lanes)],
        out_shape=[
            jax.ShapeDtypeStruct(q.shape, BF16),
            jax.ShapeDtypeStruct((seqs, features // PAIR, 8, length), F32),
        ],
        compiler_params=params(60),
        cost_estimate=cost(
            16 * q.size * (length + other), 2 * q.size * 6, q.size * (length + other) // HEAD
        ),
        name="attend",
    )(q, qm, *own, *rem)


def attend_back_part(q, qm, g, lse_ref, k, km, v, dk_ref, dv_ref):
    low = low_lanes()
    none = jnp.zeros((1, PAIR), BF16)
    pairs = q.shape[1] // PAIR
    todo = [(pair, head) for pair in range(pairs) for head in range(2)]

    def lanes_of(pair):
        return slice(pair * PAIR, (pair + 1) * PAIR)

    def mine_of(head):
        return ~low if head else low

    def products(pair, head):
        mine, lanes = mine_of(head), lanes_of(pair)
        return (
            dot(jnp.where(mine, k[:, lanes], km), jnp.where(mine, q[:, lanes], qm), NT),
            dot(jnp.where(mine, v[:, lanes], none), g[:, lanes], NT),
        )

    found = []
    ahead = products(*todo[0])
    for i, (pair, head) in enumerate(todo):
        scores, grads = ahead
        if i + 1 < len(todo):
            ahead = products(*todo[i + 1])
        lanes, mine = lanes_of(pair), mine_of(head)
        if head == 0:
            k_t = k[:, lanes].T
            dk = dv = 0.0
            dq = []
        probs = jnp.exp2(scores - lse_ref[pair, head : head + 1, :])
        grads = (probs * (grads - lse_ref[pair, 2 + head : 3 + head, :])).astype(BF16)
        dv += dot(probs.astype(BF16), jnp.where(mine, g[:, lanes], none))
        dk += dot(grads, jnp.where(mine, q[:, lanes], none))
        dq.append(dot(k_t[head * HEAD : (head + 1) * HEAD], grads))
        if head == 1:
            dk_ref[:, lanes] = (dk * (SCALE / EXPO)).astype(BF16)
            dv_ref[:, lanes] = dv.astype(BF16)
            found.append(jnp.concatenate(dq, axis=0))
    return found


def attend_back_kernel(q_ref, qm_ref, g_ref, lse_ref, ko_ref, kmo_ref, vo_ref, kr_ref, kmr_ref,
                       vr_ref, dq_ref, dko_ref, dvo_ref, dkr_ref, dvr_ref):
    parts = ((ko_ref, kmo_ref, vo_ref, dko_ref, dvo_ref), (kr_ref, kmr_ref, vr_ref, dkr_ref, dvr_ref))
    found = [
        attend_back_part(
            q_ref[0], qm_ref[0], g_ref[0], lse_ref.at[0], k[0], km[0], v[0], dk.at[0], dv.at[0]
        )
        for k, km, v, dk, dv in parts
    ]
    for pair, both in enumerate(zip(*found)):
        dq_ref[0, :, pair * PAIR : (pair + 1) * PAIR] = (sum(both) * SCALE).T.astype(BF16)


def attend_back(q, qm, o, g, lse, own, rem):
    seqs, length, features = q.shape
    delta = (g.astype(F32) * o.astype(F32)).reshape(seqs, length, features // PAIR, 2, HEAD).sum(-1)
    lse = lax.dynamic_update_slice(lse, jnp.transpose(delta, (0, 2, 3, 1)), (0, 0, 2, 0))
    lanes = math.gcd(features, 2 * PAIR)
    other = rem[0].shape[1]
    own_spec, rem_spec = pair_spec(length, lanes), pair_spec(other, lanes)
    return pl.pallas_call(
        attend_back_kernel,
        grid=(seqs, features // lanes),
        in_specs=[own_spec, mask_spec(length), own_spec, lse_spec(length, lanes)]
        + [own_spec, mask_spec(length), own_spec]
        + [rem_spec, mask_spec(other), rem_spec],
        out_specs=[own_spec] * 3 + [rem_spec] * 2,
        out_shape=[jax.ShapeDtypeStruct(q.shape, BF16)] * 3
        + [jax.ShapeDtypeStruct(rem[0].shape, BF16)] * 2,
        compiler_params=params(60),
        cost_estimate=cost(
            40 * q.size * (length + other), 2 * q.size * 14, q.size * (length + other) // HEAD
        ),
        name="attend_back",
    )(q, qm, g, lse, *own, *rem)


def gelu_and_slope(x):
    bell = jnp.exp2(x * x * (-0.5 * math.log2(math.e)))
    below = 1.0 + (0.3275911 / math.sqrt(2.0)) * jnp.abs(x)
    t = pl.reciprocal(below, approx=True)
    t = t * (2.0 - below * t)
    poly = 1.061405429 * t - 1.453152027
    poly = poly * t + 1.421413741
    poly = poly * t - 0.284496736
    poly = poly * t + 0.254829592
    tail = (0.5 * poly) * t * bell
    share = jnp.where(x >= 0.0, 1.0 - tail, tail)
    return x * share, share + x * bell * (1.0 / math.sqrt(2.0 * math.pi))


def mean(values):
    return jnp.sum(values, axis=-1, keepdims=True) * (1.0 / values.shape[-1])


def norm_parts(values):
    centred = values - mean(values)
    scale = lax.rsqrt(mean(centred * centred) + EPSILON)
    return centred * scale, scale


def norm_back(upper, normed, scale):
    return scale * (upper - mean(upper) - normed * mean(upper * normed))


def column_sum(values):
    return jnp.sum(values, axis=0, keepdims=True)


def feed_kernel(layout, tok_ref, att_ref, cot_ref, vec_ref, bu_ref, wo_ref, wu_ref, wd_ref,
                out_ref, bg_ref, ag_ref, vg_ref, dbu_ref, dwu_ref, dwd_ref, dwo_ref,
                act_s, din_s, first_t, feed_t, att_t, bg_s):
    tiles, ff_steps, chunk, wide, narrow = layout
    step = pl.program_id(0)
    tile = tok_ref.shape[0]
    hidden = act_s.shape[1]
    vec = [vec_ref[i : i + 1] for i in range(6)]
    out_bias, gain_one, shift_one, down_bias, gain_two, shift_two = vec

    @pl.when(step == 0)
    def _():
        vg_ref[...] = jnp.zeros_like(vg_ref)
        dbu_ref[...] = jnp.zeros_like(dbu_ref)

    @pl.when(step < tiles)
    def _():
        start = pl.multiple_of(step * tile, tile)
        rows = pl.ds(start, tile)
        att = att_ref[...]
        normed_one, scale_one = norm_parts(
            tok_ref[...].astype(F32) + (dot(att, wo_ref[...]) + out_bias)
        )
        first = normed_one * gain_one + shift_one
        first_low = first.astype(BF16)
        first_t[:, rows] = first_low.T
        att_t[:, rows] = att.T
        feed = jnp.zeros_like(first) + down_bias
        spans = [slice(c, c + chunk) for c in range(0, hidden, chunk)]
        ahead = dot(first_low, wu_ref[:, spans[0]])
        for i, cols in enumerate(spans):
            inner = ahead + bu_ref[:, cols]
            if i + 1 < len(spans):
                ahead = dot(first_low, wu_ref[:, spans[i + 1]])
            active, slope = gelu_and_slope(inner)
            active = active.astype(BF16)
            act_s[rows, cols] = active
            din_s[rows, cols] = slope.astype(BF16)
            feed += dot(active, wd_ref[cols])
        normed_two, scale_two = norm_parts(first + feed)
        out_ref[...] = (normed_two * gain_two + shift_two).astype(BF16)
        cot = cot_ref[...].astype(F32)
        second = norm_back(cot * gain_two, normed_two, scale_two)
        feed_low = second.astype(BF16)
        feed_t[:, rows] = feed_low.T
        back = second
        ahead = dot(feed_low, wd_ref[spans[0]], NT)
        for i, cols in enumerate(spans):
            inner = ahead
            if i + 1 < len(spans):
                ahead = dot(feed_low, wd_ref[spans[i + 1]], NT)
            inner = (inner * din_s[rows, cols].astype(F32)).astype(BF16)
            din_s[rows, cols] = inner
            dbu_ref[:, cols] += column_sum(inner.astype(F32))
            back += dot(inner, wu_ref[:, cols], NT)
        residual = norm_back(back * gain_one, normed_one, scale_one)
        branch_low = residual.astype(BF16)
        bg_ref[...] = branch_low
        bg_s[rows] = branch_low
        ag_ref[...] = dot(branch_low, wo_ref[...], NT).astype(BF16)
        for i, values in enumerate(
            (
                branch_low.astype(F32),
                back * normed_one,
                back,
                feed_low.astype(F32),
                cot * normed_two,
                cot,
            )
        ):
            vg_ref[i : i + 1] += column_sum(values)

    @pl.when((step >= tiles) & (step < tiles + ff_steps))
    def _():
        cols = pl.ds(pl.multiple_of((step - tiles) * wide, wide), wide)
        dwu = dot(first_t[...], din_s[:, cols]).astype(BF16)
        dwu_ref[...] = dwu.reshape(dwu_ref.shape)
        dwd_ref[...] = dot(feed_t[...], act_s[:, cols]).astype(BF16).T

    @pl.when(step >= tiles + ff_steps)
    def _():
        cols = pl.ds(pl.multiple_of((step - tiles - ff_steps) * narrow, narrow), narrow)
        dwo_ref[...] = dot(att_t[...], bg_s[:, cols]).astype(BF16)


def feed_both_ways(tokens, attended, cotangent, vectors, up_bias, wo, wu, wd, groups):
    rows, features = tokens.shape
    hidden = wu.shape[1]
    tile = math.gcd(rows, 256)
    tiles = rows // tile
    wide, narrow = features, math.gcd(features, 384)
    ff_steps, out_steps = hidden // wide, features // narrow
    layout = (tiles, ff_steps, math.gcd(hidden, 512), wide, narrow)
    blocked = (groups, ff_steps, features // groups, wide)
    row_spec = pl.BlockSpec((tile, features), lambda i: (jnp.minimum(i, tiles - 1), 0))

    def ff_at(i):
        return jnp.clip(i - tiles, 0, ff_steps - 1)

    return pl.pallas_call(
        functools.partial(feed_kernel, layout),
        grid=(tiles + ff_steps + out_steps,),
        in_specs=[row_spec] * 3
        + [whole_spec(a.shape) for a in (vectors, up_bias, wo, wu, wd)],
        out_specs=[row_spec] * 3
        + [
            pl.BlockSpec((8, features), lambda i: (0, 0)),
            pl.BlockSpec((1, hidden), lambda i: (0, 0)),
            pl.BlockSpec((groups, 1) + blocked[2:], lambda i: (0, ff_at(i), 0, 0)),
            pl.BlockSpec((wide, features), lambda i: (ff_at(i), 0)),
            pl.BlockSpec(
                (features, narrow),
                lambda i: (0, jnp.clip(i - tiles - ff_steps, 0, out_steps - 1)),
            ),
        ],
        out_shape=[jax.ShapeDtypeStruct(tokens.shape, BF16)] * 3
        + [
            jax.ShapeDtypeStruct((8, features), F32),
            jax.ShapeDtypeStruct((1, hidden), F32),
            jax.ShapeDtypeStruct(blocked, BF16),
            jax.ShapeDtypeStruct(wd.shape, BF16),
            jax.ShapeDtypeStruct(wo.shape, BF16),
        ],
        scratch_shapes=[
            pltpu.VMEM((rows, hidden), BF16),
            pltpu.VMEM((rows, hidden), BF16),
            pltpu.VMEM((features, rows), BF16),
            pltpu.VMEM((features, rows), BF16),
            pltpu.VMEM((features, rows), BF16),
            pltpu.VMEM((rows, features), BF16),
        ],
        compiler_params=params(60),
        cost_estimate=cost(
            6 * rows * features * (features + 2 * hidden),
            2 * (6 * rows * features + 4 * features * hidden + 2 * features * features),
            2 * rows * hidden,
        ),
        name="feed_both_ways",
    )(tokens, attended, cotangent, vectors, up_bias, wo, wu, wd)


def spread(row):
    return jnp.broadcast_to(row, (PAIR, row.shape[1])).T


def as_row(ref):
    return ref[...].astype(F32).reshape(1, ref.shape[0])


def front_kernel(tokens_ref, group_ref, valid_ref, cot_ref, bq_ref, bv_ref, bo_ref, g1_ref, s1_ref, bd_ref,
                 g2_ref, s2_ref, bu_in, wq_any, wk_any, wv_any, wo_any, wu_any, wd_any,
                 out_ref, bg_ref, ag_ref, att_ref, lse_ref, qm_ref, km_ref,
                 first_t, feed_t, vg_ref, dbu_ref, q_any, k_any, v_any, rem_any, act_any, din_any,
                 wq, wk, wv, wo, wu, wd, tok_s, q_s, k_s, v_s, kr_s, vr_s, rem_s, own_codes, code_s, act_s, din_s,
                 bu_ref, weight_sem, out_sem, send_sem, recv_sem):
    s = pl.program_id(0)
    seqs = tok_s.shape[0]
    length, features = tok_s.shape[1:]
    hidden = act_s.shape[1]
    side = lax.axis_index("blk")
    other = {"blk": 1 - side}
    query_bias, value_bias, out_bias, gain_one, shift_one, down_bias, gain_two, shift_two = [
        as_row(ref) for ref in (bq_ref, bv_ref, bo_ref, g1_ref, s1_ref, bd_ref, g2_ref, s2_ref)
    ]
    pairs_of = [(wq_any, wq), (wk_any, wk), (wv_any, wv), (wo_any, wo), (wu_any, wu), (wd_any, wd)]

    def weight(i):
        return pltpu.make_async_copy(*pairs_of[i], weight_sem.at[i])

    def remote(source, target, at):
        return pltpu.make_async_remote_copy(
            src_ref=source,
            dst_ref=target,
            send_sem=send_sem.at[at],
            recv_sem=recv_sem.at[at],
            device_id=other,
            device_id_type=pl.DeviceIdType.MESH,
        )

    def exchange(at):
        return remote(tokens_ref.at[at], rem_s.at[at], at)

    def code_exchange():
        return remote(own_codes, code_s, seqs)

    def whole_out(i):
        source, target = ((q_s, q_any), (k_s, k_any.at[0]), (v_s, v_any.at[0]))[i]
        return pltpu.make_async_copy(source, target, out_sem.at[i])

    def part_out(i, at):
        source, target = (
            (kr_s, k_any.at[1, at]),
            (vr_s, v_any.at[1, at]),
            (rem_s.at[at], rem_any.at[at]),
            (act_s, act_any.at[at]),
            (din_s, din_any.at[at]),
        )[i]
        return pltpu.make_async_copy(source, target, out_sem.at[3 + i])

    @pl.when(s == 0)
    def _():
        barrier = pltpu.get_barrier_semaphore()
        pl.semaphore_signal(barrier, inc=1, device_id=other, device_id_type=pl.DeviceIdType.MESH)
        load = pltpu.make_async_copy(tokens_ref, tok_s, weight_sem.at[len(pairs_of)])
        load.start()
        for i in range(3):
            weight(i).start()
        codes = jnp.where(valid_ref[...] == 1, group_ref[...], -1).astype(F32)
        own_codes[...] = jnp.zeros_like(own_codes)
        own_codes[0:seqs] = codes
        pl.semaphore_wait(barrier, 1)
        exchange(0).start()
        code_exchange().start()
        for i in range(3, len(pairs_of)):
            weight(i).start()
        vg_ref[...] = jnp.zeros_like(vg_ref)
        dbu_ref[...] = jnp.zeros_like(dbu_ref)
        bu_ref[...] = as_row(bu_in)
        load.wait()
        for i in range(3):
            weight(i).wait()

        def project_own(at, carry):
            x = tok_s[at]
            q_s[at] = ((dot(x, wq[...]) + query_bias) * EXPO).astype(BF16)
            k_s[at] = dot(x, wk[...]).astype(BF16)
            v_s[at] = (dot(x, wv[...]) + value_bias).astype(BF16)
            return carry

        lax.fori_loop(0, seqs, project_own, 0)
        for i in range(3):
            whole_out(i).start()
        for i in range(3, len(pairs_of)):
            weight(i).wait()
        code_exchange().wait_recv()
        exchange(0).wait_send()
        if seqs > 1:
            exchange(1).start()

    for at in range(seqs):

        @pl.when(s == at)
        def _(at=at):
            exchange(at).wait_recv()
            if at:
                for i in range(3):
                    part_out(i, at - 1).wait()

    x = rem_s[s]
    kr_s[...] = dot(x, wk[...]).astype(BF16)
    vr_s[...] = (dot(x, wv[...]) + value_bias).astype(BF16)
    slot = lax.broadcasted_iota(jnp.int32, (1, PAIR), 1) % HEAD
    slot = slot.astype(F32)
    groups_row = group_ref[pl.ds(s, 1)].astype(F32)
    qm_ref[0] = jnp.where(spread(groups_row) == slot, 1.0, 0.0).astype(BF16)
    km_ref[0, 0] = jnp.where(spread(own_codes[pl.ds(s, 1)]) == slot, 0.0, MASKED).astype(BF16)
    km_ref[1, 0] = jnp.where(spread(code_s[pl.ds(s, 1)]) == slot, 0.0, MASKED).astype(BF16)
    for at in range(seqs):

        @pl.when(s == at)
        def _(at=at):
            for i in range(3):
                part_out(i, at).start()

    groups = features // (2 * PAIR)

    def heads(group, carry):
        lanes = pl.ds(pl.multiple_of(group * 2 * PAIR, 2 * PAIR), 2 * PAIR)
        attend_group(
            q_s[s, :, lanes],
            qm_ref[0],
            [(k_s[s, :, lanes], km_ref[0, 0], v_s[s, :, lanes]), (kr_s[:, lanes], km_ref[1, 0], vr_s[:, lanes])],
            att_ref.at[0, :, lanes],
            lse_ref.at[0, pl.ds(group * 2, 2)],
        )
        return carry

    lax.fori_loop(0, groups, heads, 0)

    for at in range(1, seqs):

        @pl.when(s == at)
        def _(at=at):
            for i in range(3, 5):
                part_out(i, at - 1).wait()

    tile = math.gcd(length, FEED_ROWS)
    chunk = math.gcd(hidden, 1024)
    spans = [slice(c, c + chunk) for c in range(0, hidden, chunk)]

    def feed_rows(t, carry):
        rows = pl.ds(pl.multiple_of(t * tile, tile), tile)
        att = att_ref[0, rows]
        normed_one, scale_one = norm_parts(
            tok_s[s, rows].astype(F32) + (dot(att, wo[...]) + out_bias)
        )
        first = normed_one * gain_one + shift_one
        first_low = first.astype(BF16)
        first_t[:, rows] = first_low.T
        feed = jnp.zeros_like(first) + down_bias
        ahead = dot(first_low, wu[:, spans[0]])
        for i, cols in enumerate(spans):
            inner = ahead + bu_ref[:, cols]
            if i + 1 < len(spans):
                ahead = dot(first_low, wu[:, spans[i + 1]])
            active, slope = gelu_and_slope(inner)
            active = active.astype(BF16)
            act_s[rows, cols] = active
            din_s[rows, cols] = slope.astype(BF16)
            feed += dot(active, wd[cols])
        normed_two, scale_two = norm_parts(first + feed)
        out_ref[0, rows] = (normed_two * gain_two + shift_two).astype(BF16)
        cot = cot_ref[0, rows].astype(F32)
        second = norm_back(cot * gain_two, normed_two, scale_two)
        feed_low = second.astype(BF16)
        feed_t[:, rows] = feed_low.T
        back = second
        ahead = dot(feed_low, wd[spans[0]], NT)
        for i, cols in enumerate(spans):
            inner = ahead
            if i + 1 < len(spans):
                ahead = dot(feed_low, wd[spans[i + 1]], NT)
            inner = (inner * din_s[rows, cols].astype(F32)).astype(BF16)
            din_s[rows, cols] = inner
            dbu_ref[:, cols] += column_sum(inner.astype(F32))
            back += dot(inner, wu[:, cols], NT)
        residual = norm_back(back * gain_one, normed_one, scale_one)
        branch_low = residual.astype(BF16)
        bg_ref[0, rows] = branch_low
        att_grad = dot(branch_low, wo[...], NT).astype(BF16)
        ag_ref[0, rows] = att_grad
        product = att_grad.astype(F32) * att.astype(F32)
        coarse = product.astype(BF16)
        fine = (product - coarse.astype(F32)).astype(BF16)
        heads_count = features // HEAD
        of_head = lax.broadcasted_iota(jnp.int32, (heads_count, features), 1) // HEAD
        selector = (of_head == lax.broadcasted_iota(jnp.int32, of_head.shape, 0)).astype(F32)
        selector = selector.astype(BF16)
        delta = dot(selector, coarse, NT) + dot(selector, fine, NT)
        for pair in range(features // PAIR):
            lse_ref[0, pair, 2:4, rows] = delta[2 * pair : 2 * pair + 2]
        for i, values in enumerate(
            (
                branch_low.astype(F32),
                back * normed_one,
                back,
                feed_low.astype(F32),
                cot * normed_two,
                cot,
            )
        ):
            vg_ref[i : i + 1] += column_sum(values)
        return carry

    lax.fori_loop(0, length // tile, feed_rows, 0)

    for at in range(seqs):

        @pl.when(s == at)
        def _(at=at):
            for i in range(3, 5):
                part_out(i, at).start()
            if at < seqs - 1:
                exchange(at + 1).wait_send()
            if at + 2 < seqs:
                exchange(at + 2).start()
            if at == seqs - 1:
                for i in range(3):
                    whole_out(i).wait()
                for i in range(5):
                    part_out(i, at).wait()
                code_exchange().wait_send()


def front(tokens, group_ids, valid, cotangent, vectors, up_bias, weights):
    seqs, length, features = tokens.shape
    hidden = up_bias.shape[0]
    pairs = features // PAIR
    anywhere = pl.BlockSpec(memory_space=pl.ANY)

    def at_seq(*shape):
        return pl.BlockSpec((1,) + shape, lambda s: (s,) + (0,) * len(shape))

    def of_seqs(*shape, dtype=BF16):
        return jax.ShapeDtypeStruct((seqs,) + shape, dtype)

    def fixed(*shape):
        return pl.BlockSpec(shape, lambda s: (0,) * len(shape))

    rows, mask, lses, wide = (length, features), (length, PAIR), (pairs, 8, length), (length, hidden)
    turned = pl.BlockSpec((features, length), lambda s: (0, s))
    return pl.pallas_call(
        front_kernel,
        grid=(seqs,),
        in_specs=[anywhere, whole_spec(group_ids.shape), whole_spec(valid.shape), at_seq(*rows)]
        + [whole_spec(v.shape) for v in vectors + (up_bias,)]
        + [anywhere] * 6,
        out_specs=[at_seq(*rows)] * 4
        + [at_seq(*lses), at_seq(*mask)]
        + [pl.BlockSpec((2, 1) + mask, lambda s: (0, s, 0, 0))]
        + [turned] * 2
        + [fixed(8, features), fixed(1, hidden)]
        + [anywhere] * 6,
        out_shape=[of_seqs(*rows)] * 4
        + [of_seqs(*lses, dtype=F32), of_seqs(*mask)]
        + [jax.ShapeDtypeStruct((2, seqs) + mask, BF16)]
        + [jax.ShapeDtypeStruct((features, seqs * length), BF16)] * 2
        + [jax.ShapeDtypeStruct((8, features), F32), jax.ShapeDtypeStruct((1, hidden), F32)]
        + [of_seqs(*rows)]
        + [jax.ShapeDtypeStruct((2, seqs) + rows, BF16)] * 2
        + [of_seqs(*rows)]
        + [of_seqs(*wide)] * 2,
        scratch_shapes=[pltpu.VMEM(w.shape, BF16) for w in weights]
        + [pltpu.VMEM(tokens.shape, BF16)] * 4
        + [pltpu.VMEM(rows, BF16)] * 2
        + [pltpu.VMEM(tokens.shape, BF16)]
        + [pltpu.VMEM((seqs + -seqs % 8, length), F32)] * 2
        + [pltpu.VMEM(wide, BF16)] * 2
        + [pltpu.VMEM((1, hidden), F32)]
        + [pltpu.SemaphoreType.DMA((7,)), pltpu.SemaphoreType.DMA((8,))]
        + [pltpu.SemaphoreType.DMA((seqs + 1,))] * 2,
        compiler_params=pltpu.CompilerParams(
            collective_id=2, has_side_effects=True, vmem_limit_bytes=63 * MIB
        ),
        cost_estimate=cost(
            2 * tokens.size * (9 * features + 4 * hidden + 8 * length), 2 * 20 * tokens.size, tokens.size * 24
        ),
        name="front",
    )(tokens, group_ids, valid, cotangent, *vectors, up_bias, *weights)


def feed_weights_kernel(blocks, first_ref, din_ref, feed_ref, act_ref, att_any, bg_any,
                        dwu_ref, dwd_ref, dwo_ref, up_s, up_in, down_s, down_in, out_s, out_in,
                        att_s, bg_s, near_sem, send_sem, recv_sem):
    step = pl.program_id(0)
    features = first_ref.shape[0]
    me = lax.axis_index("dp")
    core = me % 2
    other = {"dp": me + 1 - 2 * core}

    def loads():
        return [
            pltpu.make_async_copy(att_any, att_s, near_sem.at[0]),
            pltpu.make_async_copy(bg_any, bg_s, near_sem.at[1]),
        ]

    each, deep = down_in.shape[1:3]

    def piece(i, side):
        return pl.ds(pl.multiple_of((2 * i + side) * deep, 16), deep)

    def swaps(block):
        if block == blocks:
            pairs = [(out_s.at[:, 1 - core], out_in)]
        else:
            pairs = [(up_s.at[block % 2, :, 1 - core], up_in.at[block])]
            for i in range(each):
                pairs.append((down_s.at[block % 2, piece(i, 1 - core)], down_in.at[block, i]))
        return [
            pltpu.make_async_remote_copy(
                src_ref=source,
                dst_ref=target,
                send_sem=send_sem.at[(each + 1) * block + i],
                recv_sem=recv_sem.at[(each + 1) * block + i],
                device_id=other,
                device_id_type=pl.DeviceIdType.MESH,
            )
            for i, (source, target) in enumerate(pairs)
        ]

    @pl.when(step == 0)
    def _():
        for load in loads():
            load.start()
        barrier = pltpu.get_barrier_semaphore()
        pl.semaphore_signal(barrier, inc=1, device_id=other, device_id_type=pl.DeviceIdType.MESH)
        pl.semaphore_wait(barrier, 1)

    @pl.when(step < blocks)
    def _():
        slot = step % 2
        tile = math.gcd(features, 256)
        for start in range(0, features, tile):
            cols = slice(start, start + tile)
            up = dot(first_ref[...], din_ref[:, cols]).astype(BF16)
            up_s[slot, :, :, :, cols] = up.reshape(up_s.shape[1:4] + (tile,))
            down_s[slot, cols] = dot(feed_ref[...], act_ref[:, cols]).astype(BF16).T

    for block in range(blocks):

        @pl.when(step == block)
        def _(block=block):
            for swap in swaps(block):
                swap.start()

    @pl.when(step == blocks)
    def _():
        for load in loads():
            load.wait()
        out_s[...] = dot(att_s[...].T, bg_s[...]).astype(BF16).reshape(out_s.shape)
        for swap in swaps(blocks):
            swap.start()

    for block in range(blocks):

        @pl.when(step == block + 1)
        def _(block=block):
            for swap in swaps(block):
                swap.wait()
            dwu_ref[:, 0] = (up_s[block % 2, :, core].astype(F32) + up_in[block].astype(F32)).astype(BF16)
            for i in range(each):
                mine = down_s[block % 2, piece(i, core)].astype(F32)
                dwd_ref[i] = (mine + down_in[block, i].astype(F32)).astype(BF16)

    @pl.when(step == blocks + 1)
    def _():
        for swap in swaps(blocks):
            swap.wait()
        dwo_ref[...] = (out_s[:, core].astype(F32) + out_in[...].astype(F32)).astype(BF16)


def feed_weights(first_t, din, feed_t, act, att, bg):
    dp = lax.axis_size("dp")
    features, rows = first_t.shape
    hidden = act.shape[1]
    blocks, half, low, deep = hidden // features, dp // 2, features // dp, hidden // dp
    each = half // blocks
    wide_spec = pl.BlockSpec((rows, features), lambda i: (0, jnp.minimum(i, blocks - 1)))
    anywhere = pl.BlockSpec(memory_space=pl.ANY)

    def behind(i):
        return jnp.clip(i - 1, 0, blocks - 1)

    return pl.pallas_call(
        functools.partial(feed_weights_kernel, blocks),
        grid=(blocks + 2,),
        in_specs=[
            whole_spec(first_t.shape),
            wide_spec,
            whole_spec(feed_t.shape),
            wide_spec,
            anywhere,
            anywhere,
        ],
        out_specs=[
            pl.BlockSpec((half, 1, low, features), lambda i: (0, behind(i), 0, 0)),
            pl.BlockSpec((each, deep, features), lambda i: (behind(i), 0, 0)),
            pl.BlockSpec((half, low, features), lambda i: (0, 0, 0)),
        ],
        out_shape=[
            jax.ShapeDtypeStruct((half, blocks, low, features), BF16),
            jax.ShapeDtypeStruct((half, deep, features), BF16),
            jax.ShapeDtypeStruct((half, low, features), BF16),
        ],
        scratch_shapes=[
            pltpu.VMEM((2, half, 2, low, features), BF16),
            pltpu.VMEM((blocks, half, low, features), BF16),
            pltpu.VMEM((2, features, features), BF16),
            pltpu.VMEM((blocks, each, deep, features), BF16),
            pltpu.VMEM((half, 2, low, features), BF16),
            pltpu.VMEM((half, low, features), BF16),
            pltpu.VMEM(att.shape, BF16),
            pltpu.VMEM(bg.shape, BF16),
            pltpu.SemaphoreType.DMA((2,)),
            pltpu.SemaphoreType.DMA(((each + 1) * blocks + 1,)),
            pltpu.SemaphoreType.DMA(((each + 1) * blocks + 1,)),
        ],
        compiler_params=pltpu.CompilerParams(
            collective_id=3, has_side_effects=True, vmem_limit_bytes=63 * MIB
        ),
        cost_estimate=cost(
            2 * rows * features * (2 * hidden + features), 4 * rows * (hidden + 2 * features)
        ),
        name="feed_weights",
    )(first_t, din, feed_t, act, att, bg)


def own_back_kernel(bg_ref, dq_ref, dk_ref, dv_ref, wq_ref, wk_ref, wv_ref, out_ref):
    total = bg_ref[0].astype(F32) + dot(dq_ref[0], wq_ref[...], NT)
    total += dot(dk_ref[0], wk_ref[...], NT)
    total += dot(dv_ref[0], wv_ref[...], NT)
    out_ref[0] = total.astype(BF16)


def rem_back_kernel(dk_ref, dv_ref, wk_ref, wv_ref, out_ref):
    total = dot(dk_ref[0], wk_ref[...], NT) + dot(dv_ref[0], wv_ref[...], NT)
    out_ref[0] = total.astype(BF16)


def tokens_back(kernel, rows, weights):
    seqs, length, features = rows[0].shape
    tile = math.gcd(length, 512)
    row_spec = pl.BlockSpec((1, tile, features), lambda s, i: (s, i, 0))
    size = rows[0].size
    return pl.pallas_call(
        kernel,
        grid=(seqs, length // tile),
        in_specs=[row_spec] * len(rows) + [whole_spec(w.shape) for w in weights],
        out_specs=row_spec,
        out_shape=jax.ShapeDtypeStruct(rows[0].shape, BF16),
        compiler_params=params(60),
        cost_estimate=cost(2 * size * features * len(weights), 2 * size * (1 + len(rows))),
        name="tokens_back",
    )(*rows, *weights)


def weights_back_kernel(tok_ref, rem_ref, dq_ref, dko_ref, dvo_ref, dkr_ref, dvr_ref,
                        wq_ref, wk_ref, wv_ref, bq_ref, bv_ref, tok_t, rem_t):
    @pl.when(pl.program_id(0) == 0)
    def _():
        tok_t[...] = tok_ref[...].T
        rem_t[...] = rem_ref[...].T

    wq_ref[...] = dot(tok_t[...], dq_ref[...]).astype(BF16)
    wk_ref[...] = (dot(tok_t[...], dko_ref[...]) + dot(rem_t[...], dkr_ref[...])).astype(BF16)
    wv_ref[...] = (dot(tok_t[...], dvo_ref[...]) + dot(rem_t[...], dvr_ref[...])).astype(BF16)
    bq_ref[...] = column_sum(dq_ref[...].astype(F32))
    bv_ref[...] = column_sum(dvo_ref[...].astype(F32)) + column_sum(dvr_ref[...].astype(F32))


def weights_back(tok, rem, dq, dko, dvo, dkr, dvr):
    rows, features = tok.shape
    others = rem.shape[0]
    wide = math.gcd(features, 256)
    own_spec = pl.BlockSpec((rows, wide), lambda j: (0, j))
    rem_spec = pl.BlockSpec((others, wide), lambda j: (0, j))
    bias_spec = pl.BlockSpec((1, wide), lambda j: (0, j))
    return pl.pallas_call(
        weights_back_kernel,
        grid=(features // wide,),
        in_specs=[
            whole_spec(tok.shape),
            whole_spec(rem.shape),
            own_spec,
            own_spec,
            own_spec,
            rem_spec,
            rem_spec,
        ],
        out_specs=[pl.BlockSpec((features, wide), lambda j: (0, j))] * 3 + [bias_spec] * 2,
        out_shape=[jax.ShapeDtypeStruct((features, features), BF16)] * 3
        + [jax.ShapeDtypeStruct((1, features), F32)] * 2,
        scratch_shapes=[
            pltpu.VMEM((features, rows), BF16),
            pltpu.VMEM((features, others), BF16),
        ],
        compiler_params=params(60),
        cost_estimate=cost(
            2 * features * features * (3 * rows + 2 * others),
            2 * (4 * tok.size + 3 * rem.size + 3 * features * features),
        ),
        name="weights_back",
    )(tok, rem, dq, dko, dvo, dkr, dvr)


def halve(value, axis, bit):
    size = lax.axis_size(axis)
    mine = (lax.axis_index(axis) >> bit) & 1
    pairs = value.reshape((value.shape[0] // 2, 2) + value.shape[1:])
    keep = lax.dynamic_index_in_dim(pairs, mine, 1, keepdims=False)
    send = lax.dynamic_index_in_dim(pairs, 1 - mine, 1, keepdims=False)
    came = lax.ppermute(send, axis, [(i, i ^ (1 << bit)) for i in range(size)])
    return keep.astype(F32) + came.astype(F32)


def scatter_sum(value, low=True):
    dp, blk = lax.axis_size("dp"), lax.axis_size("blk")
    if dp & (dp - 1) or blk & (blk - 1):
        return lax.psum_scatter(
            value.astype(F32), ("dp", "blk"), scatter_dimension=0, tiled=True
        )
    kept = value.dtype
    each = value.shape[0] // (dp * blk)
    value = value.reshape((dp, blk * each) + value.shape[1:])
    for bit in range(dp.bit_length() - 1):
        value = halve(value, "dp", bit).astype(kept)
    value = value.reshape((blk, each) + value.shape[2:])
    for bit in range(blk.bit_length() - 1):
        value = halve(value, "blk", bit)
        value = value if (2 << bit) == blk else value.astype(kept)
    return value.reshape(value.shape[1:]).astype(F32)


class Unit:
    def __init__(self, parts, rows, columns, halves, outs):
        self.parts, self.rows, self.columns = parts, rows, columns
        self.halves, self.outs = halves, outs
        self.first = 1 if parts else 0
        self.half = rows // (2 * halves)
        self.last_type = BF16 if (rows // 2) % 16 == 0 else F32


def timetable(units, bits, seqs, groups, slot_us, token_us):
    free, pending, table = {}, [], []
    slots = seqs * groups * 2

    def launch(key, now):
        kind, which, step = key
        if kind == "tokens":
            link, us = "blk", token_us
        elif kind == "vectors":
            link, us = None, 1.0
        else:
            us = units[which].rows * units[which].columns * 2e-5
            us *= 1 << max(bits - 1 - step, 0)
            us *= {0: 0.4, bits - 1: 3.0}.get(step, 1.25)
            link = {0: "core", bits - 1: "far", bits: "blk"}.get(step, "near")
        start = max(now, free.get(link, 0.0))
        if link:
            free[link] = start + us
        if kind != "tokens":
            pending.append((start + us + 2.5, key))

    for u, unit in enumerate(units):
        if unit.parts:
            launch(("unit", u, 1), 3.0)
    first_group = sum(1 for unit in units if unit.parts)
    now = 0.0
    while len(table) < slots or pending:
        slot = len(table)
        if slot < slots:
            now = (slot + 1) * slot_us
            part, major, minor = slot // (seqs * groups), slot // groups % seqs, slot % groups
            if part == 0 and minor == groups - 1:
                launch(("tokens", major, 0), now)
            major, minor = divmod(slot - seqs * groups, seqs)
            if part == 1 and minor == seqs - 1:
                launch(("unit", first_group + major, 0), now)
            if slot == slots - 1:
                launch(("vectors", 0, 0), now)
            due = sorted(p for p in pending if p[0] <= now)
        else:
            due = [min(pending)]
            now = max(now + 0.3, due[0][0])
        table.append([key for _, key in due])
        for found in due:
            pending.remove(found)
            kind, which, step = found[1]
            if step < bits:
                launch((kind, which, step + 1), now)
    tail = [key for keys in table[slots:] for key in keys]
    return table[:slots], tail + [("tokens", s, 0) for s in range(seqs)]


def order_of(step, seqs, groups):
    part = step // (seqs * groups)
    left = step - part * (seqs * groups)
    s = left // groups * (1 - part) + left % seqs * part
    h = left % groups * (1 - part) + left // seqs * part
    return part, s, h


def back_kernel(units, bits, groups, table, tail, n_out, *refs):
    (q_ref, qm_ref, g_ref, lse_ref, k_ref, km_ref, v_ref,
     tok_ref, rem_ref, wq_ref, wk_ref, wv_ref, vg_ref, vu_ref) = refs[:14]
    sources, refs = refs[14:17], list(refs[17:])
    tokens_any, rem_in, *outs = refs[:n_out]
    refs = refs[n_out:]
    kept = [refs.pop(0) for _ in units]
    landed = [
        [refs.pop(0) if k >= unit.first else None for k in range(bits)] for unit in units
    ]
    wide = [refs.pop(0) for _ in units]
    parting = [refs.pop(0) for _ in units]
    last = [refs.pop(0) for _ in units]
    (weight_sum, group_src, total_s, turned, dq_part, dq_s, dk_s, dv_s,
     rem_out, vec, vec_in, bias_sum, send_sem, recv_sem, local_sem, out_sem) = refs
    step = pl.program_id(0)
    steps = pl.num_programs(0)
    seqs = rem_out.shape[0]
    part, s, h = order_of(step, seqs, groups)
    features = tok_ref.shape[2]
    me, side = lax.axis_index("dp"), lax.axis_index("blk")
    core = me % 2

    def swapped(k):
        return {1: 2, 2: 1}.get(k, k) if bits > 2 else k

    def pick(values, k):
        return values[k] + (values[swapped(k)] - values[k]) * core

    bit_own = [(me // (1 << bit)) % 2 for bit in range(bits)]
    across = [me + (1 << bit) * (1 - 2 * bit_own[bit]) for bit in range(bits)]
    own = [pick(bit_own, k) for k in range(bits)]
    partner = [{"dp": pick(across, k)} for k in range(bits)] + [{"blk": 1 - side}]
    first_group = sum(1 for unit in units if unit.parts)
    lead = (slice(None),) * (bits - 1)

    def natural(digits):
        by_step = [None] + list(digits[::-1])
        return tuple(
            by_step[bit] if swapped(bit) == bit else pick(by_step, bit) for bit in range(bits - 1, 0, -1)
        )

    def digits_of(n, count):
        return [(n // (1 << (count - 1 - i))) % 2 for i in range(count)]

    sems = {}
    for u, unit in enumerate(units):
        for k in range(unit.first, bits + 1):
            sems["unit", u, k, 0] = len(sems)
    for k in range(bits + 1):
        sems["vectors", 0, k, 0] = len(sems)
    for k in range(seqs):
        sems["tokens", k, 0, 0] = len(sems)

    def remote(source, target, device, key):
        return pltpu.make_async_remote_copy(
            src_ref=source,
            dst_ref=target,
            send_sem=send_sem.at[sems[key]],
            recv_sem=recv_sem.at[sems[key]],
            device_id=device,
            device_id_type=pl.DeviceIdType.MESH,
        )

    near_sems = {}
    for u, unit in enumerate(units):
        for p in range(len(unit.parts or ())):
            for n in range(1 << min(bits - 1, 2)):
                near_sems[u, p, n] = len(near_sems)

    def spot(k, value):
        return tuple(
            own[at] if at < k else value if at == k else slice(None) for at in range(bits - 1, 0, -1)
        )

    def copies(kind, which, k):
        if kind == "tokens":
            return [remote(rem_out.at[which], rem_in.at[which], partner[bits], (kind, which, 0, 0))]
        if kind == "vectors":
            return [remote(vec.at[k], vec_in.at[k], partner[k], (kind, 0, k, 0))]
        u, unit = which, units[which]
        if k == bits:
            return [remote(parting[u], last[u], partner[bits], (kind, u, k, 0))]
        if k:
            source = kept[u].at[spot(k, 1 - own[k])]
            return [remote(source, landed[u][k], partner[k], (kind, u, k, 0))]
        source = group_src.at[(u - first_group,) + lead + (1 - core,)]
        return [remote(source, landed[u][0], partner[0], (kind, u, 0, 0))]

    def near_copies(u):
        found, row = [], 0
        for p, (source, first, rows) in enumerate(units[u].parts):
            for n in range(1 << min(bits - 1, 2)):
                digits = digits_of(n, min(bits - 1, 2))
                digits = [slice(None)] * (bits - 1 - len(digits)) + digits
                found.append(
                    pltpu.make_async_copy(
                        sources[source].at[natural(digits) + (pl.ds(first, rows),)],
                        kept[u].at[tuple(digits) + (pl.ds(row, rows),)],
                        local_sem.at[near_sems[u, p, n]],
                    )
                )
            row += rows
        return found

    def launch(*key):
        for copy in copies(*key):
            copy.start()

    def halves_of(u, which):
        unit = units[u]
        return [
            wide[u][pl.ds(pl.multiple_of(i * 2 * unit.half + which * unit.half, 8), unit.half)]
            for i in range(unit.halves)
        ]

    def receive(kind, which, k):
        for copy in copies(kind, which, k):
            copy.wait_recv()
        if kind == "tokens":
            return
        if kind == "vectors":
            vec[k + 1] = vec[k] + vec_in[k]
            if k < bits:
                launch(kind, 0, k + 1)
            return
        u, unit = which, units[which]
        if k == bits:
            for i, (mine, (out, rows, columns)) in enumerate(zip(halves_of(u, side), unit.outs)):
                came = last[u][...].astype(F32)[i * unit.half : (i + 1) * unit.half]
                outs[out][rows, columns] = mine + came
            return
        place = spot(k, own[k]) if k else lead
        open_at = [i for i, at in enumerate(place) if isinstance(at, slice)]

        def add(n, carry):
            at, where = list(place), digits_of(n, len(open_at))
            for i, digit in zip(open_at, where):
                at[i] = digit
            at = tuple(at)
            if k:
                mine, came = kept[u][at], landed[u][k][tuple(where)]
            else:
                mine = group_src[(u - first_group,) + natural(at) + (core,)]
                came = landed[u][0][natural(at)]
            total = mine.astype(F32) + came.astype(F32)
            if k == bits - 1:
                wide[u][...] = total
            else:
                kept[u][at] = total.astype(BF16)
            return carry

        if open_at:
            lax.fori_loop(0, 1 << len(open_at), add, 0)
        else:
            add(0, 0)
        if k == bits - 1:
            pieces = halves_of(u, 1 - side)
            pieces = pieces[0] if len(pieces) == 1 else jnp.concatenate(pieces, axis=0)
            parting[u][...] = pieces.astype(unit.last_type)
        launch(kind, u, k + 1)

    @pl.when(step == 0)
    def _():
        barrier = pltpu.get_barrier_semaphore()
        for other in partner:
            pl.semaphore_signal(barrier, inc=1, device_id=other, device_id_type=pl.DeviceIdType.MESH)
        pl.semaphore_wait(barrier, bits + 1)
        for u, unit in enumerate(units):
            if unit.parts:
                for copy in near_copies(u):
                    copy.start()
        for u, unit in enumerate(units):
            if unit.parts:
                for copy in near_copies(u):
                    copy.wait()
                launch("unit", u, 1)
        weight_sum[...] = jnp.zeros_like(weight_sum)
        bias_sum[...] = jnp.zeros_like(bias_sum)

    @pl.when((part == 0) & (h == 0))
    def _():
        turned[0] = rem_ref[0].T
        total_s[...] = jnp.zeros_like(total_s)

    @pl.when((part == 1) & (h == 0))
    def _():
        turned[s] = tok_ref[0].T

    width = q_ref.shape[2]
    columns = pl.ds(pl.multiple_of(h * width, width), width)

    found = attend_back_part(
        q_ref[0], qm_ref[0], g_ref[0], lse_ref.at[0], k_ref[0, 0], km_ref[0, 0], v_ref[0, 0],
        dk_s.at[s, :, columns], dv_s.at[s, :, columns],
    )
    dk, dv = dk_s[s, :, columns], dv_s[s, :, columns]
    x_t = turned[s * part]
    weight_sum[h, 1] += dot(x_t, dk)
    weight_sum[h, 2] += dot(x_t, dv)
    bias_sum[h, 1:2] += column_sum(dv.astype(F32))

    @pl.when(part == 0)
    def _():
        total_s[...] += dot(dk, wk_ref[:, columns], NT) + dot(dv, wv_ref[:, columns], NT)
        for pair, value in enumerate(found):
            dq_part[s, h, pair] = value.astype(dq_part.dtype)

    @pl.when(part == 1)
    def _():
        queries = []
        for pair, value in enumerate(found):
            value = (value + dq_part[s, h, pair].astype(F32)) * SCALE
            queries.append(value.T.astype(BF16))
        dq = jnp.concatenate(queries, axis=1)
        dq_s[s, :, columns] = dq
        weight_sum[h, 0] += dot(x_t, dq)
        bias_sum[h, 0:1] += column_sum(dq.astype(F32))

    for at in range(seqs):

        @pl.when(step == (at + 1) * groups - 1)
        def _(at=at):
            rem_out[at] = total_s[...].astype(BF16)
            launch("tokens", at, 0)

    for at in range(groups):

        @pl.when(step == steps - (groups - 1 - at) * seqs - 1)
        def _(at=at):
            rows = features // (1 << bits)
            for i in range(3):
                piece = weight_sum[at, i].astype(BF16)
                piece = piece.reshape((2,) * bits + (rows, piece.shape[1]))
                group_src[(at,) + (slice(None),) * bits + (slice(i * rows, (i + 1) * rows),)] = piece
            launch("unit", first_group + at, 0)

    @pl.when(step == steps - 1)
    def _():
        vec[0] = jnp.zeros_like(vec[0])
        vec[0, 0:6] = vg_ref[0:6]
        for at in range(groups):
            vec[0, 6:8, at * width : (at + 1) * width] = bias_sum[at, 0:2]
        blocks = vu_ref.shape[1] // features
        for at in range(blocks):
            vec[0, 8 + at : 9 + at] = vu_ref[:, at * features : (at + 1) * features]
        launch("vectors", 0, 0)

    for at, keys in enumerate(table):
        if keys:

            @pl.when(step == at)
            def _(keys=keys):
                for key in keys:
                    receive(*key)

    @pl.when(step == steps - 1)
    def _():
        def own_out(at):
            return pltpu.make_async_copy(dq_s.at[at], tokens_any.at[at], out_sem.at[at])

        left = list(tail)
        for at in range(seqs):
            total = dot(dq_s[at], wq_ref[...], NT)
            total += dot(dk_s[at], wk_ref[...], NT) + dot(dv_s[at], wv_ref[...], NT)
            dq_s[at] = total.astype(BF16)
            own_out(at).start()
            for _ in range(3):
                if left:
                    receive(*left.pop(0))
        for key in left:
            receive(*key)
        for at in range(seqs):
            own_out(at).wait()
        shards = (1 << bits) * 2
        place = me * 2 + side
        share = features // shards
        rows = pltpu.roll(vec[bits + 1, 0:8], (shards - place) * share % features, 1)
        outs[-1][0:8] = rows[:, :PAIR]
        share = vu_ref.shape[1] // shards
        each = features // share
        row = vec[bits + 1, pl.ds(8 + place // each, 1)]
        rows = pltpu.roll(jnp.broadcast_to(row, (8, features)), (each - place % each) * share % features, 1)
        outs[-1][8:16] = rows[:, :PAIR]
        for u, unit in enumerate(units):
            for k in range(unit.first, bits + 1):
                for copy in copies("unit", u, k):
                    copy.wait_send()
        for k in range(bits + 1):
            copies("vectors", 0, k)[0].wait_send()
        for k in range(seqs):
            copies("tokens", k, 0)[0].wait_send()


def back_and_sum(q, qm, g, lse, k, km, v, tokens, rem_tokens, weights, dwd, dwu, dwo, vg, vu):
    bits = lax.axis_size("dp").bit_length() - 1
    seqs, length, features = q.shape
    width = math.gcd(features, 2 * PAIR)
    groups, pairs = features // width, width // PAIR
    low, deep, blocks = dwo.shape[1], dwd.shape[1], dwu.shape[1]
    lead = (2,) * bits
    sources = [x.reshape(lead[1:] + (-1, features)) for x in (dwd, dwu, dwo)]
    every = slice(None)
    units = []
    quarter = deep // 4
    for i in range(2):
        at = slice(i * quarter, (i + 1) * quarter)
        parts = [(0, i * quarter, quarter), (0, (2 + i) * quarter, quarter)]
        units.append(Unit(parts, 2 * quarter, features, 1, [(0, at, every)]))
    for i in range(2):
        found = range(i * blocks // 2, (i + 1) * blocks // 2)
        units.append(
            Unit(
                [(1, found[0] * low, len(found) * low)],
                len(found) * low,
                features,
                len(found),
                [(1, every, slice(b * features, (b + 1) * features)) for b in found],
            )
        )
    units.append(Unit([(2, 0, low)], low, features, 1, [(2, every, every)]))
    for h in range(groups):
        columns = slice(h * width, (h + 1) * width)
        units.append(Unit(None, 3 * low, width, 3, [(3 + i, every, columns) for i in range(3)]))
    table, tail = timetable(units, bits, seqs, groups, 3.9, length * features * 4e-5)

    half = low // 2
    out_shape = [
        jax.ShapeDtypeStruct(q.shape, BF16),
        jax.ShapeDtypeStruct(q.shape, BF16),
        jax.ShapeDtypeStruct((deep // 2, features), F32),
        jax.ShapeDtypeStruct((half, blocks * features), F32),
        *(jax.ShapeDtypeStruct((half, features), F32) for _ in range(4)),
        jax.ShapeDtypeStruct((16, PAIR), F32),
    ]
    tops = lead[1:]
    scratch = [pltpu.VMEM(tops + (u.rows, u.columns), BF16) for u in units]
    for u in units:
        scratch += [pltpu.VMEM(tops[k:] + (u.rows, u.columns), BF16) for k in range(u.first, bits)]
    scratch += [pltpu.VMEM((u.rows, u.columns), F32) for u in units]
    scratch += [pltpu.VMEM((u.rows // 2, u.columns), u.last_type) for u in units] * 2
    count = len(units) * (bits + 1) + bits + 1 + seqs
    near = sum(len(u.parts) << min(bits - 1, 2) for u in units if u.parts)
    scratch += [
        pltpu.VMEM((groups, 3, features, width), F32),
        pltpu.VMEM((groups,) + lead + (3 * low, width), BF16),
        pltpu.VMEM((length, features), F32),
        pltpu.VMEM((seqs, features, length), BF16),
        pltpu.VMEM((seqs, groups, pairs, PAIR, length), F32),
        *(pltpu.VMEM((seqs, length, features), BF16) for _ in range(4)),
        pltpu.VMEM((bits + 2, 16, features), F32),
        pltpu.VMEM((bits + 1, 16, features), F32),
        pltpu.VMEM((groups, 8, width), F32),
        pltpu.SemaphoreType.DMA((count,)),
        pltpu.SemaphoreType.DMA((count,)),
        pltpu.SemaphoreType.DMA((near,)),
        pltpu.SemaphoreType.DMA((seqs,)),
    ]

    def at_step(shape, index):
        return pl.BlockSpec(shape, lambda i: index(*order_of(i, seqs, groups)))

    heads_at = at_step((1, length, width), lambda p, s, h: (s, 0, h))
    keys_at = at_step((1, 1, length, width), lambda p, s, h: (1 - p, s, 0, h))

    def rows_at(which):
        last = seqs - 1
        return pl.BlockSpec(
            (1, length, features),
            lambda i: (jnp.clip(i // groups if which == 0 else i - seqs * groups, 0, last), 0, 0),
            pipeline_mode=pl.Buffered(1),
        )

    def fixed(shape):
        return pl.BlockSpec(shape, lambda i: (0,) * len(shape), pipeline_mode=pl.Buffered(1))

    return pl.pallas_call(
        functools.partial(back_kernel, units, bits, groups, table, tail, len(out_shape)),
        grid=(2 * seqs * groups,),
        in_specs=[
            heads_at,
            at_step((1, length, PAIR), lambda p, s, h: (s, 0, 0)),
            heads_at,
            at_step((1, pairs, 8, length), lambda p, s, h: (s, h, 0, 0)),
            keys_at,
            at_step((1, 1, length, PAIR), lambda p, s, h: (1 - p, s, 0, 0)),
            keys_at,
            rows_at(1),
            rows_at(0),
        ]
        + [whole_spec(w.shape) for w in weights + (vg, vu)]
        + [pl.BlockSpec(memory_space=pl.ANY)] * 3,
        out_specs=[pl.BlockSpec(memory_space=pl.ANY)] * 2
        + [fixed(s.shape) for s in out_shape[2:]],
        out_shape=out_shape,
        scratch_shapes=scratch,
        compiler_params=pltpu.CompilerParams(
            collective_id=1, has_side_effects=True, vmem_limit_bytes=63 * MIB
        ),
        cost_estimate=cost(80 * q.size * length, 2 * q.size * 14, 2 * q.size * length // HEAD),
        name="back_and_sum",
    )(q, qm, g, lse, k, km, v, tokens, rem_tokens, *weights, vg, vu, *sources)


def finish_kernel(residual_ref, own_ref, rem_ref, *refs):
    ins, outs = refs[:7], refs[7:]
    total = residual_ref[...].astype(F32) + own_ref[...].astype(F32) + rem_ref[...].astype(F32)
    outs[0][...] = total.astype(BF16)

    @pl.when(pl.program_id(0) == 0)
    def _():
        for source, target in zip(ins[:6], outs[1:7]):
            target[...] = source[...]
        for i, target in enumerate(outs[7:]):
            target[...] = ins[6][i, : target.shape[0]]


def finish(residual, own, rem, matrices, vectors, shares):
    seqs, length, features = own.shape
    row_spec = pl.BlockSpec((1, length, features), lambda s: (s, 0, 0))

    def fixed(shape):
        return pl.BlockSpec(shape, lambda s: (0,) * len(shape))

    shapes = [m.shape for m in matrices] + [(n,) for n in shares]
    return pl.pallas_call(
        finish_kernel,
        grid=(seqs,),
        in_specs=[row_spec] * 3 + [fixed(m.shape) for m in matrices] + [fixed(vectors.shape)],
        out_specs=[row_spec] + [fixed(s) for s in shapes],
        out_shape=[jax.ShapeDtypeStruct(own.shape, BF16)] + [jax.ShapeDtypeStruct(s, F32) for s in shapes],
        compiler_params=params(60),
        cost_estimate=cost(2 * own.size, 8 * own.size),
        name="finish",
    )(residual, own, rem, *matrices, vectors)


def back_plainly(q, qm, o, g, lse, own, rem, bg, tokens, rem_tokens, weights, dwd, dwu, dwo, vg, vu):
    seqs, length, features = q.shape
    dp, blk = lax.axis_size("dp"), lax.axis_size("blk")
    dq, dko, dvo, dkr, dvr = attend_back(q, qm, o, g, lse, own, rem)
    rem_gradient = tokens_back(rem_back_kernel, (dkr, dvr), weights[1:])
    came = [
        lax.ppermute(part, "blk", [((i + r) % blk, i) for i in range(blk)])
        for r, part in enumerate(jnp.split(rem_gradient, blk - 1, axis=1), 1)
    ]
    flat = [v.reshape(-1, features) for v in (tokens, rem_tokens, dq, dko, dvo, dkr, dvr)]
    dwq, dwk, dwv, dbq, dbv = weights_back(*flat)
    total = tokens_back(own_back_kernel, (bg, dq, dko, dvo), weights).astype(F32)
    for part in came:
        total += part.astype(F32)
    dwu = jnp.moveaxis(dwu[0], 0, 1).reshape(features, -1)
    summed = [scatter_sum(w) for w in (dwd, dwu, dwo, dwq, dwk, dwv)]
    rows = [vg[i] for i in range(6)] + [dbq, dbv, vu]
    rows = [scatter_sum(v.reshape(dp * blk, -1)) for v in rows]
    return [total.astype(BF16)] + summed + [[v[0] for v in rows]]


def body(
    tokens,
    query_weight,
    query_bias,
    key_weight,
    value_weight,
    value_bias,
    out_weight,
    out_bias,
    gain_one,
    shift_one,
    up_weight,
    up_bias,
    down_weight,
    down_bias,
    gain_two,
    shift_two,
    group_ids,
    valid_mask,
    cotangent,
):
    seqs, length, features = tokens.shape
    rows = seqs * length
    blk = lax.axis_size("blk")

    def from_others(value):
        found = [
            lax.ppermute(value, "blk", [(i, (i + r) % blk) for i in range(blk)])
            for r in range(1, blk)
        ]
        return found[0] if len(found) == 1 else jnp.concatenate(found, axis=1)

    codes = jnp.where(valid_mask == 1, group_ids, -1)
    dp = lax.axis_size("dp")
    by_kernel = blk == 2 and dp & (dp - 1) == 0 and dp > 1 and (features // dp) % 16 == 0
    projections = (query_weight, key_weight, value_weight)
    vectors = (
        query_bias,
        value_bias,
        out_bias,
        gain_one,
        shift_one,
        down_bias,
        gain_two,
        shift_two,
    )

    if by_kernel:
        (block_out, branch_gradient, attended_gradient, attended, lse, query_mask, key_masks,
         first_t, feed_t, vector_gradients, up_bias_gradient, queries, keys, values,
         rem_tokens, active, inner_gradient) = front(
            tokens,
            group_ids,
            valid_mask,
            cotangent,
            vectors,
            up_bias,
            projections + (out_weight, up_weight, down_weight),
        )
        dwu, dwd, dwo = feed_weights(
            first_t,
            inner_gradient.reshape(rows, -1),
            feed_t,
            active.reshape(rows, -1),
            attended.reshape(rows, features),
            branch_gradient.reshape(rows, features),
        )
        own_gradient, rem_gradient, *matrices, vectors = back_and_sum(
            queries,
            query_mask,
            attended_gradient,
            lse,
            keys,
            key_masks,
            values,
            tokens,
            rem_tokens,
            projections,
            dwd,
            dwu,
            dwo,
            vector_gradients,
            up_bias_gradient,
        )
        shares = [features // (dp * blk)] * 8 + [up_bias.size // (dp * blk)]
        found = finish(branch_gradient, own_gradient, rem_gradient, matrices, vectors, shares)
        tokens_gradient, dwd, dwu, dwo, dwq, dwk, dwv, *rows_left = found
    else:
        rem_tokens = from_others(tokens)
        rem_codes = from_others(codes.astype(BF16)).astype(jnp.int32)
        slot = jnp.arange(PAIR, dtype=jnp.int32) % HEAD

        def key_mask(code):
            return jnp.where(code[:, :, None] == slot, 0.0, MASKED).astype(BF16)

        query_mask = (group_ids[:, :, None] == slot).astype(BF16)
        vectors = jnp.stack(vectors).astype(F32)
        queries, own_keys, own_values = project(tokens, vectors, projections)
        rem_keys, rem_values = project(rem_tokens, vectors, projections[1:])
        own = (own_keys, key_mask(codes), own_values)
        rem = (rem_keys, key_mask(rem_codes), rem_values)
        attended, lse = attend(queries, query_mask, own, rem)
        (block_out, branch_gradient, attended_gradient, vector_gradients, up_bias_gradient,
         dwu, dwd, dwo) = feed_both_ways(
            tokens.reshape(rows, features),
            attended.reshape(rows, features),
            cotangent.reshape(rows, features),
            vectors[2:],
            up_bias.astype(F32)[None],
            out_weight,
            up_weight,
            down_weight,
            1,
        )
        tokens_gradient, dwd, dwu, dwo, dwq, dwk, dwv, rows_left = back_plainly(
            queries,
            query_mask,
            attended,
            attended_gradient.reshape(tokens.shape),
            lse,
            own,
            rem,
            branch_gradient.reshape(tokens.shape),
            tokens,
            rem_tokens,
            projections,
            dwd,
            dwu,
            dwo,
            vector_gradients,
            up_bias_gradient,
        )
    dbo, dg1, ds1, dbd, dg2, ds2, dbq, dbv, dbu = rows_left
    return (
        block_out.reshape(tokens.shape),
        tokens_gradient,
        dwq,
        dbq,
        dwk,
        dwv,
        dbv,
        dwo,
        dbo,
        dg1,
        ds1,
        dwu,
        dbu,
        dwd,
        dbd,
        dg2,
        ds2,
    )


def solution(mesh):
    rows, shared, pair = P("dp", "blk", None), P(), P("dp", "blk")
    matrix, vector = P(("dp", "blk"), None), P(("dp", "blk"))
    return jax.shard_map(
        body,
        mesh=mesh,
        in_specs=(rows,) + (shared,) * 15 + (pair, pair, rows),
        out_specs=(
            rows,
            rows,
            matrix,
            vector,
            matrix,
            matrix,
            vector,
            matrix,
            vector,
            vector,
            vector,
            matrix,
            vector,
            matrix,
            vector,
            vector,
            vector,
        ),
        check_vma=False,
    )
```
